32 devices in a mesh: dp: 16 (over z, x, core), seq: 2 (over y).
Axes of the slice: x: 2, y: 2, z: 4, core: 2. Of those that a mesh axis runs over, the one named last changes fastest.
Arguments:
- tokens: bfloat16 [16, 512, 768], P('dp', 'seq'), may hold values from -6 to 6
- segment_ids: int32 [16, 512], P('dp', 'seq'), may hold values from 0 to 3, as said below
- padding: int32 [16, 512], P('dp', 'seq'), may hold values from 0 to 1, as said below
- query_weight: bfloat16 [3, 768, 768], P(None, 'dp'), may hold values from -0.21875 to 0.21875
- key_weight: bfloat16 [3, 768, 768], P(None, 'dp'), may hold values from -0.21875 to 0.21875
- value_weight: bfloat16 [3, 768, 768], P(None, 'dp'), may hold values from -0.21875 to 0.21875
- output_weight: bfloat16 [3, 768, 768], P(None, 'dp'), may hold values from -0.625 to 0.625
- query_bias: bfloat16 [3, 768], P(None, 'dp'), may hold values from -3 to 3
- value_bias: bfloat16 [3, 768], P(None, 'dp'), may hold values from -3 to 3
- output_bias: bfloat16 [3, 768], P(None, 'dp'), may hold values from -3 to 3
- attn_gain: bfloat16 [3, 768], P(None, 'dp'), may hold values from 0.5 to 1.5
- attn_shift: bfloat16 [3, 768], P(None, 'dp'), may hold values from -3 to 3
- inner_weight: bfloat16 [3, 768, 3072], P(None, 'dp'), may hold values from -0.21875 to 0.21875
- inner_bias: bfloat16 [3, 3072], P(None, 'dp'), may hold values from -3 to 3
- outer_weight: bfloat16 [3, 3072, 768], P(None, 'dp'), may hold values from -0.109375 to 0.109375
- outer_bias: bfloat16 [3, 768], P(None, 'dp'), may hold values from -3 to 3
- ffn_gain: bfloat16 [3, 768], P(None, 'dp'), may hold values from 0.5 to 1.5
- ffn_shift: bfloat16 [3, 768], P(None, 'dp'), may hold values from -3 to 3
- upstream: bfloat16 [16, 512, 768], P('dp', 'seq'), may hold values from -6 to 6
Outputs:
- hidden_out: bfloat16 [16, 512, 768], P('dp', 'seq')
- pooled: float32 [16, 4, 768], P('dp')
- tokens_grad: float32 [16, 512, 768], P('dp', 'seq')
- query_weight_grad: float32 [3, 768, 768], P(None, 'dp')
- key_weight_grad: float32 [3, 768, 768], P(None, 'dp')
- value_weight_grad: float32 [3, 768, 768], P(None, 'dp')
- output_weight_grad: float32 [3, 768, 768], P(None, 'dp')
- query_bias_grad: float32 [3, 768], P(None, 'dp')
- value_bias_grad: float32 [3, 768], P(None, 'dp')
- output_bias_grad: float32 [3, 768], P(None, 'dp')
- attn_gain_grad: float32 [3, 768], P(None, 'dp')
- attn_shift_grad: float32 [3, 768], P(None, 'dp')
- inner_weight_grad: float32 [3, 768, 3072], P(None, 'dp')
- inner_bias_grad: float32 [3, 3072], P(None, 'dp')
- outer_weight_grad: float32 [3, 3072, 768], P(None, 'dp')
- outer_bias_grad: float32 [3, 768], P(None, 'dp')
- ffn_gain_grad: float32 [3, 768], P(None, 'dp')
- ffn_shift_grad: float32 [3, 768], P(None, 'dp')
The draws below stay inside these ranges and needn't reach their ends.
Inputs may be any that keep to these rules, and one draw needn't show every extreme that they name: `segment_ids`: within each row the ids start at 0, never fall and rise by one at each new text; every id names at least one real position. `padding`: in each row the zeros form a tail that lies after position 256 and inside the last text.
All inputs are finite; a program needn't handle non-finite values.
Results may differ from the reference program's by a relative error of at most 0.025.
Values may be sent and summed in bfloat16 or wider, within the bound.
No kernel may reach another device: no remote copies, remote signals or barrier semaphores. Data moves between devices by JAX's collectives and lax.ppermute only.
A program may use at most 320 MiB of HBM per device.

```python
import jax
import jax.numpy as jnp
from jax import lax

D = 768
H = 12
HD = 64
FF = 3072
LEN = 512
SEGS = 4
LAYERS = 3
ROWS = 16


def layout(key):
    middle = LEN // 2
    row_keys = jax.random.split(jax.random.fold_in(key, 11), ROWS)
    orders = jax.vmap(lambda row_key: jax.random.permutation(row_key, LEN - 2))(row_keys)
    starts = orders[:, :SEGS - 1].astype(jnp.int32) + 1
    starts = starts + (starts >= middle).astype(jnp.int32)
    positions = jnp.arange(LEN, dtype=jnp.int32)
    flags = jnp.sum((positions[None, :, None] == starts[:, None, :]).astype(jnp.int32), axis=2)
    segment = jnp.cumsum(flags, axis=1).astype(jnp.int32)
    last_start = jnp.max(starts, axis=1)
    lowest = jnp.maximum(last_start + 1, middle + 1)
    cutoff = jax.random.randint(jax.random.fold_in(key, 12), (ROWS,), lowest, LEN + 1)
    valid = (positions[None, :] < cutoff[:, None]).astype(jnp.int32)
    return (segment, valid)


def draw_segment_ids(key, part):
    segment, valid = layout(key)
    return segment


def draw_padding(key, part):
    segment, valid = layout(key)
    return valid


def level_of(rng, shape, pieces, low, largest):
    level = 1.0
    for position, parts in pieces:
        heights = jax.random.uniform(jax.random.fold_in(jax.random.fold_in(rng, 6), position), (parts,), jnp.float32, low / len(pieces), largest / len(pieces))
        level = level * jnp.repeat(jnp.exp(heights), shape[position] // parts).reshape((-1,) + (1,) * (len(shape) - 1 - position))
    return level


def normal_values(rng, dims, scale, limit, cuts=(), held_as=jnp.bfloat16):
    level = level_of(rng, dims, cuts, -0.22, 0.18) if cuts else 1.0
    array = jax.random.normal(rng, dims, jnp.float32) * scale * level
    return jnp.minimum(jnp.maximum(array, -limit), limit).astype(held_as)


def setup_inputs(seed: int = 0) -> dict:
    key_of = jax.random.split(jax.random.key(seed), 20)
    tokens = normal_values(key_of[0], (ROWS, LEN, D), 1.0, 6.0, ((0, 16), (1, 2)))
    segment_ids = draw_segment_ids(jax.random.fold_in(key_of[19], 71), 0)
    padding = draw_padding(jax.random.fold_in(key_of[19], 71), 0)
    query_weight = normal_values(key_of[3], (LAYERS, D, D), D ** -0.5, 0.21875, ((1, 16),))
    key_weight = normal_values(key_of[4], (LAYERS, D, D), D ** -0.5, 0.21875, ((1, 16),))
    value_weight = normal_values(key_of[5], (LAYERS, D, D), D ** -0.5, 0.21875, ((1, 16),))
    output_weight = normal_values(key_of[6], (LAYERS, D, D), (D // 8) ** -0.5, 0.625, ((1, 16),))
    query_bias = normal_values(key_of[7], (LAYERS, D), 0.3, 3.0, ((1, 16),))
    value_bias = normal_values(key_of[8], (LAYERS, D), 0.3, 3.0, ((1, 16),))
    output_bias = normal_values(key_of[9], (LAYERS, D), 0.3, 3.0, ((1, 16),))
    attn_gain = jnp.clip(1.0 + 0.1 * jax.random.normal(key_of[10], (LAYERS, D), jnp.float32), 0.5, 1.5).astype(jnp.bfloat16)
    attn_shift = normal_values(key_of[11], (LAYERS, D), 0.3, 3.0, ((1, 16),))
    inner_weight = normal_values(key_of[12], (LAYERS, D, FF), D ** -0.5, 0.21875, ((1, 16),))
    inner_bias = normal_values(key_of[13], (LAYERS, FF), 0.3, 3.0, ((1, 16),))
    outer_weight = normal_values(key_of[14], (LAYERS, FF, D), FF ** -0.5, 0.109375, ((1, 16),))
    outer_bias = normal_values(key_of[15], (LAYERS, D), 0.3, 3.0, ((1, 16),))
    ffn_gain = jnp.clip(1.0 + 0.1 * jax.random.normal(key_of[16], (LAYERS, D), jnp.float32), 0.5, 1.5).astype(jnp.bfloat16)
    ffn_shift = normal_values(key_of[17], (LAYERS, D), 0.3, 3.0, ((1, 16),))
    upstream = normal_values(key_of[18], (ROWS, LEN, D), 1.0, 6.0, ((0, 16), (1, 2)))
    return dict(tokens=tokens, segment_ids=segment_ids, padding=padding, query_weight=query_weight, key_weight=key_weight, value_weight=value_weight, output_weight=output_weight, query_bias=query_bias, value_bias=value_bias, output_bias=output_bias, attn_gain=attn_gain, attn_shift=attn_shift, inner_weight=inner_weight, inner_bias=inner_bias, outer_weight=outer_weight, outer_bias=outer_bias, ffn_gain=ffn_gain, ffn_shift=ffn_shift, upstream=upstream)


@jax.custom_vjp
def low(v):
    return lax.optimization_barrier(v.astype(jnp.bfloat16)).astype(jnp.float32)

@jax.custom_vjp
def low_back(v):
    return v

def low_keep(v):
    return (low(v), None)

def low_pass(kept, grad):
    return (grad,)

def back_keep(v):
    return (v, None)

def back_low(kept, grad):
    return (low(grad),)
low.defvjp(low_keep, low_pass)
low_back.defvjp(back_keep, back_low)
epsilon = 1e-06
masked_score = -1e+30

def product(left, right):
    return jnp.dot(left, right, precision=lax.Precision.HIGHEST, preferred_element_type=jnp.float32)

def normalize(values, gain, shift):
    center = values - lax.optimization_barrier(jnp.mean(values, axis=-1, keepdims=True))
    inverse = lax.rsqrt(lax.optimization_barrier(jnp.mean(center * center, axis=-1, keepdims=True)) + epsilon)
    return center * inverse * gain + shift

def attend_row(items):
    query_row, key_row, value_row, segment_row, valid_row = items
    heads_q = query_row.reshape(LEN, H, HD)
    heads_k = key_row.reshape(LEN, H, HD)
    heads_v = value_row.reshape(LEN, H, HD)
    scores = jnp.einsum('qhd,khd->hqk', heads_q, heads_k, precision=lax.Precision.HIGHEST) * HD ** (-0.5)
    allowed = (segment_row[:, None] == segment_row[None, :]) & (valid_row[None, :] == 1)
    scores = low_back(jnp.where(allowed[None], scores, masked_score))
    probs = low(jax.nn.softmax(scores, axis=-1))
    mixed = jnp.einsum('hqk,khd->qhd', probs, heads_v, precision=lax.Precision.HIGHEST)
    return mixed.reshape(LEN, H * HD)

def encoder_layer(current, segment, valid, weights):
    tokens_low = low(current)
    queries = low(low_back(product(tokens_low, weights[0]) + weights[4]))
    keys_all = low(low_back(product(tokens_low, weights[1])))
    values_all = low(low_back(product(tokens_low, weights[2]) + weights[5]))
    mixed = lax.map(jax.checkpoint(attend_row), (queries, keys_all, values_all, segment, valid))
    mixed = low(low_back(mixed))
    branch = low_back(product(mixed, weights[3]) + weights[6])
    hidden = normalize(current + branch, weights[7], weights[8])
    inner = low_back(product(low(hidden), weights[9]) + weights[10])
    active = low(jax.nn.gelu(inner, approximate=False))
    outer = low_back(product(active, weights[11]) + weights[12])
    return normalize(hidden + outer, weights[13], weights[14])

def forward(current, segment, valid, params):
    for layer_index in range(LAYERS):
        current = encoder_layer(current, segment, valid, tuple((p[layer_index] for p in params)))
    onehot = ((segment[..., None] == jnp.arange(SEGS, dtype=jnp.int32)) & (valid[..., None] == 1)).astype(jnp.float32)
    sums = jnp.einsum('rls,rld->rsd', onehot, current, precision=lax.Precision.HIGHEST)
    pooled = sums / lax.optimization_barrier(jnp.sum(onehot, axis=1))[..., None]
    return (current, pooled)

def reference(tokens, segment_ids, padding, query_weight, key_weight, value_weight, output_weight, query_bias, value_bias, output_bias, attn_gain, attn_shift, inner_weight, inner_bias, outer_weight, outer_bias, ffn_gain, ffn_shift, upstream):
    params = tuple((p.astype(jnp.float32) for p in (query_weight, key_weight, value_weight, output_weight, query_bias, value_bias, output_bias, attn_gain, attn_shift, inner_weight, inner_bias, outer_weight, outer_bias, ffn_gain, ffn_shift)))
    groups = ROWS // 8
    items = (tokens.astype(jnp.float32).reshape(groups, 8, LEN, D), segment_ids.reshape(groups, 8, LEN), padding.reshape(groups, 8, LEN), upstream.astype(jnp.float32).reshape(groups, 8, LEN, D))

    def step(running, item):
        group_tokens, group_segment, group_valid, group_upstream = item

        def run(current, weights):
            return forward(current, group_segment, group_valid, weights)
        result, back_fn, group_pooled = jax.vjp(run, group_tokens, params, has_aux=True)
        grad_tokens, grad_params = back_fn(group_upstream)
        running = tuple((r + g for r, g in zip(running, grad_params)))
        return (running, (result, group_pooled, grad_tokens))
    zeros = tuple((jnp.zeros_like(p) for p in params))
    totals, (results, pooled_all, grads_all) = lax.scan(step, zeros, items)
    hidden_out = results.reshape(ROWS, LEN, D).astype(jnp.bfloat16)
    pooled = pooled_all.reshape(ROWS, SEGS, D)
    tokens_grad = grads_all.reshape(ROWS, LEN, D)
    return (hidden_out, pooled, tokens_grad, totals[0], totals[1], totals[2], totals[3], totals[4], totals[5], totals[6], totals[7], totals[8], totals[9], totals[10], totals[11], totals[12], totals[13], totals[14])
```

```python
import functools

import jax
import jax.numpy as jnp
from jax import lax
from jax.experimental import pallas as pl
from jax.experimental.pallas import tpu as pltpu
from jax.sharding import PartitionSpec as P

HD = 64
SEGS = 4
BLOCKS = 16
EPS = 1e-06
MASKED = -1e30
AXES = ("dp", "seq")
F32 = jnp.float32
BF16 = jnp.bfloat16
MB = 1024 * 1024

QB, VB, OB, AG, AS, UB, FG, FS, IB = range(9)


def nn(left, right):
    return lax.dot_general(left, right, (((1,), (0,)), ((), ())), preferred_element_type=F32)


def nt(left, right):
    return lax.dot_general(left, right, (((1,), (1,)), ((), ())), preferred_element_type=F32)


def params(vmem):
    return pltpu.CompilerParams(vmem_limit_bytes=vmem * MB)


def cost(flops, us):
    return pl.CostEstimate(flops=flops, bytes_accessed=int(us * 3.0e6), transcendentals=0)


VMEM = pl.BlockSpec(memory_space=pltpu.VMEM)
SMEM = pl.BlockSpec(memory_space=pltpu.SMEM)
ANY = pl.BlockSpec(memory_space=pl.ANY)


def shape(dims, dtype):
    return jax.ShapeDtypeStruct(dims, dtype)


def block_at(pos_ref, shift, dx, dc, depth):
    z, x, c = pos_ref[0], pos_ref[1], pos_ref[2]
    zz = lax.rem(z + shift, depth)
    xx = x + dx - 2 * x * dx
    cc = c + dc - 2 * c * dc
    return (zz * 2 + xx) * 2 + cc


def half_at(pos_ref, dy):
    y = pos_ref[3]
    return y + dy - 2 * y * dy


def each_buffer():
    for dy in range(2):
        for dx in range(2):
            for dc in range(2):
                yield (dy * 2 + dx) * 2 + dc, dy, dx, dc


def fetch_columns(pos_ref, bufs, member, members, full_ref, column, sem):
    depth, rows, width = bufs[0].shape
    half = width // members
    for index, dy, dx, dc in each_buffer():
        for shift in range(depth):
            row = pl.multiple_of(block_at(pos_ref, shift, dx, dc, depth) * rows, 16)
            col = pl.multiple_of(column + half_at(pos_ref, dy) * half, 128)
            pltpu.make_async_copy(
                bufs[index].at[shift, :, pl.ds(member * half, half)],
                full_ref.at[pl.ds(row, rows), pl.ds(col, half)],
                sem,
            ).start()


def fetch_rows(pos_ref, bufs, full_ref, sem):
    depth, rows, width = bufs[0].shape
    for index, dy, dx, dc in each_buffer():
        for shift in range(depth):
            block = block_at(pos_ref, shift, dx, dc, depth) * 2 + half_at(pos_ref, dy)
            row = pl.multiple_of(block * rows, 16)
            pltpu.make_async_copy(
                bufs[index].at[shift], full_ref.at[pl.ds(row, rows), :], sem
            ).start()


def wait_full(full_ref, sem):
    pltpu.make_async_copy(full_ref, full_ref, sem).wait()


def export_rows(pos_ref, depth, wide_ref, out_ref):
    rows = out_ref.shape[3]
    for dc in range(2):
        for dx in range(2):
            for shift in range(depth):
                row = pl.multiple_of(block_at(pos_ref, shift, dx, dc, depth) * rows, 16)
                out_ref[dc, dx, shift] = wide_ref[pl.ds(row, rows), :]


def export_halves(pos_ref, depth, wide_ref, out_ref):
    rows = out_ref.shape[4]
    for dc in range(2):
        for dx in range(2):
            for dy in range(2):
                for shift in range(depth):
                    block = block_at(pos_ref, shift, dx, dc, depth) * 2 + half_at(pos_ref, dy)
                    row = pl.multiple_of(block * rows, 16)
                    out_ref[dc, dx, dy, shift] = wide_ref[pl.ds(row, rows), :]


def mean_of(values):
    return jnp.mean(values, axis=-1, keepdims=True)


def normalize(values):
    center = values - mean_of(values)
    inverse = lax.rsqrt(mean_of(center * center) + EPS)
    return center * inverse, inverse


def norm_back(normed, inverse, scaled):
    return inverse * (scaled - mean_of(scaled) - normed * mean_of(scaled * normed))


def colsum(values):
    return jnp.sum(values, axis=0, keepdims=True)


def row_of(vec_ref, index):
    return vec_ref[pl.ds(index, 1), :]


def attn_kernel(depth, *refs):
    pos_w, pos_g = refs[0], refs[1]
    x_ref, xp_ref, seg_ref, lab_ref, vec_ref = refs[2:7]
    bufs = refs[7:15]
    (h_ref, n1_ref, c1_ref, q_ref, k_ref, kt_ref, v_ref, p_ref, xt_ref, ot_ref, ht_ref) = refs[15:26]
    wq, wk, wv, wo, rows_ref, vt_ref, wide_ref, bias_ref, sems = refs[26:]
    tokens, width = x_ref.shape
    for member, full in enumerate((wq, wk, wv, wo)):
        fetch_columns(pos_w, bufs, member, 4, full, 0, sems.at[member])
    bias_ref[...] = jnp.where(lab_ref[...] == seg_ref[...], 0.0, MASKED)
    low = x_ref[...].astype(BF16)
    rows_ref[:tokens] = low
    rows_ref[tokens:] = xp_ref[...]
    wide_ref[...] = low.T
    export_rows(pos_g, depth, wide_ref, xt_ref)
    wait_full(wq, sems.at[0])
    query = (nn(low, wq[...]) + row_of(vec_ref, QB)).astype(BF16)
    q_ref[...] = (query.astype(F32) * HD ** (-0.5)).astype(BF16)
    wait_full(wk, sems.at[1])
    key = nn(rows_ref[...], wk[...]).astype(BF16)
    k_ref[...] = key
    kt_ref[...] = key.T
    wait_full(wv, sems.at[2])
    value = (nn(rows_ref[...], wv[...]) + row_of(vec_ref, VB)).astype(BF16)
    v_ref[...] = value
    vt_ref[...] = value.T

    def pair(index, carry):
        lane = pl.multiple_of(index * 128, 128)
        keys = k_ref[:, pl.ds(lane, 128)]
        queries = q_ref[:, pl.ds(lane, 128)]
        first = lax.broadcasted_iota(jnp.int32, queries.shape, 1) < HD
        for which in range(2):
            mine = jnp.where(first if which == 0 else ~first, queries, jnp.zeros_like(queries))
            scores = nt(keys, mine) + bias_ref[...]
            expos = jnp.exp(scores - jnp.max(scores, axis=0, keepdims=True))
            probs = (expos * (1.0 / jnp.sum(expos, axis=0, keepdims=True))).astype(BF16)
            p_ref[index * 2 + which] = probs
            row = pl.multiple_of(index * 128 + which * HD, HD)
            wide_ref[pl.ds(row, HD), :] = nn(vt_ref[pl.ds(row, HD), :], probs).astype(BF16)
        return carry

    lax.fori_loop(0, width // 128, pair, 0)
    export_rows(pos_g, depth, wide_ref, ot_ref)
    mixed = wide_ref[...].T
    wait_full(wo, sems.at[3])
    branch = nn(mixed, wo[...]) + row_of(vec_ref, OB)
    normed, inverse = normalize(x_ref[...] + branch)
    hidden = normed * row_of(vec_ref, AG) + row_of(vec_ref, AS)
    h_ref[...] = hidden
    n1_ref[...] = normed
    c1_ref[...] = jnp.broadcast_to(inverse, c1_ref.shape)
    wide_ref[...] = hidden.astype(BF16).T
    export_rows(pos_g, depth, wide_ref, ht_ref)


def attn_forward(depth, pos_w, pos_g, x, xp, seg, lab, vec, bufs):
    tokens, width = x.shape
    heads = width // HD
    export = shape((2, 2, depth, width // BLOCKS, tokens), BF16)
    return pl.pallas_call(
        functools.partial(attn_kernel, depth),
        out_shape=(
            shape((tokens, width), F32),
            shape((tokens, width), F32),
            shape((tokens, 128), F32),
            shape((tokens, width), BF16),
            shape((2 * tokens, width), BF16),
            shape((width, 2 * tokens), BF16),
            shape((2 * tokens, width), BF16),
            shape((heads, 2 * tokens, tokens), BF16),
            export,
            export,
            export,
        ),
        in_specs=[SMEM, SMEM] + [VMEM] * 5 + [ANY] * 8,
        out_specs=[VMEM] * 11,
        scratch_shapes=[pltpu.VMEM((width, width), BF16)] * 4
        + [
            pltpu.VMEM((2 * tokens, width), BF16),
            pltpu.VMEM((width, 2 * tokens), BF16),
            pltpu.VMEM((width, tokens), BF16),
            pltpu.VMEM((2 * tokens, tokens), F32),
            pltpu.SemaphoreType.DMA((4,)),
        ],
        compiler_params=params(40),
        cost_estimate=cost(2_200_000_000, 12),
        name="attn_forward",
    )(pos_w, pos_g, x, xp, seg, lab, vec, *bufs)


def ffn_kernel(depth, tile, *refs):
    pos_w, pos_g, h_ref, vec_ref = refs[:4]
    inner_bufs, outer_bufs = refs[4:12], refs[12:20]
    x_ref, xb_ref, n2_ref, c2_ref, gp_ref, gt_ref = refs[20:26]
    wi, wu, low_ref, acc_ref, wide_ref, sems = refs[26:]
    width, hidden = wi.shape
    fetch_columns(pos_w, inner_bufs, 0, 1, wi, 0, sems.at[0])
    fetch_rows(pos_w, outer_bufs, wu, sems.at[1])
    low_ref[...] = h_ref[...].astype(BF16)
    acc_ref[...] = jnp.zeros_like(acc_ref)
    wait_full(wi, sems.at[0])
    wait_full(wu, sems.at[1])
    per_row = width // tile

    def step(index, carry):
        lane = pl.multiple_of(index * tile, tile)
        bias = vec_ref[pl.ds(IB + lax.div(index, per_row), 1), :]
        part = lax.rem(index, per_row)
        chosen = bias[:, :tile]
        for other in range(1, per_row):
            chosen = jnp.where(part == other, bias[:, other * tile : (other + 1) * tile], chosen)
        pre = nn(low_ref[...], wi[:, pl.ds(lane, tile)]) + chosen
        phi = 0.5 * (1.0 + lax.erf(pre * 0.7071067811865476))
        dens = jnp.exp(-0.5 * pre * pre) * 0.3989422804014327
        gp_ref[:, pl.ds(lane, tile)] = (phi + pre * dens).astype(BF16)
        active = (pre * phi).astype(BF16)
        acc_ref[...] += nn(active, wu[pl.ds(lane, tile), :])
        wide_ref[pl.ds(lane, tile), :] = active.T
        return carry

    lax.fori_loop(0, hidden // tile, step, 0)
    export_halves(pos_g, depth, wide_ref, gt_ref)
    normed, inverse = normalize(h_ref[...] + (acc_ref[...] + row_of(vec_ref, UB)))
    result = normed * row_of(vec_ref, FG) + row_of(vec_ref, FS)
    x_ref[...] = result
    xb_ref[...] = result.astype(BF16)
    n2_ref[...] = normed
    c2_ref[...] = jnp.broadcast_to(inverse, c2_ref.shape)


def ffn_forward(depth, pos_w, pos_g, h, vec, inner_bufs, outer_bufs):
    tokens, width = h.shape
    hidden = outer_bufs[0].shape[1] * 2 * BLOCKS
    return pl.pallas_call(
        functools.partial(ffn_kernel, depth, 384),
        out_shape=(
            shape((tokens, width), F32),
            shape((tokens, width), BF16),
            shape((tokens, width), F32),
            shape((tokens, 128), F32),
            shape((tokens, hidden), BF16),
            shape((2, 2, 2, depth, hidden // BLOCKS // 2, tokens), BF16),
        ),
        in_specs=[SMEM, SMEM, VMEM, VMEM] + [ANY] * 16,
        out_specs=[VMEM] * 6,
        scratch_shapes=[
            pltpu.VMEM((width, hidden), BF16),
            pltpu.VMEM((hidden, width), BF16),
            pltpu.VMEM((tokens, width), BF16),
            pltpu.VMEM((tokens, width), F32),
            pltpu.VMEM((hidden, tokens), BF16),
            pltpu.SemaphoreType.DMA((2,)),
        ],
        compiler_params=params(40),
        cost_estimate=cost(2_400_000_000, 12),
        name="ffn_forward",
    )(pos_w, pos_g, h, vec, *inner_bufs, *outer_bufs)


def chain_kernel(tile, *refs):
    pos_w, dx_ref, n2_ref, c2_ref, gp_ref, n1_ref, c1_ref, vec_ref = refs[:8]
    inner_bufs, outer_bufs, attn_bufs = refs[8:16], refs[16:24], refs[24:32]
    dyl_ref, du_ref, da_ref, dal_ref, do_ref, sums_ref = refs[32:38]
    wi, wu, wo, acc_ref, sems = refs[38:]
    width, hidden = wi.shape
    fetch_rows(pos_w, outer_bufs, wu, sems.at[0])
    fetch_columns(pos_w, inner_bufs, 0, 1, wi, 0, sems.at[1])
    fetch_columns(pos_w, attn_bufs, 3, 4, wo, 0, sems.at[2])
    sums_ref[...] = jnp.zeros_like(sums_ref)
    grad = dx_ref[...].astype(F32)
    normed = n2_ref[...]
    sums_ref[pl.ds(FG, 1), :] = colsum(grad * normed)
    sums_ref[pl.ds(FS, 1), :] = colsum(grad)
    back = norm_back(normed, c2_ref[:, :1], grad * row_of(vec_ref, FG))
    low = back.astype(BF16)
    dyl_ref[...] = low
    sums_ref[pl.ds(UB, 1), :] = colsum(low.astype(F32))
    acc_ref[...] = back
    wait_full(wu, sems.at[0])
    wait_full(wi, sems.at[1])
    per_row = width // tile

    for index in range(hidden // tile):
        lane = index * tile
        part = nt(dyl_ref[...], wu[pl.ds(lane, tile), :])
        part = (part * gp_ref[:, pl.ds(lane, tile)].astype(F32)).astype(BF16)
        du_ref[:, pl.ds(lane, tile)] = part
        acc_ref[...] += nt(part, wi[:, pl.ds(lane, tile)])
        sums_ref[
            pl.ds(IB + index // per_row, 1), pl.ds(index % per_row * tile, tile)
        ] = colsum(part.astype(F32))

    grad = acc_ref[...]
    normed = n1_ref[...]
    sums_ref[pl.ds(AG, 1), :] = colsum(grad * normed)
    sums_ref[pl.ds(AS, 1), :] = colsum(grad)
    back = norm_back(normed, c1_ref[:, :1], grad * row_of(vec_ref, AG))
    da_ref[...] = back
    low = back.astype(BF16)
    dal_ref[...] = low
    sums_ref[pl.ds(OB, 1), :] = colsum(low.astype(F32))
    wait_full(wo, sems.at[2])
    do_ref[...] = nt(low, wo[...]).astype(BF16)


def chain_backward(pos_w, dx, n2, c2, gp, n1, c1, vec, inner_bufs, outer_bufs, attn_bufs):
    tokens, width = n2.shape
    hidden = gp.shape[1]
    return pl.pallas_call(
        functools.partial(chain_kernel, 384),
        out_shape=(
            shape((tokens, width), BF16),
            shape((tokens, hidden), BF16),
            shape((tokens, width), F32),
            shape((tokens, width), BF16),
            shape((tokens, width), BF16),
            shape((16, width), F32),
        ),
        in_specs=[SMEM] + [VMEM] * 7 + [ANY] * 24,
        out_specs=[VMEM] * 6,
        scratch_shapes=[
            pltpu.VMEM((width, hidden), BF16),
            pltpu.VMEM((hidden, width), BF16),
            pltpu.VMEM((width, width), BF16),
            pltpu.VMEM((tokens, width), F32),
            pltpu.SemaphoreType.DMA((3,)),
        ],
        compiler_params=params(40),
        cost_estimate=cost(2_700_000_000, 12),
        name="chain_backward",
    )(pos_w, dx, n2, c2, gp, n1, c1, vec, *inner_bufs, *outer_bufs, *attn_bufs)


def attn_back_kernel(q_ref, kt_ref, v_ref, p_ref, do_ref, dq_ref, dk_ref, dv_ref, sum_ref, wide_ref):
    tokens, width = q_ref.shape

    def pair(index, carry):
        lane = pl.multiple_of(index * 128, 128)
        values = v_ref[:, pl.ds(lane, 128)]
        queries = q_ref[:, pl.ds(lane, 128)]
        grads = do_ref[:, pl.ds(lane, 128)]
        first = lax.broadcasted_iota(jnp.int32, grads.shape, 1) < HD
        keys_back, values_back = [], []
        for which in range(2):
            mine = jnp.where(first if which == 0 else ~first, grads, jnp.zeros_like(grads))
            probs_low = p_ref[index * 2 + which]
            probs = probs_low.astype(F32)
            weighted = probs * nt(values, mine)
            back = weighted - probs * jnp.sum(weighted, axis=0, keepdims=True)
            low = back.astype(BF16)
            keys_back.append(nn(low, queries))
            values_back.append(nn(probs_low, grads))
            row = pl.multiple_of(index * 128 + which * HD, HD)
            wide_ref[pl.ds(row, HD), :] = nn(kt_ref[pl.ds(row, HD), :], low)
        split = lax.broadcasted_iota(jnp.int32, keys_back[0].shape, 1) < HD
        dk_ref[:, pl.ds(lane, 128)] = jnp.where(split, keys_back[0], keys_back[1]).astype(BF16)
        dv_ref[:, pl.ds(lane, 128)] = jnp.where(split, values_back[0], values_back[1]).astype(BF16)
        return carry

    lax.fori_loop(0, width // 128, pair, 0)
    low = (wide_ref[...].T * HD ** (-0.5)).astype(BF16)
    dq_ref[...] = low
    sum_ref[...] = jnp.broadcast_to(colsum(low.astype(F32)), sum_ref.shape)


def attn_backward(q, kt, v, p, do):
    tokens, width = q.shape
    return pl.pallas_call(
        attn_back_kernel,
        out_shape=(
            shape((tokens, width), BF16),
            shape((2 * tokens, width), BF16),
            shape((2 * tokens, width), BF16),
            shape((8, width), F32),
        ),
        in_specs=[VMEM] * 5,
        out_specs=[VMEM] * 4,
        scratch_shapes=[pltpu.VMEM((width, tokens), F32)],
        compiler_params=params(40),
        cost_estimate=cost(2_000_000_000, 10),
        name="attn_backward",
    )(q, kt, v, p, do)


def input_kernel(*refs):
    pos_w, da_ref, dq_ref, dk_ref, dv_ref, rk_ref, rv_ref = refs[:7]
    bufs = refs[7:15]
    dx_ref, tk_ref, tv_ref, sum_ref = refs[15:19]
    wq, wk, wv, sems = refs[19:]
    tokens, width = da_ref.shape
    for member, full in enumerate((wq, wk, wv)):
        fetch_columns(pos_w, bufs, member, 4, full, 0, sems.at[member])
    for total, own, other in ((tk_ref, dk_ref, rk_ref), (tv_ref, dv_ref, rv_ref)):
        total[:tokens] = (own[:tokens].astype(F32) + other[tokens:].astype(F32)).astype(BF16)
        total[tokens:] = (own[tokens:].astype(F32) + other[:tokens].astype(F32)).astype(BF16)
    sum_ref[...] = jnp.broadcast_to(colsum(tv_ref[:tokens].astype(F32)), sum_ref.shape)
    wait_full(wq, sems.at[0])
    dx = da_ref[...] + nt(dq_ref[...], wq[...])
    wait_full(wk, sems.at[1])
    dx += nt(tk_ref[:tokens], wk[...])
    wait_full(wv, sems.at[2])
    dx += nt(tv_ref[:tokens], wv[...])
    dx_ref[...] = dx


def input_backward(pos_w, da, dq, dk, dv, rk, rv, bufs):
    tokens, width = da.shape
    return pl.pallas_call(
        input_kernel,
        out_shape=(
            shape((tokens, width), F32),
            shape((2 * tokens, width), BF16),
            shape((2 * tokens, width), BF16),
            shape((8, width), F32),
        ),
        in_specs=[SMEM] + [VMEM] * 6 + [ANY] * 8,
        out_specs=[VMEM] * 4,
        scratch_shapes=[pltpu.VMEM((width, width), BF16)] * 3 + [pltpu.SemaphoreType.DMA((3,))],
        compiler_params=params(40),
        cost_estimate=cost(1_000_000_000, 6),
        name="input_backward",
    )(pos_w, da, dq, dk, dv, rk, rv, *bufs)


def inner_grad_kernel(tile, pos_ref, ta_ref, tb_ref, da_ref, db_ref, *outs):
    depth, rows, half = outs[0].shape
    tokens = ta_ref.shape[-1]
    left_a = ta_ref[0].reshape(2 * depth * rows, tokens)
    left_b = tb_ref[...].reshape(2 * depth * rows, tokens)
    for dy in range(2):
        start = half_at(pos_ref, dy) * half
        for index in range(half // tile):
            lane = pl.multiple_of(start + index * tile, 128)
            part = nn(left_a, da_ref[:, pl.ds(lane, tile)]) + nn(left_b, db_ref[:, pl.ds(lane, tile)])
            part = part.astype(BF16).reshape(2, depth, rows, tile)
            for dx in range(2):
                outs[dx * 2 + dy][:, :, pl.ds(index * tile, tile)] = part[dx]


def inner_grad(pos_g, ta, tb, da, db):
    _, _, depth, rows, tokens = ta.shape
    half = da.shape[1] // 2
    return pl.pallas_call(
        functools.partial(inner_grad_kernel, 384),
        out_shape=(shape((depth, rows, half), BF16),) * 4,
        in_specs=[SMEM] + [VMEM] * 4,
        out_specs=[VMEM] * 4,
        compiler_params=params(32),
        cost_estimate=cost(1_200_000_000, 4),
        name="inner_grad",
    )(pos_g, ta, tb, da, db)


def outer_grad_kernel(ta_ref, tb_ref, da_ref, db_ref, *outs):
    depth, rows, width = outs[0].shape
    tokens = ta_ref.shape[-1]
    for dx in range(2):
        for dy in range(2):
            left_a = ta_ref[0, dx, dy].reshape(depth * rows, tokens)
            left_b = tb_ref[dx, dy].reshape(depth * rows, tokens)
            part = nn(left_a, da_ref[...]) + nn(left_b, db_ref[...])
            outs[dx * 2 + dy][...] = part.astype(BF16).reshape(depth, rows, width)


def outer_grad(ta, tb, da, db):
    _, _, _, depth, rows, tokens = ta.shape
    width = da.shape[1]
    return pl.pallas_call(
        outer_grad_kernel,
        out_shape=(shape((depth, rows, width), BF16),) * 4,
        in_specs=[VMEM] * 4,
        out_specs=[VMEM] * 4,
        compiler_params=params(32),
        cost_estimate=cost(1_200_000_000, 4),
        name="outer_grad",
    )(ta, tb, da, db)


def attn_grad_kernel(pos_ref, xa_ref, xb_ref, oa_ref, ob_ref, qa_ref, qb_ref, k_ref, v_ref, da_ref, db_ref, *outs):
    depth, rows, wide = outs[0].shape
    half = wide // 4
    tokens = xa_ref.shape[-1]
    height = 2 * depth * rows
    x_a = xa_ref[0].reshape(height, tokens)
    x_b = xb_ref[...].reshape(height, tokens)
    o_a = oa_ref[0].reshape(height, tokens)
    o_b = ob_ref[...].reshape(height, tokens)
    for dy in range(2):
        lanes = pl.ds(pl.multiple_of(half_at(pos_ref, dy) * half, 128), half)
        parts = (
            nn(x_a, qa_ref[:, lanes]) + nn(x_b, qb_ref[:, lanes]),
            nn(x_a, k_ref[:tokens, lanes]) + nn(x_b, k_ref[tokens:, lanes]),
            nn(x_a, v_ref[:tokens, lanes]) + nn(x_b, v_ref[tokens:, lanes]),
            nn(o_a, da_ref[:, lanes]) + nn(o_b, db_ref[:, lanes]),
        )
        for member, part in enumerate(parts):
            part = part.astype(BF16).reshape(2, depth, rows, half)
            for dx in range(2):
                outs[dx * 2 + dy][:, :, member * half : (member + 1) * half] = part[dx]


def attn_grad(pos_g, xa, xb, oa, ob, qa, qb, tk, tv, da, db):
    _, _, depth, rows, tokens = xa.shape
    width = da.shape[1]
    return pl.pallas_call(
        attn_grad_kernel,
        out_shape=(shape((depth, rows, 2 * width), BF16),) * 4,
        in_specs=[SMEM] + [VMEM] * 10,
        out_specs=[VMEM] * 4,
        compiler_params=params(32),
        cost_estimate=cost(1_200_000_000, 4),
        name="attn_grad",
    )(pos_g, xa, xb, oa, ob, qa, qb, tk, tv, da, db)


def build(mesh):
    count = mesh.shape["dp"]
    depth = count // 4

    def flat(dp, seq):
        return dp * 2 + seq

    def pairs(source_of):
        out = []
        for dp in range(count):
            for seq in range(2):
                out.append((flat(*source_of(dp, seq)), flat(dp, seq)))
        return out

    swap_pairs = pairs(lambda dp, seq: (dp // 2 * 2 + seq, dp % 2))
    core_pairs = pairs(lambda dp, seq: (dp ^ 1, seq))
    x_pairs = pairs(lambda dp, seq: (dp ^ 2, seq))
    y_pairs = pairs(lambda dp, seq: (dp, 1 - seq))
    z_from = [pairs(lambda dp, seq, k=k: ((dp + 4 * k) % count, seq)) for k in range(depth)]
    z_to = [pairs(lambda dp, seq, k=k: ((dp - 4 * k) % count, seq)) for k in range(depth)]

    def move(value, perm):
        return lax.ppermute(value, AXES, perm)

    def move_all(values, perm):
        return [move(value, perm) for value in values]

    def gather_chunk(piece, x_first):
        zs = [piece] + [move(piece, z_from[k]) for k in range(1, depth)]
        base = jnp.stack(zs)
        near = move(base, x_pairs if x_first else y_pairs)
        far = move_all((base, near), y_pairs if x_first else x_pairs)
        if x_first:
            table = ((base, near), (far[0], far[1]))
        else:
            table = ((base, far[0]), (near, far[1]))
        bufs = []
        for dy in range(2):
            for dx in range(2):
                bufs.append(table[dy][dx])
                bufs.append(move(table[dy][dx], core_pairs))
        return bufs

    def add(left, right):
        return (left.astype(F32) + right.astype(F32)).astype(BF16)

    def reduce_chunk(outs, x_first):
        if x_first:
            got = move_all((outs[2], outs[3]), x_pairs)
            sums = [add(outs[0], got[0]), add(outs[1], got[1])]
            rest = add(sums[0], move(sums[1], y_pairs))
        else:
            got = move_all((outs[1], outs[3]), y_pairs)
            sums = [add(outs[0], got[0]), add(outs[2], got[1])]
            rest = add(sums[0], move(sums[1], x_pairs))
        total = rest[0].astype(F32)
        for k in range(1, depth):
            total = total + move(rest[k], z_to[k]).astype(F32)
        low = total.astype(BF16)
        return total, move(low, y_pairs).astype(F32)

    def reduce_small(value):
        for perm in (core_pairs, y_pairs, x_pairs):
            value = value + move(value, perm)
        return value + sum(move(value, z_from[k]) for k in range(1, depth))

    def spread_small(value):
        value = value + sum(move(value, z_from[k]) for k in range(1, depth))
        for perm in (x_pairs, core_pairs):
            value = value + move(value, perm)
        return value

    return dict(
        count=count,
        depth=depth,
        swap=swap_pairs,
        core=core_pairs,
        move=move,
        gather=gather_chunk,
        reduce=reduce_chunk,
        reduce_small=reduce_small,
        spread_small=spread_small,
    )


def body(
    net,
    tokens,
    segment_ids,
    padding,
    query_weight,
    key_weight,
    value_weight,
    output_weight,
    query_bias,
    value_bias,
    output_bias,
    attn_gain,
    attn_shift,
    inner_weight,
    inner_bias,
    outer_weight,
    outer_bias,
    ffn_gain,
    ffn_shift,
    upstream,
):
    layers, small, width = query_weight.shape
    hidden = inner_weight.shape[2]
    count = net["count"]
    move = net["move"]
    staged = count == BLOCKS and small % 16 == 0
    dp = lax.axis_index("dp").astype(jnp.int32)
    y = lax.axis_index("seq").astype(jnp.int32)
    core = lax.rem(dp, 2)
    if staged:
        depth = net["depth"]
        pos_g = jnp.stack([lax.div(dp, 4), lax.rem(lax.div(dp, 2), 2), core, y])
        pos_w = pos_g
    else:
        depth = BLOCKS // 4
        zero = jnp.zeros((), jnp.int32)
        pos_g = jnp.stack([zero, zero, core, zero])
        pos_w = jnp.stack([zero, zero, zero, zero])

    def half(value, axis):
        size = value.shape[axis] // 2
        return lax.dynamic_slice_in_dim(value, y * size, size, axis)

    labels = jnp.where(padding == 1, segment_ids, -1)
    small_own = move(jnp.concatenate([segment_ids, labels]), net["swap"])
    small_other = move(small_own, net["core"])
    seg = small_own[0:1]
    lab = jnp.concatenate([small_own[1], small_other[1]])[:, None]
    token_low = move(tokens[0], net["swap"])
    token_other = move(token_low, net["core"])
    grad_in = move(upstream[0], net["swap"])

    onehot = (jnp.arange(count, dtype=jnp.int32) == dp).astype(BF16)
    eight = jnp.stack(
        [query_bias, value_bias, output_bias, attn_gain, attn_shift, outer_bias, ffn_gain, ffn_shift],
        axis=1,
    )
    eight = (eight[:, :, None, :] * onehot[None, None, :, None]).reshape(layers, 8, width)
    wide = (inner_bias[:, None, :] * onehot[None, :, None]).reshape(layers, hidden // width, width)
    table = jnp.concatenate([eight, wide], axis=1)
    table = net["spread_small"](table) if staged else lax.psum(table, "dp")
    table = table.astype(F32)

    chunks = []
    for layer in range(layers):
        four = (query_weight[layer], key_weight[layer], value_weight[layer], output_weight[layer])
        if staged:
            pieces = (
                jnp.concatenate([half(value, 1) for value in four], axis=1),
                half(inner_weight[layer], 1),
                half(outer_weight[layer], 0),
            )
            chunks.append(
                [net["gather"](piece, (layer * 3 + index) % 2 == 1) for index, piece in enumerate(pieces)]
            )
        else:
            full = [lax.all_gather(value, "dp", axis=0, tiled=True) for value in four]
            inner = lax.all_gather(inner_weight[layer], "dp", axis=0, tiled=True)
            outer = lax.all_gather(outer_weight[layer], "dp", axis=0, tiled=True)
            rows = width // BLOCKS

            def cut(value, dy, dx, dc):
                value = value.reshape(depth, 2, 2, rows, 2, -1)
                return value[:, dx, dc, :, dy, :]

            lists = [[], [], []]
            for index, dy, dx, dc in each_buffer():
                lists[0].append(jnp.concatenate([cut(value, dy, dx, dc) for value in full], axis=2))
                lists[1].append(cut(inner, dy, dx, dc))
                lists[2].append(
                    outer.reshape(depth, 2, 2, 2, hidden // BLOCKS // 2, width)[:, dx, dc, dy]
                )
            chunks.append(lists)

    current = token_low.astype(F32)
    other = token_other
    kept = []
    for layer in range(layers):
        attn_bufs, inner_bufs, outer_bufs = chunks[layer]
        vec = table[layer]
        h, n1, c1, q, k, kt, v, p, xt, ot, ht = attn_forward(
            depth, pos_w, pos_g, current, other, seg, lab, vec, attn_bufs
        )
        current, low, n2, c2, gp, gt = ffn_forward(depth, pos_w, pos_g, h, vec, inner_bufs, outer_bufs)
        if layer + 1 < layers:
            other = move(low, net["core"])
        kept.append((n1, c1, q, kt, v, p, n2, c2, gp, xt, ot, ht, gt))
    hidden_out = move(low, net["swap"])[None]

    range_ids = jnp.arange(SEGS, dtype=jnp.int32)
    own = (small_own[1][None, :] == range_ids[:, None]).astype(F32)
    sums = jnp.dot(own, current, precision=lax.Precision.HIGHEST)
    sums = sums + move(sums, net["core"])
    counts = jnp.sum((lab[:, 0][None, :] == range_ids[:, None]).astype(F32), axis=1)
    pooled = move(sums / counts[:, None], net["swap"])[None]

    grad = grad_in
    collected = [None] * layers
    vectors = [None] * layers
    for layer in reversed(range(layers)):
        attn_bufs, inner_bufs, outer_bufs = chunks[layer]
        vec = table[layer]
        n1, c1, q, kt, v, p, n2, c2, gp, xt, ot, ht, gt = kept[layer]
        rxt, rot, rht, rgt = (move(value[1], net["core"]) for value in (xt, ot, ht, gt))
        dyl, du, da, dal, do, sums = chain_backward(
            pos_w, grad, n2, c2, gp, n1, c1, vec, inner_bufs, outer_bufs, attn_bufs
        )
        rdyl, rdu, rdal = (move(value, net["core"]) for value in (dyl, du, dal))
        outer_parts = outer_grad(gt, rgt, dyl, rdyl)
        dq, dk, dv, qsum = attn_backward(q, kt, v, p, do)
        rdq, rdk, rdv = (move(value, net["core"]) for value in (dq, dk, dv))
        inner_parts = inner_grad(pos_g, ht, rht, du, rdu)
        grad, tk, tv, vsum = input_backward(pos_w, da, dq, dk, dv, rdk, rdv, attn_bufs)
        attn_parts = attn_grad(pos_g, xt, rxt, ot, rot, dq, rdq, tk, tv, dal, rdal)
        vectors[layer] = jnp.concatenate([qsum[:1], vsum[:1], sums[2:12]], axis=0)
        parts = (outer_parts, inner_parts, attn_parts)
        if staged:
            results = [
                net["reduce"](part, (layer * 3 + index) % 2 == 1) for index, part in enumerate(parts)
            ]

            def sides(pair, axis):
                own, got = pair
                return jnp.where(
                    y == 0, jnp.concatenate([own, got], axis), jnp.concatenate([got, own], axis)
                )

            outer = sides(results[0], 0)
            inner = sides(results[1], 1)
            size = width // 2
            four = [
                sides(tuple(value[:, member * size : (member + 1) * size] for value in results[2]), 1)
                for member in range(4)
            ]
        else:
            def whole(outs, by_rows, member=None):
                out = jnp.stack(outs).reshape((2, 2) + outs[0].shape)
                if member is not None:
                    size = out.shape[-1] // 4
                    out = out[..., member * size : (member + 1) * size]
                if by_rows:
                    out = out.transpose(2, 0, 1, 3, 4)
                    out = out.reshape(depth * 2, 1, -1, out.shape[-1])
                else:
                    out = out.transpose(2, 0, 3, 1, 4)
                    out = out.reshape(depth * 2, 1, out.shape[2], -1)
                mine = (jnp.arange(2, dtype=jnp.int32) == core)[None, :, None, None]
                out = jnp.where(mine, out, jnp.zeros_like(out)).reshape(-1, out.shape[-1])
                out = lax.psum_scatter(out, "dp", scatter_dimension=0, tiled=True)
                return lax.psum(out.astype(F32), "seq")

            outer = whole(outer_parts, True)
            inner = whole(inner_parts, False)
            four = [whole(attn_parts, False, member) for member in range(4)]
        collected[layer] = four + [inner, outer]
    tokens_grad = move(grad.astype(BF16), net["swap"]).astype(F32)[None]
    table = jnp.stack(vectors)
    table = net["reduce_small"](table) if staged else lax.psum(table, AXES)
    eight = lax.dynamic_slice_in_dim(table[:, :8], dp * small, small, 2)
    wide = lax.dynamic_slice_in_dim(
        table[:, 8:].reshape(layers, hidden), dp * (hidden // count), hidden // count, 1
    )
    stacked = [jnp.stack([collected[layer][member] for layer in range(layers)]) for member in range(6)]
    return (
        hidden_out,
        pooled,
        tokens_grad,
        stacked[0],
        stacked[1],
        stacked[2],
        stacked[3],
        eight[:, QB],
        eight[:, VB],
        eight[:, OB],
        eight[:, AG],
        eight[:, AS],
        stacked[4],
        wide,
        stacked[5],
        eight[:, UB],
        eight[:, FG],
        eight[:, FS],
    )


def solution(mesh):
    cube = P(None, "dp", None)
    flat = P(None, "dp")
    acts = P("dp", "seq", None)
    ids = P("dp", "seq")
    return jax.shard_map(
        functools.partial(body, build(mesh)),
        mesh=mesh,
        in_specs=(acts, ids, ids, cube, cube, cube, cube, flat, flat, flat, flat, flat, cube, flat, cube)
        + (flat, flat, flat, acts),
        out_specs=(acts, P("dp", None, None), acts, cube, cube, cube, cube)
        + (flat, flat, flat, flat, flat, cube, flat, cube, flat, flat, flat),
        check_vma=False,
    )
```

```python
import functools

import jax
import jax.numpy as jnp
from jax import lax
from jax.experimental import pallas as pl
from jax.experimental.pallas import tpu as pltpu
from jax.sharding import PartitionSpec as P

HD = 64
SEGS = 4
BLOCKS = 16
ZS = 4
LAG = 1
VMEM_MB = 24
EPS = 1e-06
MASKED = -1e30
AXES = ("dp", "seq")
F32 = jnp.float32
BF16 = jnp.bfloat16
MB = 1024 * 1024

QB, VB, OB, AG, AS, UB, FG, FS, IB = range(9)


def nn(left, right):
    return lax.dot_general(left, right, (((1,), (0,)), ((), ())), preferred_element_type=F32)


def nt(left, right):
    return lax.dot_general(left, right, (((1,), (1,)), ((), ())), preferred_element_type=F32)


def params(vmem):
    return pltpu.CompilerParams(vmem_limit_bytes=vmem * MB)


def cost():
    return pl.CostEstimate(flops=1, bytes_accessed=1, transcendentals=0)


def load(source, target, sem):
    pltpu.make_async_copy(source, target, sem).start()


VMEM = pl.BlockSpec(memory_space=pltpu.VMEM)
SMEM = pl.BlockSpec(memory_space=pltpu.SMEM)
ANY = pl.BlockSpec(memory_space=pl.ANY)
HBM = pl.BlockSpec(memory_space=pltpu.HBM)


def shape(dims, dtype):
    return jax.ShapeDtypeStruct(dims, dtype)


def flip(value, bit):
    return value + bit - 2 * value * bit


def block_at(pos_ref, k, dx, dc):
    z, x, c = pos_ref[0], pos_ref[1], pos_ref[2]
    low = lax.rem(z, 2)
    zz = flip(lax.div(z, 2), k // 2) * 2 + flip(low, k % 2)
    return (zz * 2 + flip(x, dx)) * 2 + flip(c, dc)


def half_at(pos_ref, dy):
    return flip(pos_ref[3], dy)


UNITS = (
    (0, 0, 0),
    (0, 1, 0),
    (0, 0, 1),
    (0, 1, 1),
    (1, 0, 0),
    (1, 0, 1),
    (1, 1, 0),
    (1, 1, 1),
)


def each_piece(bufs):
    for dc in range(2):
        for unit, (part, dy, dx) in enumerate(UNITS):
            for k in range(ZS):
                yield bufs[dc].at[unit * ZS + k], part, dy, dx, dc, k


def fetch_member(pos_ref, bufs, member, full_ref, sem):
    _, rows, width = bufs[0].shape
    half = width // 2
    for piece, part, dy, dx, dc, k in each_piece(bufs):
        if part != member // 2:
            continue
        row = pl.multiple_of(block_at(pos_ref, k, dx, dc) * rows, 16)
        col = pl.multiple_of(half_at(pos_ref, dy) * half, 128)
        pltpu.make_async_copy(
            piece.at[:, pl.ds(member % 2 * half, half)],
            full_ref.at[pl.ds(row, rows), pl.ds(col, half)],
            sem,
        ).start()


def fetch_columns(pos_ref, bufs, full_ref, sem):
    _, rows, width = bufs[0].shape
    for piece, part, dy, dx, dc, k in each_piece(bufs):
        row = pl.multiple_of(block_at(pos_ref, k, dx, dc) * rows, 16)
        col = pl.multiple_of((half_at(pos_ref, dy) * 2 + part) * width, 128)
        pltpu.make_async_copy(
            piece, full_ref.at[pl.ds(row, rows), pl.ds(col, width)], sem
        ).start()


def fetch_rows(pos_ref, bufs, full_ref, sem):
    _, rows, width = bufs[0].shape
    for piece, part, dy, dx, dc, k in each_piece(bufs):
        block = block_at(pos_ref, k, dx, dc) * 2 + half_at(pos_ref, dy)
        row = pl.multiple_of((block * 2 + part) * rows, 16)
        pltpu.make_async_copy(piece, full_ref.at[pl.ds(row, rows), :], sem).start()


def wait_full(full_ref, sem):
    pltpu.make_async_copy(full_ref, full_ref, sem).wait()


def export_rows(pos_ref, wide_ref, outs, index):
    rows = outs[0].shape[3]
    for dc in range(2):
        for dx in range(2):
            for k in range(ZS):
                row = pl.multiple_of(block_at(pos_ref, k, dx, dc) * rows, 16)
                outs[dc][index, dx, k] = wide_ref[pl.ds(row, rows), :]


def export_halves(pos_ref, wide_ref, outs):
    rows = outs[0].shape[4]
    for dc in range(2):
        for dx in range(2):
            for dy in range(2):
                for k in range(ZS):
                    block = block_at(pos_ref, k, dx, dc) * 2 + half_at(pos_ref, dy)
                    for part in range(2):
                        row = pl.multiple_of((block * 2 + part) * rows, 16)
                        outs[dc][dx, dy, part, k] = wide_ref[pl.ds(row, rows), :]


def mean_of(values):
    return jnp.mean(values, axis=-1, keepdims=True)


def normalize(values):
    center = values - mean_of(values)
    inverse = lax.rsqrt(mean_of(center * center) + EPS)
    return center * inverse, inverse


def norm_back(normed, inverse, scaled):
    return inverse * (scaled - mean_of(scaled) - normed * mean_of(scaled * normed))


def colsum(values):
    return jnp.sum(values, axis=0, keepdims=True)


def row_of(vec_ref, index):
    return vec_ref[pl.ds(index, 1), :]


def attn_kernel(*refs):
    pos_w, pos_g = refs[0], refs[1]
    x_ref, xp_ref, seg_ref, lab_ref, vec_ref = refs[2:7]
    bufs = refs[7:9]
    h_ref = refs[9]
    kept = refs[10:18]
    wq, wk, wv, wo, rows_ref, vt_ref, wide_ref, bias_ref, k_ref = refs[18:27]
    held = refs[27:35]
    n1_ref, c1_ref, q_ref, kt_ref, v_ref, p_ref = held[:6]
    exports = held[6:]
    sems, store_sems = refs[35:]

    def store(index):
        load(held[index], kept[index], store_sems.at[index])

    tokens, width = x_ref.shape
    for member, full in enumerate((wq, wk, wv, wo)):
        fetch_member(pos_w, bufs, member, full, sems.at[member])
    bias_ref[...] = jnp.where(lab_ref[...] == seg_ref[...], 0.0, MASKED)
    low = x_ref[...].astype(BF16)
    rows_ref[:tokens] = low
    rows_ref[tokens:] = xp_ref[...]
    wide_ref[...] = low.T
    export_rows(pos_g, wide_ref, exports, 0)
    wait_full(wq, sems.at[0])
    query = (nn(low, wq[...]) + row_of(vec_ref, QB)).astype(BF16)
    q_ref[...] = (query.astype(F32) * HD ** (-0.5)).astype(BF16)
    wait_full(wk, sems.at[1])
    key = nn(rows_ref[...], wk[...]).astype(BF16)
    k_ref[...] = key
    kt_ref[...] = key.T
    store(2)
    store(3)
    wait_full(wv, sems.at[2])
    value = (nn(rows_ref[...], wv[...]) + row_of(vec_ref, VB)).astype(BF16)
    v_ref[...] = value
    vt_ref[...] = value.T
    store(4)

    def pair(index, carry):
        lane = pl.multiple_of(index * 128, 128)
        keys = k_ref[:, pl.ds(lane, 128)]
        queries = q_ref[:, pl.ds(lane, 128)]
        first = lax.broadcasted_iota(jnp.int32, queries.shape, 1) < HD
        for which in range(2):
            mine = jnp.where(first if which == 0 else ~first, queries, jnp.zeros_like(queries))
            scores = nt(keys, mine) + bias_ref[...]
            expos = jnp.exp(scores - jnp.max(scores, axis=0, keepdims=True))
            probs = (expos * (1.0 / jnp.sum(expos, axis=0, keepdims=True))).astype(BF16)
            p_ref[index * 2 + which] = probs
            row = pl.multiple_of(index * 128 + which * HD, HD)
            wide_ref[pl.ds(row, HD), :] = nn(vt_ref[pl.ds(row, HD), :], probs).astype(BF16)
        both = pl.ds(index * 2, 2)
        load(p_ref.at[both], kept[5].at[both], store_sems.at[5])
        return carry

    lax.fori_loop(0, width // 128, pair, 0)
    export_rows(pos_g, wide_ref, exports, 1)
    mixed = wide_ref[...].T
    wait_full(wo, sems.at[3])
    branch = nn(mixed, wo[...]) + row_of(vec_ref, OB)
    normed, inverse = normalize(x_ref[...] + branch)
    hidden = normed * row_of(vec_ref, AG) + row_of(vec_ref, AS)
    h_ref[...] = hidden
    n1_ref[...] = normed
    c1_ref[...] = jnp.broadcast_to(inverse, c1_ref.shape)
    wide_ref[...] = hidden.astype(BF16).T
    export_rows(pos_g, wide_ref, exports, 2)
    for index in (0, 1, 6, 7):
        store(index)
    for index in range(8):
        wait_full(held[index], store_sems.at[index])


def attn_forward(pos_w, pos_g, x, xp, seg, lab, vec, bufs):
    tokens, width = x.shape
    heads = width // HD
    export = shape((3, 2, ZS, width // BLOCKS, tokens), BF16)
    kept = (
        shape((tokens, width), F32),
        shape((tokens, 128), F32),
        shape((tokens, width), BF16),
        shape((width, 2 * tokens), BF16),
        shape((2 * tokens, width), BF16),
        shape((heads, 2 * tokens, tokens), BF16),
        export,
        export,
    )
    return pl.pallas_call(
        attn_kernel,
        out_shape=(shape((tokens, width), F32),) + kept,
        in_specs=[SMEM, SMEM] + [VMEM] * 5 + [ANY] * 2,
        out_specs=[VMEM] + [HBM] * 8,
        scratch_shapes=[pltpu.VMEM((width, width), BF16)] * 4
        + [
            pltpu.VMEM((2 * tokens, width), BF16),
            pltpu.VMEM((width, 2 * tokens), BF16),
            pltpu.VMEM((width, tokens), BF16),
            pltpu.VMEM((2 * tokens, tokens), F32),
            pltpu.VMEM((2 * tokens, width), BF16),
        ]
        + [pltpu.VMEM(each.shape, each.dtype) for each in kept]
        + [pltpu.SemaphoreType.DMA((4,)), pltpu.SemaphoreType.DMA((8,))],
        compiler_params=params(VMEM_MB),
        cost_estimate=cost(),
        name="attn_forward",
    )(pos_w, pos_g, x, xp, seg, lab, vec, *bufs)


def ffn_kernel(tile, *refs):
    pos_w, pos_g, h_ref, vec_ref = refs[:4]
    inner_bufs, outer_bufs = refs[4:6], refs[6:8]
    x_ref, xb_ref = refs[8:10]
    kept = refs[10:15]
    wi, wu, low_ref, acc_ref, wide_ref = refs[15:20]
    held = refs[20:25]
    n2_ref, c2_ref, gp_ref = held[:3]
    exports = held[3:]
    sems, store_sems = refs[25:]

    def store(index):
        load(held[index], kept[index], store_sems.at[index])

    width, hidden = wi.shape
    fetch_columns(pos_w, inner_bufs, wi, sems.at[0])
    fetch_rows(pos_w, outer_bufs, wu, sems.at[1])
    low_ref[...] = h_ref[...].astype(BF16)
    acc_ref[...] = jnp.zeros_like(acc_ref)
    wait_full(wi, sems.at[0])
    wait_full(wu, sems.at[1])
    per_row = width // tile

    def step(index, carry):
        lane = pl.multiple_of(index * tile, tile)
        bias = vec_ref[pl.ds(IB + lax.div(index, per_row), 1), :]
        part = lax.rem(index, per_row)
        chosen = bias[:, :tile]
        for other in range(1, per_row):
            chosen = jnp.where(part == other, bias[:, other * tile : (other + 1) * tile], chosen)
        pre = nn(low_ref[...], wi[:, pl.ds(lane, tile)]) + chosen
        phi = 0.5 * (1.0 + lax.erf(pre * 0.7071067811865476))
        dens = jnp.exp(-0.5 * pre * pre) * 0.3989422804014327
        gp_ref[:, pl.ds(lane, tile)] = (phi + pre * dens).astype(BF16)
        active = (pre * phi).astype(BF16)
        acc_ref[...] += nn(active, wu[pl.ds(lane, tile), :])
        wide_ref[pl.ds(lane, tile), :] = active.T
        return carry

    lax.fori_loop(0, hidden // tile, step, 0)
    store(2)
    export_halves(pos_g, wide_ref, exports)
    store(3)
    store(4)
    normed, inverse = normalize(h_ref[...] + (acc_ref[...] + row_of(vec_ref, UB)))
    result = normed * row_of(vec_ref, FG) + row_of(vec_ref, FS)
    x_ref[...] = result
    xb_ref[...] = result.astype(BF16)
    n2_ref[...] = normed
    c2_ref[...] = jnp.broadcast_to(inverse, c2_ref.shape)
    store(0)
    store(1)
    for index in range(5):
        wait_full(held[index], store_sems.at[index])


def ffn_forward(pos_w, pos_g, h, vec, inner_bufs, outer_bufs):
    tokens, width = h.shape
    hidden = outer_bufs[0].shape[1] * 4 * BLOCKS
    export = shape((2, 2, 2, ZS, hidden // BLOCKS // 4, tokens), BF16)
    kept = (
        shape((tokens, width), F32),
        shape((tokens, 128), F32),
        shape((tokens, hidden), BF16),
        export,
        export,
    )
    return pl.pallas_call(
        functools.partial(ffn_kernel, 384),
        out_shape=(shape((tokens, width), F32), shape((tokens, width), BF16)) + kept,
        in_specs=[SMEM, SMEM, VMEM, VMEM] + [ANY] * 4,
        out_specs=[VMEM] * 2 + [HBM] * 5,
        scratch_shapes=[
            pltpu.VMEM((width, hidden), BF16),
            pltpu.VMEM((hidden, width), BF16),
            pltpu.VMEM((tokens, width), BF16),
            pltpu.VMEM((tokens, width), F32),
            pltpu.VMEM((hidden, tokens), BF16),
        ]
        + [pltpu.VMEM(each.shape, each.dtype) for each in kept]
        + [pltpu.SemaphoreType.DMA((2,)), pltpu.SemaphoreType.DMA((5,))],
        compiler_params=params(VMEM_MB),
        cost_estimate=cost(),
        name="ffn_forward",
    )(pos_w, pos_g, h, vec, *inner_bufs, *outer_bufs)


def chain_kernel(tile, *refs):
    pos_w, dx_ref = refs[:2]
    sources, vec_ref = refs[2:7], refs[7]
    inner_bufs, outer_bufs, attn_bufs = refs[8:10], refs[10:12], refs[12:14]
    pack_ref, da_ref, do_ref, sums_ref = refs[14:18]
    wi, wu, wo, acc_ref = refs[18:22]
    held = refs[22:27]
    n2_ref, c2_ref, gp_ref, n1_ref, c1_ref = held
    sems, load_sems = refs[27:]
    width, hidden = wi.shape
    for index in range(5):
        load(sources[index], held[index], load_sems.at[index])
    dyl_ref = pack_ref.at[:, pl.ds(0, width)]
    du_ref = pack_ref.at[:, pl.ds(width, hidden)]
    dal_ref = pack_ref.at[:, pl.ds(width + hidden, width)]
    fetch_rows(pos_w, outer_bufs, wu, sems.at[0])
    fetch_columns(pos_w, inner_bufs, wi, sems.at[1])
    fetch_member(pos_w, attn_bufs, 3, wo, sems.at[2])
    sums_ref[...] = jnp.zeros_like(sums_ref)
    grad = dx_ref[...].astype(F32)
    wait_full(n2_ref, load_sems.at[0])
    wait_full(c2_ref, load_sems.at[1])
    normed = n2_ref[...]
    sums_ref[pl.ds(FG, 1), :] = colsum(grad * normed)
    sums_ref[pl.ds(FS, 1), :] = colsum(grad)
    back = norm_back(normed, c2_ref[:, :1], grad * row_of(vec_ref, FG))
    low = back.astype(BF16)
    dyl_ref[...] = low
    sums_ref[pl.ds(UB, 1), :] = colsum(low.astype(F32))
    acc_ref[...] = back
    wait_full(gp_ref, load_sems.at[2])
    wait_full(wu, sems.at[0])
    wait_full(wi, sems.at[1])
    per_row = width // tile

    for index in range(hidden // tile):
        lane = index * tile
        part = nt(dyl_ref[...], wu[pl.ds(lane, tile), :])
        part = (part * gp_ref[:, pl.ds(lane, tile)].astype(F32)).astype(BF16)
        du_ref[:, pl.ds(lane, tile)] = part
        acc_ref[...] += nt(part, wi[:, pl.ds(lane, tile)])
        sums_ref[
            pl.ds(IB + index // per_row, 1), pl.ds(index % per_row * tile, tile)
        ] = colsum(part.astype(F32))

    grad = acc_ref[...]
    wait_full(n1_ref, load_sems.at[3])
    wait_full(c1_ref, load_sems.at[4])
    normed = n1_ref[...]
    sums_ref[pl.ds(AG, 1), :] = colsum(grad * normed)
    sums_ref[pl.ds(AS, 1), :] = colsum(grad)
    back = norm_back(normed, c1_ref[:, :1], grad * row_of(vec_ref, AG))
    da_ref[...] = back
    low = back.astype(BF16)
    dal_ref[...] = low
    sums_ref[pl.ds(OB, 1), :] = colsum(low.astype(F32))
    wait_full(wo, sems.at[2])
    do_ref[...] = nt(low, wo[...]).astype(BF16)


def chain_backward(pos_w, dx, n2, c2, gp, n1, c1, vec, inner_bufs, outer_bufs, attn_bufs):
    tokens, width = n2.shape
    hidden = gp.shape[1]
    return pl.pallas_call(
        functools.partial(chain_kernel, 384),
        out_shape=(
            shape((tokens, 2 * width + hidden), BF16),
            shape((tokens, width), F32),
            shape((tokens, width), BF16),
            shape((16, width), F32),
        ),
        in_specs=[SMEM, VMEM] + [HBM] * 5 + [VMEM] + [ANY] * 6,
        out_specs=[VMEM] * 4,
        scratch_shapes=[
            pltpu.VMEM((width, hidden), BF16),
            pltpu.VMEM((hidden, width), BF16),
            pltpu.VMEM((width, width), BF16),
            pltpu.VMEM((tokens, width), F32),
        ]
        + [pltpu.VMEM(each.shape, each.dtype) for each in (n2, c2, gp, n1, c1)]
        + [pltpu.SemaphoreType.DMA((3,)), pltpu.SemaphoreType.DMA((5,))],
        compiler_params=params(VMEM_MB),
        cost_estimate=cost(),
        name="chain_backward",
    )(pos_w, dx, n2, c2, gp, n1, c1, vec, *inner_bufs, *outer_bufs, *attn_bufs)


def attn_back_kernel(*refs):
    sources, do_ref, pack_ref, sum_ref, wide_ref = refs[:4], refs[4], refs[5], refs[6], refs[7]
    held, sems, pair_sems = refs[8:12], refs[12], refs[13]
    q_ref, kt_ref, v_ref, p_ref = held
    tokens, width = q_ref.shape
    for index in range(3):
        load(sources[index], held[index], sems.at[index])
    for index in range(width // 128):
        both = pl.ds(index * 2, 2)
        load(sources[3].at[both], p_ref.at[both], pair_sems.at[index])
    for index in range(3):
        wait_full(held[index], sems.at[index])

    def pair(index, carry):
        lane = pl.multiple_of(index * 128, 128)
        values = v_ref[:, pl.ds(lane, 128)]
        queries = q_ref[:, pl.ds(lane, 128)]
        grads = do_ref[:, pl.ds(lane, 128)]
        first = lax.broadcasted_iota(jnp.int32, grads.shape, 1) < HD
        keys_back, values_back = [], []
        wait_full(p_ref.at[pl.ds(index * 2, 2)], pair_sems.at[index])
        for which in range(2):
            mine = jnp.where(first if which == 0 else ~first, grads, jnp.zeros_like(grads))
            probs_low = p_ref[index * 2 + which]
            probs = probs_low.astype(F32)
            weighted = probs * nt(values, mine)
            back = weighted - probs * jnp.sum(weighted, axis=0, keepdims=True)
            low = back.astype(BF16)
            keys_back.append(nn(low, queries))
            values_back.append(nn(probs_low, grads))
            row = pl.multiple_of(index * 128 + which * HD, HD)
            wide_ref[pl.ds(row, HD), :] = nn(kt_ref[pl.ds(row, HD), :], low)
        split = lax.broadcasted_iota(jnp.int32, keys_back[0].shape, 1) < HD
        for at, back in ((1, keys_back), (3, values_back)):
            low = jnp.where(split, back[0], back[1]).astype(BF16)
            pack_ref[at, :, pl.ds(lane, 128)] = low[:tokens]
            pack_ref[at + 1, :, pl.ds(lane, 128)] = low[tokens:]
        return carry

    lax.fori_loop(0, width // 128, pair, 0)
    low = (wide_ref[...].T * HD ** (-0.5)).astype(BF16)
    pack_ref[0] = low
    sum_ref[...] = jnp.broadcast_to(colsum(low.astype(F32)), sum_ref.shape)


def attn_backward(q, kt, v, p, do):
    tokens, width = q.shape
    return pl.pallas_call(
        attn_back_kernel,
        out_shape=(
            shape((5, tokens, width), BF16),
            shape((8, width), F32),
        ),
        in_specs=[HBM] * 4 + [VMEM],
        out_specs=[VMEM] * 2,
        scratch_shapes=[pltpu.VMEM((width, tokens), F32)]
        + [pltpu.VMEM(each.shape, each.dtype) for each in (q, kt, v, p)]
        + [pltpu.SemaphoreType.DMA((3,)), pltpu.SemaphoreType.DMA((width // 128,))],
        compiler_params=params(VMEM_MB),
        cost_estimate=cost(),
        name="attn_backward",
    )(q, kt, v, p, do)


def input_kernel(*refs):
    pos_w, da_ref, pack_ref, got_ref = refs[:4]
    bufs = refs[4:6]
    dx_ref, total_ref, sum_ref = refs[6:9]
    wq, wk, wv, sems = refs[9:]
    tokens, width = da_ref.shape
    for member, full in enumerate((wq, wk, wv)):
        fetch_member(pos_w, bufs, member, full, sems.at[member])
    for at, (mine, theirs) in enumerate(((1, 2), (2, 1), (3, 4), (4, 3))):
        total_ref[at] = (pack_ref[mine].astype(F32) + got_ref[theirs].astype(F32)).astype(BF16)
    sum_ref[...] = jnp.broadcast_to(colsum(total_ref[2].astype(F32)), sum_ref.shape)
    wait_full(wq, sems.at[0])
    dx = da_ref[...] + nt(pack_ref[0], wq[...])
    wait_full(wk, sems.at[1])
    dx += nt(total_ref[0], wk[...])
    wait_full(wv, sems.at[2])
    dx += nt(total_ref[2], wv[...])
    dx_ref[...] = dx


def input_backward(pos_w, da, pack, got, bufs):
    tokens, width = da.shape
    return pl.pallas_call(
        input_kernel,
        out_shape=(
            shape((tokens, width), F32),
            shape((4, tokens, width), BF16),
            shape((8, width), F32),
        ),
        in_specs=[SMEM] + [VMEM] * 3 + [ANY] * 2,
        out_specs=[VMEM] * 3,
        scratch_shapes=[pltpu.VMEM((width, width), BF16)] * 3 + [pltpu.SemaphoreType.DMA((3,))],
        compiler_params=params(VMEM_MB),
        cost_estimate=cost(),
        name="input_backward",
    )(pos_w, da, pack, got, *bufs)


def place(outs, part, dy, value):
    a_keep, a_send, b_keep, b_send = outs
    if part == 0:
        a_keep[dy] = value[0]
        a_send[dy] = value[1]
    else:
        (b_send if dy else b_keep)[...] = value


def grad_shapes(rows, width):
    return (shape((2, ZS, rows, width), BF16),) * 4


def inner_grad_kernel(pos_ref, ta_ref, tb_ref, da_ref, db_ref, *refs):
    outs, left, sems = refs[:4], refs[4], refs[5]
    _, _, rows, width = outs[0].shape
    tokens = ta_ref.shape[-1]
    for side, source in enumerate((ta_ref, tb_ref)):
        load(source.at[2], left.at[side], sems.at[side])
    for side in range(2):
        wait_full(left.at[side], sems.at[side])
    left_a = left[0].reshape(2 * ZS * rows, tokens)
    left_b = left[1].reshape(2 * ZS * rows, tokens)
    for dy in range(2):
        for part in range(2):
            lanes = pl.ds(pl.multiple_of((half_at(pos_ref, dy) * 2 + part) * width + width, 128), width)
            value = nn(left_a, da_ref[:, lanes]) + nn(left_b, db_ref[:, lanes])
            place(outs, part, dy, value.astype(BF16).reshape(2, ZS, rows, width))


def inner_grad(pos_g, ta, tb, da, db):
    rows = ta.shape[3]
    return pl.pallas_call(
        inner_grad_kernel,
        out_shape=grad_shapes(rows, rows * BLOCKS),
        in_specs=[SMEM] + [HBM] * 2 + [VMEM] * 2,
        out_specs=[VMEM] * 4,
        scratch_shapes=[pltpu.VMEM((2,) + ta.shape[1:], BF16), pltpu.SemaphoreType.DMA((2,))],
        compiler_params=params(VMEM_MB),
        cost_estimate=cost(),
        name="inner_grad",
    )(pos_g, ta, tb, da, db)


def outer_grad_kernel(ta_ref, tb_ref, da_ref, db_ref, *refs):
    outs, left, sems = refs[:4], refs[4], refs[5]
    _, _, rows, width = outs[0].shape
    tokens = ta_ref.shape[-1]
    for side, source in enumerate((ta_ref, tb_ref)):
        load(source, left.at[side], sems.at[side])
    for side in range(2):
        wait_full(left.at[side], sems.at[side])
    for dy in range(2):
        for part in range(2):
            values = []
            for dx in range(2):
                left_a = left[0, dx, dy, part].reshape(ZS * rows, tokens)
                left_b = left[1, dx, dy, part].reshape(ZS * rows, tokens)
                value = nn(left_a, da_ref[:, :width]) + nn(left_b, db_ref[:, :width])
                values.append(value.astype(BF16).reshape(ZS, rows, width))
            place(outs, part, dy, jnp.stack(values))


def outer_grad(ta, tb, da, db, width):
    rows = ta.shape[4]
    return pl.pallas_call(
        outer_grad_kernel,
        out_shape=grad_shapes(rows, width),
        in_specs=[HBM] * 2 + [VMEM] * 2,
        out_specs=[VMEM] * 4,
        scratch_shapes=[pltpu.VMEM((2,) + ta.shape, BF16), pltpu.SemaphoreType.DMA((2,))],
        compiler_params=params(VMEM_MB),
        cost_estimate=cost(),
        name="outer_grad",
    )(ta, tb, da, db)


def attn_grad_kernel(pos_ref, xa_ref, xb_ref, qa_ref, qb_ref, total_ref, da_ref, db_ref, *refs):
    outs, left, sems = refs[:4], refs[4], refs[5]
    for side, source in enumerate((xa_ref, xb_ref)):
        load(source.at[pl.ds(0, 2)], left.at[side], sems.at[side])
    for side in range(2):
        wait_full(left.at[side], sems.at[side])
    _, _, rows, width = outs[0].shape
    half = width // 2
    tokens = xa_ref.shape[-1]
    height = 2 * ZS * rows
    x_a = left[0, 0].reshape(height, tokens)
    x_b = left[1, 0].reshape(height, tokens)
    o_a = left[0, 1].reshape(height, tokens)
    o_b = left[1, 1].reshape(height, tokens)
    last = da_ref.shape[1] - width
    for dy in range(2):
        start = half_at(pos_ref, dy) * half
        lanes = pl.ds(pl.multiple_of(start, 128), half)
        tail = pl.ds(pl.multiple_of(start + last, 128), half)
        members = (
            nn(x_a, qa_ref[0, :, lanes]) + nn(x_b, qb_ref[0, :, lanes]),
            nn(x_a, total_ref[0, :, lanes]) + nn(x_b, total_ref[1, :, lanes]),
            nn(x_a, total_ref[2, :, lanes]) + nn(x_b, total_ref[3, :, lanes]),
            nn(o_a, da_ref[:, tail]) + nn(o_b, db_ref[:, tail]),
        )
        for part in range(2):
            value = jnp.concatenate(members[part * 2 : part * 2 + 2], axis=1)
            place(outs, part, dy, value.astype(BF16).reshape(2, ZS, rows, width))


def attn_grad(pos_g, xa, xb, qa, qb, total, da, db):
    rows = xa.shape[3]
    return pl.pallas_call(
        attn_grad_kernel,
        out_shape=grad_shapes(rows, rows * BLOCKS),
        in_specs=[SMEM] + [HBM] * 2 + [VMEM] * 5,
        out_specs=[VMEM] * 4,
        scratch_shapes=[pltpu.VMEM((2, 2) + xa.shape[1:], BF16), pltpu.SemaphoreType.DMA((2,))],
        compiler_params=params(VMEM_MB),
        cost_estimate=cost(),
        name="attn_grad",
    )(pos_g, xa, xb, qa, qb, total, da, db)


def copy_kernel(plan, inputs, *refs):
    ins, outs, sems = refs[:inputs], refs[inputs:-1], refs[-1]
    copies = []
    for index, (out, to, source, at, size) in enumerate(plan):
        copies.append(
            pltpu.make_async_copy(
                ins[source].at[pl.ds(at, size)], outs[out].at[pl.ds(to, size)], sems.at[index]
            )
        )
    for each in copies:
        each.start()
    for each in copies:
        each.wait()


def copy_blocks(plan, inputs, sizes, name):
    piece = inputs[0].shape[1:]
    return pl.pallas_call(
        functools.partial(copy_kernel, plan, len(inputs)),
        out_shape=tuple(shape((size,) + piece, BF16) for size in sizes),
        in_specs=[ANY] * len(inputs),
        out_specs=[VMEM] * len(sizes),
        scratch_shapes=[pltpu.SemaphoreType.DMA((len(plan),))],
        compiler_params=params(VMEM_MB),
        cost_estimate=cost(),
        name=name,
    )(*inputs)


def pack_kernel(group, pos_ref, *refs):
    four, inner, outer = refs[:4], refs[4], refs[5]
    out, sem = refs[6], refs[7]
    rows, width = out.shape[1:]
    half = width // 2
    y = pos_ref[3]
    for j, chunk in enumerate(group):
        layer, kind = chunk // 3, chunk % 3
        for part in range(2):
            to = out.at[2 * j + part]
            if kind == 0:
                for side in range(2):
                    pltpu.make_async_copy(
                        four[2 * part + side].at[layer, :, pl.ds(pl.multiple_of(y * half, 128), half)],
                        to.at[:, pl.ds(side * half, half)],
                        sem,
                    ).start()
            elif kind == 1:
                lane = pl.multiple_of((2 * y + part) * width, 128)
                pltpu.make_async_copy(inner.at[layer, :, pl.ds(lane, width)], to, sem).start()
            else:
                row = pl.multiple_of((2 * y + part) * rows, 16)
                pltpu.make_async_copy(outer.at[layer, pl.ds(row, rows)], to, sem).start()
    wait_full(out, sem)


def pack_pieces(group, pos, weights):
    _, rows, width = weights[0].shape
    return pl.pallas_call(
        functools.partial(pack_kernel, group),
        out_shape=shape((2 * len(group), rows, width), BF16),
        in_specs=[SMEM] + [HBM] * 6,
        out_specs=VMEM,
        scratch_shapes=[pltpu.SemaphoreType.DMA],
        compiler_params=params(VMEM_MB),
        cost_estimate=cost(),
        name="pack",
    )(pos, *weights)


def table_kernel(at_ref, *refs):
    vectors, out = refs[:-1], refs[-1]
    width = out.shape[2]
    for index, vector in enumerate(vectors):
        size = vector.shape[1]
        start = at_ref[0] * size
        for piece in range(max(1, out.shape[1] - IB if index == IB else 1)):
            lanes = lax.broadcasted_iota(jnp.int32, (size, width), 1) + piece * width
            spot = lax.broadcasted_iota(jnp.int32, (size, width), 0) + start
            chosen = (lanes == spot).astype(F32).astype(BF16)
            out[:, index + piece, :] = nn(vector[...], chosen)


def vector_table(at, vectors, width):
    layers, last = vectors[-1].shape[0], vectors[-1].shape[1]
    rows = IB + last // vectors[0].shape[1]
    return pl.pallas_call(
        table_kernel,
        out_shape=shape((layers, rows, width), F32),
        in_specs=[SMEM] + [VMEM] * len(vectors),
        out_specs=VMEM,
        compiler_params=params(VMEM_MB),
        cost_estimate=cost(),
        name="vector_table",
    )(at, *vectors)


def finish_kernel(kind, offsets, pos_ref, *refs):
    layers = len(offsets)
    owns, gots = refs[:layers], refs[layers : 2 * layers]
    outs, buf, sems = refs[2 * layers : -2], refs[-2], refs[-1]
    rows, width = buf.shape[2:]
    half = width // 2
    y = pos_ref[3]
    copies = []
    for layer in range(layers):
        copies.append(
            pltpu.make_async_copy(
                gots[layer].at[pl.ds(offsets[layer], 2)], buf.at[layer], sems.at[layer]
            )
        )
        copies[-1].start()
    for side in range(2):
        yy = y if side == 0 else 1 - y
        if side:
            for each in copies:
                each.wait()
        for layer in range(layers):
            for part in range(2):
                value = buf[layer, part].astype(F32) if side else owns[layer][part]
                if kind == 0:
                    lanes = pl.ds(pl.multiple_of(yy * half, 128), half)
                    for member in range(2):
                        outs[2 * part + member][layer, :, lanes] = value[
                            :, member * half : (member + 1) * half
                        ]
                elif kind == 1:
                    lane = pl.multiple_of((2 * yy + part) * width, 128)
                    outs[0][layer, :, pl.ds(lane, width)] = value
                else:
                    row = pl.multiple_of((2 * yy + part) * rows, 16)
                    outs[0][layer, pl.ds(row, rows), :] = value


def finish(kind, pos, results):
    layers = len(results)
    _, rows, width = results[0][0].shape
    outs = {
        0: (shape((layers, rows, width), F32),) * 4,
        1: (shape((layers, rows, 4 * width), F32),),
        2: (shape((layers, 4 * rows, width), F32),),
    }[kind]
    return pl.pallas_call(
        functools.partial(finish_kernel, kind, tuple(value[2] for value in results)),
        out_shape=outs,
        in_specs=[SMEM] + [VMEM] * layers + [ANY] * layers,
        out_specs=[VMEM] * len(outs),
        scratch_shapes=[
            pltpu.VMEM((layers, 2, rows, width), BF16),
            pltpu.SemaphoreType.DMA((layers,)),
        ],
        compiler_params=params(VMEM_MB),
        cost_estimate=cost(),
        name="finish",
    )(pos, *[value[0] for value in results], *[value[1] for value in results])


def sum_kernel(config, *refs):
    fresh, first, second, third, fourth = config
    refs = list(refs)

    def take(count):
        out = refs[:count]
        del refs[:count]
        return out

    sends = take(2) if fresh else None
    got_x, got_y = take(2) if first or second else (None, None)
    keeps = take(2) if first else None
    rests = take(2) if second else None
    pairs = take(2) if third else None
    lasts = take(2) if fourth else None
    to_x, to_y = take(2) if fresh or first or fourth else (None, None)
    at = 0
    if fresh:
        for out, send in ((to_x, sends[0]), (to_y, sends[1])):
            for half in range(2):
                out[half * ZS : (half + 1) * ZS] = send[half]
        at = 2 * ZS
    got = 0
    if first:
        outs = take(2)
        for keep, come, rest, send in (
            (keeps[0], got_x, outs[0], to_y),
            (keeps[1], got_y, outs[1], to_x),
        ):
            rest[...] = (keep[0].astype(F32) + come[:ZS].astype(F32)).astype(BF16)
            send[at : at + ZS] = (keep[1].astype(F32) + come[ZS : 2 * ZS].astype(F32)).astype(BF16)
        got = 2 * ZS
        at += ZS
    if second:
        hold, go = take(2)
        for part, (rest, come) in enumerate(((rests[0], got_y), (rests[1], got_x))):
            for k in range(ZS):
                value = rest[k].astype(F32) + come[got + k].astype(F32)
                (go if k % 2 else hold)[k // 2, part] = value.astype(BF16)
    if third:
        hold, go = take(2)
        hold[...] = pairs[0][0].astype(F32) + pairs[1][0].astype(F32)
        go[...] = (pairs[0][1].astype(F32) + pairs[1][1].astype(F32)).astype(BF16)
    if fourth:
        (total,) = take(1)
        value = lasts[0][...] + lasts[1][...].astype(F32)
        total[...] = value
        to_y[at : at + 2] = value.astype(BF16)


def sum_round(fresh, got_x, got_y, first, second, third, fourth):
    config = tuple(value is not None for value in (fresh, first, second, third, fourth))
    sample = fresh or first or second or third or fourth
    rows, width = sample[-1].shape[-2:]
    inputs, outputs = [], []
    if fresh is not None:
        inputs += [fresh[1], fresh[3]]
    if first is not None or second is not None:
        inputs += [got_x, got_y]
    for value in (first, second, third, fourth):
        if value is not None:
            inputs += list(value)
    going = 2 * ZS * config[0] + ZS * config[1]
    if config[0] or config[1] or config[4]:
        size_y = going + 2 * config[4]
        outputs += [shape((max(going, 1), rows, width), BF16), shape((size_y, rows, width), BF16)]
    if config[1]:
        outputs += [shape((ZS, rows, width), BF16)] * 2
    if config[2]:
        outputs += [shape((2, 2, rows, width), BF16)] * 2
    if config[3]:
        outputs += [shape((2, rows, width), F32), shape((2, rows, width), BF16)]
    if config[4]:
        outputs += [shape((2, rows, width), F32)]
    outs = list(
        pl.pallas_call(
            functools.partial(sum_kernel, config),
            out_shape=tuple(outputs),
            in_specs=[VMEM] * len(inputs),
            out_specs=[VMEM] * len(outputs),
            compiler_params=params(VMEM_MB),
            cost_estimate=cost(),
            name="sum_round",
        )(*inputs)
    )

    def take(wanted, count):
        if not wanted:
            return None
        out = tuple(outs[:count])
        del outs[:count]
        return out

    sends = take(config[0] or config[1] or config[4], 2)
    return sends, going, take(config[1], 2), take(config[2], 2), take(config[3], 2), take(config[4], 1)


def fence(values):
    return lax.optimization_barrier(values)


def build(mesh):
    count = mesh.shape["dp"]

    def flat(dp, seq):
        return dp * 2 + seq

    def pairs(source_of):
        out = []
        for dp in range(count):
            for seq in range(2):
                out.append((flat(*source_of(dp, seq)), flat(dp, seq)))
        return out

    swap_pairs = pairs(lambda dp, seq: (dp // 2 * 2 + seq, dp % 2))
    core_pairs = pairs(lambda dp, seq: (dp ^ 1, seq))
    x_pairs = pairs(lambda dp, seq: (dp ^ 2, seq))
    y_pairs = pairs(lambda dp, seq: (dp, 1 - seq))
    z_pairs = [pairs(lambda dp, seq, k=k: ((dp // 4 ^ k) * 4 + dp % 4, seq)) for k in (1, 2)]

    def move(value, perm):
        return lax.ppermute(value, AXES, perm)

    return dict(
        count=count,
        swap=swap_pairs,
        core=core_pairs,
        x=x_pairs,
        y=y_pairs,
        z1=z_pairs[0],
        z2=z_pairs[1],
        move=move,
    )


def body(
    net,
    tokens,
    segment_ids,
    padding,
    query_weight,
    key_weight,
    value_weight,
    output_weight,
    query_bias,
    value_bias,
    output_bias,
    attn_gain,
    attn_shift,
    inner_weight,
    inner_bias,
    outer_weight,
    outer_bias,
    ffn_gain,
    ffn_shift,
    upstream,
):
    layers, small, width = query_weight.shape
    hidden = inner_weight.shape[2]
    count = net["count"]
    move = net["move"]
    staged = count == BLOCKS and small % 16 == 0
    dp = lax.axis_index("dp").astype(jnp.int32)
    y = lax.axis_index("seq").astype(jnp.int32)
    core = lax.rem(dp, 2)
    if staged:
        pos_g = jnp.stack([lax.div(dp, 4), lax.rem(lax.div(dp, 2), 2), core, y])
        pos_w = pos_g
    else:
        zero = jnp.zeros((), jnp.int32)
        pos_g = jnp.stack([zero, zero, core, zero])
        pos_w = jnp.stack([zero, zero, zero, zero])

    labels = jnp.where(padding == 1, segment_ids, -1)
    small_own = move(jnp.concatenate([segment_ids, labels]), net["swap"])
    token_low = move(tokens[0], net["swap"])

    vector_args = [query_bias, value_bias, output_bias, attn_gain, attn_shift, outer_bias]
    vector_args += [ffn_gain, ffn_shift, inner_bias]
    table = vector_table(dp[None], vector_args, width)
    if staged:
        table = table + move(table, net["x"])
    else:
        table = lax.psum(table, "dp")

    raw = (query_weight, key_weight, value_weight, output_weight, inner_weight, outer_weight)
    chunks = []
    for layer in range(layers):
        four = (query_weight[layer], key_weight[layer], value_weight[layer], output_weight[layer])
        if not staged:
            full = [lax.all_gather(value, "dp", axis=0, tiled=True) for value in four]
            inner = lax.all_gather(inner_weight[layer], "dp", axis=0, tiled=True)
            outer = lax.all_gather(outer_weight[layer], "dp", axis=0, tiled=True)
            rows = width // BLOCKS

            def cut(value, dy, dx, dc):
                value = value.reshape(ZS, 2, 2, rows, 2, -1)
                return value[:, dx, dc, :, dy, :]

            lists = [[[], []], [[], []], [[], []]]
            for dc in range(2):
                for part, dy, dx in UNITS:
                    lists[0][dc].append(
                        jnp.concatenate([cut(value, dy, dx, dc) for value in full[part * 2 : part * 2 + 2]], axis=2)
                    )
                    lists[1][dc].append(cut(inner, dy, dx, dc)[..., part * width : (part + 1) * width])
                    lists[2][dc].append(
                        outer.reshape(ZS, 2, 2, 2, 2, hidden // BLOCKS // 4, width)[:, dx, dc, dy, part]
                    )
            chunks.extend(tuple(jnp.concatenate(side) for side in value) for value in lists)

    total_chunks = 3 * layers
    groups = []
    if staged:
        edges = [0, 1, 2] + list(range(3, total_chunks + 1, 3))
        groups = [range(low, high) for low, high in zip(edges[:-1], edges[1:])]
    where_of = {i: (g, i - group[0]) for g, group in enumerate(groups) for i in group}
    stage_z = [None] * len(groups)

    def start_z2(g):
        own = pack_pieces(groups[g], pos_g, raw)
        stage_z[g] = (own, move(own, net["z2"]))

    def start_z1(g):
        own, come = stage_z[g]
        size = own.shape[0]
        both = copy_blocks([(0, 0, 0, 0, size), (0, size, 1, 0, size)], (own, come), [2 * size], "gather_z")[0]
        stage_z[g] = (both, move(both, net["z1"]))

    if staged:
        start_z2(0)
        stage_z[0], raw, table, small_own, token_low = fence(
            (stage_z[0], raw, table, small_own, token_low)
        )
        start_z1(0)
        start_z2(1)
        table = table + move(table, net["core"])
    small_other = move(small_own, net["core"])
    token_other = move(token_low, net["core"])
    if staged:
        stage_z[:2], raw, table, small_own, small_other, token_low, token_other, upstream = fence(
            (stage_z[:2], raw, table, small_own, small_other, token_low, token_other, upstream)
        )
    seg = small_own[0:1]
    lab = jnp.concatenate([small_own[1], small_other[1]])[:, None]
    current = token_low.astype(F32)
    other = token_other
    kept = [None] * layers
    todo = []
    for layer in range(layers):
        todo.append(("attn", layer, 3 * layer))
        todo.append(("ffn", layer, 3 * layer + 2))
    low = None
    attn_out = None
    arrived = 0 if staged else total_chunks

    def compute():
        nonlocal current, other, low, attn_out
        if not todo or todo[0][2] >= arrived:
            return
        kind, layer, _ = todo.pop(0)
        if kind == "attn":
            attn_out = attn_forward(
                pos_w, pos_g, current, other, seg, lab, table[layer], chunks[3 * layer]
            )
            return
        h, n1, c1, q, kt, v, p, xoh, far_xoh = attn_out
        current, low, n2, c2, gp, gt, far_gt = ffn_forward(
            pos_w, pos_g, h, table[layer], chunks[3 * layer + 1], chunks[3 * layer + 2]
        )
        if layer + 1 < layers:
            other = move(low, net["core"])
        kept[layer] = (n1, c1, q, kt, v, p, n2, c2, gp, xoh, gt) + (
            move(far_xoh, net["core"]),
            move(far_gt, net["core"]),
        )

    if staged:
        sent, got = {}, {}
        zplan = {
            -LAG: [(1, 1), (2, 2)],
            -LAG + 1: [(1, 2), (2, 3)],
            -LAG + 2: [(1, 3)],
            -LAG + 3: [(2, 4)],
            -LAG + 4: [(1, 4)],
        }
        spread = [net["z2"], net["z1"]]
        for r in range(-LAG, total_chunks + LAG):
            inputs, plan = [], []
            sizes = [0, 0]
            use = lambda value: (inputs.append(value), len(inputs) - 1)[1]
            fresh = r + LAG < total_chunks
            if fresh:
                g, j = where_of[r + LAG]
                n = len(groups[g])
                mine, theirs = use(stage_z[g][0]), use(stage_z[g][1])
                for out, part in ((0, 1), (1, 0)):
                    for k, (source, slot) in enumerate(((mine, 0), (theirs, 0), (mine, 1), (theirs, 1))):
                        plan.append((out, k, source, (slot * n + j) * 2 + part, 1))
                    sizes[out] = ZS
            before = r - LAG
            home = 0 <= before < total_chunks
            if before >= -LAG and (r < total_chunks or home):
                sx, sy = use(sent[before][0]), use(sent[before][1])
                rx, ry = use(got[before][0]), use(got[before][1])
                first = ZS if before + LAG < total_chunks else 0
                if r < total_chunks:
                    for out, send, come in ((0, sy, ry), (1, sx, rx)):
                        plan.append((out, sizes[out], send, 0, ZS))
                        plan.append((out, sizes[out] + ZS, come, 0, ZS))
                        sizes[out] += 2 * ZS
                if home:
                    sizes.append(8 * ZS)
                    slot = 2
                    for at, (send, come) in enumerate(((sx, rx), (sy, ry))):
                        plan.append((slot, at * 4 * ZS, send, first, 2 * ZS))
                        plan.append((slot, at * 4 * ZS + 2 * ZS, come, first, 2 * ZS))
            live = [index for index, size in enumerate(sizes) if size]
            outs = copy_blocks(
                [(live.index(each[0]),) + each[1:] for each in plan],
                inputs,
                [sizes[index] for index in live],
                "gather_round",
            )
            outs = dict(zip(live, outs))
            if 0 in outs:
                sent[r] = (outs[0], outs[1])
                got[r] = (move(outs[0], net["x"]), move(outs[1], net["y"]))
            core_pair = None
            if home:
                core_pair = (outs[2], move(outs[2], net["core"]))
            for stage, g in zplan.get(r, ()):
                if g < len(groups):
                    (start_z2 if stage == 2 else start_z1)(g)
            if spread:
                table = table + move(table, spread.pop(0))
            if r == total_chunks - 2:
                upstream = move(upstream[0], net["swap"])
            compute()
            ready = r + 1 - LAG
            state = (got.get(ready), core_pair, stage_z, current, other, attn_out, raw, table, upstream)
            state = fence(state)
            if ready in got:
                got[ready] = state[0]
            if home:
                chunks.append(state[1])
                arrived += 1
            stage_z, current, other, attn_out, raw, table, upstream = (list(state[2]),) + tuple(state[3:])
    while todo:
        compute()
    range_ids = jnp.arange(SEGS, dtype=jnp.int32)
    own = (small_own[1][None, :] == range_ids[:, None]).astype(F32)
    sums = jnp.dot(own, current, precision=lax.Precision.HIGHEST)
    pool_sums = sums
    counts = jnp.sum((lab[:, 0][None, :] == range_ids[:, None]).astype(F32), axis=1)
    loose = {}
    if staged:
        loose["hidden"] = move(low, net["swap"])
        loose["pool"] = pool_sums + move(pool_sums, net["core"])

    grad = upstream if staged else move(upstream[0], net["swap"])
    parts = []
    vectors = [None] * layers
    rounds = []
    ends = []

    def side_work():
        step = len(rounds)
        last = total_chunks
        if step == 0:
            loose["pooled"] = move(loose.pop("pool") / counts[:, None], net["swap"])
        if step == last - 2:
            loose["table"] = jnp.stack(vectors)
            loose["table"] = loose["table"] + move(loose["table"], net["core"])
        order = {last - 1: "z1", last: "z2", last + 1: "x", last + 2: "y"}
        if step in order:
            loose["table"] = loose["table"] + move(loose["table"], net[order[step]])
        if step == last:
            loose["grad"] = move(loose.pop("grad").astype(BF16), net["swap"])

    def settle(state):
        nonlocal loose
        state, loose = fence((state, loose))
        return state

    def advance(fresh, state):
        nonlocal loose
        if not staged:
            if fresh is not None:
                parts.append(fresh)
            return state
        side_work()
        s = len(rounds)
        past = rounds[s - LAG] if s >= LAG else {}
        pick = lambda key: past.get(key)
        has_home = pick("first") is not None or pick("second") is not None
        sends, going, first, second, third, fourth = sum_round(
            fresh,
            pick("got_x") if has_home else None,
            pick("got_y") if has_home else None,
            pick("first"),
            pick("second"),
            pick("third"),
            pick("fourth"),
        )
        now = {}
        if fresh is not None:
            now["first"] = (fresh[0], fresh[2])
        if first is not None:
            now["second"] = first
        if sends is not None:
            if going:
                now["got_x"] = move(sends[0], net["x"])
            now["got_y"] = move(sends[1], net["y"])
        if second is not None:
            now["third"] = (second[0], move(second[1], net["z1"]))
        if third is not None:
            now["fourth"] = (third[0], move(third[1], net["z2"]))
        if fourth is not None:
            now["total"] = fourth[0]
            ends.append(going)
        rounds.append(now)
        ready = s + 1 - LAG
        if ready < 0:
            state, loose = fence((state, loose))
            return state
        rounds[ready], state, loose = fence((rounds[ready], state, loose))
        return state

    ready = None
    for layer in reversed(range(layers)):
        attn_bufs, inner_bufs, outer_bufs = chunks[3 * layer : 3 * layer + 3]
        vec = table[layer]
        n1, c1, q, kt, v, p, n2, c2, gp, xoh, gt, far_xoh, far_gt = kept[layer]
        pack, da, do, sums = chain_backward(
            pos_w, grad, n2, c2, gp, n1, c1, vec, inner_bufs, outer_bufs, attn_bufs
        )
        if layer + 1 < layers:
            attn_parts = attn_grad(*attn_args)
            (pack, da, do, sums), attn_parts = advance(ready, ((pack, da, do, sums), attn_parts))
            ready = attn_parts
        got_pack = move(pack, net["core"])
        back, qsum = attn_backward(q, kt, v, p, do)
        outer_parts = outer_grad(gt, far_gt, pack, got_pack, width)
        state = (back, qsum, outer_parts, pack, got_pack, da)
        back, qsum, outer_parts, pack, got_pack, da = (
            advance(ready, state) if ready is not None else settle(state)
        )
        got_back = move(back, net["core"])
        inner_parts = inner_grad(pos_g, xoh, far_xoh, pack, got_pack)
        grad, total, vsum = input_backward(pos_w, da, back, got_back, attn_bufs)
        state = (grad, total, vsum, inner_parts, back, got_back)
        grad, total, vsum, inner_parts, back, got_back = advance(outer_parts, state)
        ready = inner_parts
        attn_args = (pos_g, xoh, far_xoh, back, got_back, total, pack, got_pack)
        vectors[layer] = jnp.concatenate([qsum[:1], vsum[:1], sums[2:12]], axis=0)
    loose["grad"] = grad
    attn_parts = attn_grad(*attn_args)
    attn_parts = advance(ready, attn_parts)
    advance(attn_parts, None)
    results = []
    if staged:
        for _ in range(4 * LAG):
            advance(None, None)
        for s, now in enumerate(rounds):
            if "total" in now:
                results.append((now["total"], now["got_y"], ends[len(results)]))

    if staged:
        stacked = []
        for kind, first in ((0, 2), (1, 1), (2, 0)):
            stacked += list(finish(kind, pos_g, results[first::3][::-1]))
        hidden_out, pooled, tokens_grad, table = (
            loose[key] for key in ("hidden", "pooled", "grad", "table")
        )
    else:
        collected = [None] * layers
        for place_at, layer in enumerate(reversed(range(layers))):
            outer_parts, inner_parts, attn_parts = parts[3 * place_at : 3 * place_at + 3]

            def spread(outs):
                a_keep, a_send, b_keep, b_send = outs
                a = jnp.stack([a_keep, a_send])
                b = jnp.stack([b_keep, b_send], axis=1)
                return jnp.stack([a, b], axis=2)

            def total(out):
                out = out.reshape(ZS * 2, 1, out.shape[2], out.shape[3])
                mine = (jnp.arange(2, dtype=jnp.int32) == core)[None, :, None, None]
                out = jnp.where(mine, out, jnp.zeros_like(out)).reshape(-1, out.shape[-1])
                out = lax.psum_scatter(out, "dp", scatter_dimension=0, tiled=True)
                return lax.psum(out.astype(F32), "seq")

            outer = spread(outer_parts).transpose(3, 0, 1, 2, 4, 5)
            outer = total(outer.reshape(ZS, 2, -1, width))
            inner = spread(inner_parts).transpose(3, 0, 4, 1, 2, 5)
            inner = total(inner.reshape(ZS, 2, inner.shape[2], -1))
            attn = spread(attn_parts)
            attn = attn.reshape(attn.shape[:5] + (2, width // 2)).transpose(2, 5, 3, 0, 4, 1, 6)
            attn = attn.reshape(4, ZS, 2, attn.shape[4], width)
            four = [total(attn[index]) for index in range(4)]
            collected[layer] = four + [inner, outer]
        stacked = [
            jnp.stack([collected[layer][member] for layer in range(layers)]) for member in range(6)
        ]
        hidden_out = move(low, net["swap"])
        pooled = move((pool_sums + move(pool_sums, net["core"])) / counts[:, None], net["swap"])
        tokens_grad = move(grad.astype(BF16), net["swap"])
        table = lax.psum(jnp.stack(vectors), AXES)
    eight = lax.dynamic_slice_in_dim(table[:, :8], dp * small, small, 2)
    wide = lax.dynamic_slice_in_dim(
        table[:, 8:].reshape(layers, hidden), dp * (hidden // count), hidden // count, 1
    )
    return (
        hidden_out[None],
        pooled[None],
        tokens_grad.astype(F32)[None],
        stacked[0],
        stacked[1],
        stacked[2],
        stacked[3],
        eight[:, QB],
        eight[:, VB],
        eight[:, OB],
        eight[:, AG],
        eight[:, AS],
        stacked[4],
        wide,
        stacked[5],
        eight[:, UB],
        eight[:, FG],
        eight[:, FS],
    )


def solution(mesh):
    cube = P(None, "dp", None)
    flat = P(None, "dp")
    acts = P("dp", "seq", None)
    ids = P("dp", "seq")
    return jax.shard_map(
        functools.partial(body, build(mesh)),
        mesh=mesh,
        in_specs=(acts, ids, ids, cube, cube, cube, cube, flat, flat, flat, flat, flat, cube, flat, cube)
        + (flat, flat, flat, acts),
        out_specs=(acts, P("dp", None, None), acts, cube, cube, cube, cube)
        + (flat, flat, flat, flat, flat, cube, flat, cube, flat, flat, flat),
        check_vma=False,
    )
```

```python
import functools

import jax
import jax.numpy as jnp
from jax import lax
from jax.experimental import pallas as pl
from jax.experimental.pallas import tpu as pltpu
from jax.sharding import PartitionSpec as P

HD = 64
SEGS = 4
BLOCKS = 16
ZS = 4
LAG = 1
VMEM_MB = 24
EPS = 1e-06
MASKED = -1e30
AXES = ("dp", "seq")
F32 = jnp.float32
BF16 = jnp.bfloat16
MB = 1024 * 1024

QB, VB, OB, AG, AS, UB, FG, FS, IB = range(9)


def nn(left, right):
    return lax.dot_general(left, right, (((1,), (0,)), ((), ())), preferred_element_type=F32)


def nt(left, right):
    return lax.dot_general(left, right, (((1,), (1,)), ((), ())), preferred_element_type=F32)


def params(vmem):
    return pltpu.CompilerParams(vmem_limit_bytes=vmem * MB)


def cost():
    return pl.CostEstimate(flops=1, bytes_accessed=1, transcendentals=0)


def load(source, target, sem):
    pltpu.make_async_copy(source, target, sem).start()


VMEM = pl.BlockSpec(memory_space=pltpu.VMEM)
SMEM = pl.BlockSpec(memory_space=pltpu.SMEM)
ANY = pl.BlockSpec(memory_space=pl.ANY)
HBM = pl.BlockSpec(memory_space=pltpu.HBM)


def shape(dims, dtype):
    return jax.ShapeDtypeStruct(dims, dtype)


def flip(value, bit):
    return value + bit - 2 * value * bit


def block_at(pos_ref, k, dx, dc):
    z, x, c = pos_ref[0], pos_ref[1], pos_ref[2]
    low = lax.rem(z, 2)
    zz = flip(lax.div(z, 2), k // 2) * 2 + flip(low, k % 2)
    return (zz * 2 + flip(x, dx)) * 2 + flip(c, dc)


def half_at(pos_ref, dy):
    return flip(pos_ref[3], dy)


UNITS = (
    (0, 0, 0),
    (0, 1, 0),
    (0, 0, 1),
    (0, 1, 1),
    (1, 0, 0),
    (1, 0, 1),
    (1, 1, 0),
    (1, 1, 1),
)


def each_unit(pos_ref, bufs):
    for dc in range(2):
        for unit, (part, dy, dx) in enumerate(UNITS):
            at = flip(pos_ref[1], dx) * 2 + flip(pos_ref[2], dc)
            yield bufs[dc].at[pl.ds(unit * ZS, ZS)], part, dy, at


def fetch_member(pos_ref, bufs, member, full_ref, sem):
    half = full_ref.shape[3] // 2
    for unit, part, dy, at in each_unit(pos_ref, bufs):
        if part == member // 2:
            col = pl.multiple_of(half_at(pos_ref, dy) * half, 128)
            load(
                unit.at[:, :, pl.ds(member % 2 * half, half)],
                full_ref.at[:, at, :, pl.ds(col, half)],
                sem,
            )


def fetch_columns(pos_ref, bufs, full_ref, sem):
    width = full_ref.shape[3] // 4
    for unit, part, dy, at in each_unit(pos_ref, bufs):
        col = pl.multiple_of((half_at(pos_ref, dy) * 2 + part) * width, 128)
        load(unit, full_ref.at[:, at, :, pl.ds(col, width)], sem)


def fetch_rows(pos_ref, bufs, full_ref, sem):
    for unit, part, dy, at in each_unit(pos_ref, bufs):
        load(unit, full_ref.at[:, at, half_at(pos_ref, dy) * 2 + part], sem)


def flat(values):
    return values.reshape(-1, values.shape[-1])


def square(width):
    return pltpu.VMEM((ZS, BLOCKS // ZS, width // BLOCKS, width), BF16)


def wide_matrix(width, hidden):
    return pltpu.VMEM((ZS, BLOCKS // ZS, width // BLOCKS, hidden), BF16)


def tall_matrix(hidden, width):
    return pltpu.VMEM((ZS, BLOCKS // ZS, 4, hidden // BLOCKS // 4, width), BF16)


def wait_full(full_ref, sem):
    pltpu.make_async_copy(full_ref, full_ref, sem).wait()


def export_rows(pos_ref, wide_ref, outs, index):
    rows = outs[0].shape[3]
    for dc in range(2):
        for dx in range(2):
            for k in range(ZS):
                row = pl.multiple_of(block_at(pos_ref, k, dx, dc) * rows, 16)
                outs[dc][index, dx, k] = wide_ref[pl.ds(row, rows), :]


def export_halves(pos_ref, wide_ref, outs):
    rows = outs[0].shape[4]
    for dc in range(2):
        for dx in range(2):
            for dy in range(2):
                for k in range(ZS):
                    block = block_at(pos_ref, k, dx, dc) * 2 + half_at(pos_ref, dy)
                    for part in range(2):
                        row = pl.multiple_of((block * 2 + part) * rows, 16)
                        outs[dc][dx, dy, part, k] = wide_ref[pl.ds(row, rows), :]


def mean_of(values):
    return jnp.mean(values, axis=-1, keepdims=True)


def normalize(values):
    center = values - mean_of(values)
    inverse = lax.rsqrt(mean_of(center * center) + EPS)
    return center * inverse, inverse


def norm_back(normed, inverse, scaled):
    return inverse * (scaled - mean_of(scaled) - normed * mean_of(scaled * normed))


def colsum(values):
    return jnp.sum(values, axis=0, keepdims=True)


def row_of(vec_ref, index):
    return vec_ref[pl.ds(index, 1), :]


def attn_kernel(*refs):
    pos_w, pos_g = refs[0], refs[1]
    x_ref, xp_ref, seg_ref, lab_ref, vec_ref = refs[2:7]
    bufs = refs[7:9]
    h_ref = refs[9]
    kept = refs[10:18]
    wq, wk, wv, wo, rows_ref, vt_ref, wide_ref, bias_ref, k_ref = refs[18:27]
    held = refs[27:35]
    n1_ref, c1_ref, q_ref, kt_ref, v_ref, p_ref = held[:6]
    exports = held[6:]
    sems, store_sems = refs[35:]

    def store(index):
        load(held[index], kept[index], store_sems.at[index])

    tokens, width = x_ref.shape
    for member, full in enumerate((wq, wk, wv, wo)):
        fetch_member(pos_w, bufs, member, full, sems.at[member])
    bias_ref[...] = jnp.where(lab_ref[...] == seg_ref[...], 0.0, MASKED)
    low = x_ref[...].astype(BF16)
    rows_ref[:tokens] = low
    rows_ref[tokens:] = xp_ref[...]
    wide_ref[...] = low.T
    export_rows(pos_g, wide_ref, exports, 0)
    wait_full(wq, sems.at[0])
    query = (nn(low, flat(wq[...])) + row_of(vec_ref, QB)).astype(BF16)
    q_ref[...] = (query.astype(F32) * HD ** (-0.5)).astype(BF16)
    wait_full(wk, sems.at[1])
    key = nn(rows_ref[...], flat(wk[...])).astype(BF16)
    k_ref[...] = key
    kt_ref[...] = key.T
    store(2)
    store(3)
    wait_full(wv, sems.at[2])
    value = (nn(rows_ref[...], flat(wv[...])) + row_of(vec_ref, VB)).astype(BF16)
    v_ref[...] = value
    vt_ref[...] = value.T
    store(4)

    def pair(index, carry):
        lane = pl.multiple_of(index * 128, 128)
        keys = k_ref[:, pl.ds(lane, 128)]
        queries = q_ref[:, pl.ds(lane, 128)]
        first = lax.broadcasted_iota(jnp.int32, queries.shape, 1) < HD
        for which in range(2):
            mine = jnp.where(first if which == 0 else ~first, queries, jnp.zeros_like(queries))
            scores = nt(keys, mine) + bias_ref[...]
            expos = jnp.exp(scores - jnp.max(scores, axis=0, keepdims=True))
            probs = (expos * (1.0 / jnp.sum(expos, axis=0, keepdims=True))).astype(BF16)
            p_ref[index * 2 + which] = probs
            row = pl.multiple_of(index * 128 + which * HD, HD)
            wide_ref[pl.ds(row, HD), :] = nn(vt_ref[pl.ds(row, HD), :], probs).astype(BF16)
        both = pl.ds(index * 2, 2)
        load(p_ref.at[both], kept[5].at[both], store_sems.at[5])
        return carry

    lax.fori_loop(0, width // 128, pair, 0)
    export_rows(pos_g, wide_ref, exports, 1)
    mixed = wide_ref[...].T
    wait_full(wo, sems.at[3])
    branch = nn(mixed, flat(wo[...])) + row_of(vec_ref, OB)
    normed, inverse = normalize(x_ref[...] + branch)
    hidden = normed * row_of(vec_ref, AG) + row_of(vec_ref, AS)
    h_ref[...] = hidden
    n1_ref[...] = normed
    c1_ref[...] = jnp.broadcast_to(inverse, c1_ref.shape)
    wide_ref[...] = hidden.astype(BF16).T
    export_rows(pos_g, wide_ref, exports, 2)
    for index in (0, 1, 6, 7):
        store(index)
    for index in range(8):
        wait_full(held[index], store_sems.at[index])


def attn_forward(pos_w, pos_g, x, xp, seg, lab, vec, bufs):
    tokens, width = x.shape
    heads = width // HD
    export = shape((3, 2, ZS, width // BLOCKS, tokens), BF16)
    kept = (
        shape((tokens, width), F32),
        shape((tokens, 128), F32),
        shape((tokens, width), BF16),
        shape((width, 2 * tokens), BF16),
        shape((2 * tokens, width), BF16),
        shape((heads, 2 * tokens, tokens), BF16),
        export,
        export,
    )
    return pl.pallas_call(
        attn_kernel,
        out_shape=(shape((tokens, width), F32),) + kept,
        in_specs=[SMEM, SMEM] + [VMEM] * 5 + [ANY] * 2,
        out_specs=[VMEM] + [HBM] * 8,
        scratch_shapes=[square(width)] * 4
        + [
            pltpu.VMEM((2 * tokens, width), BF16),
            pltpu.VMEM((width, 2 * tokens), BF16),
            pltpu.VMEM((width, tokens), BF16),
            pltpu.VMEM((2 * tokens, tokens), F32),
            pltpu.VMEM((2 * tokens, width), BF16),
        ]
        + [pltpu.VMEM(each.shape, each.dtype) for each in kept]
        + [pltpu.SemaphoreType.DMA((4,)), pltpu.SemaphoreType.DMA((8,))],
        compiler_params=params(VMEM_MB),
        cost_estimate=cost(),
        name="attn_forward",
    )(pos_w, pos_g, x, xp, seg, lab, vec, *bufs)


def head_back(grad, normed, inverse, gain, low_ref, back_ref, sums_ref):
    sums_ref[...] = jnp.zeros_like(sums_ref)
    sums_ref[pl.ds(0, 1), :] = colsum(grad * normed)
    sums_ref[pl.ds(1, 1), :] = colsum(grad)
    back = norm_back(normed, inverse, grad * gain)
    low = back.astype(BF16)
    low_ref[...] = low
    back_ref[...] = back
    sums_ref[pl.ds(2, 1), :] = colsum(low.astype(F32))


def head_shapes(tokens, width):
    return (
        shape((tokens, width), BF16),
        shape((tokens, width), F32),
        shape((8, width), F32),
    )


def inner_kernel(tile, *refs):
    pos_w, pos_g, h_ref, vec_ref = refs[:4]
    bufs, active_ref, kept = refs[4:6], refs[6], refs[7:10]
    wi, low_ref, wide_ref = refs[10:13]
    held = refs[13:16]
    gp_ref, exports = held[0], held[1:]
    sem, store_sems = refs[16:]
    width, hidden = h_ref.shape[1], wi.shape[3]
    fetch_columns(pos_w, bufs, wi, sem)
    low_ref[...] = h_ref[...].astype(BF16)
    wait_full(wi, sem)
    per_row = width // tile

    def step(index, carry):
        lanes = pl.ds(pl.multiple_of(index * tile, tile), tile)
        bias = vec_ref[pl.ds(IB + lax.div(index, per_row), 1), :]
        part = lax.rem(index, per_row)
        chosen = bias[:, :tile]
        for other in range(1, per_row):
            chosen = jnp.where(part == other, bias[:, other * tile : (other + 1) * tile], chosen)
        pre = nn(low_ref[...], flat(wi[:, :, :, lanes])) + chosen
        phi = 0.5 * (1.0 + lax.erf(pre * 0.7071067811865476))
        dens = jnp.exp(-0.5 * pre * pre) * 0.3989422804014327
        gp_ref[:, lanes] = (phi + pre * dens).astype(BF16)
        active = (pre * phi).astype(BF16)
        active_ref[:, lanes] = active
        wide_ref[lanes, :] = active.T
        return carry

    lax.fori_loop(0, hidden // tile, step, 0)
    load(held[0], kept[0], store_sems.at[0])
    export_halves(pos_g, wide_ref, exports)
    for index in (1, 2):
        load(held[index], kept[index], store_sems.at[index])
    for index in range(3):
        wait_full(held[index], store_sems.at[index])


def inner_forward(pos_w, pos_g, h, vec, bufs):
    tokens, width = h.shape
    hidden = bufs[0].shape[2] * 4
    export = shape((2, 2, 2, ZS, hidden // BLOCKS // 4, tokens), BF16)
    kept = (shape((tokens, hidden), BF16), export, export)
    return pl.pallas_call(
        functools.partial(inner_kernel, 384),
        out_shape=(shape((tokens, hidden), BF16),) + kept,
        in_specs=[SMEM, SMEM, VMEM, VMEM] + [ANY] * 2,
        out_specs=[VMEM] + [HBM] * 3,
        scratch_shapes=[
            wide_matrix(width, hidden),
            pltpu.VMEM((tokens, width), BF16),
            pltpu.VMEM((hidden, tokens), BF16),
        ]
        + [pltpu.VMEM(each.shape, each.dtype) for each in kept]
        + [pltpu.SemaphoreType.DMA, pltpu.SemaphoreType.DMA((3,))],
        compiler_params=params(VMEM_MB),
        cost_estimate=cost(),
        name="inner_forward",
    )(pos_w, pos_g, h, vec, *bufs)


def outer_kernel(last, *refs):
    pos_w, h_ref, active_ref, vec_ref = refs[:4]
    grad_ref = refs[4] if last else None
    refs = refs[4 + last :]
    bufs = refs[:2]
    outs, wu, acc_ref, sem = refs[2:-3], refs[-3], refs[-2], refs[-1]
    fetch_rows(pos_w, bufs, wu, sem)
    acc_ref[...] = h_ref[...] + row_of(vec_ref, UB)
    wait_full(wu, sem)
    tile = active_ref.shape[1] // ZS
    for z in range(ZS):
        acc_ref[...] += nn(active_ref[:, pl.ds(z * tile, tile)], flat(wu[z]))
    normed, inverse = normalize(acc_ref[...])
    result = normed * row_of(vec_ref, FG) + row_of(vec_ref, FS)
    outs[0][...] = result
    outs[1][...] = result.astype(BF16)
    if last:
        head_back(
            grad_ref[...].astype(F32), normed, inverse, row_of(vec_ref, FG), outs[2], outs[3], outs[4]
        )
    else:
        outs[2][...] = normed
        outs[3][...] = jnp.broadcast_to(inverse, outs[3].shape)


def outer_forward(pos_w, h, active, vec, bufs, grad):
    tokens, width = h.shape
    hidden = active.shape[1]
    last = grad is not None
    outs = (shape((tokens, width), F32), shape((tokens, width), BF16))
    if last:
        outs += head_shapes(tokens, width)
    else:
        outs += (shape((tokens, width), F32), shape((tokens, 128), F32))
    return pl.pallas_call(
        functools.partial(outer_kernel, int(last)),
        out_shape=outs,
        in_specs=[SMEM] + [VMEM] * (3 + last) + [ANY] * 2,
        out_specs=[VMEM] * len(outs),
        scratch_shapes=[
            tall_matrix(hidden, width),
            pltpu.VMEM((tokens, width), F32),
            pltpu.SemaphoreType.DMA,
        ],
        compiler_params=params(VMEM_MB),
        cost_estimate=cost(),
        name="outer_forward",
    )(pos_w, h, active, vec, *((grad,) if last else ()), *bufs)


def chain_kernel(tile, waits, *refs):
    pos_w, dyl_ref, dy_ref = refs[:3]
    sources, vec_ref = refs[3:6], refs[6]
    inner_bufs, outer_bufs, attn_bufs = refs[7:9], refs[9:11], refs[11:13]
    refs = refs[13 + waits :]
    pack_ref, da_ref, do_ref, sums_ref = refs[:4]
    wi, wu, wo, acc_ref = refs[4:8]
    held = refs[8:11]
    gp_ref, n1_ref, c1_ref = held
    sems, load_sems = refs[11:]
    width, hidden = dy_ref.shape[1], wi.shape[3]
    for index in range(3):
        load(sources[index], held[index], load_sems.at[index])
    du_ref = pack_ref.at[:, pl.ds(0, hidden)]
    dal_ref = pack_ref.at[:, pl.ds(hidden, width)]
    fetch_rows(pos_w, outer_bufs, wu, sems.at[0])
    fetch_columns(pos_w, inner_bufs, wi, sems.at[1])
    fetch_member(pos_w, attn_bufs, 3, wo, sems.at[2])
    sums_ref[...] = jnp.zeros_like(sums_ref)
    acc_ref[...] = dy_ref[...]
    wait_full(gp_ref, load_sems.at[0])
    wait_full(wu, sems.at[0])
    wait_full(wi, sems.at[1])
    per_row = width // tile

    for index in range(hidden // tile):
        lane = index * tile
        rows = wu[index * ZS * tile // hidden, pl.ds(lane % (hidden // ZS) * BLOCKS // hidden, tile * BLOCKS // hidden)]
        part = nt(dyl_ref[...], flat(rows))
        part = (part * gp_ref[:, pl.ds(lane, tile)].astype(F32)).astype(BF16)
        du_ref[:, pl.ds(lane, tile)] = part
        acc_ref[...] += nt(part, flat(wi[:, :, :, pl.ds(lane, tile)]))
        sums_ref[
            pl.ds(IB + index // per_row, 1), pl.ds(index % per_row * tile, tile)
        ] = colsum(part.astype(F32))

    grad = acc_ref[...]
    wait_full(n1_ref, load_sems.at[1])
    wait_full(c1_ref, load_sems.at[2])
    normed = n1_ref[...]
    sums_ref[pl.ds(AG, 1), :] = colsum(grad * normed)
    sums_ref[pl.ds(AS, 1), :] = colsum(grad)
    back = norm_back(normed, c1_ref[:, :1], grad * row_of(vec_ref, AG))
    da_ref[...] = back
    low = back.astype(BF16)
    dal_ref[...] = low
    sums_ref[pl.ds(OB, 1), :] = colsum(low.astype(F32))
    wait_full(wo, sems.at[2])
    do_ref[...] = nt(low, flat(wo[...])).astype(BF16)


def chain_backward(pos_w, dyl, dy, gp, n1, c1, vec, inner_bufs, outer_bufs, attn_bufs, after=()):
    tokens, width = n1.shape
    hidden = gp.shape[1]
    return pl.pallas_call(
        functools.partial(chain_kernel, 384, len(after)),
        out_shape=(
            shape((tokens, hidden + width), BF16),
            shape((tokens, width), F32),
            shape((tokens, width), BF16),
            shape((16, width), F32),
        ),
        in_specs=[SMEM] + [VMEM] * 2 + [HBM] * 3 + [VMEM] + [ANY] * (6 + len(after)),
        out_specs=[VMEM] * 4,
        scratch_shapes=[
            wide_matrix(width, hidden),
            tall_matrix(hidden, width),
            square(width),
            pltpu.VMEM((tokens, width), F32),
        ]
        + [pltpu.VMEM(each.shape, each.dtype) for each in (gp, n1, c1)]
        + [pltpu.SemaphoreType.DMA((3,)), pltpu.SemaphoreType.DMA((3,))],
        compiler_params=params(VMEM_MB),
        cost_estimate=cost(),
        name="chain_backward",
    )(pos_w, dyl, dy, gp, n1, c1, vec, *inner_bufs, *outer_bufs, *attn_bufs, *after)


def attn_back_kernel(*refs):
    sources, do_ref, pack_ref, sum_ref, wide_ref = refs[:4], refs[4], refs[5], refs[6], refs[7]
    held, sems, pair_sems = refs[8:12], refs[12], refs[13]
    q_ref, kt_ref, v_ref, p_ref = held
    tokens, width = q_ref.shape
    for index in range(3):
        load(sources[index], held[index], sems.at[index])
    for index in range(width // 128):
        both = pl.ds(index * 2, 2)
        load(sources[3].at[both], p_ref.at[both], pair_sems.at[index])
    for index in range(3):
        wait_full(held[index], sems.at[index])

    def pair(index, carry):
        lane = pl.multiple_of(index * 128, 128)
        values = v_ref[:, pl.ds(lane, 128)]
        queries = q_ref[:, pl.ds(lane, 128)]
        grads = do_ref[:, pl.ds(lane, 128)]
        first = lax.broadcasted_iota(jnp.int32, grads.shape, 1) < HD
        keys_back, values_back = [], []
        wait_full(p_ref.at[pl.ds(index * 2, 2)], pair_sems.at[index])
        for which in range(2):
            mine = jnp.where(first if which == 0 else ~first, grads, jnp.zeros_like(grads))
            probs_low = p_ref[index * 2 + which]
            probs = probs_low.astype(F32)
            weighted = probs * nt(values, mine)
            back = weighted - probs * jnp.sum(weighted, axis=0, keepdims=True)
            low = back.astype(BF16)
            keys_back.append(nn(low, queries))
            values_back.append(nn(probs_low, grads))
            row = pl.multiple_of(index * 128 + which * HD, HD)
            wide_ref[pl.ds(row, HD), :] = nn(kt_ref[pl.ds(row, HD), :], low)
        split = lax.broadcasted_iota(jnp.int32, keys_back[0].shape, 1) < HD
        for at, back in ((1, keys_back), (3, values_back)):
            low = jnp.where(split, back[0], back[1]).astype(BF16)
            pack_ref[at, :, pl.ds(lane, 128)] = low[:tokens]
            pack_ref[at + 1, :, pl.ds(lane, 128)] = low[tokens:]
        return carry

    lax.fori_loop(0, width // 128, pair, 0)
    low = (wide_ref[...].T * HD ** (-0.5)).astype(BF16)
    pack_ref[0] = low
    sum_ref[...] = jnp.broadcast_to(colsum(low.astype(F32)), sum_ref.shape)


def attn_backward(q, kt, v, p, do):
    tokens, width = q.shape
    return pl.pallas_call(
        attn_back_kernel,
        out_shape=(
            shape((5, tokens, width), BF16),
            shape((8, width), F32),
        ),
        in_specs=[HBM] * 4 + [VMEM],
        out_specs=[VMEM] * 2,
        scratch_shapes=[pltpu.VMEM((width, tokens), F32)]
        + [pltpu.VMEM(each.shape, each.dtype) for each in (q, kt, v, p)]
        + [pltpu.SemaphoreType.DMA((3,)), pltpu.SemaphoreType.DMA((width // 128,))],
        compiler_params=params(VMEM_MB),
        cost_estimate=cost(),
        name="attn_backward",
    )(q, kt, v, p, do)


def input_kernel(first, *refs):
    pos_w, da_ref, pack_ref, got_ref = refs[:4]
    bufs = refs[4:6]
    refs = refs[6:]
    if not first:
        n2_ref, c2_ref, vec_ref = refs[:3]
        refs = refs[3:]
    total_ref, sum_ref = refs[:2]
    heads = refs[2:-4]
    wq, wk, wv, sems = refs[-4:]
    tokens, width = da_ref.shape
    for member, full in enumerate((wq, wk, wv)):
        fetch_member(pos_w, bufs, member, full, sems.at[member])
    for at, (mine, theirs) in enumerate(((1, 2), (2, 1), (3, 4), (4, 3))):
        total_ref[at] = (pack_ref[mine].astype(F32) + got_ref[theirs].astype(F32)).astype(BF16)
    sum_ref[...] = jnp.broadcast_to(colsum(total_ref[2].astype(F32)), sum_ref.shape)
    wait_full(wq, sems.at[0])
    dx = da_ref[...] + nt(pack_ref[0], flat(wq[...]))
    wait_full(wk, sems.at[1])
    dx += nt(total_ref[0], flat(wk[...]))
    wait_full(wv, sems.at[2])
    dx += nt(total_ref[2], flat(wv[...]))
    if first:
        heads[0][...] = dx.astype(BF16)
    else:
        head_back(dx, n2_ref[...], c2_ref[:, :1], row_of(vec_ref, FG), *heads)


def input_backward(pos_w, da, pack, got, bufs, below):
    tokens, width = da.shape
    first = below is None
    outs = (shape((4, tokens, width), BF16), shape((8, width), F32))
    outs += (shape((tokens, width), BF16),) if first else head_shapes(tokens, width)
    return pl.pallas_call(
        functools.partial(input_kernel, first),
        out_shape=outs,
        in_specs=[SMEM] + [VMEM] * 3 + [ANY] * 2 + ([] if first else [VMEM] * 3),
        out_specs=[VMEM] * len(outs),
        scratch_shapes=[square(width)] * 3 + [pltpu.SemaphoreType.DMA((3,))],
        compiler_params=params(VMEM_MB),
        cost_estimate=cost(),
        name="input_backward",
    )(pos_w, da, pack, got, *bufs, *(() if first else below))


def place(outs, part, dy, value):
    a_keep, a_send, b_keep, b_send = outs
    if part == 0:
        a_keep[dy] = value[0]
        a_send[dy] = value[1]
    else:
        (b_send if dy else b_keep)[...] = value


def grad_shapes(rows, width):
    return (shape((2, ZS, rows, width), BF16),) * 4


def inner_grad_kernel(pos_ref, ta_ref, tb_ref, da_ref, db_ref, *refs):
    outs, left, sems = refs[:4], refs[4], refs[5]
    _, _, rows, width = outs[0].shape
    tokens = ta_ref.shape[-1]
    for side, source in enumerate((ta_ref, tb_ref)):
        load(source.at[2], left.at[side], sems.at[side])
    for side in range(2):
        wait_full(left.at[side], sems.at[side])
    left_a = left[0].reshape(2 * ZS * rows, tokens)
    left_b = left[1].reshape(2 * ZS * rows, tokens)
    for dy in range(2):
        for part in range(2):
            lanes = pl.ds(pl.multiple_of((half_at(pos_ref, dy) * 2 + part) * width, 128), width)
            value = nn(left_a, da_ref[:, lanes]) + nn(left_b, db_ref[:, lanes])
            place(outs, part, dy, value.astype(BF16).reshape(2, ZS, rows, width))


def inner_grad(pos_g, ta, tb, da, db):
    rows = ta.shape[3]
    return pl.pallas_call(
        inner_grad_kernel,
        out_shape=grad_shapes(rows, rows * BLOCKS),
        in_specs=[SMEM] + [HBM] * 2 + [VMEM] * 2,
        out_specs=[VMEM] * 4,
        scratch_shapes=[pltpu.VMEM((2,) + ta.shape[1:], BF16), pltpu.SemaphoreType.DMA((2,))],
        compiler_params=params(VMEM_MB),
        cost_estimate=cost(),
        name="inner_grad",
    )(pos_g, ta, tb, da, db)


def outer_grad_kernel(ta_ref, tb_ref, da_ref, db_ref, *refs):
    outs, left, sems = refs[:4], refs[4], refs[5]
    _, _, rows, width = outs[0].shape
    tokens = ta_ref.shape[-1]
    for side, source in enumerate((ta_ref, tb_ref)):
        load(source, left.at[side], sems.at[side])
    for side in range(2):
        wait_full(left.at[side], sems.at[side])
    for dy in range(2):
        for part in range(2):
            values = []
            for dx in range(2):
                left_a = left[0, dx, dy, part].reshape(ZS * rows, tokens)
                left_b = left[1, dx, dy, part].reshape(ZS * rows, tokens)
                value = nn(left_a, da_ref[...]) + nn(left_b, db_ref[...])
                values.append(value.astype(BF16).reshape(ZS, rows, width))
            place(outs, part, dy, jnp.stack(values))


def outer_grad(ta, tb, da, db):
    rows, width = ta.shape[4], da.shape[1]
    return pl.pallas_call(
        outer_grad_kernel,
        out_shape=grad_shapes(rows, width),
        in_specs=[HBM] * 2 + [VMEM] * 2,
        out_specs=[VMEM] * 4,
        scratch_shapes=[pltpu.VMEM((2,) + ta.shape, BF16), pltpu.SemaphoreType.DMA((2,))],
        compiler_params=params(VMEM_MB),
        cost_estimate=cost(),
        name="outer_grad",
    )(ta, tb, da, db)


def attn_grad_kernel(pos_ref, xa_ref, xb_ref, qa_ref, qb_ref, total_ref, da_ref, db_ref, *refs):
    outs, left, sems = refs[:4], refs[4], refs[5]
    for side, source in enumerate((xa_ref, xb_ref)):
        load(source.at[pl.ds(0, 2)], left.at[side], sems.at[side])
    for side in range(2):
        wait_full(left.at[side], sems.at[side])
    _, _, rows, width = outs[0].shape
    half = width // 2
    tokens = xa_ref.shape[-1]
    height = 2 * ZS * rows
    x_a = left[0, 0].reshape(height, tokens)
    x_b = left[1, 0].reshape(height, tokens)
    o_a = left[0, 1].reshape(height, tokens)
    o_b = left[1, 1].reshape(height, tokens)
    last = da_ref.shape[1] - width
    for dy in range(2):
        start = half_at(pos_ref, dy) * half
        lanes = pl.ds(pl.multiple_of(start, 128), half)
        tail = pl.ds(pl.multiple_of(start + last, 128), half)
        members = (
            nn(x_a, qa_ref[0, :, lanes]) + nn(x_b, qb_ref[0, :, lanes]),
            nn(x_a, total_ref[0, :, lanes]) + nn(x_b, total_ref[1, :, lanes]),
            nn(x_a, total_ref[2, :, lanes]) + nn(x_b, total_ref[3, :, lanes]),
            nn(o_a, da_ref[:, tail]) + nn(o_b, db_ref[:, tail]),
        )
        for part in range(2):
            value = jnp.concatenate(members[part * 2 : part * 2 + 2], axis=1)
            place(outs, part, dy, value.astype(BF16).reshape(2, ZS, rows, width))


def attn_grad(pos_g, xa, xb, qa, qb, total, da, db):
    rows = xa.shape[3]
    return pl.pallas_call(
        attn_grad_kernel,
        out_shape=grad_shapes(rows, rows * BLOCKS),
        in_specs=[SMEM] + [HBM] * 2 + [VMEM] * 5,
        out_specs=[VMEM] * 4,
        scratch_shapes=[pltpu.VMEM((2, 2) + xa.shape[1:], BF16), pltpu.SemaphoreType.DMA((2,))],
        compiler_params=params(VMEM_MB),
        cost_estimate=cost(),
        name="attn_grad",
    )(pos_g, xa, xb, qa, qb, total, da, db)


def copy_kernel(plan, inputs, pos_ref, *refs):
    ins, outs, sems = refs[:inputs], refs[inputs:-1], refs[-1]
    copies = []
    for index, (out, to, source, at, size, by_z) in enumerate(plan):
        if by_z:
            z = pos_ref[0]
            to = flip(lax.div(z, 2), to // 2) * 2 + flip(lax.rem(z, 2), to % 2)
        copies.append(
            pltpu.make_async_copy(
                ins[source].at[pl.ds(at, size)], outs[out].at[pl.ds(to, size)], sems.at[index]
            )
        )
    for each in copies:
        each.start()
    for each in copies:
        each.wait()


def copy_blocks(pos, plan, inputs, sizes, name):
    piece = inputs[0].shape[1:]
    return pl.pallas_call(
        functools.partial(copy_kernel, plan, len(inputs)),
        out_shape=tuple(shape((size,) + piece, BF16) for size in sizes),
        in_specs=[SMEM] + [ANY] * len(inputs),
        out_specs=[VMEM] * len(sizes),
        scratch_shapes=[pltpu.SemaphoreType.DMA((len(plan),))],
        compiler_params=params(VMEM_MB),
        cost_estimate=cost(),
        name=name,
    )(pos, *inputs)


def pack_kernel(group, pos_ref, *refs):
    four, inner, outer = refs[:4], refs[4], refs[5]
    out, sem = refs[6], refs[7]
    rows, width = out.shape[1:]
    half = width // 2
    y = pos_ref[3]
    for j, chunk in enumerate(group):
        layer, kind = chunk // 3, chunk % 3
        for part in range(2):
            to = out.at[2 * j + part]
            if kind == 0:
                for side in range(2):
                    pltpu.make_async_copy(
                        four[2 * part + side].at[layer, :, pl.ds(pl.multiple_of(y * half, 128), half)],
                        to.at[:, pl.ds(side * half, half)],
                        sem,
                    ).start()
            elif kind == 1:
                lane = pl.multiple_of((2 * y + part) * width, 128)
                pltpu.make_async_copy(inner.at[layer, :, pl.ds(lane, width)], to, sem).start()
            else:
                row = pl.multiple_of((2 * y + part) * rows, 16)
                pltpu.make_async_copy(outer.at[layer, pl.ds(row, rows)], to, sem).start()
    wait_full(out, sem)


def pack_pieces(group, pos, weights):
    _, rows, width = weights[0].shape
    return pl.pallas_call(
        functools.partial(pack_kernel, group),
        out_shape=shape((2 * len(group), rows, width), BF16),
        in_specs=[SMEM] + [HBM] * 6,
        out_specs=VMEM,
        scratch_shapes=[pltpu.SemaphoreType.DMA],
        compiler_params=params(VMEM_MB),
        cost_estimate=cost(),
        name="pack",
    )(pos, *weights)


def table_kernel(at_ref, *refs):
    vectors, out = refs[:-1], refs[-1]
    width = out.shape[2]
    for index, vector in enumerate(vectors):
        size = vector.shape[1]
        start = at_ref[0] * size
        for piece in range(max(1, out.shape[1] - IB if index == IB else 1)):
            lanes = lax.broadcasted_iota(jnp.int32, (size, width), 1) + piece * width
            spot = lax.broadcasted_iota(jnp.int32, (size, width), 0) + start
            chosen = (lanes == spot).astype(F32).astype(BF16)
            out[:, index + piece, :] = nn(vector[...], chosen)


def vector_table(at, vectors, width):
    layers, last = vectors[-1].shape[0], vectors[-1].shape[1]
    rows = IB + last // vectors[0].shape[1]
    return pl.pallas_call(
        table_kernel,
        out_shape=shape((layers, rows, width), F32),
        in_specs=[SMEM] + [VMEM] * len(vectors),
        out_specs=VMEM,
        compiler_params=params(VMEM_MB),
        cost_estimate=cost(),
        name="vector_table",
    )(at, *vectors)


def finish_kernel(kind, offsets, pos_ref, *refs):
    layers = len(offsets)
    owns, gots = refs[:layers], refs[layers : 2 * layers]
    outs, buf, sems = refs[2 * layers : -2], refs[-2], refs[-1]
    rows, width = buf.shape[2:]
    half = width // 2
    y = pos_ref[3]
    copies = []
    for layer in range(layers):
        copies.append(
            pltpu.make_async_copy(
                gots[layer].at[pl.ds(offsets[layer], 2)], buf.at[layer], sems.at[layer]
            )
        )
        copies[-1].start()
    for side in range(2):
        yy = y if side == 0 else 1 - y
        if side:
            for each in copies:
                each.wait()
        for layer in range(layers):
            for part in range(2):
                value = (buf[layer, part] if side else owns[layer][part].astype(BF16)).astype(F32)
                if kind == 0:
                    lanes = pl.ds(pl.multiple_of(yy * half, 128), half)
                    for member in range(2):
                        outs[2 * part + member][layer, :, lanes] = value[
                            :, member * half : (member + 1) * half
                        ]
                elif kind == 1:
                    lane = pl.multiple_of((2 * yy + part) * width, 128)
                    outs[0][layer, :, pl.ds(lane, width)] = value
                else:
                    row = pl.multiple_of((2 * yy + part) * rows, 16)
                    outs[0][layer, pl.ds(row, rows), :] = value


def finish(kind, pos, results):
    layers = len(results)
    _, rows, width = results[0][0].shape
    outs = {
        0: (shape((layers, rows, width), F32),) * 4,
        1: (shape((layers, rows, 4 * width), F32),),
        2: (shape((layers, 4 * rows, width), F32),),
    }[kind]
    return pl.pallas_call(
        functools.partial(finish_kernel, kind, tuple(value[2] for value in results)),
        out_shape=outs,
        in_specs=[SMEM] + [VMEM] * layers + [ANY] * layers,
        out_specs=[VMEM] * len(outs),
        scratch_shapes=[
            pltpu.VMEM((layers, 2, rows, width), BF16),
            pltpu.SemaphoreType.DMA((layers,)),
        ],
        compiler_params=params(VMEM_MB),
        cost_estimate=cost(),
        name="finish",
    )(pos, *[value[0] for value in results], *[value[1] for value in results])


def sum_kernel(config, *refs):
    fresh, first, second, third, fourth, small = config
    refs = list(refs)

    def take(count):
        out = refs[:count]
        del refs[:count]
        return out

    sends = take(2) if fresh else None
    got_x, got_y = take(2) if first or second else (None, None)
    keeps = take(2) if first else None
    rests = take(2) if second else None
    pairs = take(2) if third else None
    lasts = take(2) if fourth else None
    tables = take(2 if small == 1 else 1) if small else None
    to_x, to_y = take(2) if fresh or first or fourth else (None, None)
    at = 0
    if fresh:
        for out, send in ((to_x, sends[0]), (to_y, sends[1])):
            for half in range(2):
                out[half * ZS : (half + 1) * ZS] = send[half]
        at = 2 * ZS
    got = 0
    if first:
        outs = take(2)
        for keep, come, rest, send in (
            (keeps[0], got_x, outs[0], to_y),
            (keeps[1], got_y, outs[1], to_x),
        ):
            rest[...] = (keep[0].astype(F32) + come[:ZS].astype(F32)).astype(BF16)
            send[at : at + ZS] = (keep[1].astype(F32) + come[ZS : 2 * ZS].astype(F32)).astype(BF16)
        got = 2 * ZS
        at += ZS
    if second:
        hold, to_z1 = take(2)
        for part, (rest, come) in enumerate(((rests[0], got_y), (rests[1], got_x))):
            for k in range(ZS):
                value = rest[k].astype(F32) + come[got + k].astype(F32)
                (to_z1 if k % 2 else hold)[k // 2 * 2 + part] = value.astype(BF16)
    if third:
        hold, to_z2 = take(2)
        for part in range(2):
            hold[part] = pairs[0][part].astype(F32) + pairs[1][part].astype(F32)
            value = pairs[0][2 + part].astype(F32) + pairs[1][2 + part].astype(F32)
            to_z2[part] = value.astype(BF16)
    if fourth:
        (total,) = take(1)
        value = lasts[0][...] + lasts[1][:2].astype(F32)
        total[...] = value
        to_y[at : at + 2] = value.astype(BF16)
    if small:
        come = (None, None, got_x, pairs and pairs[1], lasts and lasts[1])[small]
        come = tables[1][...] if small == 1 else come[come.shape[0] - 1]
        value = tables[0][...] + come.astype(F32)
        refs[0][...] = value
        to = (None, to_x, to_z1 if second else None, to_z2 if third else None, to_y)[small]
        to[to.shape[0] - 1] = value.astype(BF16)


def sum_round(fresh, got_x, got_y, first, second, third, fourth, small):
    stage, table = small
    config = tuple(value is not None for value in (fresh, first, second, third, fourth)) + (stage,)
    sample = fresh or first or second or third or fourth
    rows, width = sample[-1].shape[-2:]
    inputs, outputs = [], []
    if fresh is not None:
        inputs += [fresh[1], fresh[3]]
    if first is not None or second is not None:
        inputs += [got_x, got_y]
    for value in (first, second, third, fourth, table):
        if value is not None:
            inputs += list(value)
    going = 2 * ZS * config[0] + ZS * config[1]
    if config[0] or config[1] or config[4]:
        size_x, size_y = max(going, 1) + (stage == 1), going + 2 * config[4] + (stage == 4)
        outputs += [shape((size_x, rows, width), BF16), shape((size_y, rows, width), BF16)]
    if config[1]:
        outputs += [shape((ZS, rows, width), BF16)] * 2
    if config[2]:
        outputs += [shape((4, rows, width), BF16), shape((4 + (stage == 2), rows, width), BF16)]
    if config[3]:
        outputs += [shape((2, rows, width), F32), shape((2 + (stage == 3), rows, width), BF16)]
    if config[4]:
        outputs += [shape((2, rows, width), F32)]
    if config[5]:
        outputs += [shape(table[0].shape, F32)]
    outs = list(
        pl.pallas_call(
            functools.partial(sum_kernel, config),
            out_shape=tuple(outputs),
            in_specs=[VMEM] * len(inputs),
            out_specs=[VMEM] * len(outputs),
            compiler_params=params(VMEM_MB),
            cost_estimate=cost(),
            name="sum_round",
        )(*inputs)
    )

    def take(wanted, count):
        if not wanted:
            return None
        out = tuple(outs[:count])
        del outs[:count]
        return out

    sends = take(config[0] or config[1] or config[4], 2)
    return (
        sends,
        going,
        take(config[1], 2),
        take(config[2], 2),
        take(config[3], 2),
        take(config[4], 1),
        take(stage > 0, 1),
    )


def collect_kernel(*refs):
    out = refs[-1]
    for layer in range(out.shape[0]):
        query_ref, value_ref, head_ref, chain_ref = refs[4 * layer : 4 * layer + 4]
        out[layer] = chain_ref[...]
        out[layer, pl.ds(QB, 1), :] = query_ref[:1]
        out[layer, pl.ds(VB, 1), :] = value_ref[:1]
        for at, index in enumerate((FG, FS, UB)):
            out[layer, pl.ds(index, 1), :] = head_ref[at : at + 1]


def collect(vectors, rows):
    flat = [value for layer in vectors for value in layer]
    width = flat[0].shape[1]
    return pl.pallas_call(
        collect_kernel,
        out_shape=shape((len(vectors), rows, width), F32),
        in_specs=[VMEM] * len(flat),
        out_specs=VMEM,
        compiler_params=params(VMEM_MB),
        cost_estimate=cost(),
        name="collect",
    )(*flat)


def vectors_kernel(last, at_ref, table_ref, got_ref, *outs):
    layers, width = outs[0].shape[0], table_ref.shape[1]
    at = at_ref[0]
    for index, out in enumerate(outs):
        size = out.shape[1]
        start = at * size
        shift = lax.rem(width - lax.rem(start, width), width)
        for layer in range(layers):
            spot = pl.ds(layer * 16 + index + lax.div(start, width), 1)
            value = table_ref[spot, :]
            if last is not None:
                value = value.astype(BF16).astype(F32) + got_ref[spot, :]
            value = jnp.broadcast_to(value, (8, width))
            out[pl.ds(layer, 1), :] = pltpu.roll(value, shift, 1)[:1, :size]


def own_vectors(at, table, got, layers, size, wide):
    sizes = [size] * IB + [wide]
    last = None if got is None else 0
    return pl.pallas_call(
        functools.partial(vectors_kernel, last),
        out_shape=tuple(shape((layers, each), F32) for each in sizes),
        in_specs=[SMEM, VMEM, VMEM],
        out_specs=[VMEM] * len(sizes),
        compiler_params=params(VMEM_MB),
        cost_estimate=cost(),
        name="own_vectors",
    )(at, table, table if got is None else got)


def fence(values):
    return lax.optimization_barrier(values)


def build(mesh):
    count = mesh.shape["dp"]

    def flat(dp, seq):
        return dp * 2 + seq

    def pairs(source_of):
        out = []
        for dp in range(count):
            for seq in range(2):
                out.append((flat(*source_of(dp, seq)), flat(dp, seq)))
        return out

    swap_pairs = pairs(lambda dp, seq: (dp // 2 * 2 + seq, dp % 2))
    core_pairs = pairs(lambda dp, seq: (dp ^ 1, seq))
    x_pairs = pairs(lambda dp, seq: (dp ^ 2, seq))
    y_pairs = pairs(lambda dp, seq: (dp, 1 - seq))
    z_pairs = [pairs(lambda dp, seq, k=k: ((dp // 4 ^ k) * 4 + dp % 4, seq)) for k in (1, 2)]

    def move(value, perm):
        return lax.ppermute(value, AXES, perm)

    return dict(
        count=count,
        swap=swap_pairs,
        core=core_pairs,
        x=x_pairs,
        y=y_pairs,
        z1=z_pairs[0],
        z2=z_pairs[1],
        move=move,
    )


def body(
    net,
    tokens,
    segment_ids,
    padding,
    query_weight,
    key_weight,
    value_weight,
    output_weight,
    query_bias,
    value_bias,
    output_bias,
    attn_gain,
    attn_shift,
    inner_weight,
    inner_bias,
    outer_weight,
    outer_bias,
    ffn_gain,
    ffn_shift,
    upstream,
):
    layers, small, width = query_weight.shape
    hidden = inner_weight.shape[2]
    count = net["count"]
    move = net["move"]
    staged = count == BLOCKS and small == 16 * layers
    dp = lax.axis_index("dp").astype(jnp.int32)
    y = lax.axis_index("seq").astype(jnp.int32)
    core = lax.rem(dp, 2)
    if staged:
        pos_g = jnp.stack([lax.div(dp, 4), lax.rem(lax.div(dp, 2), 2), core, y])
        pos_w = pos_g
    else:
        zero = jnp.zeros((), jnp.int32)
        pos_g = jnp.stack([zero, zero, core, zero])
        pos_w = jnp.stack([zero, zero, zero, zero])

    labels = jnp.where(padding == 1, segment_ids, -1)
    small_own = move(jnp.concatenate([segment_ids, labels]), net["swap"])
    token_low = move(tokens[0], net["swap"])

    vector_args = [query_bias, value_bias, output_bias, attn_gain, attn_shift, outer_bias]
    vector_args += [ffn_gain, ffn_shift, inner_bias]
    table = vector_table(dp[None], vector_args, width)
    if staged:
        table = table + move(table, net["x"])
    else:
        table = lax.psum(table, "dp")

    raw = (query_weight, key_weight, value_weight, output_weight, inner_weight, outer_weight)
    chunks = []
    for layer in range(layers):
        four = (query_weight[layer], key_weight[layer], value_weight[layer], output_weight[layer])
        if not staged:
            full = [lax.all_gather(value, "dp", axis=0, tiled=True) for value in four]
            inner = lax.all_gather(inner_weight[layer], "dp", axis=0, tiled=True)
            outer = lax.all_gather(outer_weight[layer], "dp", axis=0, tiled=True)
            rows = width // BLOCKS

            def cut(value, dy, dx, dc):
                value = value.reshape(ZS, 2, 2, rows, 2, -1)
                return value[:, dx, dc, :, dy, :]

            lists = [[[], []], [[], []], [[], []]]
            for dc in range(2):
                for part, dy, dx in UNITS:
                    lists[0][dc].append(
                        jnp.concatenate([cut(value, dy, dx, dc) for value in full[part * 2 : part * 2 + 2]], axis=2)
                    )
                    lists[1][dc].append(cut(inner, dy, dx, dc)[..., part * width : (part + 1) * width])
                    lists[2][dc].append(
                        outer.reshape(ZS, 2, 2, 2, 2, hidden // BLOCKS // 4, width)[:, dx, dc, dy, part]
                    )
            chunks.extend(tuple(jnp.concatenate(side) for side in value) for value in lists)

    total_chunks = 3 * layers
    groups = []
    if staged:
        edges = [0, 1, 2] + list(range(3, total_chunks + 1, 3))
        groups = [range(low, high) for low, high in zip(edges[:-1], edges[1:])]
    where_of = {i: (g, i - group[0]) for g, group in enumerate(groups) for i in group}
    stage_z = [None] * len(groups)

    def start_z2(g):
        own = pack_pieces(groups[g], pos_g, raw)
        stage_z[g] = (own, move(own, net["z2"]))

    def start_z1(g):
        own, come = stage_z[g]
        size = own.shape[0]
        both = copy_blocks(
            pos_g,
            [(0, 0, 0, 0, size, False), (0, size, 1, 0, size, False)],
            (own, come),
            [2 * size],
            "gather_z",
        )[0]
        stage_z[g] = (both, move(both, net["z1"]))

    if staged:
        start_z2(0)
        stage_z[0], raw, table, small_own, token_low = fence(
            (stage_z[0], raw, table, small_own, token_low)
        )
        start_z1(0)
        start_z2(1)
        table = table + move(table, net["core"])
    small_other = move(small_own, net["core"])
    token_other = move(token_low, net["core"])
    if staged:
        stage_z[:2], raw, table, small_own, small_other, token_low, token_other, upstream = fence(
            (stage_z[:2], raw, table, small_own, small_other, token_low, token_other, upstream)
        )
    seg = small_own[0:1]
    lab = jnp.concatenate([small_own[1], small_other[1]])[:, None]
    current = token_low.astype(F32)
    other = token_other
    kept = [None] * layers
    todo = []
    for layer in range(layers):
        todo.append(("attn", layer, 3 * layer))
        todo.append(("inner", layer, 3 * layer + 1))
        todo.append(("outer", layer, 3 * layer + 2))
    low = None
    attn_out = None
    arrived = 0 if staged else total_chunks

    mid = None

    def compute():
        nonlocal current, other, low, attn_out, mid, head
        if not todo or todo[0][2] >= arrived:
            return
        kind, layer, _ = todo.pop(0)
        vec = table[layer]
        if kind == "attn":
            attn_out = attn_forward(pos_w, pos_g, current, other, seg, lab, vec, chunks[3 * layer])
            return
        h, n1, c1, q, kt, v, p, xoh, far_xoh = attn_out
        if kind == "inner":
            active, gp, gt, far_gt = inner_forward(pos_w, pos_g, h, vec, chunks[3 * layer + 1])
            mid = (active, gp, gt, move(far_gt, net["core"]), move(far_xoh, net["core"]))
            return
        active, gp, gt, far_gt, far_xoh = mid
        last = layer + 1 == layers
        current, low, *rest = outer_forward(
            pos_w, h, active, vec, chunks[3 * layer + 2], upstream if last else None
        )
        if last:
            head, rest = rest, (None, None)
        else:
            other = move(low, net["core"])
        kept[layer] = (n1, c1, q, kt, v, p, *rest, gp, xoh, gt, far_xoh, far_gt)

    head = None
    if not staged:
        upstream = move(upstream[0], net["swap"])
    if staged:
        sent, got = {}, {}
        zplan = {
            -LAG: [(1, 1), (2, 2)],
            -LAG + 1: [(1, 2), (2, 3)],
            -LAG + 2: [(1, 3)],
            -LAG + 3: [(2, 4)],
            -LAG + 4: [(1, 4)],
        }
        spread = [net["z2"], net["z1"]]
        for r in range(-LAG, total_chunks + LAG):
            inputs, plan = [], []
            sizes = [0, 0]
            use = lambda value: (inputs.append(value), len(inputs) - 1)[1]
            fresh = r + LAG < total_chunks
            if fresh:
                g, j = where_of[r + LAG]
                n = len(groups[g])
                mine, theirs = use(stage_z[g][0]), use(stage_z[g][1])
                for out, part in ((0, 1), (1, 0)):
                    for k, (source, slot) in enumerate(((mine, 0), (theirs, 0), (mine, 1), (theirs, 1))):
                        plan.append((out, k, source, (slot * n + j) * 2 + part, 1, True))
                    sizes[out] = ZS
            before = r - LAG
            home = 0 <= before < total_chunks
            if before >= -LAG and (r < total_chunks or home):
                sx, sy = use(sent[before][0]), use(sent[before][1])
                rx, ry = use(got[before][0]), use(got[before][1])
                first = ZS if before + LAG < total_chunks else 0
                if r < total_chunks:
                    for out, send, come in ((0, sy, ry), (1, sx, rx)):
                        plan.append((out, sizes[out], send, 0, ZS, False))
                        plan.append((out, sizes[out] + ZS, come, 0, ZS, False))
                        sizes[out] += 2 * ZS
                if home:
                    sizes.append(8 * ZS)
                    slot = 2
                    for at, (send, come) in enumerate(((sx, rx), (sy, ry))):
                        plan.append((slot, at * 4 * ZS, send, first, 2 * ZS, False))
                        plan.append((slot, at * 4 * ZS + 2 * ZS, come, first, 2 * ZS, False))
            live = [index for index, size in enumerate(sizes) if size]
            outs = copy_blocks(
                pos_g,
                [(live.index(each[0]),) + each[1:] for each in plan],
                inputs,
                [sizes[index] for index in live],
                "gather_round",
            )
            outs = dict(zip(live, outs))
            if 0 in outs:
                sent[r] = (outs[0], outs[1])
                got[r] = (move(outs[0], net["x"]), move(outs[1], net["y"]))
            core_pair = None
            if home:
                core_pair = (outs[2], move(outs[2], net["core"]))
            for stage, g in zplan.get(r, ()):
                if g < len(groups):
                    (start_z2 if stage == 2 else start_z1)(g)
            if spread:
                table = table + move(table, spread.pop(0))
            if r == total_chunks - 1:
                upstream = move(upstream[0], net["swap"])
            compute()
            ready = r + 1 - LAG
            state = (got.get(ready), core_pair, stage_z, current, other, attn_out, raw, table, upstream, mid)
            state = fence(state)
            if ready in got:
                got[ready] = state[0]
            if home:
                chunks.append(state[1])
                arrived += 1
            stage_z, current, other, attn_out, raw, table, upstream, mid = (list(state[2]),) + tuple(state[3:])
    while todo:
        compute()
    range_ids = jnp.arange(SEGS, dtype=jnp.int32)
    own = (small_own[1][None, :] == range_ids[:, None]).astype(F32)
    sums = jnp.dot(own, current, precision=lax.Precision.HIGHEST)
    pool_sums = sums
    counts = jnp.sum((lab[:, 0][None, :] == range_ids[:, None]).astype(F32), axis=1)
    loose = {}
    if staged:
        loose["hidden"] = move(low, net["swap"])
        loose["pool"] = pool_sums + move(pool_sums, net["core"])

    parts = []
    vectors = [None] * layers
    rounds = []
    ends = []
    table_stage = 1

    def side_work():
        step = len(rounds)
        last = total_chunks
        if step == 0:
            loose["pooled"] = move(loose.pop("pool") / counts[:, None], net["swap"])
        if step == last + 2:
            loose["grad"] = move(loose.pop("grad"), net["swap"])

    def settle(state):
        return fence(state)

    def advance(fresh, state):
        if not staged:
            if fresh is not None:
                parts.append(fresh)
            return state(()) if callable(state) else state
        side_work()
        s = len(rounds)
        past = rounds[s - LAG] if s >= LAG else {}
        pick = lambda key: past.get(key)
        has_home = pick("first") is not None or pick("second") is not None
        sends, going, first, second, third, fourth, small = sum_round(
            fresh,
            pick("got_x") if has_home else None,
            pick("got_y") if has_home else None,
            pick("first"),
            pick("second"),
            pick("third"),
            pick("fourth"),
            loose.pop("small", (0, None)),
        )
        now = {}
        if fresh is not None:
            now["first"] = (fresh[0], fresh[2])
        if first is not None:
            now["second"] = first
        if sends is not None:
            if going:
                now["got_x"] = move(sends[0], net["x"])
            now["got_y"] = move(sends[1], net["y"])
        if second is not None:
            now["third"] = (second[0], move(second[1], net["z1"]))
        if third is not None:
            now["fourth"] = (third[0], move(third[1], net["z2"]))
        if fourth is not None:
            now["total"] = fourth[0]
            ends.append(going)
        if "vectors" in loose:
            small = loose.pop("vectors").reshape(-1, width)
            loose["small"] = (1, (small, move(small, net["core"])))
        elif small is not None:
            nonlocal table_stage
            table_stage += 1
            loose["small"] = (table_stage, small)
        if callable(state):
            state = state(sends)
        rounds.append(now)
        ready = s + 1 - LAG
        if ready < 0:
            return fence(state)
        rounds[ready], state = fence((rounds[ready], state))
        return state

    top = layers - 1
    attn_parts = None
    dyl, dy, head_sums = head
    for layer in reversed(range(layers)):
        attn_bufs, inner_bufs, outer_bufs = chunks[3 * layer : 3 * layer + 3]
        n1, c1, q, kt, v, p, n2, c2, gp, xoh, gt, far_xoh, far_gt = kept[layer]
        got_dyl = move(dyl, net["core"])
        chain_args = (pos_w, dyl, dy, gp, n1, c1, table[layer], inner_bufs, outer_bufs, attn_bufs)
        if layer == top:
            outer_parts = settle(outer_grad(gt, far_gt, dyl, got_dyl))

            def first_chain(sends):
                pack, da, do, sums = chain_backward(*chain_args, after=sends)
                got_pack = move(pack, net["core"])
                inner_parts = inner_grad(pos_g, xoh, far_xoh, pack, got_pack)
                return pack, da, do, sums, got_pack, inner_parts

            pack, da, do, sums, got_pack, inner_parts = advance(outer_parts, first_chain)
            back, qsum = attn_backward(q, kt, v, p, do)
        else:
            pack, da, do, sums = chain_backward(*chain_args)
            outer_parts = outer_grad(gt, far_gt, dyl, got_dyl)
            state = advance(attn_parts, (pack, da, do, sums, outer_parts))
            pack, da, do, sums, outer_parts = state
            got_pack = move(pack, net["core"])
            back, qsum = attn_backward(q, kt, v, p, do)
            inner_parts = inner_grad(pos_g, xoh, far_xoh, pack, got_pack)
            state = advance(outer_parts, (back, qsum, got_pack, inner_parts))
            back, qsum, got_pack, inner_parts = state
        got_back = move(back, net["core"])
        below = None if layer == 0 else (kept[layer - 1][6], kept[layer - 1][7], table[layer - 1])
        total, vsum, *head = input_backward(pos_w, da, back, got_back, attn_bufs, below)
        attn_parts = attn_grad(pos_g, xoh, far_xoh, back, got_back, total, pack, got_pack)
        vectors[layer] = (qsum, vsum, head_sums, sums)
        attn_parts, head, vectors[layer] = advance(inner_parts, (attn_parts, head, vectors[layer]))
        if layer:
            dyl, dy, head_sums = head
    grad = head[0]
    vectors = collect(vectors, 16)
    loose["vectors"], loose["grad"] = vectors, grad
    advance(attn_parts, None)
    results = []
    if staged:
        for _ in range(4 * LAG):
            advance(None, None)
        for s, now in enumerate(rounds):
            if "total" in now:
                results.append((now["total"], now["got_y"], ends[len(results)]))

    if staged:
        stacked = []
        for kind, first in ((0, 2), (1, 1), (2, 0)):
            stacked += list(finish(kind, pos_g, results[first::3][::-1]))
        hidden_out, pooled, tokens_grad = (loose[key] for key in ("hidden", "pooled", "grad"))
        vectors = loose["small"][1][0]
        got_vectors = rounds[-1]["got_y"][-1].astype(F32)
    else:
        collected = [None] * layers
        for place_at, layer in enumerate(reversed(range(layers))):
            outer_parts, inner_parts, attn_parts = parts[3 * place_at : 3 * place_at + 3]

            def spread(outs):
                a_keep, a_send, b_keep, b_send = outs
                a = jnp.stack([a_keep, a_send])
                b = jnp.stack([b_keep, b_send], axis=1)
                return jnp.stack([a, b], axis=2)

            def total(out):
                out = out.reshape(ZS * 2, 1, out.shape[2], out.shape[3])
                mine = (jnp.arange(2, dtype=jnp.int32) == core)[None, :, None, None]
                out = jnp.where(mine, out, jnp.zeros_like(out)).reshape(-1, out.shape[-1])
                out = lax.psum_scatter(out, "dp", scatter_dimension=0, tiled=True)
                return lax.psum(out.astype(F32), "seq")

            outer = spread(outer_parts).transpose(3, 0, 1, 2, 4, 5)
            outer = total(outer.reshape(ZS, 2, -1, width))
            inner = spread(inner_parts).transpose(3, 0, 4, 1, 2, 5)
            inner = total(inner.reshape(ZS, 2, inner.shape[2], -1))
            attn = spread(attn_parts)
            attn = attn.reshape(attn.shape[:5] + (2, width // 2)).transpose(2, 5, 3, 0, 4, 1, 6)
            attn = attn.reshape(4, ZS, 2, attn.shape[4], width)
            four = [total(attn[index]) for index in range(4)]
            collected[layer] = four + [inner, outer]
        stacked = [
            jnp.stack([collected[layer][member] for layer in range(layers)]) for member in range(6)
        ]
        hidden_out = move(low, net["swap"])
        pooled = move((pool_sums + move(pool_sums, net["core"])) / counts[:, None], net["swap"])
        tokens_grad = move(grad, net["swap"])
        vectors = lax.psum(vectors, AXES).reshape(-1, width)
        got_vectors = None
    own = own_vectors(dp[None], vectors, got_vectors, layers, small, hidden // count)
    return (
        hidden_out[None],
        pooled[None],
        tokens_grad.astype(F32)[None],
        stacked[0],
        stacked[1],
        stacked[2],
        stacked[3],
        own[QB],
        own[VB],
        own[OB],
        own[AG],
        own[AS],
        stacked[4],
        own[IB],
        stacked[5],
        own[UB],
        own[FG],
        own[FS],
    )


def solution(mesh):
    cube = P(None, "dp", None)
    flat = P(None, "dp")
    acts = P("dp", "seq", None)
    ids = P("dp", "seq")
    return jax.shard_map(
        functools.partial(body, build(mesh)),
        mesh=mesh,
        in_specs=(acts, ids, ids, cube, cube, cube, cube, flat, flat, flat, flat, flat, cube, flat, cube)
        + (flat, flat, flat, acts),
        out_specs=(acts, P("dp", None, None), acts, cube, cube, cube, cube)
        + (flat, flat, flat, flat, flat, cube, flat, cube, flat, flat, flat),
        check_vma=False,
    )
```

```python
import functools

import jax
import jax.numpy as jnp
from jax import lax
from jax.experimental import pallas as pl
from jax.experimental.pallas import tpu as pltpu
from jax.sharding import PartitionSpec as P

HD = 64
SEGS = 4
BLOCKS = 16
ZS = 4
LAG = 1
VMEM_MB = 24
EPS = 1e-06
MASKED = -1e30
AXES = ("dp", "seq")
F32 = jnp.float32
BF16 = jnp.bfloat16
MB = 1024 * 1024

QB, VB, OB, AG, AS, UB, FG, FS, IB = range(9)


def nn(left, right):
    return lax.dot_general(left, right, (((1,), (0,)), ((), ())), preferred_element_type=F32)


def nt(left, right):
    return lax.dot_general(left, right, (((1,), (1,)), ((), ())), preferred_element_type=F32)


def params(vmem):
    return pltpu.CompilerParams(vmem_limit_bytes=vmem * MB)


def cost():
    return pl.CostEstimate(flops=1, bytes_accessed=1, transcendentals=0)


def load(source, target, sem):
    pltpu.make_async_copy(source, target, sem).start()


VMEM = pl.BlockSpec(memory_space=pltpu.VMEM)
SMEM = pl.BlockSpec(memory_space=pltpu.SMEM)
ANY = pl.BlockSpec(memory_space=pl.ANY)
HBM = pl.BlockSpec(memory_space=pltpu.HBM)


def shape(dims, dtype):
    return jax.ShapeDtypeStruct(dims, dtype)


def flip(value, bit):
    return value + bit - 2 * value * bit


def block_at(pos_ref, k, dx, dc):
    z, x, c = pos_ref[0], pos_ref[1], pos_ref[2]
    low = lax.rem(z, 2)
    zz = flip(lax.div(z, 2), k // 2) * 2 + flip(low, k % 2)
    return (zz * 2 + flip(x, dx)) * 2 + flip(c, dc)


def half_at(pos_ref, dy):
    return flip(pos_ref[3], dy)


UNITS = (
    (0, 0, 0),
    (0, 1, 0),
    (0, 0, 1),
    (0, 1, 1),
    (1, 0, 0),
    (1, 0, 1),
    (1, 1, 0),
    (1, 1, 1),
)


def each_unit(pos_ref, bufs):
    for dc in range(2):
        for unit, (part, dy, dx) in enumerate(UNITS):
            at = flip(pos_ref[1], dx) * 2 + flip(pos_ref[2], dc)
            yield bufs[dc].at[pl.ds(unit * ZS, ZS)], part, dy, at


def fetch_member(pos_ref, bufs, member, full_ref, sem):
    half = full_ref.shape[3] // 2
    for unit, part, dy, at in each_unit(pos_ref, bufs):
        if part == member // 2:
            col = pl.multiple_of(half_at(pos_ref, dy) * half, 128)
            load(
                unit.at[:, :, pl.ds(member % 2 * half, half)],
                full_ref.at[:, at, :, pl.ds(col, half)],
                sem,
            )


def fetch_columns(pos_ref, bufs, full_ref, sem):
    width = full_ref.shape[3] // 4
    for unit, part, dy, at in each_unit(pos_ref, bufs):
        col = pl.multiple_of((half_at(pos_ref, dy) * 2 + part) * width, 128)
        load(unit, full_ref.at[:, at, :, pl.ds(col, width)], sem)


def fetch_rows(pos_ref, bufs, full_ref, sem):
    for unit, part, dy, at in each_unit(pos_ref, bufs):
        load(unit, full_ref.at[:, at, half_at(pos_ref, dy) * 2 + part], sem)


def flat(values):
    return values.reshape(-1, values.shape[-1])


def square(width):
    return pltpu.VMEM((ZS, BLOCKS // ZS, width // BLOCKS, width), BF16)


def wide_matrix(width, hidden):
    return pltpu.VMEM((ZS, BLOCKS // ZS, width // BLOCKS, hidden), BF16)


def tall_matrix(hidden, width):
    return pltpu.VMEM((ZS, BLOCKS // ZS, 4, hidden // BLOCKS // 4, width), BF16)


def wait_full(full_ref, sem):
    pltpu.make_async_copy(full_ref, full_ref, sem).wait()


def export_rows(pos_ref, wide_ref, outs, index):
    rows = outs[0].shape[3]
    for dc in range(2):
        for dx in range(2):
            for k in range(ZS):
                row = pl.multiple_of(block_at(pos_ref, k, dx, dc) * rows, 16)
                outs[dc][index, dx, k] = wide_ref[pl.ds(row, rows), :]


def export_halves(pos_ref, wide_ref, outs):
    rows = outs[0].shape[4]
    for dc in range(2):
        for dx in range(2):
            for dy in range(2):
                for k in range(ZS):
                    block = block_at(pos_ref, k, dx, dc) * 2 + half_at(pos_ref, dy)
                    for part in range(2):
                        row = pl.multiple_of((block * 2 + part) * rows, 16)
                        outs[dc][dx, dy, part, k] = wide_ref[pl.ds(row, rows), :]


def mean_of(values):
    return jnp.mean(values, axis=-1, keepdims=True)


def normalize(values):
    center = values - mean_of(values)
    inverse = lax.rsqrt(mean_of(center * center) + EPS)
    return center * inverse, inverse


def norm_back(normed, inverse, scaled):
    return inverse * (scaled - mean_of(scaled) - normed * mean_of(scaled * normed))


def colsum(values):
    return jnp.sum(values, axis=0, keepdims=True)


def row_of(vec_ref, index):
    return vec_ref[pl.ds(index, 1), :]


def attn_kernel(*refs):
    pos_w, pos_g = refs[0], refs[1]
    x_ref, xp_ref, seg_ref, lab_ref, vec_ref = refs[2:7]
    bufs = refs[7:9]
    h_ref = refs[9]
    kept = refs[10:18]
    wq, wk, wv, wo, rows_ref, vt_ref, wide_ref, bias_ref, k_ref = refs[18:27]
    held = refs[27:35]
    n1_ref, c1_ref, q_ref, kt_ref, v_ref, p_ref = held[:6]
    exports = held[6:]
    sems, store_sems = refs[35:]

    def store(index):
        load(held[index], kept[index], store_sems.at[index])

    tokens, width = x_ref.shape
    for member, full in enumerate((wq, wk, wv, wo)):
        fetch_member(pos_w, bufs, member, full, sems.at[member])
    bias_ref[...] = jnp.where(lab_ref[...] == seg_ref[...], 0.0, MASKED)
    low = x_ref[...].astype(BF16)
    rows_ref[:tokens] = low
    rows_ref[tokens:] = xp_ref[...]
    wide_ref[...] = low.T
    export_rows(pos_g, wide_ref, exports, 0)
    wait_full(wq, sems.at[0])
    query = (nn(low, flat(wq[...])) + row_of(vec_ref, QB)).astype(BF16)
    q_ref[...] = (query.astype(F32) * HD ** (-0.5)).astype(BF16)
    wait_full(wk, sems.at[1])
    key = nn(rows_ref[...], flat(wk[...])).astype(BF16)
    k_ref[...] = key
    kt_ref[...] = key.T
    store(2)
    store(3)
    wait_full(wv, sems.at[2])
    value = (nn(rows_ref[...], flat(wv[...])) + row_of(vec_ref, VB)).astype(BF16)
    v_ref[...] = value
    vt_ref[...] = value.T
    store(4)

    def pair(index, carry):
        lane = pl.multiple_of(index * 128, 128)
        keys = k_ref[:, pl.ds(lane, 128)]
        queries = q_ref[:, pl.ds(lane, 128)]
        first = lax.broadcasted_iota(jnp.int32, queries.shape, 1) < HD
        for which in range(2):
            mine = jnp.where(first if which == 0 else ~first, queries, jnp.zeros_like(queries))
            scores = nt(keys, mine) + bias_ref[...]
            expos = jnp.exp(scores - jnp.max(scores, axis=0, keepdims=True))
            probs = (expos * (1.0 / jnp.sum(expos, axis=0, keepdims=True))).astype(BF16)
            p_ref[index * 2 + which] = probs
            row = pl.multiple_of(index * 128 + which * HD, HD)
            wide_ref[pl.ds(row, HD), :] = nn(vt_ref[pl.ds(row, HD), :], probs).astype(BF16)
        both = pl.ds(index * 2, 2)
        load(p_ref.at[both], kept[5].at[both], store_sems.at[5])
        return carry

    lax.fori_loop(0, width // 128, pair, 0)
    export_rows(pos_g, wide_ref, exports, 1)
    mixed = wide_ref[...].T
    wait_full(wo, sems.at[3])
    branch = nn(mixed, flat(wo[...])) + row_of(vec_ref, OB)
    normed, inverse = normalize(x_ref[...] + branch)
    hidden = normed * row_of(vec_ref, AG) + row_of(vec_ref, AS)
    h_ref[...] = hidden
    n1_ref[...] = normed
    c1_ref[...] = jnp.broadcast_to(inverse, c1_ref.shape)
    wide_ref[...] = hidden.astype(BF16).T
    export_rows(pos_g, wide_ref, exports, 2)
    for index in (0, 1, 6, 7):
        store(index)
    for index in range(8):
        wait_full(held[index], store_sems.at[index])


def attn_forward(pos_w, pos_g, x, xp, seg, lab, vec, bufs):
    tokens, width = x.shape
    heads = width // HD
    export = shape((3, 2, ZS, width // BLOCKS, tokens), BF16)
    kept = (
        shape((tokens, width), F32),
        shape((tokens, 128), F32),
        shape((tokens, width), BF16),
        shape((width, 2 * tokens), BF16),
        shape((2 * tokens, width), BF16),
        shape((heads, 2 * tokens, tokens), BF16),
        export,
        export,
    )
    return pl.pallas_call(
        attn_kernel,
        out_shape=(shape((tokens, width), F32),) + kept,
        in_specs=[SMEM, SMEM] + [VMEM] * 5 + [ANY] * 2,
        out_specs=[VMEM] + [HBM] * 8,
        scratch_shapes=[square(width)] * 4
        + [
            pltpu.VMEM((2 * tokens, width), BF16),
            pltpu.VMEM((width, 2 * tokens), BF16),
            pltpu.VMEM((width, tokens), BF16),
            pltpu.VMEM((2 * tokens, tokens), F32),
            pltpu.VMEM((2 * tokens, width), BF16),
        ]
        + [pltpu.VMEM(each.shape, each.dtype) for each in kept]
        + [pltpu.SemaphoreType.DMA((4,)), pltpu.SemaphoreType.DMA((8,))],
        compiler_params=params(VMEM_MB),
        cost_estimate=cost(),
        name="attn_forward",
    )(pos_w, pos_g, x, xp, seg, lab, vec, *bufs)


def head_back(grad, normed, inverse, gain, low_ref, back_ref, sums_ref):
    sums_ref[...] = jnp.zeros_like(sums_ref)
    sums_ref[pl.ds(0, 1), :] = colsum(grad * normed)
    sums_ref[pl.ds(1, 1), :] = colsum(grad)
    back = norm_back(normed, inverse, grad * gain)
    low = back.astype(BF16)
    low_ref[...] = low
    back_ref[...] = back
    sums_ref[pl.ds(2, 1), :] = colsum(low.astype(F32))


def head_shapes(tokens, width):
    return (
        shape((tokens, width), BF16),
        shape((tokens, width), F32),
        shape((8, width), F32),
    )


def inner_kernel(tile, *refs):
    pos_w, pos_g, h_ref, vec_ref = refs[:4]
    bufs, active_ref, kept = refs[4:6], refs[6], refs[7:10]
    wi, low_ref, wide_ref = refs[10:13]
    held = refs[13:16]
    gp_ref, exports = held[0], held[1:]
    sem, store_sems = refs[16:]
    width, hidden = h_ref.shape[1], wi.shape[3]
    fetch_columns(pos_w, bufs, wi, sem)
    low_ref[...] = h_ref[...].astype(BF16)
    wait_full(wi, sem)
    per_row = width // tile

    def step(index, carry):
        lanes = pl.ds(pl.multiple_of(index * tile, tile), tile)
        bias = vec_ref[pl.ds(IB + lax.div(index, per_row), 1), :]
        part = lax.rem(index, per_row)
        chosen = bias[:, :tile]
        for other in range(1, per_row):
            chosen = jnp.where(part == other, bias[:, other * tile : (other + 1) * tile], chosen)
        pre = nn(low_ref[...], flat(wi[:, :, :, lanes])) + chosen
        phi = 0.5 * (1.0 + lax.erf(pre * 0.7071067811865476))
        dens = jnp.exp(-0.5 * pre * pre) * 0.3989422804014327
        gp_ref[:, lanes] = (phi + pre * dens).astype(BF16)
        active = (pre * phi).astype(BF16)
        active_ref[:, lanes] = active
        wide_ref[lanes, :] = active.T
        return carry

    lax.fori_loop(0, hidden // tile, step, 0)
    load(held[0], kept[0], store_sems.at[0])
    export_halves(pos_g, wide_ref, exports)
    for index in (1, 2):
        load(held[index], kept[index], store_sems.at[index])
    for index in range(3):
        wait_full(held[index], store_sems.at[index])


def inner_forward(pos_w, pos_g, h, vec, bufs):
    tokens, width = h.shape
    hidden = bufs[0].shape[2] * 4
    export = shape((2, 2, 2, ZS, hidden // BLOCKS // 4, tokens), BF16)
    kept = (shape((tokens, hidden), BF16), export, export)
    return pl.pallas_call(
        functools.partial(inner_kernel, 384),
        out_shape=(shape((tokens, hidden), BF16),) + kept,
        in_specs=[SMEM, SMEM, VMEM, VMEM] + [ANY] * 2,
        out_specs=[VMEM] + [HBM] * 3,
        scratch_shapes=[
            wide_matrix(width, hidden),
            pltpu.VMEM((tokens, width), BF16),
            pltpu.VMEM((hidden, tokens), BF16),
        ]
        + [pltpu.VMEM(each.shape, each.dtype) for each in kept]
        + [pltpu.SemaphoreType.DMA, pltpu.SemaphoreType.DMA((3,))],
        compiler_params=params(VMEM_MB),
        cost_estimate=cost(),
        name="inner_forward",
    )(pos_w, pos_g, h, vec, *bufs)


def outer_kernel(last, *refs):
    pos_w, h_ref, active_ref, vec_ref = refs[:4]
    grad_ref = refs[4] if last else None
    refs = refs[4 + last :]
    bufs = refs[:2]
    outs, wu, acc_ref, sem = refs[2:-3], refs[-3], refs[-2], refs[-1]
    fetch_rows(pos_w, bufs, wu, sem)
    acc_ref[...] = h_ref[...] + row_of(vec_ref, UB)
    wait_full(wu, sem)
    tile = active_ref.shape[1] // ZS
    for z in range(ZS):
        acc_ref[...] += nn(active_ref[:, pl.ds(z * tile, tile)], flat(wu[z]))
    normed, inverse = normalize(acc_ref[...])
    result = normed * row_of(vec_ref, FG) + row_of(vec_ref, FS)
    outs[0][...] = result
    outs[1][...] = result.astype(BF16)
    if last:
        head_back(
            grad_ref[...].astype(F32), normed, inverse, row_of(vec_ref, FG), outs[2], outs[3], outs[4]
        )
    else:
        outs[2][...] = normed
        outs[3][...] = jnp.broadcast_to(inverse, outs[3].shape)


def outer_forward(pos_w, h, active, vec, bufs, grad):
    tokens, width = h.shape
    hidden = active.shape[1]
    last = grad is not None
    outs = (shape((tokens, width), F32), shape((tokens, width), BF16))
    if last:
        outs += head_shapes(tokens, width)
    else:
        outs += (shape((tokens, width), F32), shape((tokens, 128), F32))
    return pl.pallas_call(
        functools.partial(outer_kernel, int(last)),
        out_shape=outs,
        in_specs=[SMEM] + [VMEM] * (3 + last) + [ANY] * 2,
        out_specs=[VMEM] * len(outs),
        scratch_shapes=[
            tall_matrix(hidden, width),
            pltpu.VMEM((tokens, width), F32),
            pltpu.SemaphoreType.DMA,
        ],
        compiler_params=params(VMEM_MB),
        cost_estimate=cost(),
        name="outer_forward",
    )(pos_w, h, active, vec, *((grad,) if last else ()), *bufs)


def chain_kernel(tile, waits, *refs):
    pos_w, dyl_ref, dy_ref = refs[:3]
    sources, vec_ref = refs[3:6], refs[6]
    inner_bufs, outer_bufs, attn_bufs = refs[7:9], refs[9:11], refs[11:13]
    refs = refs[13 + waits :]
    pack_ref, da_ref, do_ref, sums_ref = refs[:4]
    wi, wu, wo, acc_ref = refs[4:8]
    held = refs[8:11]
    gp_ref, n1_ref, c1_ref = held
    sems, load_sems = refs[11:]
    width, hidden = dy_ref.shape[1], wi.shape[3]
    for index in range(3):
        load(sources[index], held[index], load_sems.at[index])
    du_ref = pack_ref.at[:, pl.ds(0, hidden)]
    dal_ref = pack_ref.at[:, pl.ds(hidden, width)]
    fetch_rows(pos_w, outer_bufs, wu, sems.at[0])
    fetch_columns(pos_w, inner_bufs, wi, sems.at[1])
    fetch_member(pos_w, attn_bufs, 3, wo, sems.at[2])
    sums_ref[...] = jnp.zeros_like(sums_ref)
    acc_ref[...] = dy_ref[...]
    wait_full(gp_ref, load_sems.at[0])
    wait_full(wu, sems.at[0])
    wait_full(wi, sems.at[1])
    per_row = width // tile

    for index in range(hidden // tile):
        lane = index * tile
        rows = wu[index * ZS * tile // hidden, pl.ds(lane % (hidden // ZS) * BLOCKS // hidden, tile * BLOCKS // hidden)]
        part = nt(dyl_ref[...], flat(rows))
        part = (part * gp_ref[:, pl.ds(lane, tile)].astype(F32)).astype(BF16)
        du_ref[:, pl.ds(lane, tile)] = part
        acc_ref[...] += nt(part, flat(wi[:, :, :, pl.ds(lane, tile)]))
        sums_ref[
            pl.ds(IB + index // per_row, 1), pl.ds(index % per_row * tile, tile)
        ] = colsum(part.astype(F32))

    grad = acc_ref[...]
    wait_full(n1_ref, load_sems.at[1])
    wait_full(c1_ref, load_sems.at[2])
    normed = n1_ref[...]
    sums_ref[pl.ds(AG, 1), :] = colsum(grad * normed)
    sums_ref[pl.ds(AS, 1), :] = colsum(grad)
    back = norm_back(normed, c1_ref[:, :1], grad * row_of(vec_ref, AG))
    da_ref[...] = back
    low = back.astype(BF16)
    dal_ref[...] = low
    sums_ref[pl.ds(OB, 1), :] = colsum(low.astype(F32))
    wait_full(wo, sems.at[2])
    do_ref[...] = nt(low, flat(wo[...])).astype(BF16)


def chain_backward(pos_w, dyl, dy, gp, n1, c1, vec, inner_bufs, outer_bufs, attn_bufs, after=()):
    tokens, width = n1.shape
    hidden = gp.shape[1]
    return pl.pallas_call(
        functools.partial(chain_kernel, 384, len(after)),
        out_shape=(
            shape((tokens, hidden + width), BF16),
            shape((tokens, width), F32),
            shape((tokens, width), BF16),
            shape((16, width), F32),
        ),
        in_specs=[SMEM] + [VMEM] * 2 + [HBM] * 3 + [VMEM] + [ANY] * (6 + len(after)),
        out_specs=[VMEM] * 4,
        scratch_shapes=[
            wide_matrix(width, hidden),
            tall_matrix(hidden, width),
            square(width),
            pltpu.VMEM((tokens, width), F32),
        ]
        + [pltpu.VMEM(each.shape, each.dtype) for each in (gp, n1, c1)]
        + [pltpu.SemaphoreType.DMA((3,)), pltpu.SemaphoreType.DMA((3,))],
        compiler_params=params(VMEM_MB),
        cost_estimate=cost(),
        name="chain_backward",
    )(pos_w, dyl, dy, gp, n1, c1, vec, *inner_bufs, *outer_bufs, *attn_bufs, *after)


def attn_back_kernel(waits, *refs):
    sources, do_ref = refs[:4], refs[4]
    refs = refs[waits:]
    pack_ref, sum_ref, wide_ref = refs[5], refs[6], refs[7]
    held, sems, pair_sems = refs[8:12], refs[12], refs[13]
    q_ref, kt_ref, v_ref, p_ref = held
    tokens, width = q_ref.shape
    for index in range(3):
        load(sources[index], held[index], sems.at[index])
    for index in range(width // 128):
        both = pl.ds(index * 2, 2)
        load(sources[3].at[both], p_ref.at[both], pair_sems.at[index])
    for index in range(3):
        wait_full(held[index], sems.at[index])

    def pair(index, carry):
        lane = pl.multiple_of(index * 128, 128)
        values = v_ref[:, pl.ds(lane, 128)]
        queries = q_ref[:, pl.ds(lane, 128)]
        grads = do_ref[:, pl.ds(lane, 128)]
        first = lax.broadcasted_iota(jnp.int32, grads.shape, 1) < HD
        keys_back, values_back = [], []
        wait_full(p_ref.at[pl.ds(index * 2, 2)], pair_sems.at[index])
        for which in range(2):
            mine = jnp.where(first if which == 0 else ~first, grads, jnp.zeros_like(grads))
            probs_low = p_ref[index * 2 + which]
            probs = probs_low.astype(F32)
            weighted = probs * nt(values, mine)
            back = weighted - probs * jnp.sum(weighted, axis=0, keepdims=True)
            low = back.astype(BF16)
            keys_back.append(nn(low, queries))
            values_back.append(nn(probs_low, grads))
            row = pl.multiple_of(index * 128 + which * HD, HD)
            wide_ref[pl.ds(row, HD), :] = nn(kt_ref[pl.ds(row, HD), :], low)
        split = lax.broadcasted_iota(jnp.int32, keys_back[0].shape, 1) < HD
        for at, back in ((1, keys_back), (3, values_back)):
            low = jnp.where(split, back[0], back[1]).astype(BF16)
            pack_ref[at, :, pl.ds(lane, 128)] = low[:tokens]
            pack_ref[at + 1, :, pl.ds(lane, 128)] = low[tokens:]
        return carry

    lax.fori_loop(0, width // 128, pair, 0)
    low = (wide_ref[...].T * HD ** (-0.5)).astype(BF16)
    pack_ref[0] = low
    sum_ref[...] = jnp.broadcast_to(colsum(low.astype(F32)), sum_ref.shape)


def attn_backward(q, kt, v, p, do, after=()):
    tokens, width = q.shape
    return pl.pallas_call(
        functools.partial(attn_back_kernel, len(after)),
        out_shape=(
            shape((5, tokens, width), BF16),
            shape((8, width), F32),
        ),
        in_specs=[HBM] * 4 + [VMEM] + [ANY] * len(after),
        out_specs=[VMEM] * 2,
        scratch_shapes=[pltpu.VMEM((width, tokens), F32)]
        + [pltpu.VMEM(each.shape, each.dtype) for each in (q, kt, v, p)]
        + [pltpu.SemaphoreType.DMA((3,)), pltpu.SemaphoreType.DMA((width // 128,))],
        compiler_params=params(VMEM_MB),
        cost_estimate=cost(),
        name="attn_backward",
    )(q, kt, v, p, do, *after)


def input_kernel(first, *refs):
    pos_w, da_ref, pack_ref, got_ref = refs[:4]
    bufs = refs[4:6]
    refs = refs[6:]
    if not first:
        n2_ref, c2_ref, vec_ref = refs[:3]
        refs = refs[3:]
    total_ref, sum_ref = refs[:2]
    heads = refs[2:-4]
    wq, wk, wv, sems = refs[-4:]
    tokens, width = da_ref.shape
    for member, full in enumerate((wq, wk, wv)):
        fetch_member(pos_w, bufs, member, full, sems.at[member])
    for at, (mine, theirs) in enumerate(((1, 2), (2, 1), (3, 4), (4, 3))):
        total_ref[at] = (pack_ref[mine].astype(F32) + got_ref[theirs].astype(F32)).astype(BF16)
    sum_ref[...] = jnp.broadcast_to(colsum(total_ref[2].astype(F32)), sum_ref.shape)
    wait_full(wq, sems.at[0])
    dx = da_ref[...] + nt(pack_ref[0], flat(wq[...]))
    wait_full(wk, sems.at[1])
    dx += nt(total_ref[0], flat(wk[...]))
    wait_full(wv, sems.at[2])
    dx += nt(total_ref[2], flat(wv[...]))
    if first:
        heads[0][...] = dx.astype(BF16)
    else:
        head_back(dx, n2_ref[...], c2_ref[:, :1], row_of(vec_ref, FG), *heads)


def input_backward(pos_w, da, pack, got, bufs, below):
    tokens, width = da.shape
    first = below is None
    outs = (shape((4, tokens, width), BF16), shape((8, width), F32))
    outs += (shape((tokens, width), BF16),) if first else head_shapes(tokens, width)
    return pl.pallas_call(
        functools.partial(input_kernel, first),
        out_shape=outs,
        in_specs=[SMEM] + [VMEM] * 3 + [ANY] * 2 + ([] if first else [VMEM] * 3),
        out_specs=[VMEM] * len(outs),
        scratch_shapes=[square(width)] * 3 + [pltpu.SemaphoreType.DMA((3,))],
        compiler_params=params(VMEM_MB),
        cost_estimate=cost(),
        name="input_backward",
    )(pos_w, da, pack, got, *bufs, *(() if first else below))


def place(outs, part, dy, value):
    a_keep, a_send, b_keep, b_send = outs
    if part == 0:
        a_keep[dy] = value[0]
        a_send[dy] = value[1]
    else:
        (b_send if dy else b_keep)[...] = value


def grad_shapes(rows, width):
    return (shape((2, ZS, rows, width), BF16),) * 4


def inner_grad_kernel(pos_ref, ta_ref, tb_ref, da_ref, db_ref, *refs):
    outs, left, sems = refs[:4], refs[4], refs[5]
    _, _, rows, width = outs[0].shape
    tokens = ta_ref.shape[-1]
    for side, source in enumerate((ta_ref, tb_ref)):
        load(source.at[2], left.at[side], sems.at[side])
    for side in range(2):
        wait_full(left.at[side], sems.at[side])
    left_a = left[0].reshape(2 * ZS * rows, tokens)
    left_b = left[1].reshape(2 * ZS * rows, tokens)
    for dy in range(2):
        for part in range(2):
            lanes = pl.ds(pl.multiple_of((half_at(pos_ref, dy) * 2 + part) * width, 128), width)
            value = nn(left_a, da_ref[:, lanes]) + nn(left_b, db_ref[:, lanes])
            place(outs, part, dy, value.astype(BF16).reshape(2, ZS, rows, width))


def inner_grad(pos_g, ta, tb, da, db):
    rows = ta.shape[3]
    return pl.pallas_call(
        inner_grad_kernel,
        out_shape=grad_shapes(rows, rows * BLOCKS),
        in_specs=[SMEM] + [HBM] * 2 + [VMEM] * 2,
        out_specs=[VMEM] * 4,
        scratch_shapes=[pltpu.VMEM((2,) + ta.shape[1:], BF16), pltpu.SemaphoreType.DMA((2,))],
        compiler_params=params(VMEM_MB),
        cost_estimate=cost(),
        name="inner_grad",
    )(pos_g, ta, tb, da, db)


def outer_grad_kernel(ta_ref, tb_ref, da_ref, db_ref, *refs):
    outs, left, sems = refs[:4], refs[4], refs[5]
    _, _, rows, width = outs[0].shape
    tokens = ta_ref.shape[-1]
    for side, source in enumerate((ta_ref, tb_ref)):
        load(source, left.at[side], sems.at[side])
    for side in range(2):
        wait_full(left.at[side], sems.at[side])
    for dy in range(2):
        for part in range(2):
            values = []
            for dx in range(2):
                left_a = left[0, dx, dy, part].reshape(ZS * rows, tokens)
                left_b = left[1, dx, dy, part].reshape(ZS * rows, tokens)
                value = nn(left_a, da_ref[...]) + nn(left_b, db_ref[...])
                values.append(value.astype(BF16).reshape(ZS, rows, width))
            place(outs, part, dy, jnp.stack(values))


def outer_grad(ta, tb, da, db):
    rows, width = ta.shape[4], da.shape[1]
    return pl.pallas_call(
        outer_grad_kernel,
        out_shape=grad_shapes(rows, width),
        in_specs=[HBM] * 2 + [VMEM] * 2,
        out_specs=[VMEM] * 4,
        scratch_shapes=[pltpu.VMEM((2,) + ta.shape, BF16), pltpu.SemaphoreType.DMA((2,))],
        compiler_params=params(VMEM_MB),
        cost_estimate=cost(),
        name="outer_grad",
    )(ta, tb, da, db)


def attn_grad_kernel(pos_ref, xa_ref, xb_ref, qa_ref, qb_ref, total_ref, da_ref, db_ref, *refs):
    outs, left, sems = refs[:4], refs[4], refs[5]
    for side, source in enumerate((xa_ref, xb_ref)):
        load(source.at[pl.ds(0, 2)], left.at[side], sems.at[side])
    for side in range(2):
        wait_full(left.at[side], sems.at[side])
    _, _, rows, width = outs[0].shape
    half = width // 2
    tokens = xa_ref.shape[-1]
    height = 2 * ZS * rows
    x_a = left[0, 0].reshape(height, tokens)
    x_b = left[1, 0].reshape(height, tokens)
    o_a = left[0, 1].reshape(height, tokens)
    o_b = left[1, 1].reshape(height, tokens)
    last = da_ref.shape[1] - width
    for dy in range(2):
        start = half_at(pos_ref, dy) * half
        lanes = pl.ds(pl.multiple_of(start, 128), half)
        tail = pl.ds(pl.multiple_of(start + last, 128), half)
        members = (
            nn(x_a, qa_ref[0, :, lanes]) + nn(x_b, qb_ref[0, :, lanes]),
            nn(x_a, total_ref[0, :, lanes]) + nn(x_b, total_ref[1, :, lanes]),
            nn(x_a, total_ref[2, :, lanes]) + nn(x_b, total_ref[3, :, lanes]),
            nn(o_a, da_ref[:, tail]) + nn(o_b, db_ref[:, tail]),
        )
        for part in range(2):
            value = jnp.concatenate(members[part * 2 : part * 2 + 2], axis=1)
            place(outs, part, dy, value.astype(BF16).reshape(2, ZS, rows, width))


def attn_grad(pos_g, xa, xb, qa, qb, total, da, db):
    rows = xa.shape[3]
    return pl.pallas_call(
        attn_grad_kernel,
        out_shape=grad_shapes(rows, rows * BLOCKS),
        in_specs=[SMEM] + [HBM] * 2 + [VMEM] * 5,
        out_specs=[VMEM] * 4,
        scratch_shapes=[pltpu.VMEM((2, 2) + xa.shape[1:], BF16), pltpu.SemaphoreType.DMA((2,))],
        compiler_params=params(VMEM_MB),
        cost_estimate=cost(),
        name="attn_grad",
    )(pos_g, xa, xb, qa, qb, total, da, db)


def copy_kernel(plan, inputs, pos_ref, *refs):
    ins, outs, sems = refs[:inputs], refs[inputs:-1], refs[-1]
    copies = []
    for index, (out, to, source, at, size, by_z) in enumerate(plan):
        if by_z:
            z = pos_ref[0]
            to = flip(lax.div(z, 2), to // 2) * 2 + flip(lax.rem(z, 2), to % 2)
        copies.append(
            pltpu.make_async_copy(
                ins[source].at[pl.ds(at, size)], outs[out].at[pl.ds(to, size)], sems.at[index]
            )
        )
    for each in copies:
        each.start()
    for each in copies:
        each.wait()


def copy_blocks(pos, plan, inputs, sizes, name):
    piece = inputs[0].shape[1:]
    return pl.pallas_call(
        functools.partial(copy_kernel, plan, len(inputs)),
        out_shape=tuple(shape((size,) + piece, BF16) for size in sizes),
        in_specs=[SMEM] + [ANY] * len(inputs),
        out_specs=[VMEM] * len(sizes),
        scratch_shapes=[pltpu.SemaphoreType.DMA((len(plan),))],
        compiler_params=params(VMEM_MB),
        cost_estimate=cost(),
        name=name,
    )(pos, *inputs)


def pack_kernel(group, pos_ref, *refs):
    four, inner, outer = refs[:4], refs[4], refs[5]
    out, sem = refs[6], refs[7]
    rows, width = out.shape[1:]
    half = width // 2
    y = pos_ref[3]
    for j, chunk in enumerate(group):
        layer, kind = chunk // 3, chunk % 3
        for part in range(2):
            to = out.at[2 * j + part]
            if kind == 0:
                for side in range(2):
                    pltpu.make_async_copy(
                        four[2 * part + side].at[layer, :, pl.ds(pl.multiple_of(y * half, 128), half)],
                        to.at[:, pl.ds(side * half, half)],
                        sem,
                    ).start()
            elif kind == 1:
                lane = pl.multiple_of((2 * y + part) * width, 128)
                pltpu.make_async_copy(inner.at[layer, :, pl.ds(lane, width)], to, sem).start()
            else:
                row = pl.multiple_of((2 * y + part) * rows, 16)
                pltpu.make_async_copy(outer.at[layer, pl.ds(row, rows)], to, sem).start()
    wait_full(out, sem)


def pack_pieces(group, pos, weights):
    _, rows, width = weights[0].shape
    return pl.pallas_call(
        functools.partial(pack_kernel, group),
        out_shape=shape((2 * len(group), rows, width), BF16),
        in_specs=[SMEM] + [HBM] * 6,
        out_specs=VMEM,
        scratch_shapes=[pltpu.SemaphoreType.DMA],
        compiler_params=params(VMEM_MB),
        cost_estimate=cost(),
        name="pack",
    )(pos, *weights)


def table_kernel(at_ref, *refs):
    vectors, out = refs[:-1], refs[-1]
    width = out.shape[2]
    for index, vector in enumerate(vectors):
        size = vector.shape[1]
        start = at_ref[0] * size
        for piece in range(max(1, out.shape[1] - IB if index == IB else 1)):
            lanes = lax.broadcasted_iota(jnp.int32, (size, width), 1) + piece * width
            spot = lax.broadcasted_iota(jnp.int32, (size, width), 0) + start
            chosen = (lanes == spot).astype(F32).astype(BF16)
            out[:, index + piece, :] = nn(vector[...], chosen)


def vector_table(at, vectors, width):
    layers, last = vectors[-1].shape[0], vectors[-1].shape[1]
    rows = IB + last // vectors[0].shape[1]
    return pl.pallas_call(
        table_kernel,
        out_shape=shape((layers, rows, width), F32),
        in_specs=[SMEM] + [VMEM] * len(vectors),
        out_specs=VMEM,
        compiler_params=params(VMEM_MB),
        cost_estimate=cost(),
        name="vector_table",
    )(at, *vectors)


def finish_kernel(kind, offsets, pos_ref, *refs):
    layers = len(offsets)
    owns, gots = refs[:layers], refs[layers : 2 * layers]
    outs, buf, sems = refs[2 * layers : -2], refs[-2], refs[-1]
    rows, width = buf.shape[2:]
    half = width // 2
    y = pos_ref[3]
    copies = []
    for layer in range(layers):
        copies.append(
            pltpu.make_async_copy(
                gots[layer].at[pl.ds(offsets[layer], 2)], buf.at[layer], sems.at[layer]
            )
        )
        copies[-1].start()
    for side in range(2):
        yy = y if side == 0 else 1 - y
        if side:
            for each in copies:
                each.wait()
        for layer in range(layers):
            for part in range(2):
                value = (buf[layer, part] if side else owns[layer][part].astype(BF16)).astype(F32)
                if kind == 0:
                    lanes = pl.ds(pl.multiple_of(yy * half, 128), half)
                    for member in range(2):
                        outs[2 * part + member][layer, :, lanes] = value[
                            :, member * half : (member + 1) * half
                        ]
                elif kind == 1:
                    lane = pl.multiple_of((2 * yy + part) * width, 128)
                    outs[0][layer, :, pl.ds(lane, width)] = value
                else:
                    row = pl.multiple_of((2 * yy + part) * rows, 16)
                    outs[0][layer, pl.ds(row, rows), :] = value


def finish(kind, pos, results):
    layers = len(results)
    _, rows, width = results[0][0].shape
    outs = {
        0: (shape((layers, rows, width), F32),) * 4,
        1: (shape((layers, rows, 4 * width), F32),),
        2: (shape((layers, 4 * rows, width), F32),),
    }[kind]
    return pl.pallas_call(
        functools.partial(finish_kernel, kind, tuple(value[2] for value in results)),
        out_shape=outs,
        in_specs=[SMEM] + [VMEM] * layers + [ANY] * layers,
        out_specs=[VMEM] * len(outs),
        scratch_shapes=[
            pltpu.VMEM((layers, 2, rows, width), BF16),
            pltpu.SemaphoreType.DMA((layers,)),
        ],
        compiler_params=params(VMEM_MB),
        cost_estimate=cost(),
        name="finish",
    )(pos, *[value[0] for value in results], *[value[1] for value in results])


def sum_kernel(config, *refs):
    fresh, first, second, third, fourth, small, waits = config
    refs = list(refs)

    def take(count):
        out = refs[:count]
        del refs[:count]
        return out

    sends = take(2) if fresh else None
    got_x, got_y = take(2) if first or second else (None, None)
    keeps = take(2) if first else None
    rests = take(2) if second else None
    pairs = take(2) if third else None
    lasts = take(2) if fourth else None
    tables = take(2 if small == 1 else 1) if small else None
    take(waits)
    to_x, to_y = take(2) if fresh or first or fourth else (None, None)
    at = 0
    if fresh:
        for out, send in ((to_x, sends[0]), (to_y, sends[1])):
            for half in range(2):
                out[half * ZS : (half + 1) * ZS] = send[half]
        at = 2 * ZS
    got = 0
    if first:
        outs = take(2)
        for keep, come, rest, send in (
            (keeps[0], got_x, outs[0], to_y),
            (keeps[1], got_y, outs[1], to_x),
        ):
            rest[...] = (keep[0].astype(F32) + come[:ZS].astype(F32)).astype(BF16)
            send[at : at + ZS] = (keep[1].astype(F32) + come[ZS : 2 * ZS].astype(F32)).astype(BF16)
        got = 2 * ZS
        at += ZS
    if second:
        hold, to_z1 = take(2)
        for part, (rest, come) in enumerate(((rests[0], got_y), (rests[1], got_x))):
            for k in range(ZS):
                value = rest[k].astype(F32) + come[got + k].astype(F32)
                (to_z1 if k % 2 else hold)[k // 2 * 2 + part] = value.astype(BF16)
    if third:
        hold, to_z2 = take(2)
        for part in range(2):
            hold[part] = pairs[0][part].astype(F32) + pairs[1][part].astype(F32)
            value = pairs[0][2 + part].astype(F32) + pairs[1][2 + part].astype(F32)
            to_z2[part] = value.astype(BF16)
    if fourth:
        (total,) = take(1)
        value = lasts[0][...] + lasts[1][:2].astype(F32)
        total[...] = value
        to_y[at : at + 2] = value.astype(BF16)
    if small:
        come = (None, None, got_x, pairs and pairs[1], lasts and lasts[1])[small]
        come = tables[1][...] if small == 1 else come[come.shape[0] - 1]
        value = tables[0][...] + come.astype(F32)
        refs[0][...] = value
        to = (None, to_x, to_z1 if second else None, to_z2 if third else None, to_y)[small]
        to[to.shape[0] - 1] = value.astype(BF16)


def sum_round(fresh, got_x, got_y, first, second, third, fourth, small, after):
    stage, table = small
    config = tuple(value is not None for value in (fresh, first, second, third, fourth)) + (stage, len(after))
    sample = fresh or first or second or third or fourth
    rows, width = sample[-1].shape[-2:]
    inputs, outputs = [], []
    if fresh is not None:
        inputs += [fresh[1], fresh[3]]
    if first is not None or second is not None:
        inputs += [got_x, got_y]
    for value in (first, second, third, fourth, table):
        if value is not None:
            inputs += list(value)
    going = 2 * ZS * config[0] + ZS * config[1]
    if config[0] or config[1] or config[4]:
        size_x, size_y = max(going, 1) + (stage == 1), going + 2 * config[4] + (stage == 4)
        outputs += [shape((size_x, rows, width), BF16), shape((size_y, rows, width), BF16)]
    if config[1]:
        outputs += [shape((ZS, rows, width), BF16)] * 2
    if config[2]:
        outputs += [shape((4, rows, width), BF16), shape((4 + (stage == 2), rows, width), BF16)]
    if config[3]:
        outputs += [shape((2, rows, width), F32), shape((2 + (stage == 3), rows, width), BF16)]
    if config[4]:
        outputs += [shape((2, rows, width), F32)]
    if config[5]:
        outputs += [shape(table[0].shape, F32)]
    outs = list(
        pl.pallas_call(
            functools.partial(sum_kernel, config),
            out_shape=tuple(outputs),
            in_specs=[VMEM] * len(inputs) + [ANY] * len(after),
            out_specs=[VMEM] * len(outputs),
            compiler_params=params(VMEM_MB),
            cost_estimate=cost(),
            name="sum_round",
        )(*inputs, *after)
    )

    def take(wanted, count):
        if not wanted:
            return None
        out = tuple(outs[:count])
        del outs[:count]
        return out

    sends = take(config[0] or config[1] or config[4], 2)
    return (
        sends,
        going,
        take(config[1], 2),
        take(config[2], 2),
        take(config[3], 2),
        take(config[4], 1),
        take(stage > 0, 1),
    )


def collect_kernel(*refs):
    out = refs[-1]
    for layer in range(out.shape[0]):
        query_ref, value_ref, head_ref, chain_ref = refs[4 * layer : 4 * layer + 4]
        out[layer] = chain_ref[...]
        out[layer, pl.ds(QB, 1), :] = query_ref[:1]
        out[layer, pl.ds(VB, 1), :] = value_ref[:1]
        for at, index in enumerate((FG, FS, UB)):
            out[layer, pl.ds(index, 1), :] = head_ref[at : at + 1]


def collect(vectors, rows):
    flat = [value for layer in vectors for value in layer]
    width = flat[0].shape[1]
    return pl.pallas_call(
        collect_kernel,
        out_shape=shape((len(vectors), rows, width), F32),
        in_specs=[VMEM] * len(flat),
        out_specs=VMEM,
        compiler_params=params(VMEM_MB),
        cost_estimate=cost(),
        name="collect",
    )(*flat)


def vectors_kernel(last, at_ref, table_ref, got_ref, *outs):
    layers, width = outs[0].shape[0], table_ref.shape[1]
    at = at_ref[0]
    for index, out in enumerate(outs):
        size = out.shape[1]
        start = at * size
        shift = lax.rem(width - lax.rem(start, width), width)
        for layer in range(layers):
            spot = pl.ds(layer * 16 + index + lax.div(start, width), 1)
            value = table_ref[spot, :]
            if last is not None:
                value = value.astype(BF16).astype(F32) + got_ref[spot, :]
            value = jnp.broadcast_to(value, (8, width))
            out[pl.ds(layer, 1), :] = pltpu.roll(value, shift, 1)[:1, :size]


def own_vectors(at, table, got, layers, size, wide):
    sizes = [size] * IB + [wide]
    last = None if got is None else 0
    return pl.pallas_call(
        functools.partial(vectors_kernel, last),
        out_shape=tuple(shape((layers, each), F32) for each in sizes),
        in_specs=[SMEM, VMEM, VMEM],
        out_specs=[VMEM] * len(sizes),
        compiler_params=params(VMEM_MB),
        cost_estimate=cost(),
        name="own_vectors",
    )(at, table, table if got is None else got)


def fence(values):
    return lax.optimization_barrier(values)


def build(mesh):
    count = mesh.shape["dp"]

    def flat(dp, seq):
        return dp * 2 + seq

    def pairs(source_of):
        out = []
        for dp in range(count):
            for seq in range(2):
                out.append((flat(*source_of(dp, seq)), flat(dp, seq)))
        return out

    swap_pairs = pairs(lambda dp, seq: (dp // 2 * 2 + seq, dp % 2))
    core_pairs = pairs(lambda dp, seq: (dp ^ 1, seq))
    x_pairs = pairs(lambda dp, seq: (dp ^ 2, seq))
    y_pairs = pairs(lambda dp, seq: (dp, 1 - seq))
    z_pairs = [pairs(lambda dp, seq, k=k: ((dp // 4 ^ k) * 4 + dp % 4, seq)) for k in (1, 2)]

    def move(value, perm):
        return lax.ppermute(value, AXES, perm)

    return dict(
        count=count,
        swap=swap_pairs,
        core=core_pairs,
        x=x_pairs,
        y=y_pairs,
        z1=z_pairs[0],
        z2=z_pairs[1],
        move=move,
    )


def body(
    net,
    tokens,
    segment_ids,
    padding,
    query_weight,
    key_weight,
    value_weight,
    output_weight,
    query_bias,
    value_bias,
    output_bias,
    attn_gain,
    attn_shift,
    inner_weight,
    inner_bias,
    outer_weight,
    outer_bias,
    ffn_gain,
    ffn_shift,
    upstream,
):
    layers, small, width = query_weight.shape
    hidden = inner_weight.shape[2]
    count = net["count"]
    move = net["move"]
    staged = count == BLOCKS and small == 16 * layers
    dp = lax.axis_index("dp").astype(jnp.int32)
    y = lax.axis_index("seq").astype(jnp.int32)
    core = lax.rem(dp, 2)
    if staged:
        pos_g = jnp.stack([lax.div(dp, 4), lax.rem(lax.div(dp, 2), 2), core, y])
        pos_w = pos_g
    else:
        zero = jnp.zeros((), jnp.int32)
        pos_g = jnp.stack([zero, zero, core, zero])
        pos_w = jnp.stack([zero, zero, zero, zero])

    labels = jnp.where(padding == 1, segment_ids, -1)
    small_own = move(jnp.concatenate([segment_ids, labels]), net["swap"])
    token_low = move(tokens[0], net["swap"])

    vector_args = [query_bias, value_bias, output_bias, attn_gain, attn_shift, outer_bias]
    vector_args += [ffn_gain, ffn_shift, inner_bias]
    table = vector_table(dp[None], vector_args, width)
    if staged:
        table = table + move(table, net["x"])
    else:
        table = lax.psum(table, "dp")

    raw = (query_weight, key_weight, value_weight, output_weight, inner_weight, outer_weight)
    chunks = []
    for layer in range(layers):
        four = (query_weight[layer], key_weight[layer], value_weight[layer], output_weight[layer])
        if not staged:
            full = [lax.all_gather(value, "dp", axis=0, tiled=True) for value in four]
            inner = lax.all_gather(inner_weight[layer], "dp", axis=0, tiled=True)
            outer = lax.all_gather(outer_weight[layer], "dp", axis=0, tiled=True)
            rows = width // BLOCKS

            def cut(value, dy, dx, dc):
                value = value.reshape(ZS, 2, 2, rows, 2, -1)
                return value[:, dx, dc, :, dy, :]

            lists = [[[], []], [[], []], [[], []]]
            for dc in range(2):
                for part, dy, dx in UNITS:
                    lists[0][dc].append(
                        jnp.concatenate([cut(value, dy, dx, dc) for value in full[part * 2 : part * 2 + 2]], axis=2)
                    )
                    lists[1][dc].append(cut(inner, dy, dx, dc)[..., part * width : (part + 1) * width])
                    lists[2][dc].append(
                        outer.reshape(ZS, 2, 2, 2, 2, hidden // BLOCKS // 4, width)[:, dx, dc, dy, part]
                    )
            chunks.extend(tuple(jnp.concatenate(side) for side in value) for value in lists)

    total_chunks = 3 * layers
    groups = []
    if staged:
        edges = [0, 1, 2, 3] + list(range(4, total_chunks, 2)) + [total_chunks]
        groups = [range(low, high) for low, high in zip(edges[:-1], edges[1:])]
    where_of = {i: (g, i - group[0]) for g, group in enumerate(groups) for i in group}
    stage_z = [None] * len(groups)

    def start_z2(g):
        own = pack_pieces(groups[g], pos_g, raw)
        stage_z[g] = (own, move(own, net["z2"]))

    def start_z1(g):
        own, come = stage_z[g]
        size = own.shape[0]
        both = copy_blocks(
            pos_g,
            [(0, 0, 0, 0, size, False), (0, size, 1, 0, size, False)],
            (own, come),
            [2 * size],
            "gather_z",
        )[0]
        stage_z[g] = (both, move(both, net["z1"]))

    if staged:
        start_z2(0)
        stage_z[0], raw, table, small_own, token_low = fence(
            (stage_z[0], raw, table, small_own, token_low)
        )
        start_z1(0)
        start_z2(1)
        table = table + move(table, net["core"])
    small_other = move(small_own, net["core"])
    token_other = move(token_low, net["core"])
    if staged:
        stage_z[:2], raw, table, small_own, small_other, token_low, token_other, upstream = fence(
            (stage_z[:2], raw, table, small_own, small_other, token_low, token_other, upstream)
        )
    seg = small_own[0:1]
    lab = jnp.concatenate([small_own[1], small_other[1]])[:, None]
    current = token_low.astype(F32)
    other = token_other
    kept = [None] * layers
    todo = []
    for layer in range(layers):
        todo.append(("attn", layer, 3 * layer))
        todo.append(("inner", layer, 3 * layer + 1))
        todo.append(("outer", layer, 3 * layer + 2))
    low = None
    attn_out = None
    arrived = 0 if staged else total_chunks

    mid = None

    def compute():
        nonlocal current, other, low, attn_out, mid, head
        if not todo or todo[0][2] >= arrived:
            return
        kind, layer, _ = todo.pop(0)
        vec = table[layer]
        if kind == "attn":
            attn_out = attn_forward(pos_w, pos_g, current, other, seg, lab, vec, chunks[3 * layer])
            return
        h, n1, c1, q, kt, v, p, xoh, far_xoh = attn_out
        if kind == "inner":
            active, gp, gt, far_gt = inner_forward(pos_w, pos_g, h, vec, chunks[3 * layer + 1])
            mid = (active, gp, gt, move(far_gt, net["core"]), move(far_xoh, net["core"]))
            return
        active, gp, gt, far_gt, far_xoh = mid
        last = layer + 1 == layers
        current, low, *rest = outer_forward(
            pos_w, h, active, vec, chunks[3 * layer + 2], upstream if last else None
        )
        if last:
            head, rest = rest, (None, None)
        else:
            other = move(low, net["core"])
        kept[layer] = (n1, c1, q, kt, v, p, *rest, gp, xoh, gt, far_xoh, far_gt)

    head = None
    if not staged:
        upstream = move(upstream[0], net["swap"])
    if staged:
        sent, got = {}, {}
        zplan = {r: [(1, r + 2), (2, r + 3)] for r in range(-1, 2)}
        for r in range(2, 2 * len(groups)):
            g = (r + 6) // 2 + (r % 2)
            zplan[r] = [(1 + r % 2, g)]
        spread = [net["z2"], net["z1"]]
        for r in range(-LAG, total_chunks + LAG):
            inputs, plan = [], []
            sizes = [0, 0]
            use = lambda value: (inputs.append(value), len(inputs) - 1)[1]
            fresh = r + LAG < total_chunks
            if fresh:
                g, j = where_of[r + LAG]
                n = len(groups[g])
                mine, theirs = use(stage_z[g][0]), use(stage_z[g][1])
                for out, part in ((0, 1), (1, 0)):
                    for k, (source, slot) in enumerate(((mine, 0), (theirs, 0), (mine, 1), (theirs, 1))):
                        plan.append((out, k, source, (slot * n + j) * 2 + part, 1, True))
                    sizes[out] = ZS
            before = r - LAG
            home = 0 <= before < total_chunks
            if before >= -LAG and (r < total_chunks or home):
                sx, sy = use(sent[before][0]), use(sent[before][1])
                rx, ry = use(got[before][0]), use(got[before][1])
                first = ZS if before + LAG < total_chunks else 0
                if r < total_chunks:
                    for out, send, come in ((0, sy, ry), (1, sx, rx)):
                        plan.append((out, sizes[out], send, 0, ZS, False))
                        plan.append((out, sizes[out] + ZS, come, 0, ZS, False))
                        sizes[out] += 2 * ZS
                if home:
                    sizes.append(8 * ZS)
                    slot = 2
                    for at, (send, come) in enumerate(((sx, rx), (sy, ry))):
                        plan.append((slot, at * 4 * ZS, send, first, 2 * ZS, False))
                        plan.append((slot, at * 4 * ZS + 2 * ZS, come, first, 2 * ZS, False))
            live = [index for index, size in enumerate(sizes) if size]
            outs = copy_blocks(
                pos_g,
                [(live.index(each[0]),) + each[1:] for each in plan],
                inputs,
                [sizes[index] for index in live],
                "gather_round",
            )
            outs = dict(zip(live, outs))
            if 0 in outs:
                sent[r] = (outs[0], outs[1])
                got[r] = (move(outs[0], net["x"]), move(outs[1], net["y"]))
            core_pair = None
            if home:
                core_pair = (outs[2], move(outs[2], net["core"]))
            for stage, g in zplan.get(r, ()):
                if g < len(groups):
                    (start_z2 if stage == 2 else start_z1)(g)
            if spread:
                table = table + move(table, spread.pop(0))
            if r == total_chunks - 1:
                upstream = move(upstream[0], net["swap"])
            compute()
            ready = r + 1 - LAG
            state = (got.get(ready), core_pair, stage_z, current, other, attn_out, raw, table, upstream, mid)
            state = fence(state)
            if ready in got:
                got[ready] = state[0]
            if home:
                chunks.append(state[1])
                arrived += 1
            stage_z, current, other, attn_out, raw, table, upstream, mid = (list(state[2]),) + tuple(state[3:])
    while todo:
        compute()
    range_ids = jnp.arange(SEGS, dtype=jnp.int32)
    own = (small_own[1][None, :] == range_ids[:, None]).astype(F32)
    sums = jnp.dot(own, current, precision=lax.Precision.HIGHEST)
    pool_sums = sums
    counts = jnp.sum((lab[:, 0][None, :] == range_ids[:, None]).astype(F32), axis=1)
    loose = {}
    if staged:
        loose["hidden"] = move(low, net["swap"])
        loose["pool"] = pool_sums + move(pool_sums, net["core"])

    parts = []
    vectors = [None] * layers
    rounds = []
    ends = []
    table_stage = 1

    def side_work():
        step = len(rounds)
        last = total_chunks + 1
        if step == 2:
            loose["after"] = (loose["hidden"], loose["pool"])
        if step == 3:
            loose["pooled"] = move(loose.pop("pool") / counts[:, None], net["swap"])
            loose["after"] = (loose["pooled"],)
        if step == last + 1:
            loose["grad"] = move(loose.pop("grad"), net["swap"])
            loose["after"] = (loose["grad"],)
        if step == last + 2:
            done = list(finish(2, pos_g, ended()[0::3][::-1]))
            loose["outer"] = done
            loose["after"] = (done[0],)

    def ended():
        found = []
        for now in rounds:
            if "total" in now:
                found.append((now["total"], now["got_y"], ends[len(found)]))
        return found

    def settle(state):
        return fence(state)

    def advance(fresh, state):
        if not staged:
            if fresh is not None:
                parts.append(fresh)
            return state(()) if callable(state) else state
        s = len(rounds)
        past = rounds[s - LAG] if s >= LAG else {}
        pick = lambda key: past.get(key)
        has_home = pick("first") is not None or pick("second") is not None
        sends, going, first, second, third, fourth, small = sum_round(
            fresh,
            pick("got_x") if has_home else None,
            pick("got_y") if has_home else None,
            pick("first"),
            pick("second"),
            pick("third"),
            pick("fourth"),
            loose.pop("small", (0, None)),
            tuple(loose.pop("after", ())),
        )
        now = {}
        if fresh is not None:
            now["first"] = (fresh[0], fresh[2])
        if first is not None:
            now["second"] = first
        if sends is not None:
            if going:
                now["got_x"] = move(sends[0], net["x"])
            now["got_y"] = move(sends[1], net["y"])
        if second is not None:
            now["third"] = (second[0], move(second[1], net["z1"]))
        if third is not None:
            now["fourth"] = (third[0], move(third[1], net["z2"]))
        if fourth is not None:
            now["total"] = fourth[0]
            ends.append(going)
        if "vectors" in loose:
            small = loose.pop("vectors").reshape(-1, width)
            loose["small"] = (1, (small, move(small, net["core"])))
        elif small is not None:
            nonlocal table_stage
            table_stage += 1
            loose["small"] = (table_stage, small)
        side_work()
        if callable(state):
            state = state(sends)
        rounds.append(now)
        ready = s + 1 - LAG
        if ready < 0:
            return fence(state)
        rounds[ready], state = fence((rounds[ready], state))
        return state

    top = layers - 1
    ready = []
    dyl, dy, head_sums = head
    for layer in reversed(range(layers)):
        attn_bufs, inner_bufs, outer_bufs = chunks[3 * layer : 3 * layer + 3]
        n1, c1, q, kt, v, p, n2, c2, gp, xoh, gt, far_xoh, far_gt = kept[layer]
        got_dyl = move(dyl, net["core"])
        chain_args = (pos_w, dyl, dy, gp, n1, c1, table[layer], inner_bufs, outer_bufs, attn_bufs)
        if layer == top:
            outer_parts = settle(outer_grad(gt, far_gt, dyl, got_dyl))

            def first_round(sends):
                return chain_backward(*chain_args, after=sends)

            pack, da, do, sums = advance(outer_parts, first_round)
            got_pack = move(pack, net["core"])

            def second_round(sends):
                back, qsum = attn_backward(q, kt, v, p, do, after=sends)
                return back, qsum, got_pack, inner_grad(pos_g, xoh, far_xoh, pack, got_pack)

            back, qsum, got_pack, inner_parts = advance(None, second_round)
            ready.append(inner_parts)
            got_back = move(back, net["core"])
        else:
            pack, da, do, sums = chain_backward(*chain_args)
            outer_parts = outer_grad(gt, far_gt, dyl, got_dyl)
            state = advance(ready.pop(0), (pack, da, do, sums, outer_parts))
            pack, da, do, sums, outer_parts = state
            ready.append(outer_parts)
            got_pack = move(pack, net["core"])
            back, qsum = attn_backward(q, kt, v, p, do)
            inner_parts = inner_grad(pos_g, xoh, far_xoh, pack, got_pack)
            state = advance(ready.pop(0), (back, qsum, got_pack, inner_parts))
            back, qsum, got_pack, inner_parts = state
            ready.append(inner_parts)
            got_back = move(back, net["core"])
        below = None if layer == 0 else (kept[layer - 1][6], kept[layer - 1][7], table[layer - 1])
        total, vsum, *head = input_backward(pos_w, da, back, got_back, attn_bufs, below)
        attn_parts = attn_grad(pos_g, xoh, far_xoh, back, got_back, total, pack, got_pack)
        attn_parts, head, vsum = advance(ready.pop(0), (attn_parts, head, vsum))
        ready.append(attn_parts)
        vectors[layer] = (qsum, vsum, head_sums, sums)
        if layer:
            dyl, dy, head_sums = head
    grad = head[0]
    vectors = collect(vectors, 16)
    loose["grad"] = grad
    while ready:
        if len(ready) == 1:
            loose["vectors"] = vectors
        advance(ready.pop(0), None)
    results = []
    if staged:
        for _ in range(4 * LAG):
            advance(None, None)
        results = ended()

    if staged:
        stacked = []
        for kind, first in ((0, 2), (1, 1)):
            stacked += list(finish(kind, pos_g, results[first::3][::-1]))
        stacked += loose["outer"]
        hidden_out, pooled, tokens_grad = (loose[key] for key in ("hidden", "pooled", "grad"))
        vectors = loose["small"][1][0]
        got_vectors = rounds[-1]["got_y"][-1].astype(F32)
    else:
        collected = [None] * layers
        for place_at, layer in enumerate(reversed(range(layers))):
            outer_parts, inner_parts, attn_parts = parts[3 * place_at : 3 * place_at + 3]

            def spread(outs):
                a_keep, a_send, b_keep, b_send = outs
                a = jnp.stack([a_keep, a_send])
                b = jnp.stack([b_keep, b_send], axis=1)
                return jnp.stack([a, b], axis=2)

            def total(out):
                out = out.reshape(ZS * 2, 1, out.shape[2], out.shape[3])
                mine = (jnp.arange(2, dtype=jnp.int32) == core)[None, :, None, None]
                out = jnp.where(mine, out, jnp.zeros_like(out)).reshape(-1, out.shape[-1])
                out = lax.psum_scatter(out, "dp", scatter_dimension=0, tiled=True)
                return lax.psum(out.astype(F32), "seq")

            outer = spread(outer_parts).transpose(3, 0, 1, 2, 4, 5)
            outer = total(outer.reshape(ZS, 2, -1, width))
            inner = spread(inner_parts).transpose(3, 0, 4, 1, 2, 5)
            inner = total(inner.reshape(ZS, 2, inner.shape[2], -1))
            attn = spread(attn_parts)
            attn = attn.reshape(attn.shape[:5] + (2, width // 2)).transpose(2, 5, 3, 0, 4, 1, 6)
            attn = attn.reshape(4, ZS, 2, attn.shape[4], width)
            four = [total(attn[index]) for index in range(4)]
            collected[layer] = four + [inner, outer]
        stacked = [
            jnp.stack([collected[layer][member] for layer in range(layers)]) for member in range(6)
        ]
        hidden_out = move(low, net["swap"])
        pooled = move((pool_sums + move(pool_sums, net["core"])) / counts[:, None], net["swap"])
        tokens_grad = move(grad, net["swap"])
        vectors = lax.psum(vectors, AXES).reshape(-1, width)
        got_vectors = None
    own = own_vectors(dp[None], vectors, got_vectors, layers, small, hidden // count)
    return (
        hidden_out[None],
        pooled[None],
        tokens_grad.astype(F32)[None],
        stacked[0],
        stacked[1],
        stacked[2],
        stacked[3],
        own[QB],
        own[VB],
        own[OB],
        own[AG],
        own[AS],
        stacked[4],
        own[IB],
        stacked[5],
        own[UB],
        own[FG],
        own[FS],
    )


def solution(mesh):
    cube = P(None, "dp", None)
    flat = P(None, "dp")
    acts = P("dp", "seq", None)
    ids = P("dp", "seq")
    return jax.shard_map(
        functools.partial(body, build(mesh)),
        mesh=mesh,
        in_specs=(acts, ids, ids, cube, cube, cube, cube, flat, flat, flat, flat, flat, cube, flat, cube)
        + (flat, flat, flat, acts),
        out_specs=(acts, P("dp", None, None), acts, cube, cube, cube, cube)
        + (flat, flat, flat, flat, flat, cube, flat, cube, flat, flat, flat),
        check_vma=False,
    )
```

```python
import functools

import jax
import jax.numpy as jnp
from jax import lax
from jax.experimental import pallas as pl
from jax.experimental.pallas import tpu as pltpu
from jax.sharding import PartitionSpec as P

HD = 64
SEGS = 4
BLOCKS = 16
ZS = 4
LAG = 1
VMEM_MB = 24
EPS = 1e-06
MASKED = -1e30
AXES = ("dp", "seq")
F32 = jnp.float32
BF16 = jnp.bfloat16
MB = 1024 * 1024

QB, VB, OB, AG, AS, UB, FG, FS, IB = range(9)


def nn(left, right):
    return lax.dot_general(left, right, (((1,), (0,)), ((), ())), preferred_element_type=F32)


def nt(left, right):
    return lax.dot_general(left, right, (((1,), (1,)), ((), ())), preferred_element_type=F32)


def params(vmem):
    return pltpu.CompilerParams(vmem_limit_bytes=vmem * MB)


def cost():
    return pl.CostEstimate(flops=1, bytes_accessed=1, transcendentals=0)


def load(source, target, sem):
    pltpu.make_async_copy(source, target, sem).start()


VMEM = pl.BlockSpec(memory_space=pltpu.VMEM)
SMEM = pl.BlockSpec(memory_space=pltpu.SMEM)
ANY = pl.BlockSpec(memory_space=pl.ANY)
HBM = pl.BlockSpec(memory_space=pltpu.HBM)


def shape(dims, dtype):
    return jax.ShapeDtypeStruct(dims, dtype)


def flip(value, bit):
    return value + bit - 2 * value * bit


def block_at(pos_ref, k, dx, dc):
    z, x, c = pos_ref[0], pos_ref[1], pos_ref[2]
    low = lax.rem(z, 2)
    zz = flip(lax.div(z, 2), k // 2) * 2 + flip(low, k % 2)
    return (zz * 2 + flip(x, dx)) * 2 + flip(c, dc)


def half_at(pos_ref, dy):
    return flip(pos_ref[3], dy)


UNITS = (
    (0, 0, 0),
    (0, 1, 0),
    (0, 0, 1),
    (0, 1, 1),
    (1, 0, 0),
    (1, 0, 1),
    (1, 1, 0),
    (1, 1, 1),
)


def each_unit(pos_ref, bufs):
    for dc in range(2):
        for unit, (part, dy, dx) in enumerate(UNITS):
            at = flip(pos_ref[1], dx) * 2 + flip(pos_ref[2], dc)
            yield bufs[dc].at[pl.ds(unit * ZS, ZS)], part, dy, at


def fetch_member(pos_ref, bufs, member, full_ref, sem):
    half = full_ref.shape[3] // 2
    for unit, part, dy, at in each_unit(pos_ref, bufs):
        if part == member // 2:
            col = pl.multiple_of(half_at(pos_ref, dy) * half, 128)
            load(
                unit.at[:, :, pl.ds(member % 2 * half, half)],
                full_ref.at[:, at, :, pl.ds(col, half)],
                sem,
            )


def fetch_columns(pos_ref, bufs, full_ref, sem):
    width = full_ref.shape[3] // 4
    for unit, part, dy, at in each_unit(pos_ref, bufs):
        col = pl.multiple_of((half_at(pos_ref, dy) * 2 + part) * width, 128)
        load(unit, full_ref.at[:, at, :, pl.ds(col, width)], sem)


def fetch_rows(pos_ref, bufs, full_ref, sem):
    for unit, part, dy, at in each_unit(pos_ref, bufs):
        load(unit, full_ref.at[:, at, half_at(pos_ref, dy) * 2 + part], sem)


def flat(values):
    return values.reshape(-1, values.shape[-1])


def square(width):
    return pltpu.VMEM((ZS, BLOCKS // ZS, width // BLOCKS, width), BF16)


def wide_matrix(width, hidden):
    return pltpu.VMEM((ZS, BLOCKS // ZS, width // BLOCKS, hidden), BF16)


def tall_matrix(hidden, width):
    return pltpu.VMEM((ZS, BLOCKS // ZS, 4, hidden // BLOCKS // 4, width), BF16)


def wait_full(full_ref, sem):
    pltpu.make_async_copy(full_ref, full_ref, sem).wait()


def export_rows(pos_ref, wide_ref, outs, index):
    rows = outs[0].shape[3]
    for dc in range(2):
        for dx in range(2):
            for k in range(ZS):
                row = pl.multiple_of(block_at(pos_ref, k, dx, dc) * rows, 16)
                outs[dc][index, dx, k] = wide_ref[pl.ds(row, rows), :]


def export_halves(pos_ref, wide_ref, outs):
    rows = outs[0].shape[4]
    for dc in range(2):
        for dx in range(2):
            for dy in range(2):
                for k in range(ZS):
                    block = block_at(pos_ref, k, dx, dc) * 2 + half_at(pos_ref, dy)
                    for part in range(2):
                        row = pl.multiple_of((block * 2 + part) * rows, 16)
                        outs[dc][dx, dy, part, k] = wide_ref[pl.ds(row, rows), :]


def mean_of(values):
    return jnp.mean(values, axis=-1, keepdims=True)


def normalize(values):
    center = values - mean_of(values)
    inverse = lax.rsqrt(mean_of(center * center) + EPS)
    return center * inverse, inverse


def norm_back(normed, inverse, scaled):
    return inverse * (scaled - mean_of(scaled) - normed * mean_of(scaled * normed))


def colsum(values):
    return jnp.sum(values, axis=0, keepdims=True)


def row_of(vec_ref, index):
    return vec_ref[pl.ds(index, 1), :]


def attn_kernel(*refs):
    pos_w, pos_g = refs[0], refs[1]
    x_ref, xp_ref, seg_ref, lab_ref, vec_ref = refs[2:7]
    bufs = refs[7:9]
    h_ref = refs[9]
    kept = refs[10:18]
    wq, wk, wv, wo, rows_ref, vt_ref, wide_ref, bias_ref, k_ref = refs[18:27]
    held = refs[27:35]
    n1_ref, c1_ref, q_ref, kt_ref, v_ref, p_ref = held[:6]
    exports = held[6:]
    sems, store_sems = refs[35:]

    def store(index):
        load(held[index], kept[index], store_sems.at[index])

    tokens, width = x_ref.shape
    for member, full in enumerate((wq, wk, wv, wo)):
        fetch_member(pos_w, bufs, member, full, sems.at[member])
    bias_ref[...] = jnp.where(lab_ref[...] == seg_ref[...], 0.0, MASKED)
    low = x_ref[...].astype(BF16)
    rows_ref[:tokens] = low
    rows_ref[tokens:] = xp_ref[...]
    wide_ref[...] = low.T
    export_rows(pos_g, wide_ref, exports, 0)
    wait_full(wq, sems.at[0])
    query = (nn(low, flat(wq[...])) + row_of(vec_ref, QB)).astype(BF16)
    q_ref[...] = (query.astype(F32) * HD ** (-0.5)).astype(BF16)
    wait_full(wk, sems.at[1])
    key = nn(rows_ref[...], flat(wk[...])).astype(BF16)
    k_ref[...] = key
    kt_ref[...] = key.T
    store(2)
    store(3)
    wait_full(wv, sems.at[2])
    value = (nn(rows_ref[...], flat(wv[...])) + row_of(vec_ref, VB)).astype(BF16)
    v_ref[...] = value
    vt_ref[...] = value.T
    store(4)

    def pair(index, carry):
        lane = pl.multiple_of(index * 128, 128)
        keys = k_ref[:, pl.ds(lane, 128)]
        queries = q_ref[:, pl.ds(lane, 128)]
        first = lax.broadcasted_iota(jnp.int32, queries.shape, 1) < HD
        for which in range(2):
            mine = jnp.where(first if which == 0 else ~first, queries, jnp.zeros_like(queries))
            scores = nt(keys, mine) + bias_ref[...]
            expos = jnp.exp(scores - jnp.max(scores, axis=0, keepdims=True))
            probs = (expos * (1.0 / jnp.sum(expos, axis=0, keepdims=True))).astype(BF16)
            p_ref[index * 2 + which] = probs
            row = pl.multiple_of(index * 128 + which * HD, HD)
            wide_ref[pl.ds(row, HD), :] = nn(vt_ref[pl.ds(row, HD), :], probs).astype(BF16)
        both = pl.ds(index * 2, 2)
        load(p_ref.at[both], kept[5].at[both], store_sems.at[5])
        return carry

    lax.fori_loop(0, width // 128, pair, 0)
    export_rows(pos_g, wide_ref, exports, 1)
    mixed = wide_ref[...].T
    wait_full(wo, sems.at[3])
    branch = nn(mixed, flat(wo[...])) + row_of(vec_ref, OB)
    normed, inverse = normalize(x_ref[...] + branch)
    hidden = normed * row_of(vec_ref, AG) + row_of(vec_ref, AS)
    h_ref[...] = hidden
    n1_ref[...] = normed
    c1_ref[...] = jnp.broadcast_to(inverse, c1_ref.shape)
    wide_ref[...] = hidden.astype(BF16).T
    export_rows(pos_g, wide_ref, exports, 2)
    for index in (0, 1, 6, 7):
        store(index)
    for index in range(8):
        wait_full(held[index], store_sems.at[index])


def attn_forward(pos_w, pos_g, x, xp, seg, lab, vec, bufs):
    tokens, width = x.shape
    heads = width // HD
    export = shape((3, 2, ZS, width // BLOCKS, tokens), BF16)
    kept = (
        shape((tokens, width), F32),
        shape((tokens, 128), F32),
        shape((tokens, width), BF16),
        shape((width, 2 * tokens), BF16),
        shape((2 * tokens, width), BF16),
        shape((heads, 2 * tokens, tokens), BF16),
        export,
        export,
    )
    return pl.pallas_call(
        attn_kernel,
        out_shape=(shape((tokens, width), F32),) + kept,
        in_specs=[SMEM, SMEM] + [VMEM] * 5 + [ANY] * 2,
        out_specs=[VMEM] + [HBM] * 8,
        scratch_shapes=[square(width)] * 4
        + [
            pltpu.VMEM((2 * tokens, width), BF16),
            pltpu.VMEM((width, 2 * tokens), BF16),
            pltpu.VMEM((width, tokens), BF16),
            pltpu.VMEM((2 * tokens, tokens), F32),
            pltpu.VMEM((2 * tokens, width), BF16),
        ]
        + [pltpu.VMEM(each.shape, each.dtype) for each in kept]
        + [pltpu.SemaphoreType.DMA((4,)), pltpu.SemaphoreType.DMA((8,))],
        compiler_params=params(VMEM_MB),
        cost_estimate=cost(),
        name="attn_forward",
    )(pos_w, pos_g, x, xp, seg, lab, vec, *bufs)


def head_back(grad, normed, inverse, gain, low_ref, back_ref, sums_ref):
    sums_ref[...] = jnp.zeros_like(sums_ref)
    sums_ref[pl.ds(0, 1), :] = colsum(grad * normed)
    sums_ref[pl.ds(1, 1), :] = colsum(grad)
    back = norm_back(normed, inverse, grad * gain)
    low = back.astype(BF16)
    low_ref[...] = low
    back_ref[...] = back
    sums_ref[pl.ds(2, 1), :] = colsum(low.astype(F32))


def head_shapes(tokens, width):
    return (
        shape((tokens, width), BF16),
        shape((tokens, width), F32),
        shape((8, width), F32),
    )


def inner_kernel(tile, *refs):
    pos_w, pos_g, h_ref, vec_ref = refs[:4]
    bufs, active_ref, kept = refs[4:6], refs[6], refs[7:10]
    wi, low_ref, wide_ref = refs[10:13]
    held = refs[13:16]
    gp_ref, exports = held[0], held[1:]
    sem, store_sems = refs[16:]
    width, hidden = h_ref.shape[1], wi.shape[3]
    fetch_columns(pos_w, bufs, wi, sem)
    low_ref[...] = h_ref[...].astype(BF16)
    wait_full(wi, sem)
    per_row = width // tile

    def step(index, carry):
        lanes = pl.ds(pl.multiple_of(index * tile, tile), tile)
        bias = vec_ref[pl.ds(IB + lax.div(index, per_row), 1), :]
        part = lax.rem(index, per_row)
        chosen = bias[:, :tile]
        for other in range(1, per_row):
            chosen = jnp.where(part == other, bias[:, other * tile : (other + 1) * tile], chosen)
        pre = nn(low_ref[...], flat(wi[:, :, :, lanes])) + chosen
        phi = 0.5 * (1.0 + lax.erf(pre * 0.7071067811865476))
        dens = jnp.exp(-0.5 * pre * pre) * 0.3989422804014327
        gp_ref[:, lanes] = (phi + pre * dens).astype(BF16)
        active = (pre * phi).astype(BF16)
        active_ref[:, lanes] = active
        wide_ref[lanes, :] = active.T
        return carry

    lax.fori_loop(0, hidden // tile, step, 0)
    load(held[0], kept[0], store_sems.at[0])
    export_halves(pos_g, wide_ref, exports)
    for index in (1, 2):
        load(held[index], kept[index], store_sems.at[index])
    for index in range(3):
        wait_full(held[index], store_sems.at[index])


def inner_forward(pos_w, pos_g, h, vec, bufs):
    tokens, width = h.shape
    hidden = bufs[0].shape[2] * 4
    export = shape((2, 2, 2, ZS, hidden // BLOCKS // 4, tokens), BF16)
    kept = (shape((tokens, hidden), BF16), export, export)
    return pl.pallas_call(
        functools.partial(inner_kernel, 384),
        out_shape=(shape((tokens, hidden), BF16),) + kept,
        in_specs=[SMEM, SMEM, VMEM, VMEM] + [ANY] * 2,
        out_specs=[VMEM] + [HBM] * 3,
        scratch_shapes=[
            wide_matrix(width, hidden),
            pltpu.VMEM((tokens, width), BF16),
            pltpu.VMEM((hidden, tokens), BF16),
        ]
        + [pltpu.VMEM(each.shape, each.dtype) for each in kept]
        + [pltpu.SemaphoreType.DMA, pltpu.SemaphoreType.DMA((3,))],
        compiler_params=params(VMEM_MB),
        cost_estimate=cost(),
        name="inner_forward",
    )(pos_w, pos_g, h, vec, *bufs)


def outer_kernel(last, *refs):
    pos_w, h_ref, active_ref, vec_ref = refs[:4]
    grad_ref = refs[4] if last else None
    refs = refs[4 + last :]
    bufs = refs[:2]
    outs, wu, acc_ref, sem = refs[2:-3], refs[-3], refs[-2], refs[-1]
    fetch_rows(pos_w, bufs, wu, sem)
    acc_ref[...] = h_ref[...] + row_of(vec_ref, UB)
    wait_full(wu, sem)
    tile = active_ref.shape[1] // ZS
    for z in range(ZS):
        acc_ref[...] += nn(active_ref[:, pl.ds(z * tile, tile)], flat(wu[z]))
    normed, inverse = normalize(acc_ref[...])
    result = normed * row_of(vec_ref, FG) + row_of(vec_ref, FS)
    outs[0][...] = result
    outs[1][...] = result.astype(BF16)
    if last:
        head_back(
            grad_ref[...].astype(F32), normed, inverse, row_of(vec_ref, FG), outs[2], outs[3], outs[4]
        )
    else:
        outs[2][...] = normed
        outs[3][...] = jnp.broadcast_to(inverse, outs[3].shape)


def outer_forward(pos_w, h, active, vec, bufs, grad):
    tokens, width = h.shape
    hidden = active.shape[1]
    last = grad is not None
    outs = (shape((tokens, width), F32), shape((tokens, width), BF16))
    if last:
        outs += head_shapes(tokens, width)
    else:
        outs += (shape((tokens, width), F32), shape((tokens, 128), F32))
    return pl.pallas_call(
        functools.partial(outer_kernel, int(last)),
        out_shape=outs,
        in_specs=[SMEM] + [VMEM] * (3 + last) + [ANY] * 2,
        out_specs=[VMEM] * len(outs),
        scratch_shapes=[
            tall_matrix(hidden, width),
            pltpu.VMEM((tokens, width), F32),
            pltpu.SemaphoreType.DMA,
        ],
        compiler_params=params(VMEM_MB),
        cost_estimate=cost(),
        name="outer_forward",
    )(pos_w, h, active, vec, *((grad,) if last else ()), *bufs)


def chain_kernel(tile, waits, *refs):
    pos_w, dyl_ref, dy_ref = refs[:3]
    sources, vec_ref = refs[3:6], refs[6]
    inner_bufs, outer_bufs, attn_bufs = refs[7:9], refs[9:11], refs[11:13]
    refs = refs[13 + waits :]
    pack_ref, da_ref, do_ref, sums_ref = refs[:4]
    wi, wu, wo, acc_ref = refs[4:8]
    held = refs[8:11]
    gp_ref, n1_ref, c1_ref = held
    sems, load_sems = refs[11:]
    width, hidden = dy_ref.shape[1], wi.shape[3]
    for index in range(3):
        load(sources[index], held[index], load_sems.at[index])
    du_ref = pack_ref.at[:, pl.ds(0, hidden)]
    dal_ref = pack_ref.at[:, pl.ds(hidden, width)]
    fetch_rows(pos_w, outer_bufs, wu, sems.at[0])
    fetch_columns(pos_w, inner_bufs, wi, sems.at[1])
    fetch_member(pos_w, attn_bufs, 3, wo, sems.at[2])
    sums_ref[...] = jnp.zeros_like(sums_ref)
    acc_ref[...] = dy_ref[...]
    wait_full(gp_ref, load_sems.at[0])
    wait_full(wu, sems.at[0])
    wait_full(wi, sems.at[1])
    per_row = width // tile

    for index in range(hidden // tile):
        lane = index * tile
        rows = wu[index * ZS * tile // hidden, pl.ds(lane % (hidden // ZS) * BLOCKS // hidden, tile * BLOCKS // hidden)]
        part = nt(dyl_ref[...], flat(rows))
        part = (part * gp_ref[:, pl.ds(lane, tile)].astype(F32)).astype(BF16)
        du_ref[:, pl.ds(lane, tile)] = part
        acc_ref[...] += nt(part, flat(wi[:, :, :, pl.ds(lane, tile)]))
        sums_ref[
            pl.ds(IB + index // per_row, 1), pl.ds(index % per_row * tile, tile)
        ] = colsum(part.astype(F32))

    grad = acc_ref[...]
    wait_full(n1_ref, load_sems.at[1])
    wait_full(c1_ref, load_sems.at[2])
    normed = n1_ref[...]
    sums_ref[pl.ds(AG, 1), :] = colsum(grad * normed)
    sums_ref[pl.ds(AS, 1), :] = colsum(grad)
    back = norm_back(normed, c1_ref[:, :1], grad * row_of(vec_ref, AG))
    da_ref[...] = back
    low = back.astype(BF16)
    dal_ref[...] = low
    sums_ref[pl.ds(OB, 1), :] = colsum(low.astype(F32))
    wait_full(wo, sems.at[2])
    do_ref[...] = nt(low, flat(wo[...])).astype(BF16)


def chain_backward(pos_w, dyl, dy, gp, n1, c1, vec, inner_bufs, outer_bufs, attn_bufs, after=()):
    tokens, width = n1.shape
    hidden = gp.shape[1]
    return pl.pallas_call(
        functools.partial(chain_kernel, 384, len(after)),
        out_shape=(
            shape((tokens, hidden + width), BF16),
            shape((tokens, width), F32),
            shape((tokens, width), BF16),
            shape((16, width), F32),
        ),
        in_specs=[SMEM] + [VMEM] * 2 + [HBM] * 3 + [VMEM] + [ANY] * (6 + len(after)),
        out_specs=[VMEM] * 4,
        scratch_shapes=[
            wide_matrix(width, hidden),
            tall_matrix(hidden, width),
            square(width),
            pltpu.VMEM((tokens, width), F32),
        ]
        + [pltpu.VMEM(each.shape, each.dtype) for each in (gp, n1, c1)]
        + [pltpu.SemaphoreType.DMA((3,)), pltpu.SemaphoreType.DMA((3,))],
        compiler_params=params(VMEM_MB),
        cost_estimate=cost(),
        name="chain_backward",
    )(pos_w, dyl, dy, gp, n1, c1, vec, *inner_bufs, *outer_bufs, *attn_bufs, *after)


def attn_back_kernel(waits, *refs):
    sources, do_ref = refs[:4], refs[4]
    refs = refs[waits:]
    pack_ref, sum_ref, wide_ref = refs[5], refs[6], refs[7]
    held, sems, pair_sems = refs[8:12], refs[12], refs[13]
    q_ref, kt_ref, v_ref, p_ref = held
    tokens, width = q_ref.shape
    for index in range(3):
        load(sources[index], held[index], sems.at[index])
    for index in range(width // 128):
        both = pl.ds(index * 2, 2)
        load(sources[3].at[both], p_ref.at[both], pair_sems.at[index])
    for index in range(3):
        wait_full(held[index], sems.at[index])

    def pair(index, carry):
        lane = pl.multiple_of(index * 128, 128)
        values = v_ref[:, pl.ds(lane, 128)]
        queries = q_ref[:, pl.ds(lane, 128)]
        grads = do_ref[:, pl.ds(lane, 128)]
        first = lax.broadcasted_iota(jnp.int32, grads.shape, 1) < HD
        keys_back, values_back = [], []
        wait_full(p_ref.at[pl.ds(index * 2, 2)], pair_sems.at[index])
        for which in range(2):
            mine = jnp.where(first if which == 0 else ~first, grads, jnp.zeros_like(grads))
            probs_low = p_ref[index * 2 + which]
            probs = probs_low.astype(F32)
            weighted = probs * nt(values, mine)
            back = weighted - probs * jnp.sum(weighted, axis=0, keepdims=True)
            low = back.astype(BF16)
            keys_back.append(nn(low, queries))
            values_back.append(nn(probs_low, grads))
            row = pl.multiple_of(index * 128 + which * HD, HD)
            wide_ref[pl.ds(row, HD), :] = nn(kt_ref[pl.ds(row, HD), :], low)
        split = lax.broadcasted_iota(jnp.int32, keys_back[0].shape, 1) < HD
        for at, back in ((1, keys_back), (3, values_back)):
            low = jnp.where(split, back[0], back[1]).astype(BF16)
            pack_ref[at, :, pl.ds(lane, 128)] = low[:tokens]
            pack_ref[at + 1, :, pl.ds(lane, 128)] = low[tokens:]
        return carry

    lax.fori_loop(0, width // 128, pair, 0)
    low = (wide_ref[...].T * HD ** (-0.5)).astype(BF16)
    pack_ref[0] = low
    sum_ref[...] = jnp.broadcast_to(colsum(low.astype(F32)), sum_ref.shape)


def attn_backward(q, kt, v, p, do, after=()):
    tokens, width = q.shape
    return pl.pallas_call(
        functools.partial(attn_back_kernel, len(after)),
        out_shape=(
            shape((5, tokens, width), BF16),
            shape((8, width), F32),
        ),
        in_specs=[HBM] * 4 + [VMEM] + [ANY] * len(after),
        out_specs=[VMEM] * 2,
        scratch_shapes=[pltpu.VMEM((width, tokens), F32)]
        + [pltpu.VMEM(each.shape, each.dtype) for each in (q, kt, v, p)]
        + [pltpu.SemaphoreType.DMA((3,)), pltpu.SemaphoreType.DMA((width // 128,))],
        compiler_params=params(VMEM_MB),
        cost_estimate=cost(),
        name="attn_backward",
    )(q, kt, v, p, do, *after)


def input_kernel(first, *refs):
    pos_w, da_ref, pack_ref, got_ref = refs[:4]
    bufs = refs[4:6]
    refs = refs[6:]
    if not first:
        n2_ref, c2_ref, vec_ref = refs[:3]
        refs = refs[3:]
    total_ref, sum_ref = refs[:2]
    heads = refs[2:-4]
    wq, wk, wv, sems = refs[-4:]
    tokens, width = da_ref.shape
    for member, full in enumerate((wq, wk, wv)):
        fetch_member(pos_w, bufs, member, full, sems.at[member])
    for at, (mine, theirs) in enumerate(((1, 2), (2, 1), (3, 4), (4, 3))):
        total_ref[at] = (pack_ref[mine].astype(F32) + got_ref[theirs].astype(F32)).astype(BF16)
    sum_ref[...] = jnp.broadcast_to(colsum(total_ref[2].astype(F32)), sum_ref.shape)
    wait_full(wq, sems.at[0])
    dx = da_ref[...] + nt(pack_ref[0], flat(wq[...]))
    wait_full(wk, sems.at[1])
    dx += nt(total_ref[0], flat(wk[...]))
    wait_full(wv, sems.at[2])
    dx += nt(total_ref[2], flat(wv[...]))
    if first:
        heads[0][...] = dx.astype(BF16)
    else:
        head_back(dx, n2_ref[...], c2_ref[:, :1], row_of(vec_ref, FG), *heads)


def input_backward(pos_w, da, pack, got, bufs, below):
    tokens, width = da.shape
    first = below is None
    outs = (shape((4, tokens, width), BF16), shape((8, width), F32))
    outs += (shape((tokens, width), BF16),) if first else head_shapes(tokens, width)
    return pl.pallas_call(
        functools.partial(input_kernel, first),
        out_shape=outs,
        in_specs=[SMEM] + [VMEM] * 3 + [ANY] * 2 + ([] if first else [VMEM] * 3),
        out_specs=[VMEM] * len(outs),
        scratch_shapes=[square(width)] * 3 + [pltpu.SemaphoreType.DMA((3,))],
        compiler_params=params(VMEM_MB),
        cost_estimate=cost(),
        name="input_backward",
    )(pos_w, da, pack, got, *bufs, *(() if first else below))


def place(outs, part, dy, value):
    a_keep, a_send, b_keep, b_send = outs
    if part == 0:
        a_keep[dy] = value[0]
        a_send[dy] = value[1]
    else:
        (b_send if dy else b_keep)[...] = value


def grad_shapes(rows, width):
    return (shape((2, ZS, rows, width), BF16),) * 4


def inner_grad_kernel(pos_ref, ta_ref, tb_ref, da_ref, db_ref, *refs):
    outs, left, sems = refs[:4], refs[4], refs[5]
    _, _, rows, width = outs[0].shape
    tokens = ta_ref.shape[-1]
    for side, source in enumerate((ta_ref, tb_ref)):
        load(source.at[2], left.at[side], sems.at[side])
    for side in range(2):
        wait_full(left.at[side], sems.at[side])
    left_a = left[0].reshape(2 * ZS * rows, tokens)
    left_b = left[1].reshape(2 * ZS * rows, tokens)
    for dy in range(2):
        for part in range(2):
            lanes = pl.ds(pl.multiple_of((half_at(pos_ref, dy) * 2 + part) * width, 128), width)
            value = nn(left_a, da_ref[:, lanes]) + nn(left_b, db_ref[:, lanes])
            place(outs, part, dy, value.astype(BF16).reshape(2, ZS, rows, width))


def inner_grad(pos_g, ta, tb, da, db):
    rows = ta.shape[3]
    return pl.pallas_call(
        inner_grad_kernel,
        out_shape=grad_shapes(rows, rows * BLOCKS),
        in_specs=[SMEM] + [HBM] * 2 + [VMEM] * 2,
        out_specs=[VMEM] * 4,
        scratch_shapes=[pltpu.VMEM((2,) + ta.shape[1:], BF16), pltpu.SemaphoreType.DMA((2,))],
        compiler_params=params(VMEM_MB),
        cost_estimate=cost(),
        name="inner_grad",
    )(pos_g, ta, tb, da, db)


def outer_grad_kernel(ta_ref, tb_ref, da_ref, db_ref, *refs):
    outs, left, sems = refs[:4], refs[4], refs[5]
    _, _, rows, width = outs[0].shape
    tokens = ta_ref.shape[-1]
    for side, source in enumerate((ta_ref, tb_ref)):
        load(source, left.at[side], sems.at[side])
    for side in range(2):
        wait_full(left.at[side], sems.at[side])
    for dy in range(2):
        for part in range(2):
            values = []
            for dx in range(2):
                left_a = left[0, dx, dy, part].reshape(ZS * rows, tokens)
                left_b = left[1, dx, dy, part].reshape(ZS * rows, tokens)
                value = nn(left_a, da_ref[...]) + nn(left_b, db_ref[...])
                values.append(value.astype(BF16).reshape(ZS, rows, width))
            place(outs, part, dy, jnp.stack(values))


def outer_grad(ta, tb, da, db):
    rows, width = ta.shape[4], da.shape[1]
    return pl.pallas_call(
        outer_grad_kernel,
        out_shape=grad_shapes(rows, width),
        in_specs=[HBM] * 2 + [VMEM] * 2,
        out_specs=[VMEM] * 4,
        scratch_shapes=[pltpu.VMEM((2,) + ta.shape, BF16), pltpu.SemaphoreType.DMA((2,))],
        compiler_params=params(VMEM_MB),
        cost_estimate=cost(),
        name="outer_grad",
    )(ta, tb, da, db)


def attn_grad_kernel(pos_ref, xa_ref, xb_ref, qa_ref, qb_ref, total_ref, da_ref, db_ref, *refs):
    outs, left, sems = refs[:4], refs[4], refs[5]
    for side, source in enumerate((xa_ref, xb_ref)):
        load(source.at[pl.ds(0, 2)], left.at[side], sems.at[side])
    for side in range(2):
        wait_full(left.at[side], sems.at[side])
    _, _, rows, width = outs[0].shape
    half = width // 2
    tokens = xa_ref.shape[-1]
    height = 2 * ZS * rows
    x_a = left[0, 0].reshape(height, tokens)
    x_b = left[1, 0].reshape(height, tokens)
    o_a = left[0, 1].reshape(height, tokens)
    o_b = left[1, 1].reshape(height, tokens)
    last = da_ref.shape[1] - width
    for dy in range(2):
        start = half_at(pos_ref, dy) * half
        lanes = pl.ds(pl.multiple_of(start, 128), half)
        tail = pl.ds(pl.multiple_of(start + last, 128), half)
        members = (
            nn(x_a, qa_ref[0, :, lanes]) + nn(x_b, qb_ref[0, :, lanes]),
            nn(x_a, total_ref[0, :, lanes]) + nn(x_b, total_ref[1, :, lanes]),
            nn(x_a, total_ref[2, :, lanes]) + nn(x_b, total_ref[3, :, lanes]),
            nn(o_a, da_ref[:, tail]) + nn(o_b, db_ref[:, tail]),
        )
        for part in range(2):
            value = jnp.concatenate(members[part * 2 : part * 2 + 2], axis=1)
            place(outs, part, dy, value.astype(BF16).reshape(2, ZS, rows, width))


def attn_grad(pos_g, xa, xb, qa, qb, total, da, db):
    rows = xa.shape[3]
    return pl.pallas_call(
        attn_grad_kernel,
        out_shape=grad_shapes(rows, rows * BLOCKS),
        in_specs=[SMEM] + [HBM] * 2 + [VMEM] * 5,
        out_specs=[VMEM] * 4,
        scratch_shapes=[pltpu.VMEM((2, 2) + xa.shape[1:], BF16), pltpu.SemaphoreType.DMA((2,))],
        compiler_params=params(VMEM_MB),
        cost_estimate=cost(),
        name="attn_grad",
    )(pos_g, xa, xb, qa, qb, total, da, db)


def copy_kernel(plan, inputs, pos_ref, *refs):
    ins, outs, sems = refs[:inputs], refs[inputs:-1], refs[-1]
    copies = []
    for index, (out, to, source, at, size, by_z) in enumerate(plan):
        if by_z:
            z = pos_ref[0]
            to = flip(lax.div(z, 2), to // 2) * 2 + flip(lax.rem(z, 2), to % 2)
        copies.append(
            pltpu.make_async_copy(
                ins[source].at[pl.ds(at, size)], outs[out].at[pl.ds(to, size)], sems.at[index]
            )
        )
    for each in copies:
        each.start()
    for each in copies:
        each.wait()


def copy_blocks(pos, plan, inputs, sizes, name):
    piece = inputs[0].shape[1:]
    return pl.pallas_call(
        functools.partial(copy_kernel, plan, len(inputs)),
        out_shape=tuple(shape((size,) + piece, BF16) for size in sizes),
        in_specs=[SMEM] + [ANY] * len(inputs),
        out_specs=[VMEM] * len(sizes),
        scratch_shapes=[pltpu.SemaphoreType.DMA((len(plan),))],
        compiler_params=params(VMEM_MB),
        cost_estimate=cost(),
        name=name,
    )(pos, *inputs)


def pack_kernel(group, pos_ref, *refs):
    four, inner, outer = refs[:4], refs[4], refs[5]
    out, sem = refs[6], refs[7]
    rows, width = out.shape[1:]
    half = width // 2
    y = pos_ref[3]
    for j, chunk in enumerate(group):
        layer, kind = chunk // 3, chunk % 3
        for part in range(2):
            to = out.at[2 * j + part]
            if kind == 0:
                for side in range(2):
                    pltpu.make_async_copy(
                        four[2 * part + side].at[layer, :, pl.ds(pl.multiple_of(y * half, 128), half)],
                        to.at[:, pl.ds(side * half, half)],
                        sem,
                    ).start()
            elif kind == 1:
                lane = pl.multiple_of((2 * y + part) * width, 128)
                pltpu.make_async_copy(inner.at[layer, :, pl.ds(lane, width)], to, sem).start()
            else:
                row = pl.multiple_of((2 * y + part) * rows, 16)
                pltpu.make_async_copy(outer.at[layer, pl.ds(row, rows)], to, sem).start()
    wait_full(out, sem)


def pack_pieces(group, pos, weights):
    _, rows, width = weights[0].shape
    return pl.pallas_call(
        functools.partial(pack_kernel, group),
        out_shape=shape((2 * len(group), rows, width), BF16),
        in_specs=[SMEM] + [HBM] * 6,
        out_specs=VMEM,
        scratch_shapes=[pltpu.SemaphoreType.DMA],
        compiler_params=params(VMEM_MB),
        cost_estimate=cost(),
        name="pack",
    )(pos, *weights)


def table_kernel(at_ref, *refs):
    vectors, out = refs[:-1], refs[-1]
    width = out.shape[2]
    for index, vector in enumerate(vectors):
        size = vector.shape[1]
        start = at_ref[0] * size
        for piece in range(max(1, out.shape[1] - IB if index == IB else 1)):
            lanes = lax.broadcasted_iota(jnp.int32, (size, width), 1) + piece * width
            spot = lax.broadcasted_iota(jnp.int32, (size, width), 0) + start
            chosen = (lanes == spot).astype(F32).astype(BF16)
            out[:, index + piece, :] = nn(vector[...], chosen)


def vector_table(at, vectors, width):
    layers, last = vectors[-1].shape[0], vectors[-1].shape[1]
    rows = IB + last // vectors[0].shape[1]
    return pl.pallas_call(
        table_kernel,
        out_shape=shape((layers, rows, width), F32),
        in_specs=[SMEM] + [VMEM] * len(vectors),
        out_specs=VMEM,
        compiler_params=params(VMEM_MB),
        cost_estimate=cost(),
        name="vector_table",
    )(at, *vectors)


def finish_kernel(kind, offsets, pos_ref, *refs):
    layers = len(offsets)
    owns, gots = refs[:layers], refs[layers : 2 * layers]
    outs, buf, sems = refs[2 * layers : -2], refs[-2], refs[-1]
    rows, width = buf.shape[2:]
    half = width // 2
    y = pos_ref[3]
    copies = []
    for layer in range(layers):
        copies.append(
            pltpu.make_async_copy(
                gots[layer].at[pl.ds(offsets[layer], 3)], buf.at[layer], sems.at[layer]
            )
        )
        copies[-1].start()
    for each in copies:
        each.wait()
    for side in range(2):
        yy = y if side == 0 else 1 - y
        for layer in range(layers):
            for part in range(2):
                if part == 0:
                    value = owns[layer][side].astype(BF16).astype(F32)
                    value = value + buf[layer, 1 - side].astype(F32)
                else:
                    value = (buf[layer, 2] if side else owns[layer][2].astype(BF16)).astype(F32)
                if kind == 0:
                    lanes = pl.ds(pl.multiple_of(yy * half, 128), half)
                    for member in range(2):
                        outs[2 * part + member][layer, :, lanes] = value[
                            :, member * half : (member + 1) * half
                        ]
                elif kind == 1:
                    lane = pl.multiple_of((2 * yy + part) * width, 128)
                    outs[0][layer, :, pl.ds(lane, width)] = value
                else:
                    row = pl.multiple_of((2 * yy + part) * rows, 16)
                    outs[0][layer, pl.ds(row, rows), :] = value


def finish(kind, pos, results):
    layers = len(results)
    _, rows, width = results[0][0].shape
    outs = {
        0: (shape((layers, rows, width), F32),) * 4,
        1: (shape((layers, rows, 4 * width), F32),),
        2: (shape((layers, 4 * rows, width), F32),),
    }[kind]
    return pl.pallas_call(
        functools.partial(finish_kernel, kind, tuple(value[2] for value in results)),
        out_shape=outs,
        in_specs=[SMEM] + [VMEM] * layers + [ANY] * layers,
        out_specs=[VMEM] * len(outs),
        scratch_shapes=[
            pltpu.VMEM((layers, 3, rows, width), BF16),
            pltpu.SemaphoreType.DMA((layers,)),
        ],
        compiler_params=params(VMEM_MB),
        cost_estimate=cost(),
        name="finish",
    )(pos, *[value[0] for value in results], *[value[1] for value in results])


def sum_kernel(config, *refs):
    fresh, first, second, third, fourth, small, waits = config
    refs = list(refs)

    def take(count):
        out = refs[:count]
        del refs[:count]
        return out

    sends = take(2) if fresh else None
    got_x = take(1)[0] if first or second else None
    got_y = take(1)[0] if first else None
    keeps = take(2) if first else None
    rests = take(2) if second else None
    pairs = take(2) if third else None
    lasts = take(2) if fourth else None
    tables = take(2 if small == 1 else 1) if small else None
    take(waits)
    to_x = take(1)[0] if fresh or first else None
    to_y = take(1)[0] if fresh or fourth else None
    at = 0
    if fresh:
        for out, send in ((to_x, sends[0]), (to_y, sends[1])):
            for half in range(2):
                out[half * ZS : (half + 1) * ZS] = send[half]
        at = 2 * ZS
    if first:
        a_rest, b_rest = take(2)
        for half in range(2):
            come = got_x[half * ZS : (half + 1) * ZS].astype(F32)
            a_rest[half] = (keeps[0][half].astype(F32) + come).astype(BF16)
        b_rest[...] = (keeps[1][0].astype(F32) + got_y[:ZS].astype(F32)).astype(BF16)
        value = keeps[1][1].astype(F32) + got_y[ZS : 2 * ZS].astype(F32)
        to_x[at : at + ZS] = value.astype(BF16)
    if second:
        hold, to_z1 = take(2)
        begin = 2 * ZS if first else 0
        for k in range(ZS):
            out = to_z1 if k % 2 else hold
            for half in range(2):
                out[k // 2 * 3 + half] = rests[0][half, k]
            value = rests[1][k].astype(F32) + got_x[begin + k].astype(F32)
            out[k // 2 * 3 + 2] = value.astype(BF16)
    if third:
        hold, to_z2 = take(2)
        for index in range(3):
            hold[index] = pairs[0][index].astype(F32) + pairs[1][index].astype(F32)
            value = pairs[0][3 + index].astype(F32) + pairs[1][3 + index].astype(F32)
            to_z2[index] = value.astype(BF16)
    if fourth:
        (total,) = take(1)
        value = lasts[0][...] + lasts[1][:3].astype(F32)
        total[...] = value
        to_y[at : at + 3] = value.astype(BF16)
    if small:
        come = (None, None, got_x, pairs and pairs[1], lasts and lasts[1])[small]
        come = tables[1][...] if small == 1 else come[come.shape[0] - 1]
        value = tables[0][...] + come.astype(F32)
        refs[0][...] = value
        to = (None, to_x, to_z1 if second else None, to_z2 if third else None, to_y)[small]
        to[to.shape[0] - 1] = value.astype(BF16)


def sum_round(fresh, got_x, got_y, first, second, third, fourth, small, after):
    stage, table = small
    config = tuple(value is not None for value in (fresh, first, second, third, fourth)) + (stage, len(after))
    sample = fresh or first or second or third or fourth
    rows, width = sample[-1].shape[-2:]
    inputs, outputs = [], []
    if fresh is not None:
        inputs += [fresh[1], fresh[3]]
    if first is not None or second is not None:
        inputs += [got_x]
    if first is not None:
        inputs += [got_y]
    for value in (first, second, third, fourth, table):
        if value is not None:
            inputs += list(value)
    begin = 2 * ZS * config[0]
    if config[0] or config[1]:
        outputs += [shape((begin + ZS * config[1] + (stage == 1), rows, width), BF16)]
    if config[0] or config[4]:
        outputs += [shape((begin + 3 * config[4] + (stage == 4), rows, width), BF16)]
    if config[1]:
        outputs += [shape((2, ZS, rows, width), BF16), shape((ZS, rows, width), BF16)]
    if config[2]:
        outputs += [shape((6, rows, width), BF16), shape((6 + (stage == 2), rows, width), BF16)]
    if config[3]:
        outputs += [shape((3, rows, width), F32), shape((3 + (stage == 3), rows, width), BF16)]
    if config[4]:
        outputs += [shape((3, rows, width), F32)]
    if config[5]:
        outputs += [shape(table[0].shape, F32)]
    outs = list(
        pl.pallas_call(
            functools.partial(sum_kernel, config),
            out_shape=tuple(outputs),
            in_specs=[VMEM] * len(inputs) + [ANY] * len(after),
            out_specs=[VMEM] * len(outputs),
            compiler_params=params(VMEM_MB),
            cost_estimate=cost(),
            name="sum_round",
        )(*inputs, *after)
    )

    def take(wanted, count):
        if not wanted:
            return None
        out = tuple(outs[:count])
        del outs[:count]
        return out

    to_x = take(config[0] or config[1], 1)
    to_y = take(config[0] or config[4], 1)
    return (
        to_x,
        to_y,
        begin,
        take(config[1], 2),
        take(config[2], 2),
        take(config[3], 2),
        take(config[4], 1),
        take(stage > 0, 1),
    )


def collect_kernel(*refs):
    out = refs[-1]
    for layer in range(out.shape[0]):
        query_ref, value_ref, head_ref, chain_ref = refs[4 * layer : 4 * layer + 4]
        out[layer] = chain_ref[...]
        out[layer, pl.ds(QB, 1), :] = query_ref[:1]
        out[layer, pl.ds(VB, 1), :] = value_ref[:1]
        for at, index in enumerate((FG, FS, UB)):
            out[layer, pl.ds(index, 1), :] = head_ref[at : at + 1]


def collect(vectors, rows):
    flat = [value for layer in vectors for value in layer]
    width = flat[0].shape[1]
    return pl.pallas_call(
        collect_kernel,
        out_shape=shape((len(vectors), rows, width), F32),
        in_specs=[VMEM] * len(flat),
        out_specs=VMEM,
        compiler_params=params(VMEM_MB),
        cost_estimate=cost(),
        name="collect",
    )(*flat)


def vectors_kernel(last, at_ref, table_ref, got_ref, *outs):
    layers, width = outs[0].shape[0], table_ref.shape[1]
    at = at_ref[0]
    for index, out in enumerate(outs):
        size = out.shape[1]
        start = at * size
        shift = lax.rem(width - lax.rem(start, width), width)
        for layer in range(layers):
            spot = pl.ds(layer * 16 + index + lax.div(start, width), 1)
            value = table_ref[spot, :]
            if last is not None:
                value = value.astype(BF16).astype(F32) + got_ref[spot, :]
            value = jnp.broadcast_to(value, (8, width))
            out[pl.ds(layer, 1), :] = pltpu.roll(value, shift, 1)[:1, :size]


def own_vectors(at, table, got, layers, size, wide):
    sizes = [size] * IB + [wide]
    last = None if got is None else 0
    return pl.pallas_call(
        functools.partial(vectors_kernel, last),
        out_shape=tuple(shape((layers, each), F32) for each in sizes),
        in_specs=[SMEM, VMEM, VMEM],
        out_specs=[VMEM] * len(sizes),
        compiler_params=params(VMEM_MB),
        cost_estimate=cost(),
        name="own_vectors",
    )(at, table, table if got is None else got)


def fence(values):
    return lax.optimization_barrier(values)


def build(mesh):
    count = mesh.shape["dp"]

    def flat(dp, seq):
        return dp * 2 + seq

    def pairs(source_of):
        out = []
        for dp in range(count):
            for seq in range(2):
                out.append((flat(*source_of(dp, seq)), flat(dp, seq)))
        return out

    swap_pairs = pairs(lambda dp, seq: (dp // 2 * 2 + seq, dp % 2))
    core_pairs = pairs(lambda dp, seq: (dp ^ 1, seq))
    x_pairs = pairs(lambda dp, seq: (dp ^ 2, seq))
    y_pairs = pairs(lambda dp, seq: (dp, 1 - seq))
    z_pairs = [pairs(lambda dp, seq, k=k: ((dp // 4 ^ k) * 4 + dp % 4, seq)) for k in (1, 2)]

    def move(value, perm):
        return lax.ppermute(value, AXES, perm)

    return dict(
        count=count,
        swap=swap_pairs,
        core=core_pairs,
        x=x_pairs,
        y=y_pairs,
        z1=z_pairs[0],
        z2=z_pairs[1],
        move=move,
    )


def body(
    net,
    tokens,
    segment_ids,
    padding,
    query_weight,
    key_weight,
    value_weight,
    output_weight,
    query_bias,
    value_bias,
    output_bias,
    attn_gain,
    attn_shift,
    inner_weight,
    inner_bias,
    outer_weight,
    outer_bias,
    ffn_gain,
    ffn_shift,
    upstream,
):
    layers, small, width = query_weight.shape
    hidden = inner_weight.shape[2]
    count = net["count"]
    move = net["move"]
    staged = count == BLOCKS and small == 16 * layers
    dp = lax.axis_index("dp").astype(jnp.int32)
    y = lax.axis_index("seq").astype(jnp.int32)
    core = lax.rem(dp, 2)
    if staged:
        pos_g = jnp.stack([lax.div(dp, 4), lax.rem(lax.div(dp, 2), 2), core, y])
        pos_w = pos_g
    else:
        zero = jnp.zeros((), jnp.int32)
        pos_g = jnp.stack([zero, zero, core, zero])
        pos_w = jnp.stack([zero, zero, zero, zero])

    labels = jnp.where(padding == 1, segment_ids, -1)
    small_own = move(jnp.concatenate([segment_ids, labels]), net["swap"])
    token_low = move(tokens[0], net["swap"])

    vector_args = [query_bias, value_bias, output_bias, attn_gain, attn_shift, outer_bias]
    vector_args += [ffn_gain, ffn_shift, inner_bias]
    table = vector_table(dp[None], vector_args, width)
    if staged:
        table = table + move(table, net["x"])
    else:
        table = lax.psum(table, "dp")

    raw = (query_weight, key_weight, value_weight, output_weight, inner_weight, outer_weight)
    chunks = []
    for layer in range(layers):
        four = (query_weight[layer], key_weight[layer], value_weight[layer], output_weight[layer])
        if not staged:
            full = [lax.all_gather(value, "dp", axis=0, tiled=True) for value in four]
            inner = lax.all_gather(inner_weight[layer], "dp", axis=0, tiled=True)
            outer = lax.all_gather(outer_weight[layer], "dp", axis=0, tiled=True)
            rows = width // BLOCKS

            def cut(value, dy, dx, dc):
                value = value.reshape(ZS, 2, 2, rows, 2, -1)
                return value[:, dx, dc, :, dy, :]

            lists = [[[], []], [[], []], [[], []]]
            for dc in range(2):
                for part, dy, dx in UNITS:
                    lists[0][dc].append(
                        jnp.concatenate([cut(value, dy, dx, dc) for value in full[part * 2 : part * 2 + 2]], axis=2)
                    )
                    lists[1][dc].append(cut(inner, dy, dx, dc)[..., part * width : (part + 1) * width])
                    lists[2][dc].append(
                        outer.reshape(ZS, 2, 2, 2, 2, hidden // BLOCKS // 4, width)[:, dx, dc, dy, part]
                    )
            chunks.extend(tuple(jnp.concatenate(side) for side in value) for value in lists)

    total_chunks = 3 * layers
    groups = []
    if staged:
        edges = [0, 1, 2, 3] + list(range(4, total_chunks, 2)) + [total_chunks]
        groups = [range(low, high) for low, high in zip(edges[:-1], edges[1:])]
    where_of = {i: (g, i - group[0]) for g, group in enumerate(groups) for i in group}
    stage_z = [None] * len(groups)

    def start_z2(g):
        own = pack_pieces(groups[g], pos_g, raw)
        stage_z[g] = (own, move(own, net["z2"]))

    def start_z1(g):
        own, come = stage_z[g]
        size = own.shape[0]
        both = copy_blocks(
            pos_g,
            [(0, 0, 0, 0, size, False), (0, size, 1, 0, size, False)],
            (own, come),
            [2 * size],
            "gather_z",
        )[0]
        stage_z[g] = (both, move(both, net["z1"]))

    if staged:
        start_z2(0)
        stage_z[0], raw, table, small_own, token_low = fence(
            (stage_z[0], raw, table, small_own, token_low)
        )
        start_z1(0)
        start_z2(1)
        table = table + move(table, net["core"])
    small_other = move(small_own, net["core"])
    token_other = move(token_low, net["core"])
    if staged:
        stage_z[:2], raw, table, small_own, small_other, token_low, token_other, upstream = fence(
            (stage_z[:2], raw, table, small_own, small_other, token_low, token_other, upstream)
        )
    seg = small_own[0:1]
    lab = jnp.concatenate([small_own[1], small_other[1]])[:, None]
    current = token_low.astype(F32)
    other = token_other
    kept = [None] * layers
    todo = []
    for layer in range(layers):
        todo.append(("attn", layer, 3 * layer))
        todo.append(("inner", layer, 3 * layer + 1))
        todo.append(("outer", layer, 3 * layer + 2))
    low = None
    attn_out = None
    arrived = 0 if staged else total_chunks

    mid = None

    def compute():
        nonlocal current, other, low, attn_out, mid, head
        if not todo or todo[0][2] >= arrived:
            return
        kind, layer, _ = todo.pop(0)
        vec = table[layer]
        if kind == "attn":
            attn_out = attn_forward(pos_w, pos_g, current, other, seg, lab, vec, chunks[3 * layer])
            return
        h, n1, c1, q, kt, v, p, xoh, far_xoh = attn_out
        if kind == "inner":
            active, gp, gt, far_gt = inner_forward(pos_w, pos_g, h, vec, chunks[3 * layer + 1])
            mid = (active, gp, gt, move(far_gt, net["core"]), move(far_xoh, net["core"]))
            return
        active, gp, gt, far_gt, far_xoh = mid
        last = layer + 1 == layers
        current, low, *rest = outer_forward(
            pos_w, h, active, vec, chunks[3 * layer + 2], upstream if last else None
        )
        if last:
            head, rest = rest, (None, None)
        else:
            other = move(low, net["core"])
        kept[layer] = (n1, c1, q, kt, v, p, *rest, gp, xoh, gt, far_xoh, far_gt)

    head = None
    if not staged:
        upstream = move(upstream[0], net["swap"])
    if staged:
        sent, got = {}, {}
        zplan = {r: [(1, r + 2), (2, r + 3)] for r in range(-1, 2)}
        for r in range(2, 2 * len(groups)):
            g = (r + 6) // 2 + (r % 2)
            zplan[r] = [(1 + r % 2, g)]
        spread = [net["z2"], net["z1"]]
        for r in range(-LAG, total_chunks + LAG):
            inputs, plan = [], []
            sizes = [0, 0]
            use = lambda value: (inputs.append(value), len(inputs) - 1)[1]
            fresh = r + LAG < total_chunks
            if fresh:
                g, j = where_of[r + LAG]
                n = len(groups[g])
                mine, theirs = use(stage_z[g][0]), use(stage_z[g][1])
                for out, part in ((0, 1), (1, 0)):
                    for k, (source, slot) in enumerate(((mine, 0), (theirs, 0), (mine, 1), (theirs, 1))):
                        plan.append((out, k, source, (slot * n + j) * 2 + part, 1, True))
                    sizes[out] = ZS
            before = r - LAG
            home = 0 <= before < total_chunks
            if before >= -LAG and (r < total_chunks or home):
                sx, sy = use(sent[before][0]), use(sent[before][1])
                rx, ry = use(got[before][0]), use(got[before][1])
                first = ZS if before + LAG < total_chunks else 0
                if r < total_chunks:
                    for out, send, come in ((0, sy, ry), (1, sx, rx)):
                        plan.append((out, sizes[out], send, 0, ZS, False))
                        plan.append((out, sizes[out] + ZS, come, 0, ZS, False))
                        sizes[out] += 2 * ZS
                if home:
                    sizes.append(8 * ZS)
                    slot = 2
                    for at, (send, come) in enumerate(((sx, rx), (sy, ry))):
                        plan.append((slot, at * 4 * ZS, send, first, 2 * ZS, False))
                        plan.append((slot, at * 4 * ZS + 2 * ZS, come, first, 2 * ZS, False))
            live = [index for index, size in enumerate(sizes) if size]
            outs = copy_blocks(
                pos_g,
                [(live.index(each[0]),) + each[1:] for each in plan],
                inputs,
                [sizes[index] for index in live],
                "gather_round",
            )
            outs = dict(zip(live, outs))
            if 0 in outs:
                sent[r] = (outs[0], outs[1])
                got[r] = (move(outs[0], net["x"]), move(outs[1], net["y"]))
            core_pair = None
            if home:
                core_pair = (outs[2], move(outs[2], net["core"]))
            for stage, g in zplan.get(r, ()):
                if g < len(groups):
                    (start_z2 if stage == 2 else start_z1)(g)
            if spread and r >= 0:
                table = table + move(table, spread.pop(0))
            if r == total_chunks - 1:
                upstream = move(upstream[0], net["swap"])
            compute()
            ready = r + 1 - LAG
            state = (got.get(ready), core_pair, stage_z, current, other, attn_out, raw, table, upstream, mid)
            state = fence(state)
            if ready in got:
                got[ready] = state[0]
            if home:
                chunks.append(state[1])
                arrived += 1
            stage_z, current, other, attn_out, raw, table, upstream, mid = (list(state[2]),) + tuple(state[3:])
    while todo:
        compute()
    range_ids = jnp.arange(SEGS, dtype=jnp.int32)
    own = (small_own[1][None, :] == range_ids[:, None]).astype(F32)
    sums = jnp.dot(own, current, precision=lax.Precision.HIGHEST)
    pool_sums = sums
    counts = jnp.sum((lab[:, 0][None, :] == range_ids[:, None]).astype(F32), axis=1)
    loose = {}
    if staged:
        loose["hidden"] = move(low, net["swap"])
        loose["pool"] = pool_sums + move(pool_sums, net["core"])

    parts = []
    vectors = [None] * layers
    rounds = []
    ends = []
    table_stage = 1

    def side_work():
        step = len(rounds)
        last = total_chunks + 1
        if step == 2:
            loose["after"] = (loose["hidden"], loose["pool"])
        if step == 3:
            loose["pooled"] = move(loose.pop("pool") / counts[:, None], net["swap"])
            loose["after"] = (loose["pooled"],)
        if step == last + 1:
            loose["grad"] = move(loose.pop("grad"), net["swap"])
            loose["after"] = (loose["grad"],)
        if step == last + 2:
            done = list(finish(2, pos_g, ended()[0::3][::-1]))
            loose["outer"] = done
            loose["after"] = (done[0],)

    def ended():
        found = []
        for now in rounds:
            if "total" in now:
                found.append((now["total"], now["got_y"], ends[len(found)]))
        return found

    def settle(state):
        return fence(state)

    def advance(fresh, state):
        if not staged:
            if fresh is not None:
                parts.append(fresh)
            return state(()) if callable(state) else state
        s = len(rounds)
        past = rounds[s - LAG] if s >= LAG else {}
        pick = lambda key: past.get(key)
        has_home = pick("first") is not None or pick("second") is not None
        to_x, to_y, going, first, second, third, fourth, small = sum_round(
            fresh,
            pick("got_x") if has_home else None,
            pick("got_y") if pick("first") is not None else None,
            pick("first"),
            pick("second"),
            pick("third"),
            pick("fourth"),
            loose.pop("small", (0, None)),
            tuple(loose.pop("after", ())),
        )
        sends = (to_x or ()) + (to_y or ())
        now = {}
        if fresh is not None:
            now["first"] = (fresh[0], fresh[2])
        if first is not None:
            now["second"] = first
        if to_x is not None:
            now["got_x"] = move(to_x[0], net["x"])
        if to_y is not None:
            now["got_y"] = move(to_y[0], net["y"])
        if second is not None:
            now["third"] = (second[0], move(second[1], net["z1"]))
        if third is not None:
            now["fourth"] = (third[0], move(third[1], net["z2"]))
        if fourth is not None:
            now["total"] = fourth[0]
            ends.append(going)
        if "vectors" in loose:
            small = loose.pop("vectors").reshape(-1, width)
            loose["small"] = (1, (small, move(small, net["core"])))
        elif small is not None:
            nonlocal table_stage
            table_stage += 1
            loose["small"] = (table_stage, small)
        side_work()
        if callable(state):
            state = state(sends)
        rounds.append(now)
        ready = s + 1 - LAG
        if ready < 0:
            return fence(state)
        rounds[ready], state = fence((rounds[ready], state))
        return state

    top = layers - 1
    ready = []
    dyl, dy, head_sums = head
    for layer in reversed(range(layers)):
        attn_bufs, inner_bufs, outer_bufs = chunks[3 * layer : 3 * layer + 3]
        n1, c1, q, kt, v, p, n2, c2, gp, xoh, gt, far_xoh, far_gt = kept[layer]
        got_dyl = move(dyl, net["core"])
        chain_args = (pos_w, dyl, dy, gp, n1, c1, table[layer], inner_bufs, outer_bufs, attn_bufs)
        if layer == top:
            outer_parts = settle(outer_grad(gt, far_gt, dyl, got_dyl))

            def first_round(sends):
                return chain_backward(*chain_args, after=sends)

            pack, da, do, sums = advance(outer_parts, first_round)
            got_pack = move(pack, net["core"])

            def second_round(sends):
                back, qsum = attn_backward(q, kt, v, p, do, after=sends)
                return back, qsum, got_pack, inner_grad(pos_g, xoh, far_xoh, pack, got_pack)

            back, qsum, got_pack, inner_parts = advance(None, second_round)
            ready.append(inner_parts)
            got_back = move(back, net["core"])
        else:
            pack, da, do, sums = chain_backward(*chain_args)
            outer_parts = outer_grad(gt, far_gt, dyl, got_dyl)
            state = advance(ready.pop(0), (pack, da, do, sums, outer_parts))
            pack, da, do, sums, outer_parts = state
            ready.append(outer_parts)
            got_pack = move(pack, net["core"])
            back, qsum = attn_backward(q, kt, v, p, do)
            inner_parts = inner_grad(pos_g, xoh, far_xoh, pack, got_pack)
            state = advance(ready.pop(0), (back, qsum, got_pack, inner_parts))
            back, qsum, got_pack, inner_parts = state
            ready.append(inner_parts)
            got_back = move(back, net["core"])
        below = None if layer == 0 else (kept[layer - 1][6], kept[layer - 1][7], table[layer - 1])
        total, vsum, *head = input_backward(pos_w, da, back, got_back, attn_bufs, below)
        attn_parts = attn_grad(pos_g, xoh, far_xoh, back, got_back, total, pack, got_pack)
        attn_parts, head, vsum = advance(ready.pop(0), (attn_parts, head, vsum))
        ready.append(attn_parts)
        vectors[layer] = (qsum, vsum, head_sums, sums)
        if layer:
            dyl, dy, head_sums = head
    grad = head[0]
    vectors = collect(vectors, 16)
    loose["grad"] = grad
    while ready:
        if len(ready) == 1:
            loose["vectors"] = vectors
        advance(ready.pop(0), None)
    results = []
    if staged:
        for _ in range(4 * LAG):
            advance(None, None)
        results = ended()

    if staged:
        stacked = []
        for kind, first in ((0, 2), (1, 1)):
            stacked += list(finish(kind, pos_g, results[first::3][::-1]))
        stacked += loose["outer"]
        hidden_out, pooled, tokens_grad = (loose[key] for key in ("hidden", "pooled", "grad"))
        vectors = loose["small"][1][0]
        got_vectors = rounds[-1]["got_y"][-1].astype(F32)
    else:
        collected = [None] * layers
        for place_at, layer in enumerate(reversed(range(layers))):
            outer_parts, inner_parts, attn_parts = parts[3 * place_at : 3 * place_at + 3]

            def spread(outs):
                a_keep, a_send, b_keep, b_send = outs
                a = jnp.stack([a_keep, a_send])
                b = jnp.stack([b_keep, b_send], axis=1)
                return jnp.stack([a, b], axis=2)

            def total(out):
                out = out.reshape(ZS * 2, 1, out.shape[2], out.shape[3])
                mine = (jnp.arange(2, dtype=jnp.int32) == core)[None, :, None, None]
                out = jnp.where(mine, out, jnp.zeros_like(out)).reshape(-1, out.shape[-1])
                out = lax.psum_scatter(out, "dp", scatter_dimension=0, tiled=True)
                return lax.psum(out.astype(F32), "seq")

            outer = spread(outer_parts).transpose(3, 0, 1, 2, 4, 5)
            outer = total(outer.reshape(ZS, 2, -1, width))
            inner = spread(inner_parts).transpose(3, 0, 4, 1, 2, 5)
            inner = total(inner.reshape(ZS, 2, inner.shape[2], -1))
            attn = spread(attn_parts)
            attn = attn.reshape(attn.shape[:5] + (2, width // 2)).transpose(2, 5, 3, 0, 4, 1, 6)
            attn = attn.reshape(4, ZS, 2, attn.shape[4], width)
            four = [total(attn[index]) for index in range(4)]
            collected[layer] = four + [inner, outer]
        stacked = [
            jnp.stack([collected[layer][member] for layer in range(layers)]) for member in range(6)
        ]
        hidden_out = move(low, net["swap"])
        pooled = move((pool_sums + move(pool_sums, net["core"])) / counts[:, None], net["swap"])
        tokens_grad = move(grad, net["swap"])
        vectors = lax.psum(vectors, AXES).reshape(-1, width)
        got_vectors = None
    own = own_vectors(dp[None], vectors, got_vectors, layers, small, hidden // count)
    return (
        hidden_out[None],
        pooled[None],
        tokens_grad.astype(F32)[None],
        stacked[0],
        stacked[1],
        stacked[2],
        stacked[3],
        own[QB],
        own[VB],
        own[OB],
        own[AG],
        own[AS],
        stacked[4],
        own[IB],
        stacked[5],
        own[UB],
        own[FG],
        own[FS],
    )


def solution(mesh):
    cube = P(None, "dp", None)
    flat = P(None, "dp")
    acts = P("dp", "seq", None)
    ids = P("dp", "seq")
    return jax.shard_map(
        functools.partial(body, build(mesh)),
        mesh=mesh,
        in_specs=(acts, ids, ids, cube, cube, cube, cube, flat, flat, flat, flat, flat, cube, flat, cube)
        + (flat, flat, flat, acts),
        out_specs=(acts, P("dp", None, None), acts, cube, cube, cube, cube)
        + (flat, flat, flat, flat, flat, cube, flat, cube, flat, flat, flat),
        check_vma=False,
    )
```

```python
import functools

import jax
import jax.numpy as jnp
from jax import lax
from jax.experimental import pallas as pl
from jax.experimental.pallas import tpu as pltpu
from jax.sharding import PartitionSpec as P

HD = 64
SEGS = 4
BLOCKS = 16
ZS = 4
LAG = 1
VMEM_MB = 24
EPS = 1e-06
MASKED = -1e30
AXES = ("dp", "seq")
F32 = jnp.float32
BF16 = jnp.bfloat16
MB = 1024 * 1024

QB, VB, OB, AG, AS, UB, FG, FS, IB = range(9)


def nn(left, right):
    return lax.dot_general(left, right, (((1,), (0,)), ((), ())), preferred_element_type=F32)


def nt(left, right):
    return lax.dot_general(left, right, (((1,), (1,)), ((), ())), preferred_element_type=F32)


def params(vmem):
    return pltpu.CompilerParams(vmem_limit_bytes=vmem * MB)


def cost():
    return pl.CostEstimate(flops=1, bytes_accessed=1, transcendentals=0)


def load(source, target, sem):
    pltpu.make_async_copy(source, target, sem).start()


VMEM = pl.BlockSpec(memory_space=pltpu.VMEM)
SMEM = pl.BlockSpec(memory_space=pltpu.SMEM)
ANY = pl.BlockSpec(memory_space=pl.ANY)
HBM = pl.BlockSpec(memory_space=pltpu.HBM)


def shape(dims, dtype):
    return jax.ShapeDtypeStruct(dims, dtype)


def flip(value, bit):
    return value + bit - 2 * value * bit


def block_at(pos_ref, k, dx, dc):
    z, x, c = pos_ref[0], pos_ref[1], pos_ref[2]
    low = lax.rem(z, 2)
    zz = flip(lax.div(z, 2), k // 2) * 2 + flip(low, k % 2)
    return (zz * 2 + flip(x, dx)) * 2 + flip(c, dc)


def half_at(pos_ref, dy):
    return flip(pos_ref[3], dy)


UNITS = (
    (0, 0, 0),
    (0, 1, 0),
    (0, 0, 1),
    (0, 1, 1),
    (1, 0, 0),
    (1, 0, 1),
    (1, 1, 0),
    (1, 1, 1),
)


def each_unit(pos_ref, bufs):
    for dc in range(2):
        for unit, (part, dy, dx) in enumerate(UNITS):
            at = flip(pos_ref[1], dx) * 2 + flip(pos_ref[2], dc)
            yield bufs[dc].at[pl.ds(unit * ZS, ZS)], part, dy, at


def fetch_member(pos_ref, bufs, member, full_ref, sem):
    half = full_ref.shape[3] // 2
    for unit, part, dy, at in each_unit(pos_ref, bufs):
        if part == member // 2:
            col = pl.multiple_of(half_at(pos_ref, dy) * half, 128)
            load(
                unit.at[:, :, pl.ds(member % 2 * half, half)],
                full_ref.at[:, at, :, pl.ds(col, half)],
                sem,
            )


def fetch_columns(pos_ref, bufs, full_ref, sem):
    width = full_ref.shape[3] // 4
    for unit, part, dy, at in each_unit(pos_ref, bufs):
        col = pl.multiple_of((half_at(pos_ref, dy) * 2 + part) * width, 128)
        load(unit, full_ref.at[:, at, :, pl.ds(col, width)], sem)


def fetch_rows(pos_ref, bufs, full_ref, sem):
    for unit, part, dy, at in each_unit(pos_ref, bufs):
        load(unit, full_ref.at[:, at, half_at(pos_ref, dy) * 2 + part], sem)


def flat(values):
    return values.reshape(-1, values.shape[-1])


def square(width):
    return pltpu.VMEM((ZS, BLOCKS // ZS, width // BLOCKS, width), BF16)


def wide_matrix(width, hidden):
    return pltpu.VMEM((ZS, BLOCKS // ZS, width // BLOCKS, hidden), BF16)


def tall_matrix(hidden, width):
    return pltpu.VMEM((ZS, BLOCKS // ZS, 4, hidden // BLOCKS // 4, width), BF16)


def wait_full(full_ref, sem):
    pltpu.make_async_copy(full_ref, full_ref, sem).wait()


def export_rows(pos_ref, wide_ref, outs, index):
    rows = outs[0].shape[3]
    for dc in range(2):
        for dx in range(2):
            for k in range(ZS):
                row = pl.multiple_of(block_at(pos_ref, k, dx, dc) * rows, 16)
                outs[dc][index, dx, k] = wide_ref[pl.ds(row, rows), :]


def export_halves(pos_ref, wide_ref, outs):
    rows = outs[0].shape[4]
    for dc in range(2):
        for dx in range(2):
            for dy in range(2):
                for k in range(ZS):
                    block = block_at(pos_ref, k, dx, dc) * 2 + half_at(pos_ref, dy)
                    for part in range(2):
                        row = pl.multiple_of((block * 2 + part) * rows, 16)
                        outs[dc][dx, dy, part, k] = wide_ref[pl.ds(row, rows), :]


def mean_of(values):
    return jnp.mean(values, axis=-1, keepdims=True)


def normalize(values):
    center = values - mean_of(values)
    inverse = lax.rsqrt(mean_of(center * center) + EPS)
    return center * inverse, inverse


def norm_back(normed, inverse, scaled):
    return inverse * (scaled - mean_of(scaled) - normed * mean_of(scaled * normed))


def colsum(values):
    return jnp.sum(values, axis=0, keepdims=True)


def row_of(vec_ref, index):
    return vec_ref[pl.ds(index, 1), :]


def attn_kernel(*refs):
    pos_w, pos_g = refs[0], refs[1]
    x_ref, xp_ref, seg_ref, lab_ref, vec_ref = refs[2:7]
    bufs = refs[7:9]
    h_ref = refs[9]
    kept = refs[10:18]
    wq, wk, wv, wo, rows_ref, vt_ref, wide_ref, bias_ref, k_ref = refs[18:27]
    held = refs[27:35]
    n1_ref, c1_ref, q_ref, kt_ref, v_ref, p_ref = held[:6]
    exports = held[6:]
    sems, store_sems = refs[35:]

    def store(index):
        load(held[index], kept[index], store_sems.at[index])

    tokens, width = x_ref.shape
    for member, full in enumerate((wq, wk, wv, wo)):
        fetch_member(pos_w, bufs, member, full, sems.at[member])
    bias_ref[...] = jnp.where(lab_ref[...] == seg_ref[...], 0.0, MASKED)
    low = x_ref[...].astype(BF16)
    rows_ref[:tokens] = low
    rows_ref[tokens:] = xp_ref[...]
    wide_ref[...] = low.T
    export_rows(pos_g, wide_ref, exports, 0)
    wait_full(wq, sems.at[0])
    query = (nn(low, flat(wq[...])) + row_of(vec_ref, QB)).astype(BF16)
    q_ref[...] = (query.astype(F32) * HD ** (-0.5)).astype(BF16)
    wait_full(wk, sems.at[1])
    key = nn(rows_ref[...], flat(wk[...])).astype(BF16)
    k_ref[...] = key
    kt_ref[...] = key.T
    store(2)
    store(3)
    wait_full(wv, sems.at[2])
    value = (nn(rows_ref[...], flat(wv[...])) + row_of(vec_ref, VB)).astype(BF16)
    v_ref[...] = value
    vt_ref[...] = value.T
    store(4)

    def pair(index, carry):
        lane = pl.multiple_of(index * 128, 128)
        keys = k_ref[:, pl.ds(lane, 128)]
        queries = q_ref[:, pl.ds(lane, 128)]
        first = lax.broadcasted_iota(jnp.int32, queries.shape, 1) < HD
        for which in range(2):
            mine = jnp.where(first if which == 0 else ~first, queries, jnp.zeros_like(queries))
            scores = nt(keys, mine) + bias_ref[...]
            expos = jnp.exp(scores - jnp.max(scores, axis=0, keepdims=True))
            probs = (expos * (1.0 / jnp.sum(expos, axis=0, keepdims=True))).astype(BF16)
            p_ref[index * 2 + which] = probs
            row = pl.multiple_of(index * 128 + which * HD, HD)
            wide_ref[pl.ds(row, HD), :] = nn(vt_ref[pl.ds(row, HD), :], probs).astype(BF16)
        both = pl.ds(index * 2, 2)
        load(p_ref.at[both], kept[5].at[both], store_sems.at[5])
        return carry

    lax.fori_loop(0, width // 128, pair, 0)
    export_rows(pos_g, wide_ref, exports, 1)
    mixed = wide_ref[...].T
    wait_full(wo, sems.at[3])
    branch = nn(mixed, flat(wo[...])) + row_of(vec_ref, OB)
    normed, inverse = normalize(x_ref[...] + branch)
    hidden = normed * row_of(vec_ref, AG) + row_of(vec_ref, AS)
    h_ref[...] = hidden
    n1_ref[...] = normed
    c1_ref[...] = jnp.broadcast_to(inverse, c1_ref.shape)
    wide_ref[...] = hidden.astype(BF16).T
    export_rows(pos_g, wide_ref, exports, 2)
    for index in (0, 1, 6, 7):
        store(index)
    for index in range(8):
        wait_full(held[index], store_sems.at[index])


def attn_forward(pos_w, pos_g, x, xp, seg, lab, vec, bufs):
    tokens, width = x.shape
    heads = width // HD
    export = shape((3, 2, ZS, width // BLOCKS, tokens), BF16)
    kept = (
        shape((tokens, width), F32),
        shape((tokens, 128), F32),
        shape((tokens, width), BF16),
        shape((width, 2 * tokens), BF16),
        shape((2 * tokens, width), BF16),
        shape((heads, 2 * tokens, tokens), BF16),
        export,
        export,
    )
    return pl.pallas_call(
        attn_kernel,
        out_shape=(shape((tokens, width), F32),) + kept,
        in_specs=[SMEM, SMEM] + [VMEM] * 5 + [ANY] * 2,
        out_specs=[VMEM] + [HBM] * 8,
        scratch_shapes=[square(width)] * 4
        + [
            pltpu.VMEM((2 * tokens, width), BF16),
            pltpu.VMEM((width, 2 * tokens), BF16),
            pltpu.VMEM((width, tokens), BF16),
            pltpu.VMEM((2 * tokens, tokens), F32),
            pltpu.VMEM((2 * tokens, width), BF16),
        ]
        + [pltpu.VMEM(each.shape, each.dtype) for each in kept]
        + [pltpu.SemaphoreType.DMA((4,)), pltpu.SemaphoreType.DMA((8,))],
        compiler_params=params(VMEM_MB),
        cost_estimate=cost(),
        name="attn_forward",
    )(pos_w, pos_g, x, xp, seg, lab, vec, *bufs)


def head_back(grad, normed, inverse, gain, low_ref, back_ref, sums_ref):
    sums_ref[...] = jnp.zeros_like(sums_ref)
    sums_ref[pl.ds(0, 1), :] = colsum(grad * normed)
    sums_ref[pl.ds(1, 1), :] = colsum(grad)
    back = norm_back(normed, inverse, grad * gain)
    low = back.astype(BF16)
    low_ref[...] = low
    back_ref[...] = back
    sums_ref[pl.ds(2, 1), :] = colsum(low.astype(F32))


def head_shapes(tokens, width):
    return (
        shape((tokens, width), BF16),
        shape((tokens, width), F32),
        shape((8, width), F32),
    )


def inner_kernel(tile, *refs):
    pos_w, pos_g, h_ref, vec_ref = refs[:4]
    bufs, active_ref, kept = refs[4:6], refs[6], refs[7:10]
    wi, low_ref, wide_ref = refs[10:13]
    held = refs[13:16]
    gp_ref, exports = held[0], held[1:]
    sem, store_sems = refs[16:]
    width, hidden = h_ref.shape[1], wi.shape[3]
    fetch_columns(pos_w, bufs, wi, sem)
    low_ref[...] = h_ref[...].astype(BF16)
    wait_full(wi, sem)
    per_row = width // tile

    def step(index, carry):
        lanes = pl.ds(pl.multiple_of(index * tile, tile), tile)
        bias = vec_ref[pl.ds(IB + lax.div(index, per_row), 1), :]
        part = lax.rem(index, per_row)
        chosen = bias[:, :tile]
        for other in range(1, per_row):
            chosen = jnp.where(part == other, bias[:, other * tile : (other + 1) * tile], chosen)
        pre = nn(low_ref[...], flat(wi[:, :, :, lanes])) + chosen
        phi = 0.5 * (1.0 + lax.erf(pre * 0.7071067811865476))
        dens = jnp.exp(-0.5 * pre * pre) * 0.3989422804014327
        gp_ref[:, lanes] = (phi + pre * dens).astype(BF16)
        active = (pre * phi).astype(BF16)
        active_ref[:, lanes] = active
        wide_ref[lanes, :] = active.T
        return carry

    lax.fori_loop(0, hidden // tile, step, 0)
    load(held[0], kept[0], store_sems.at[0])
    export_halves(pos_g, wide_ref, exports)
    for index in (1, 2):
        load(held[index], kept[index], store_sems.at[index])
    for index in range(3):
        wait_full(held[index], store_sems.at[index])


def inner_forward(pos_w, pos_g, h, vec, bufs):
    tokens, width = h.shape
    hidden = bufs[0].shape[2] * 4
    export = shape((2, 2, 2, ZS, hidden // BLOCKS // 4, tokens), BF16)
    kept = (shape((tokens, hidden), BF16), export, export)
    return pl.pallas_call(
        functools.partial(inner_kernel, 384),
        out_shape=(shape((tokens, hidden), BF16),) + kept,
        in_specs=[SMEM, SMEM, VMEM, VMEM] + [ANY] * 2,
        out_specs=[VMEM] + [HBM] * 3,
        scratch_shapes=[
            wide_matrix(width, hidden),
            pltpu.VMEM((tokens, width), BF16),
            pltpu.VMEM((hidden, tokens), BF16),
        ]
        + [pltpu.VMEM(each.shape, each.dtype) for each in kept]
        + [pltpu.SemaphoreType.DMA, pltpu.SemaphoreType.DMA((3,))],
        compiler_params=params(VMEM_MB),
        cost_estimate=cost(),
        name="inner_forward",
    )(pos_w, pos_g, h, vec, *bufs)


def outer_kernel(last, *refs):
    pos_w, h_ref, active_ref, vec_ref = refs[:4]
    grad_ref = refs[4] if last else None
    refs = refs[4 + last :]
    bufs = refs[:2]
    outs, wu, acc_ref, sem = refs[2:-3], refs[-3], refs[-2], refs[-1]
    fetch_rows(pos_w, bufs, wu, sem)
    acc_ref[...] = h_ref[...] + row_of(vec_ref, UB)
    wait_full(wu, sem)
    tile = active_ref.shape[1] // ZS
    for z in range(ZS):
        acc_ref[...] += nn(active_ref[:, pl.ds(z * tile, tile)], flat(wu[z]))
    normed, inverse = normalize(acc_ref[...])
    result = normed * row_of(vec_ref, FG) + row_of(vec_ref, FS)
    outs[0][...] = result
    outs[1][...] = result.astype(BF16)
    if last:
        head_back(
            grad_ref[...].astype(F32), normed, inverse, row_of(vec_ref, FG), outs[2], outs[3], outs[4]
        )
    else:
        outs[2][...] = normed
        outs[3][...] = jnp.broadcast_to(inverse, outs[3].shape)


def outer_forward(pos_w, h, active, vec, bufs, grad):
    tokens, width = h.shape
    hidden = active.shape[1]
    last = grad is not None
    outs = (shape((tokens, width), F32), shape((tokens, width), BF16))
    if last:
        outs += head_shapes(tokens, width)
    else:
        outs += (shape((tokens, width), F32), shape((tokens, 128), F32))
    return pl.pallas_call(
        functools.partial(outer_kernel, int(last)),
        out_shape=outs,
        in_specs=[SMEM] + [VMEM] * (3 + last) + [ANY] * 2,
        out_specs=[VMEM] * len(outs),
        scratch_shapes=[
            tall_matrix(hidden, width),
            pltpu.VMEM((tokens, width), F32),
            pltpu.SemaphoreType.DMA,
        ],
        compiler_params=params(VMEM_MB),
        cost_estimate=cost(),
        name="outer_forward",
    )(pos_w, h, active, vec, *((grad,) if last else ()), *bufs)


def chain_kernel(tile, waits, *refs):
    pos_w, dyl_ref, dy_ref = refs[:3]
    sources, vec_ref = refs[3:6], refs[6]
    inner_bufs, outer_bufs, attn_bufs = refs[7:9], refs[9:11], refs[11:13]
    refs = refs[13 + waits :]
    pack_ref, da_ref, do_ref, sums_ref = refs[:4]
    wi, wu, wo, acc_ref = refs[4:8]
    held = refs[8:11]
    gp_ref, n1_ref, c1_ref = held
    sems, load_sems = refs[11:]
    width, hidden = dy_ref.shape[1], wi.shape[3]
    for index in range(3):
        load(sources[index], held[index], load_sems.at[index])
    du_ref = pack_ref.at[:, pl.ds(0, hidden)]
    dal_ref = pack_ref.at[:, pl.ds(hidden, width)]
    fetch_rows(pos_w, outer_bufs, wu, sems.at[0])
    fetch_columns(pos_w, inner_bufs, wi, sems.at[1])
    fetch_member(pos_w, attn_bufs, 3, wo, sems.at[2])
    sums_ref[...] = jnp.zeros_like(sums_ref)
    acc_ref[...] = dy_ref[...]
    wait_full(gp_ref, load_sems.at[0])
    wait_full(wu, sems.at[0])
    wait_full(wi, sems.at[1])
    per_row = width // tile

    for index in range(hidden // tile):
        lane = index * tile
        rows = wu[index * ZS * tile // hidden, pl.ds(lane % (hidden // ZS) * BLOCKS // hidden, tile * BLOCKS // hidden)]
        part = nt(dyl_ref[...], flat(rows))
        part = (part * gp_ref[:, pl.ds(lane, tile)].astype(F32)).astype(BF16)
        du_ref[:, pl.ds(lane, tile)] = part
        acc_ref[...] += nt(part, flat(wi[:, :, :, pl.ds(lane, tile)]))
        sums_ref[
            pl.ds(IB + index // per_row, 1), pl.ds(index % per_row * tile, tile)
        ] = colsum(part.astype(F32))

    grad = acc_ref[...]
    wait_full(n1_ref, load_sems.at[1])
    wait_full(c1_ref, load_sems.at[2])
    normed = n1_ref[...]
    sums_ref[pl.ds(AG, 1), :] = colsum(grad * normed)
    sums_ref[pl.ds(AS, 1), :] = colsum(grad)
    back = norm_back(normed, c1_ref[:, :1], grad * row_of(vec_ref, AG))
    da_ref[...] = back
    low = back.astype(BF16)
    dal_ref[...] = low
    sums_ref[pl.ds(OB, 1), :] = colsum(low.astype(F32))
    wait_full(wo, sems.at[2])
    do_ref[...] = nt(low, flat(wo[...])).astype(BF16)


def chain_backward(pos_w, dyl, dy, gp, n1, c1, vec, inner_bufs, outer_bufs, attn_bufs, after=()):
    tokens, width = n1.shape
    hidden = gp.shape[1]
    return pl.pallas_call(
        functools.partial(chain_kernel, 384, len(after)),
        out_shape=(
            shape((tokens, hidden + width), BF16),
            shape((tokens, width), F32),
            shape((tokens, width), BF16),
            shape((16, width), F32),
        ),
        in_specs=[SMEM] + [VMEM] * 2 + [HBM] * 3 + [VMEM] + [ANY] * (6 + len(after)),
        out_specs=[VMEM] * 4,
        scratch_shapes=[
            wide_matrix(width, hidden),
            tall_matrix(hidden, width),
            square(width),
            pltpu.VMEM((tokens, width), F32),
        ]
        + [pltpu.VMEM(each.shape, each.dtype) for each in (gp, n1, c1)]
        + [pltpu.SemaphoreType.DMA((3,)), pltpu.SemaphoreType.DMA((3,))],
        compiler_params=params(VMEM_MB),
        cost_estimate=cost(),
        name="chain_backward",
    )(pos_w, dyl, dy, gp, n1, c1, vec, *inner_bufs, *outer_bufs, *attn_bufs, *after)


def attn_back_kernel(waits, *refs):
    sources, do_ref = refs[:4], refs[4]
    refs = refs[waits:]
    pack_ref, sum_ref, wide_ref = refs[5], refs[6], refs[7]
    held, sems, pair_sems = refs[8:12], refs[12], refs[13]
    q_ref, kt_ref, v_ref, p_ref = held
    tokens, width = q_ref.shape
    for index in range(3):
        load(sources[index], held[index], sems.at[index])
    for index in range(width // 128):
        both = pl.ds(index * 2, 2)
        load(sources[3].at[both], p_ref.at[both], pair_sems.at[index])
    for index in range(3):
        wait_full(held[index], sems.at[index])

    def pair(index, carry):
        lane = pl.multiple_of(index * 128, 128)
        values = v_ref[:, pl.ds(lane, 128)]
        queries = q_ref[:, pl.ds(lane, 128)]
        grads = do_ref[:, pl.ds(lane, 128)]
        first = lax.broadcasted_iota(jnp.int32, grads.shape, 1) < HD
        keys_back, values_back = [], []
        wait_full(p_ref.at[pl.ds(index * 2, 2)], pair_sems.at[index])
        for which in range(2):
            mine = jnp.where(first if which == 0 else ~first, grads, jnp.zeros_like(grads))
            probs_low = p_ref[index * 2 + which]
            probs = probs_low.astype(F32)
            weighted = probs * nt(values, mine)
            back = weighted - probs * jnp.sum(weighted, axis=0, keepdims=True)
            low = back.astype(BF16)
            keys_back.append(nn(low, queries))
            values_back.append(nn(probs_low, grads))
            row = pl.multiple_of(index * 128 + which * HD, HD)
            wide_ref[pl.ds(row, HD), :] = nn(kt_ref[pl.ds(row, HD), :], low)
        split = lax.broadcasted_iota(jnp.int32, keys_back[0].shape, 1) < HD
        for at, back in ((1, keys_back), (3, values_back)):
            low = jnp.where(split, back[0], back[1]).astype(BF16)
            pack_ref[at, :, pl.ds(lane, 128)] = low[:tokens]
            pack_ref[at + 1, :, pl.ds(lane, 128)] = low[tokens:]
        return carry

    lax.fori_loop(0, width // 128, pair, 0)
    low = (wide_ref[...].T * HD ** (-0.5)).astype(BF16)
    pack_ref[0] = low
    sum_ref[...] = jnp.broadcast_to(colsum(low.astype(F32)), sum_ref.shape)


def attn_backward(q, kt, v, p, do, after=()):
    tokens, width = q.shape
    return pl.pallas_call(
        functools.partial(attn_back_kernel, len(after)),
        out_shape=(
            shape((5, tokens, width), BF16),
            shape((8, width), F32),
        ),
        in_specs=[HBM] * 4 + [VMEM] + [ANY] * len(after),
        out_specs=[VMEM] * 2,
        scratch_shapes=[pltpu.VMEM((width, tokens), F32)]
        + [pltpu.VMEM(each.shape, each.dtype) for each in (q, kt, v, p)]
        + [pltpu.SemaphoreType.DMA((3,)), pltpu.SemaphoreType.DMA((width // 128,))],
        compiler_params=params(VMEM_MB),
        cost_estimate=cost(),
        name="attn_backward",
    )(q, kt, v, p, do, *after)


def input_kernel(first, *refs):
    pos_w, da_ref, pack_ref, got_ref = refs[:4]
    bufs = refs[4:6]
    refs = refs[6:]
    if not first:
        n2_ref, c2_ref, vec_ref = refs[:3]
        refs = refs[3:]
    total_ref, sum_ref = refs[:2]
    heads = refs[2:-4]
    wq, wk, wv, sems = refs[-4:]
    tokens, width = da_ref.shape
    for member, full in enumerate((wq, wk, wv)):
        fetch_member(pos_w, bufs, member, full, sems.at[member])
    for at, (mine, theirs) in enumerate(((1, 2), (2, 1), (3, 4), (4, 3))):
        total_ref[at] = (pack_ref[mine].astype(F32) + got_ref[theirs].astype(F32)).astype(BF16)
    sum_ref[...] = jnp.broadcast_to(colsum(total_ref[2].astype(F32)), sum_ref.shape)
    wait_full(wq, sems.at[0])
    dx = da_ref[...] + nt(pack_ref[0], flat(wq[...]))
    wait_full(wk, sems.at[1])
    dx += nt(total_ref[0], flat(wk[...]))
    wait_full(wv, sems.at[2])
    dx += nt(total_ref[2], flat(wv[...]))
    if first:
        heads[0][...] = dx.astype(BF16)
    else:
        head_back(dx, n2_ref[...], c2_ref[:, :1], row_of(vec_ref, FG), *heads)


def input_backward(pos_w, da, pack, got, bufs, below):
    tokens, width = da.shape
    first = below is None
    outs = (shape((4, tokens, width), BF16), shape((8, width), F32))
    outs += (shape((tokens, width), BF16),) if first else head_shapes(tokens, width)
    return pl.pallas_call(
        functools.partial(input_kernel, first),
        out_shape=outs,
        in_specs=[SMEM] + [VMEM] * 3 + [ANY] * 2 + ([] if first else [VMEM] * 3),
        out_specs=[VMEM] * len(outs),
        scratch_shapes=[square(width)] * 3 + [pltpu.SemaphoreType.DMA((3,))],
        compiler_params=params(VMEM_MB),
        cost_estimate=cost(),
        name="input_backward",
    )(pos_w, da, pack, got, *bufs, *(() if first else below))


def place(outs, part, dy, value):
    a_keep, a_send, b_keep, b_send = outs
    if part == 0:
        a_keep[dy] = value[0]
        a_send[dy] = value[1]
    else:
        (b_send if dy else b_keep)[...] = value


def grad_shapes(rows, width):
    return (shape((2, ZS, rows, width), BF16),) * 4


def inner_grad_kernel(pos_ref, ta_ref, tb_ref, da_ref, db_ref, *refs):
    outs, left, sems = refs[:4], refs[4], refs[5]
    _, _, rows, width = outs[0].shape
    tokens = ta_ref.shape[-1]
    for side, source in enumerate((ta_ref, tb_ref)):
        load(source.at[2], left.at[side], sems.at[side])
    for side in range(2):
        wait_full(left.at[side], sems.at[side])
    left_a = left[0].reshape(2 * ZS * rows, tokens)
    left_b = left[1].reshape(2 * ZS * rows, tokens)
    for dy in range(2):
        for part in range(2):
            lanes = pl.ds(pl.multiple_of((half_at(pos_ref, dy) * 2 + part) * width, 128), width)
            value = nn(left_a, da_ref[:, lanes]) + nn(left_b, db_ref[:, lanes])
            place(outs, part, dy, value.astype(BF16).reshape(2, ZS, rows, width))


def inner_grad(pos_g, ta, tb, da, db):
    rows = ta.shape[3]
    return pl.pallas_call(
        inner_grad_kernel,
        out_shape=grad_shapes(rows, rows * BLOCKS),
        in_specs=[SMEM] + [HBM] * 2 + [VMEM] * 2,
        out_specs=[VMEM] * 4,
        scratch_shapes=[pltpu.VMEM((2,) + ta.shape[1:], BF16), pltpu.SemaphoreType.DMA((2,))],
        compiler_params=params(VMEM_MB),
        cost_estimate=cost(),
        name="inner_grad",
    )(pos_g, ta, tb, da, db)


def outer_grad_kernel(ta_ref, tb_ref, da_ref, db_ref, *refs):
    outs, left, sems = refs[:4], refs[4], refs[5]
    _, _, rows, width = outs[0].shape
    tokens = ta_ref.shape[-1]
    for side, source in enumerate((ta_ref, tb_ref)):
        load(source, left.at[side], sems.at[side])
    for side in range(2):
        wait_full(left.at[side], sems.at[side])
    for dy in range(2):
        for part in range(2):
            values = []
            for dx in range(2):
                left_a = left[0, dx, dy, part].reshape(ZS * rows, tokens)
                left_b = left[1, dx, dy, part].reshape(ZS * rows, tokens)
                value = nn(left_a, da_ref[...]) + nn(left_b, db_ref[...])
                values.append(value.astype(BF16).reshape(ZS, rows, width))
            place(outs, part, dy, jnp.stack(values))


def outer_grad(ta, tb, da, db):
    rows, width = ta.shape[4], da.shape[1]
    return pl.pallas_call(
        outer_grad_kernel,
        out_shape=grad_shapes(rows, width),
        in_specs=[HBM] * 2 + [VMEM] * 2,
        out_specs=[VMEM] * 4,
        scratch_shapes=[pltpu.VMEM((2,) + ta.shape, BF16), pltpu.SemaphoreType.DMA((2,))],
        compiler_params=params(VMEM_MB),
        cost_estimate=cost(),
        name="outer_grad",
    )(ta, tb, da, db)


def attn_grad_kernel(pos_ref, xa_ref, xb_ref, qa_ref, qb_ref, total_ref, da_ref, db_ref, *refs):
    outs, left, sems = refs[:4], refs[4], refs[5]
    for side, source in enumerate((xa_ref, xb_ref)):
        load(source.at[pl.ds(0, 2)], left.at[side], sems.at[side])
    for side in range(2):
        wait_full(left.at[side], sems.at[side])
    _, _, rows, width = outs[0].shape
    half = width // 2
    tokens = xa_ref.shape[-1]
    height = 2 * ZS * rows
    x_a = left[0, 0].reshape(height, tokens)
    x_b = left[1, 0].reshape(height, tokens)
    o_a = left[0, 1].reshape(height, tokens)
    o_b = left[1, 1].reshape(height, tokens)
    last = da_ref.shape[1] - width
    for dy in range(2):
        start = half_at(pos_ref, dy) * half
        lanes = pl.ds(pl.multiple_of(start, 128), half)
        tail = pl.ds(pl.multiple_of(start + last, 128), half)
        members = (
            nn(x_a, qa_ref[0, :, lanes]) + nn(x_b, qb_ref[0, :, lanes]),
            nn(x_a, total_ref[0, :, lanes]) + nn(x_b, total_ref[1, :, lanes]),
            nn(x_a, total_ref[2, :, lanes]) + nn(x_b, total_ref[3, :, lanes]),
            nn(o_a, da_ref[:, tail]) + nn(o_b, db_ref[:, tail]),
        )
        for part in range(2):
            value = jnp.concatenate(members[part * 2 : part * 2 + 2], axis=1)
            place(outs, part, dy, value.astype(BF16).reshape(2, ZS, rows, width))


def attn_grad(pos_g, xa, xb, qa, qb, total, da, db):
    rows = xa.shape[3]
    return pl.pallas_call(
        attn_grad_kernel,
        out_shape=grad_shapes(rows, rows * BLOCKS),
        in_specs=[SMEM] + [HBM] * 2 + [VMEM] * 5,
        out_specs=[VMEM] * 4,
        scratch_shapes=[pltpu.VMEM((2, 2) + xa.shape[1:], BF16), pltpu.SemaphoreType.DMA((2,))],
        compiler_params=params(VMEM_MB),
        cost_estimate=cost(),
        name="attn_grad",
    )(pos_g, xa, xb, qa, qb, total, da, db)


def copy_kernel(plan, inputs, pos_ref, *refs):
    ins, outs, sems = refs[:inputs], refs[inputs:-1], refs[-1]
    copies = []
    for index, (out, to, source, at, size, by_z) in enumerate(plan):
        if by_z:
            z = pos_ref[0]
            to = flip(lax.div(z, 2), to // 2) * 2 + flip(lax.rem(z, 2), to % 2)
        copies.append(
            pltpu.make_async_copy(
                ins[source].at[pl.ds(at, size)], outs[out].at[pl.ds(to, size)], sems.at[index]
            )
        )
    for each in copies:
        each.start()
    for each in copies:
        each.wait()


def copy_blocks(pos, plan, inputs, sizes, name):
    piece = inputs[0].shape[1:]
    return pl.pallas_call(
        functools.partial(copy_kernel, plan, len(inputs)),
        out_shape=tuple(shape((size,) + piece, BF16) for size in sizes),
        in_specs=[SMEM] + [ANY] * len(inputs),
        out_specs=[VMEM] * len(sizes),
        scratch_shapes=[pltpu.SemaphoreType.DMA((len(plan),))],
        compiler_params=params(VMEM_MB),
        cost_estimate=cost(),
        name=name,
    )(pos, *inputs)


def pack_kernel(group, pos_ref, *refs):
    four, inner, outer = refs[:4], refs[4], refs[5]
    out, sem = refs[6], refs[7]
    rows, width = out.shape[1:]
    half = width // 2
    y = pos_ref[3]
    for j, chunk in enumerate(group):
        layer, kind = chunk // 3, chunk % 3
        for part in range(2):
            to = out.at[2 * j + part]
            if kind == 0:
                for side in range(2):
                    pltpu.make_async_copy(
                        four[2 * part + side].at[layer, :, pl.ds(pl.multiple_of(y * half, 128), half)],
                        to.at[:, pl.ds(side * half, half)],
                        sem,
                    ).start()
            elif kind == 1:
                lane = pl.multiple_of((2 * y + part) * width, 128)
                pltpu.make_async_copy(inner.at[layer, :, pl.ds(lane, width)], to, sem).start()
            else:
                row = pl.multiple_of((2 * y + part) * rows, 16)
                pltpu.make_async_copy(outer.at[layer, pl.ds(row, rows)], to, sem).start()
    wait_full(out, sem)


def pack_pieces(group, pos, weights):
    _, rows, width = weights[0].shape
    return pl.pallas_call(
        functools.partial(pack_kernel, group),
        out_shape=shape((2 * len(group), rows, width), BF16),
        in_specs=[SMEM] + [HBM] * 6,
        out_specs=VMEM,
        scratch_shapes=[pltpu.SemaphoreType.DMA],
        compiler_params=params(VMEM_MB),
        cost_estimate=cost(),
        name="pack",
    )(pos, *weights)


def table_kernel(at_ref, *refs):
    vectors, out = refs[:-1], refs[-1]
    width = out.shape[2]
    for index, vector in enumerate(vectors):
        size = vector.shape[1]
        start = at_ref[0] * size
        for piece in range(max(1, out.shape[1] - IB if index == IB else 1)):
            lanes = lax.broadcasted_iota(jnp.int32, (size, width), 1) + piece * width
            spot = lax.broadcasted_iota(jnp.int32, (size, width), 0) + start
            chosen = (lanes == spot).astype(F32).astype(BF16)
            out[:, index + piece, :] = nn(vector[...], chosen)


def vector_table(at, vectors, width):
    layers, last = vectors[-1].shape[0], vectors[-1].shape[1]
    rows = IB + last // vectors[0].shape[1]
    return pl.pallas_call(
        table_kernel,
        out_shape=shape((layers, rows, width), F32),
        in_specs=[SMEM] + [VMEM] * len(vectors),
        out_specs=VMEM,
        compiler_params=params(VMEM_MB),
        cost_estimate=cost(),
        name="vector_table",
    )(at, *vectors)


def finish_kernel(kind, offsets, pos_ref, *refs):
    layers = len(offsets)
    owns, gots = refs[: 2 * layers], refs[2 * layers : 4 * layers]
    outs, buf, sems = refs[4 * layers : -2], refs[-2], refs[-1]
    rows, width = buf.shape[2:]
    half = width // 2
    y = pos_ref[3]
    copies = []
    for layer in range(layers):
        for part, at in enumerate(offsets[layer]):
            copies.append(
                pltpu.make_async_copy(
                    gots[2 * layer + part].at[pl.ds(at, 2 - part)],
                    buf.at[layer, pl.ds(2 * part, 2 - part)],
                    sems.at[2 * layer + part],
                )
            )
            copies[-1].start()
    for each in copies:
        each.wait()
    for side in range(2):
        yy = y if side == 0 else 1 - y
        for layer in range(layers):
            for part in range(2):
                if part == 0:
                    value = owns[2 * layer][side].astype(BF16).astype(F32)
                    value = value + buf[layer, 1 - side].astype(F32)
                else:
                    value = (buf[layer, 2] if side else owns[2 * layer + 1][0].astype(BF16)).astype(F32)
                if kind == 0:
                    lanes = pl.ds(pl.multiple_of(yy * half, 128), half)
                    for member in range(2):
                        outs[2 * part + member][layer, :, lanes] = value[
                            :, member * half : (member + 1) * half
                        ]
                elif kind == 1:
                    lane = pl.multiple_of((2 * yy + part) * width, 128)
                    outs[0][layer, :, pl.ds(lane, width)] = value
                else:
                    row = pl.multiple_of((2 * yy + part) * rows, 16)
                    outs[0][layer, pl.ds(row, rows), :] = value


def finish(kind, pos, results):
    layers = len(results)
    _, rows, width = results[0][0][0].shape
    outs = {
        0: (shape((layers, rows, width), F32),) * 4,
        1: (shape((layers, rows, 4 * width), F32),),
        2: (shape((layers, 4 * rows, width), F32),),
    }[kind]
    return pl.pallas_call(
        functools.partial(finish_kernel, kind, tuple((a[2], b[2]) for a, b in results)),
        out_shape=outs,
        in_specs=[SMEM] + [VMEM] * (2 * layers) + [ANY] * (2 * layers),
        out_specs=[VMEM] * len(outs),
        scratch_shapes=[
            pltpu.VMEM((layers, 3, rows, width), BF16),
            pltpu.SemaphoreType.DMA((2 * layers,)),
        ],
        compiler_params=params(VMEM_MB),
        cost_estimate=cost(),
        name="finish",
    )(pos, *[part[0] for value in results for part in value], *[part[1] for value in results for part in value])


def sum_kernel(config, *refs):
    fresh, first, second, third_a, third_b, fourth_a, fourth_b, small, waits = config
    refs = list(refs)

    def take(count):
        out = refs[:count]
        del refs[:count]
        return out

    sends = take(2) if fresh else None
    got_x = take(1)[0] if first or second else None
    got_y = take(1)[0] if first else None
    keeps = take(2) if first else None
    rest = take(1)[0] if second else None
    got_z1 = take(1)[0] if third_a or third_b else None
    pair_a = take(1)[0] if third_a else None
    pair_b = take(1)[0] if third_b else None
    got_z2 = take(1)[0] if fourth_a or fourth_b else None
    last_a = take(1)[0] if fourth_a else None
    last_b = take(1)[0] if fourth_b else None
    tables = take(2 if small == 1 else 1) if small else None
    take(waits)
    to_x = take(1)[0] if fresh or first else None
    to_y = take(1)[0] if fresh or fourth_a or fourth_b else None
    to_z1 = take(1)[0] if first or second else None
    to_z2 = take(1)[0] if third_a or third_b else None
    at = 0
    if fresh:
        for out, send in ((to_x, sends[0]), (to_y, sends[1])):
            for half in range(2):
                out[half * ZS : (half + 1) * ZS] = send[half]
        at = 2 * ZS
    if first:
        b_rest, hold = take(2)
        for k in range(ZS):
            for half in range(2):
                value = keeps[0][half, k].astype(F32) + got_x[half * ZS + k].astype(F32)
                (to_z1 if k % 2 else hold)[k // 2 * 2 + half] = value.astype(BF16)
        b_rest[...] = (keeps[1][0].astype(F32) + got_y[:ZS].astype(F32)).astype(BF16)
        value = keeps[1][1].astype(F32) + got_y[ZS : 2 * ZS].astype(F32)
        to_x[at : at + ZS] = value.astype(BF16)
    if second:
        (hold,) = take(1)
        begin = 2 * ZS if first else 0
        for k in range(ZS):
            value = (rest[k].astype(F32) + got_x[begin + k].astype(F32)).astype(BF16)
            if k % 2:
                to_z1[4 * first + k // 2] = value
            else:
                hold[k // 2] = value
    for here, pair, begin, size, to in (
        (third_a, pair_a, 0, 2, 0),
        (third_b, pair_b, 4 * third_a, 1, 2 * third_a),
    ):
        if here:
            (hold,) = take(1)
            for index in range(size):
                hold[index] = pair[index].astype(F32) + got_z1[begin + index].astype(F32)
                value = pair[size + index].astype(F32) + got_z1[begin + size + index].astype(F32)
                to_z2[to + index] = value.astype(BF16)
    for here, last, begin, size in ((fourth_a, last_a, 0, 2), (fourth_b, last_b, 2 * fourth_a, 1)):
        if here:
            (total,) = take(1)
            for index in range(size):
                value = last[index] + got_z2[begin + index].astype(F32)
                total[index] = value
                to_y[at + begin + index] = value.astype(BF16)
    if small:
        come = (None, None, got_x, got_z1, got_z2)[small]
        come = tables[1][...] if small == 1 else come[come.shape[0] - 1]
        value = tables[0][...] + come.astype(F32)
        refs[0][...] = value
        to = (None, to_x, to_z1, to_z2, to_y)[small]
        to[to.shape[0] - 1] = value.astype(BF16)


def sum_round(fresh, past, small, after):
    names = ("first", "second", "third_a", "third_b", "fourth_a", "fourth_b")
    stage, table = small
    config = (fresh is not None,) + tuple(name in past for name in names) + (stage, len(after))
    is_fresh, first, second, third_a, third_b, fourth_a, fourth_b = (int(value) for value in config[:7])
    sample = fresh[1] if fresh is not None else past[[name for name in names if name in past][0]][0]
    rows, width = sample.shape[-2:]
    inputs = []
    if is_fresh:
        inputs += [fresh[1], fresh[3]]
    if first or second:
        inputs += [past["got_x"]]
    if first:
        inputs += [past["got_y"]] + list(past["first"])
    if second:
        inputs += list(past["second"])
    if third_a or third_b:
        inputs += [past["got_z1"]]
    for name in ("third_a", "third_b"):
        inputs += list(past.get(name, ()))
    if fourth_a or fourth_b:
        inputs += [past["got_z2"]]
    for name in ("fourth_a", "fourth_b"):
        inputs += list(past.get(name, ()))
    if table is not None:
        inputs += list(table)
    begin = 2 * ZS * is_fresh
    sizes = (
        (is_fresh or first, begin + ZS * first + (stage == 1)),
        (is_fresh or fourth_a or fourth_b, begin + 2 * fourth_a + fourth_b + (stage == 4)),
        (first or second, 4 * first + 2 * second + (stage == 2)),
        (third_a or third_b, 2 * third_a + third_b + (stage == 3)),
    )
    outputs = [shape((size, rows, width), BF16) for there, size in sizes if there]
    if first:
        outputs += [shape((ZS, rows, width), BF16), shape((4, rows, width), BF16)]
    if second:
        outputs += [shape((2, rows, width), BF16)]
    if third_a:
        outputs += [shape((2, rows, width), F32)]
    if third_b:
        outputs += [shape((1, rows, width), F32)]
    if fourth_a:
        outputs += [shape((2, rows, width), F32)]
    if fourth_b:
        outputs += [shape((1, rows, width), F32)]
    if stage:
        outputs += [shape(table[0].shape, F32)]
    outs = list(
        pl.pallas_call(
            functools.partial(sum_kernel, config),
            out_shape=tuple(outputs),
            in_specs=[VMEM] * len(inputs) + [ANY] * len(after),
            out_specs=[VMEM] * len(outputs),
            compiler_params=params(VMEM_MB),
            cost_estimate=cost(),
            name="sum_round",
        )(*inputs, *after)
    )

    def take(wanted, count):
        if not wanted:
            return None
        out = tuple(outs[:count])
        del outs[:count]
        return out

    sends = tuple(take(there, 1) for there, _ in sizes)
    b_rest = take(first, 1)
    holds = (take(first, 1), take(second, 1))
    lasts = (take(third_a, 1), take(third_b, 1))
    totals = (take(fourth_a, 1), take(fourth_b, 1))
    return sends, begin, b_rest, holds, lasts, totals, take(stage > 0, 1)


def collect_kernel(*refs):
    out = refs[-1]
    for layer in range(out.shape[0]):
        query_ref, value_ref, head_ref, chain_ref = refs[4 * layer : 4 * layer + 4]
        out[layer] = chain_ref[...]
        out[layer, pl.ds(QB, 1), :] = query_ref[:1]
        out[layer, pl.ds(VB, 1), :] = value_ref[:1]
        for at, index in enumerate((FG, FS, UB)):
            out[layer, pl.ds(index, 1), :] = head_ref[at : at + 1]


def collect(vectors, rows):
    flat = [value for layer in vectors for value in layer]
    width = flat[0].shape[1]
    return pl.pallas_call(
        collect_kernel,
        out_shape=shape((len(vectors), rows, width), F32),
        in_specs=[VMEM] * len(flat),
        out_specs=VMEM,
        compiler_params=params(VMEM_MB),
        cost_estimate=cost(),
        name="collect",
    )(*flat)


def vectors_kernel(last, at_ref, table_ref, got_ref, *outs):
    layers, width = outs[0].shape[0], table_ref.shape[1]
    at = at_ref[0]
    for index, out in enumerate(outs):
        size = out.shape[1]
        start = at * size
        shift = lax.rem(width - lax.rem(start, width), width)
        for layer in range(layers):
            spot = pl.ds(layer * 16 + index + lax.div(start, width), 1)
            value = table_ref[spot, :]
            if last is not None:
                value = value.astype(BF16).astype(F32) + got_ref[spot, :]
            value = jnp.broadcast_to(value, (8, width))
            out[pl.ds(layer, 1), :] = pltpu.roll(value, shift, 1)[:1, :size]


def own_vectors(at, table, got, layers, size, wide):
    sizes = [size] * IB + [wide]
    last = None if got is None else 0
    return pl.pallas_call(
        functools.partial(vectors_kernel, last),
        out_shape=tuple(shape((layers, each), F32) for each in sizes),
        in_specs=[SMEM, VMEM, VMEM],
        out_specs=[VMEM] * len(sizes),
        compiler_params=params(VMEM_MB),
        cost_estimate=cost(),
        name="own_vectors",
    )(at, table, table if got is None else got)


def fence(values):
    return lax.optimization_barrier(values)


def build(mesh):
    count = mesh.shape["dp"]

    def flat(dp, seq):
        return dp * 2 + seq

    def pairs(source_of):
        out = []
        for dp in range(count):
            for seq in range(2):
                out.append((flat(*source_of(dp, seq)), flat(dp, seq)))
        return out

    swap_pairs = pairs(lambda dp, seq: (dp // 2 * 2 + seq, dp % 2))
    core_pairs = pairs(lambda dp, seq: (dp ^ 1, seq))
    x_pairs = pairs(lambda dp, seq: (dp ^ 2, seq))
    y_pairs = pairs(lambda dp, seq: (dp, 1 - seq))
    z_pairs = [pairs(lambda dp, seq, k=k: ((dp // 4 ^ k) * 4 + dp % 4, seq)) for k in (1, 2)]

    def move(value, perm):
        return lax.ppermute(value, AXES, perm)

    return dict(
        count=count,
        swap=swap_pairs,
        core=core_pairs,
        x=x_pairs,
        y=y_pairs,
        z1=z_pairs[0],
        z2=z_pairs[1],
        move=move,
    )


def body(
    net,
    tokens,
    segment_ids,
    padding,
    query_weight,
    key_weight,
    value_weight,
    output_weight,
    query_bias,
    value_bias,
    output_bias,
    attn_gain,
    attn_shift,
    inner_weight,
    inner_bias,
    outer_weight,
    outer_bias,
    ffn_gain,
    ffn_shift,
    upstream,
):
    layers, small, width = query_weight.shape
    hidden = inner_weight.shape[2]
    count = net["count"]
    move = net["move"]
    staged = count == BLOCKS and small == 16 * layers
    dp = lax.axis_index("dp").astype(jnp.int32)
    y = lax.axis_index("seq").astype(jnp.int32)
    core = lax.rem(dp, 2)
    if staged:
        pos_g = jnp.stack([lax.div(dp, 4), lax.rem(lax.div(dp, 2), 2), core, y])
        pos_w = pos_g
    else:
        zero = jnp.zeros((), jnp.int32)
        pos_g = jnp.stack([zero, zero, core, zero])
        pos_w = jnp.stack([zero, zero, zero, zero])

    labels = jnp.where(padding == 1, segment_ids, -1)
    small_own = move(jnp.concatenate([segment_ids, labels]), net["swap"])
    token_low = move(tokens[0], net["swap"])

    vector_args = [query_bias, value_bias, output_bias, attn_gain, attn_shift, outer_bias]
    vector_args += [ffn_gain, ffn_shift, inner_bias]
    table = vector_table(dp[None], vector_args, width)
    if staged:
        table = table + move(table, net["x"])
    else:
        table = lax.psum(table, "dp")

    raw = (query_weight, key_weight, value_weight, output_weight, inner_weight, outer_weight)
    chunks = []
    for layer in range(layers):
        four = (query_weight[layer], key_weight[layer], value_weight[layer], output_weight[layer])
        if not staged:
            full = [lax.all_gather(value, "dp", axis=0, tiled=True) for value in four]
            inner = lax.all_gather(inner_weight[layer], "dp", axis=0, tiled=True)
            outer = lax.all_gather(outer_weight[layer], "dp", axis=0, tiled=True)
            rows = width // BLOCKS

            def cut(value, dy, dx, dc):
                value = value.reshape(ZS, 2, 2, rows, 2, -1)
                return value[:, dx, dc, :, dy, :]

            lists = [[[], []], [[], []], [[], []]]
            for dc in range(2):
                for part, dy, dx in UNITS:
                    lists[0][dc].append(
                        jnp.concatenate([cut(value, dy, dx, dc) for value in full[part * 2 : part * 2 + 2]], axis=2)
                    )
                    lists[1][dc].append(cut(inner, dy, dx, dc)[..., part * width : (part + 1) * width])
                    lists[2][dc].append(
                        outer.reshape(ZS, 2, 2, 2, 2, hidden // BLOCKS // 4, width)[:, dx, dc, dy, part]
                    )
            chunks.extend(tuple(jnp.concatenate(side) for side in value) for value in lists)

    total_chunks = 3 * layers
    groups = []
    if staged:
        edges = [0, 1, 2, 3] + list(range(4, total_chunks, 2)) + [total_chunks]
        groups = [range(low, high) for low, high in zip(edges[:-1], edges[1:])]
    where_of = {i: (g, i - group[0]) for g, group in enumerate(groups) for i in group}
    stage_z = [None] * len(groups)

    def start_z2(g):
        own = pack_pieces(groups[g], pos_g, raw)
        stage_z[g] = (own, move(own, net["z2"]))

    def start_z1(g):
        own, come = stage_z[g]
        size = own.shape[0]
        both = copy_blocks(
            pos_g,
            [(0, 0, 0, 0, size, False), (0, size, 1, 0, size, False)],
            (own, come),
            [2 * size],
            "gather_z",
        )[0]
        stage_z[g] = (both, move(both, net["z1"]))

    if staged:
        start_z2(0)
        stage_z[0], raw, table, small_own, token_low = fence(
            (stage_z[0], raw, table, small_own, token_low)
        )
        start_z1(0)
        start_z2(1)
        table = table + move(table, net["core"])
    small_other = move(small_own, net["core"])
    token_other = move(token_low, net["core"])
    if staged:
        stage_z[:2], raw, table, small_own, small_other, token_low, token_other, upstream = fence(
            (stage_z[:2], raw, table, small_own, small_other, token_low, token_other, upstream)
        )
    seg = small_own[0:1]
    lab = jnp.concatenate([small_own[1], small_other[1]])[:, None]
    current = token_low.astype(F32)
    other = token_other
    kept = [None] * layers
    todo = []
    for layer in range(layers):
        todo.append(("attn", layer, 3 * layer))
        todo.append(("inner", layer, 3 * layer + 1))
        todo.append(("outer", layer, 3 * layer + 2))
    low = None
    attn_out = None
    arrived = 0 if staged else total_chunks

    mid = None

    def compute():
        nonlocal current, other, low, attn_out, mid, head
        if not todo or todo[0][2] >= arrived:
            return
        kind, layer, _ = todo.pop(0)
        vec = table[layer]
        if kind == "attn":
            attn_out = attn_forward(pos_w, pos_g, current, other, seg, lab, vec, chunks[3 * layer])
            return
        h, n1, c1, q, kt, v, p, xoh, far_xoh = attn_out
        if kind == "inner":
            active, gp, gt, far_gt = inner_forward(pos_w, pos_g, h, vec, chunks[3 * layer + 1])
            mid = (active, gp, gt, move(far_gt, net["core"]), move(far_xoh, net["core"]))
            return
        active, gp, gt, far_gt, far_xoh = mid
        last = layer + 1 == layers
        current, low, *rest = outer_forward(
            pos_w, h, active, vec, chunks[3 * layer + 2], upstream if last else None
        )
        if last:
            head, rest = rest, (None, None)
        else:
            other = move(low, net["core"])
        kept[layer] = (n1, c1, q, kt, v, p, *rest, gp, xoh, gt, far_xoh, far_gt)

    head = None
    if not staged:
        upstream = move(upstream[0], net["swap"])
    if staged:
        sent, got = {}, {}
        zplan = {r: [(1, r + 2), (2, r + 3)] for r in range(-1, 2)}
        for r in range(2, 2 * len(groups)):
            g = (r + 6) // 2 + (r % 2)
            zplan[r] = [(1 + r % 2, g)]
        spread = [net["z2"], net["z1"]]
        for r in range(-LAG, total_chunks + LAG):
            inputs, plan = [], []
            sizes = [0, 0]
            use = lambda value: (inputs.append(value), len(inputs) - 1)[1]
            fresh = r + LAG < total_chunks
            if fresh:
                g, j = where_of[r + LAG]
                n = len(groups[g])
                mine, theirs = use(stage_z[g][0]), use(stage_z[g][1])
                for out, part in ((0, 1), (1, 0)):
                    for k, (source, slot) in enumerate(((mine, 0), (theirs, 0), (mine, 1), (theirs, 1))):
                        plan.append((out, k, source, (slot * n + j) * 2 + part, 1, True))
                    sizes[out] = ZS
            before = r - LAG
            home = 0 <= before < total_chunks
            if before >= -LAG and (r < total_chunks or home):
                sx, sy = use(sent[before][0]), use(sent[before][1])
                rx, ry = use(got[before][0]), use(got[before][1])
                first = ZS if before + LAG < total_chunks else 0
                if r < total_chunks:
                    for out, send, come in ((0, sy, ry), (1, sx, rx)):
                        plan.append((out, sizes[out], send, 0, ZS, False))
                        plan.append((out, sizes[out] + ZS, come, 0, ZS, False))
                        sizes[out] += 2 * ZS
                if home:
                    sizes.append(8 * ZS)
                    slot = 2
                    for at, (send, come) in enumerate(((sx, rx), (sy, ry))):
                        plan.append((slot, at * 4 * ZS, send, first, 2 * ZS, False))
                        plan.append((slot, at * 4 * ZS + 2 * ZS, come, first, 2 * ZS, False))
            live = [index for index, size in enumerate(sizes) if size]
            outs = copy_blocks(
                pos_g,
                [(live.index(each[0]),) + each[1:] for each in plan],
                inputs,
                [sizes[index] for index in live],
                "gather_round",
            )
            outs = dict(zip(live, outs))
            if 0 in outs:
                sent[r] = (outs[0], outs[1])
                got[r] = (move(outs[0], net["x"]), move(outs[1], net["y"]))
            core_pair = None
            if home:
                core_pair = (outs[2], move(outs[2], net["core"]))
            for stage, g in zplan.get(r, ()):
                if g < len(groups):
                    (start_z2 if stage == 2 else start_z1)(g)
            if spread and r >= 0:
                table = table + move(table, spread.pop(0))
            if r == total_chunks - 1:
                upstream = move(upstream[0], net["swap"])
            compute()
            ready = r + 1 - LAG
            state = (got.get(ready), core_pair, stage_z, current, other, attn_out, raw, table, upstream, mid)
            state = fence(state)
            if ready in got:
                got[ready] = state[0]
            if home:
                chunks.append(state[1])
                arrived += 1
            stage_z, current, other, attn_out, raw, table, upstream, mid = (list(state[2]),) + tuple(state[3:])
    while todo:
        compute()
    range_ids = jnp.arange(SEGS, dtype=jnp.int32)
    own = (small_own[1][None, :] == range_ids[:, None]).astype(F32)
    sums = jnp.dot(own, current, precision=lax.Precision.HIGHEST)
    pool_sums = sums
    counts = jnp.sum((lab[:, 0][None, :] == range_ids[:, None]).astype(F32), axis=1)
    loose = {}
    if staged:
        loose["hidden"] = move(low, net["swap"])
        loose["pool"] = pool_sums + move(pool_sums, net["core"])

    parts = []
    vectors = [None] * layers
    rounds = []
    ends = [], []
    table_stage = 1

    def side_work():
        step = len(rounds)
        last = total_chunks + 1
        if step == 2:
            loose["after"] = (loose["hidden"], loose["pool"])
        if step == 3:
            loose["pooled"] = move(loose.pop("pool") / counts[:, None], net["swap"])
            loose["after"] = (loose["pooled"],)
        if step == last + 1:
            loose["grad"] = move(loose.pop("grad"), net["swap"])
            loose["after"] = (loose["grad"],)
        if step == last + 2:
            done = list(finish(2, pos_g, ended()[0::3][::-1]))
            loose["outer"] = done
            loose["after"] = (done[0],)

    def ended():
        out = []
        for each in zip(*ends):
            if each[1][0] < len(rounds):
                out.append(tuple((own, rounds[s]["got_y"], at) for s, own, at in each))
        return out

    def settle(state):
        return fence(state)

    def advance(fresh, state):
        if not staged:
            if fresh is not None:
                parts.append(fresh)
            return state(()) if callable(state) else state
        s = len(rounds)
        past = rounds[s - 1] if s else {}
        sends, begin, b_rest, holds, lasts, totals, small = sum_round(
            fresh, past, loose.pop("small", (0, None)), tuple(loose.pop("after", ()))
        )
        now = {}
        for name, way, value in zip(
            ("got_x", "got_y", "got_z1", "got_z2"), ("x", "y", "z1", "z2"), sends
        ):
            if value is not None:
                now[name] = move(value[0], net[way])
        for name, value in (
            ("first", fresh and (fresh[0], fresh[2])),
            ("second", b_rest),
            ("third_a", holds[0]),
            ("third_b", holds[1]),
            ("fourth_a", lasts[0]),
            ("fourth_b", lasts[1]),
        ):
            if value is not None:
                now[name] = value
        for part, value in enumerate(totals):
            if value is not None:
                ends[part].append((s, value[0], begin + (2 if part and totals[0] is not None else 0)))
        sends = tuple(value[0] for value in sends if value is not None)
        if "vectors" in loose:
            small = loose.pop("vectors").reshape(-1, width)
            loose["small"] = (1, (small, move(small, net["core"])))
        elif small is not None:
            nonlocal table_stage
            table_stage += 1
            loose["small"] = (table_stage, small)
        side_work()
        if callable(state):
            state = state(sends)
        rounds.append(now)
        ready = s + 1 - LAG
        if ready < 0:
            return fence(state)
        rounds[ready], state = fence((rounds[ready], state))
        return state

    top = layers - 1
    ready = []
    dyl, dy, head_sums = head
    for layer in reversed(range(layers)):
        attn_bufs, inner_bufs, outer_bufs = chunks[3 * layer : 3 * layer + 3]
        n1, c1, q, kt, v, p, n2, c2, gp, xoh, gt, far_xoh, far_gt = kept[layer]
        got_dyl = move(dyl, net["core"])
        chain_args = (pos_w, dyl, dy, gp, n1, c1, table[layer], inner_bufs, outer_bufs, attn_bufs)
        if layer == top:
            outer_parts = settle(outer_grad(gt, far_gt, dyl, got_dyl))

            def first_round(sends):
                return chain_backward(*chain_args, after=sends)

            pack, da, do, sums = advance(outer_parts, first_round)
            got_pack = move(pack, net["core"])

            def second_round(sends):
                back, qsum = attn_backward(q, kt, v, p, do, after=sends)
                return back, qsum, got_pack, inner_grad(pos_g, xoh, far_xoh, pack, got_pack)

            back, qsum, got_pack, inner_parts = advance(None, second_round)
            ready.append(inner_parts)
            got_back = move(back, net["core"])
        else:
            pack, da, do, sums = chain_backward(*chain_args)
            outer_parts = outer_grad(gt, far_gt, dyl, got_dyl)
            state = advance(ready.pop(0), (pack, da, do, sums, outer_parts))
            pack, da, do, sums, outer_parts = state
            ready.append(outer_parts)
            got_pack = move(pack, net["core"])
            back, qsum = attn_backward(q, kt, v, p, do)
            inner_parts = inner_grad(pos_g, xoh, far_xoh, pack, got_pack)
            state = advance(ready.pop(0), (back, qsum, got_pack, inner_parts))
            back, qsum, got_pack, inner_parts = state
            ready.append(inner_parts)
            got_back = move(back, net["core"])
        below = None if layer == 0 else (kept[layer - 1][6], kept[layer - 1][7], table[layer - 1])
        total, vsum, *head = input_backward(pos_w, da, back, got_back, attn_bufs, below)
        attn_parts = attn_grad(pos_g, xoh, far_xoh, back, got_back, total, pack, got_pack)
        attn_parts, head, vsum = advance(ready.pop(0), (attn_parts, head, vsum))
        ready.append(attn_parts)
        vectors[layer] = (qsum, vsum, head_sums, sums)
        if layer:
            dyl, dy, head_sums = head
    grad = head[0]
    vectors = collect(vectors, 16)
    loose["grad"] = grad
    while ready:
        if len(ready) == 1:
            loose["vectors"] = vectors
        advance(ready.pop(0), None)
    results = []
    if staged:
        for _ in range(4 * LAG):
            advance(None, None)
        results = ended()

    if staged:
        stacked = []
        for kind, first in ((0, 2), (1, 1)):
            stacked += list(finish(kind, pos_g, results[first::3][::-1]))
        stacked += loose["outer"]
        hidden_out, pooled, tokens_grad = (loose[key] for key in ("hidden", "pooled", "grad"))
        vectors = loose["small"][1][0]
        got_vectors = rounds[-1]["got_y"][-1].astype(F32)
    else:
        collected = [None] * layers
        for place_at, layer in enumerate(reversed(range(layers))):
            outer_parts, inner_parts, attn_parts = parts[3 * place_at : 3 * place_at + 3]

            def spread(outs):
                a_keep, a_send, b_keep, b_send = outs
                a = jnp.stack([a_keep, a_send])
                b = jnp.stack([b_keep, b_send], axis=1)
                return jnp.stack([a, b], axis=2)

            def total(out):
                out = out.reshape(ZS * 2, 1, out.shape[2], out.shape[3])
                mine = (jnp.arange(2, dtype=jnp.int32) == core)[None, :, None, None]
                out = jnp.where(mine, out, jnp.zeros_like(out)).reshape(-1, out.shape[-1])
                out = lax.psum_scatter(out, "dp", scatter_dimension=0, tiled=True)
                return lax.psum(out.astype(F32), "seq")

            outer = spread(outer_parts).transpose(3, 0, 1, 2, 4, 5)
            outer = total(outer.reshape(ZS, 2, -1, width))
            inner = spread(inner_parts).transpose(3, 0, 4, 1, 2, 5)
            inner = total(inner.reshape(ZS, 2, inner.shape[2], -1))
            attn = spread(attn_parts)
            attn = attn.reshape(attn.shape[:5] + (2, width // 2)).transpose(2, 5, 3, 0, 4, 1, 6)
            attn = attn.reshape(4, ZS, 2, attn.shape[4], width)
            four = [total(attn[index]) for index in range(4)]
            collected[layer] = four + [inner, outer]
        stacked = [
            jnp.stack([collected[layer][member] for layer in range(layers)]) for member in range(6)
        ]
        hidden_out = move(low, net["swap"])
        pooled = move((pool_sums + move(pool_sums, net["core"])) / counts[:, None], net["swap"])
        tokens_grad = move(grad, net["swap"])
        vectors = lax.psum(vectors, AXES).reshape(-1, width)
        got_vectors = None
    own = own_vectors(dp[None], vectors, got_vectors, layers, small, hidden // count)
    return (
        hidden_out[None],
        pooled[None],
        tokens_grad.astype(F32)[None],
        stacked[0],
        stacked[1],
        stacked[2],
        stacked[3],
        own[QB],
        own[VB],
        own[OB],
        own[AG],
        own[AS],
        stacked[4],
        own[IB],
        stacked[5],
        own[UB],
        own[FG],
        own[FS],
    )


def solution(mesh):
    cube = P(None, "dp", None)
    flat = P(None, "dp")
    acts = P("dp", "seq", None)
    ids = P("dp", "seq")
    return jax.shard_map(
        functools.partial(body, build(mesh)),
        mesh=mesh,
        in_specs=(acts, ids, ids, cube, cube, cube, cube, flat, flat, flat, flat, flat, cube, flat, cube)
        + (flat, flat, flat, acts),
        out_specs=(acts, P("dp", None, None), acts, cube, cube, cube, cube)
        + (flat, flat, flat, flat, flat, cube, flat, cube, flat, flat, flat),
        check_vma=False,
    )
```

```python
import functools

import jax
import jax.numpy as jnp
from jax import lax
from jax.experimental import pallas as pl
from jax.experimental.pallas import tpu as pltpu
from jax.sharding import PartitionSpec as P

HD = 64
SEGS = 4
BLOCKS = 16
ZS = 4
LAG = 1
VMEM_MB = 20
EPS = 1e-06
MASKED = -1e30
AXES = ("dp", "seq")
F32 = jnp.float32
BF16 = jnp.bfloat16
MB = 1024 * 1024

QB, VB, OB, AG, AS, UB, FG, FS, IB = range(9)


def nn(left, right):
    return lax.dot_general(left, right, (((1,), (0,)), ((), ())), preferred_element_type=F32)


def nt(left, right):
    return lax.dot_general(left, right, (((1,), (1,)), ((), ())), preferred_element_type=F32)


def params(vmem):
    return pltpu.CompilerParams(vmem_limit_bytes=vmem * MB)


def cost():
    return pl.CostEstimate(flops=1, bytes_accessed=1, transcendentals=0)


def load(source, target, sem):
    pltpu.make_async_copy(source, target, sem).start()


VMEM = pl.BlockSpec(memory_space=pltpu.VMEM)
SMEM = pl.BlockSpec(memory_space=pltpu.SMEM)
ANY = pl.BlockSpec(memory_space=pl.ANY)
HBM = pl.BlockSpec(memory_space=pltpu.HBM)


def shape(dims, dtype):
    return jax.ShapeDtypeStruct(dims, dtype)


def flip(value, bit):
    return value + bit - 2 * value * bit


def block_at(pos_ref, k, dx, dc):
    z, x, c = pos_ref[0], pos_ref[1], pos_ref[2]
    low = lax.rem(z, 2)
    zz = flip(lax.div(z, 2), k // 2) * 2 + flip(low, k % 2)
    return (zz * 2 + flip(x, dx)) * 2 + flip(c, dc)


def half_at(pos_ref, dy):
    return flip(pos_ref[3], dy)


UNITS = (
    (0, 0, 0),
    (0, 1, 0),
    (0, 0, 1),
    (0, 1, 1),
    (1, 0, 0),
    (1, 0, 1),
    (1, 1, 0),
    (1, 1, 1),
)


def each_unit(pos_ref, bufs):
    for dc in range(2):
        for unit, (part, dy, dx) in enumerate(UNITS):
            at = flip(pos_ref[1], dx) * 2 + flip(pos_ref[2], dc)
            yield bufs[dc].at[pl.ds(unit * ZS, ZS)], part, dy, at


def fetch_member(pos_ref, bufs, member, full_ref, sem):
    half = full_ref.shape[3] // 2
    for unit, part, dy, at in each_unit(pos_ref, bufs):
        if part == member // 2:
            col = pl.multiple_of(half_at(pos_ref, dy) * half, 128)
            load(
                unit.at[:, :, pl.ds(member % 2 * half, half)],
                full_ref.at[:, at, :, pl.ds(col, half)],
                sem,
            )


def fetch_columns(pos_ref, bufs, full_ref, sem):
    width = full_ref.shape[3] // 4
    for unit, part, dy, at in each_unit(pos_ref, bufs):
        col = pl.multiple_of((half_at(pos_ref, dy) * 2 + part) * width, 128)
        load(unit, full_ref.at[:, at, :, pl.ds(col, width)], sem)


def fetch_rows(pos_ref, bufs, full_ref, sem):
    for unit, part, dy, at in each_unit(pos_ref, bufs):
        load(unit, full_ref.at[:, at, half_at(pos_ref, dy) * 2 + part], sem)


def flat(values):
    return values.reshape(-1, values.shape[-1])


def square(width):
    return pltpu.VMEM((ZS, BLOCKS // ZS, width // BLOCKS, width), BF16)


def wide_matrix(width, hidden):
    return pltpu.VMEM((ZS, BLOCKS // ZS, width // BLOCKS, hidden), BF16)


def tall_matrix(hidden, width):
    return pltpu.VMEM((ZS, BLOCKS // ZS, 4, hidden // BLOCKS // 4, width), BF16)


def wait_full(full_ref, sem):
    pltpu.make_async_copy(full_ref, full_ref, sem).wait()


def export_rows(pos_ref, wide_ref, outs, index):
    rows = outs[0].shape[3]
    for dc in range(2):
        for dx in range(2):
            for k in range(ZS):
                row = pl.multiple_of(block_at(pos_ref, k, dx, dc) * rows, 16)
                outs[dc][index, dx, k] = wide_ref[pl.ds(row, rows), :]


def export_halves(pos_ref, wide_ref, outs):
    rows = outs[0].shape[4]
    for dc in range(2):
        for dx in range(2):
            for dy in range(2):
                for k in range(ZS):
                    block = block_at(pos_ref, k, dx, dc) * 2 + half_at(pos_ref, dy)
                    for part in range(2):
                        row = pl.multiple_of((block * 2 + part) * rows, 16)
                        outs[dc][dx, dy, part, k] = wide_ref[pl.ds(row, rows), :]


def mean_of(values):
    return jnp.mean(values, axis=-1, keepdims=True)


def normalize(values):
    center = values - mean_of(values)
    inverse = lax.rsqrt(mean_of(center * center) + EPS)
    return center * inverse, inverse


def norm_back(normed, inverse, scaled):
    return inverse * (scaled - mean_of(scaled) - normed * mean_of(scaled * normed))


def colsum(values):
    return jnp.sum(values, axis=0, keepdims=True)


def row_of(vec_ref, index):
    return vec_ref[pl.ds(index, 1), :]


def attn_kernel(*refs):
    pos_w, pos_g = refs[0], refs[1]
    x_ref, xp_ref, seg_ref, lab_ref, vec_ref = refs[2:7]
    bufs = refs[7:9]
    h_ref = refs[9]
    kept = refs[10:18]
    wq, wk, wv, wo, rows_ref, vt_ref, wide_ref, bias_ref, k_ref = refs[18:27]
    held = refs[27:35]
    n1_ref, c1_ref, q_ref, kt_ref, v_ref, p_ref = held[:6]
    exports = held[6:]
    sems, store_sems = refs[35:]

    def store(index):
        load(held[index], kept[index], store_sems.at[index])

    tokens, width = x_ref.shape
    for member, full in enumerate((wq, wk, wv, wo)):
        fetch_member(pos_w, bufs, member, full, sems.at[member])
    bias_ref[...] = jnp.where(lab_ref[...] == seg_ref[...], 0.0, MASKED)
    low = x_ref[...].astype(BF16)
    rows_ref[:tokens] = low
    rows_ref[tokens:] = xp_ref[...]
    wide_ref[...] = low.T
    export_rows(pos_g, wide_ref, exports, 0)
    wait_full(wq, sems.at[0])
    query = (nn(low, flat(wq[...])) + row_of(vec_ref, QB)).astype(BF16)
    q_ref[...] = (query.astype(F32) * HD ** (-0.5)).astype(BF16)
    wait_full(wk, sems.at[1])
    key = nn(rows_ref[...], flat(wk[...])).astype(BF16)
    k_ref[...] = key
    kt_ref[...] = key.T
    store(2)
    store(3)
    wait_full(wv, sems.at[2])
    value = (nn(rows_ref[...], flat(wv[...])) + row_of(vec_ref, VB)).astype(BF16)
    v_ref[...] = value
    vt_ref[...] = value.T
    store(4)

    def pair(index, carry):
        lane = pl.multiple_of(index * 128, 128)
        keys = k_ref[:, pl.ds(lane, 128)]
        queries = q_ref[:, pl.ds(lane, 128)]
        first = lax.broadcasted_iota(jnp.int32, queries.shape, 1) < HD
        for which in range(2):
            mine = jnp.where(first if which == 0 else ~first, queries, jnp.zeros_like(queries))
            scores = nt(keys, mine) + bias_ref[...]
            expos = jnp.exp(scores - jnp.max(scores, axis=0, keepdims=True))
            probs = (expos * (1.0 / jnp.sum(expos, axis=0, keepdims=True))).astype(BF16)
            p_ref[index * 2 + which] = probs
            row = pl.multiple_of(index * 128 + which * HD, HD)
            wide_ref[pl.ds(row, HD), :] = nn(vt_ref[pl.ds(row, HD), :], probs).astype(BF16)
        both = pl.ds(index * 2, 2)
        load(p_ref.at[both], kept[5].at[both], store_sems.at[5])
        return carry

    lax.fori_loop(0, width // 128, pair, 0)
    export_rows(pos_g, wide_ref, exports, 1)
    mixed = wide_ref[...].T
    wait_full(wo, sems.at[3])
    branch = nn(mixed, flat(wo[...])) + row_of(vec_ref, OB)
    normed, inverse = normalize(x_ref[...] + branch)
    hidden = normed * row_of(vec_ref, AG) + row_of(vec_ref, AS)
    h_ref[...] = hidden
    n1_ref[...] = normed
    c1_ref[...] = jnp.broadcast_to(inverse, c1_ref.shape)
    wide_ref[...] = hidden.astype(BF16).T
    export_rows(pos_g, wide_ref, exports, 2)
    for index in (0, 1, 6, 7):
        store(index)
    for index in range(8):
        wait_full(held[index], store_sems.at[index])


def attn_forward(pos_w, pos_g, x, xp, seg, lab, vec, bufs):
    tokens, width = x.shape
    heads = width // HD
    export = shape((3, 2, ZS, width // BLOCKS, tokens), BF16)
    kept = (
        shape((tokens, width), F32),
        shape((tokens, 128), F32),
        shape((tokens, width), BF16),
        shape((width, 2 * tokens), BF16),
        shape((2 * tokens, width), BF16),
        shape((heads, 2 * tokens, tokens), BF16),
        export,
        export,
    )
    return pl.pallas_call(
        attn_kernel,
        out_shape=(shape((tokens, width), F32),) + kept,
        in_specs=[SMEM, SMEM] + [VMEM] * 5 + [ANY] * 2,
        out_specs=[VMEM] + [HBM] * 8,
        scratch_shapes=[square(width)] * 4
        + [
            pltpu.VMEM((2 * tokens, width), BF16),
            pltpu.VMEM((width, 2 * tokens), BF16),
            pltpu.VMEM((width, tokens), BF16),
            pltpu.VMEM((2 * tokens, tokens), F32),
            pltpu.VMEM((2 * tokens, width), BF16),
        ]
        + [pltpu.VMEM(each.shape, each.dtype) for each in kept]
        + [pltpu.SemaphoreType.DMA((4,)), pltpu.SemaphoreType.DMA((8,))],
        compiler_params=params(VMEM_MB),
        cost_estimate=cost(),
        name="attn_forward",
    )(pos_w, pos_g, x, xp, seg, lab, vec, *bufs)


def head_back(grad, normed, inverse, gain, low_ref, back_ref, sums_ref):
    sums_ref[...] = jnp.zeros_like(sums_ref)
    sums_ref[pl.ds(0, 1), :] = colsum(grad * normed)
    sums_ref[pl.ds(1, 1), :] = colsum(grad)
    back = norm_back(normed, inverse, grad * gain)
    low = back.astype(BF16)
    low_ref[...] = low
    back_ref[...] = back
    sums_ref[pl.ds(2, 1), :] = colsum(low.astype(F32))


def head_shapes(tokens, width):
    return (
        shape((tokens, width), BF16),
        shape((tokens, width), F32),
        shape((8, width), F32),
    )


def inner_kernel(tile, *refs):
    pos_w, pos_g, h_ref, vec_ref = refs[:4]
    bufs, active_ref, kept = refs[4:6], refs[6], refs[7:10]
    wi, low_ref, wide_ref = refs[10:13]
    held = refs[13:16]
    gp_ref, exports = held[0], held[1:]
    sem, store_sems = refs[16:]
    width, hidden = h_ref.shape[1], wi.shape[3]
    fetch_columns(pos_w, bufs, wi, sem)
    low_ref[...] = h_ref[...].astype(BF16)
    wait_full(wi, sem)
    per_row = width // tile

    def step(index, carry):
        lanes = pl.ds(pl.multiple_of(index * tile, tile), tile)
        bias = vec_ref[pl.ds(IB + lax.div(index, per_row), 1), :]
        part = lax.rem(index, per_row)
        chosen = bias[:, :tile]
        for other in range(1, per_row):
            chosen = jnp.where(part == other, bias[:, other * tile : (other + 1) * tile], chosen)
        pre = nn(low_ref[...], flat(wi[:, :, :, lanes])) + chosen
        phi = 0.5 * (1.0 + lax.erf(pre * 0.7071067811865476))
        dens = jnp.exp(-0.5 * pre * pre) * 0.3989422804014327
        gp_ref[:, lanes] = (phi + pre * dens).astype(BF16)
        active = (pre * phi).astype(BF16)
        active_ref[:, lanes] = active
        wide_ref[lanes, :] = active.T
        return carry

    lax.fori_loop(0, hidden // tile, step, 0)
    load(held[0], kept[0], store_sems.at[0])
    export_halves(pos_g, wide_ref, exports)
    for index in (1, 2):
        load(held[index], kept[index], store_sems.at[index])
    for index in range(3):
        wait_full(held[index], store_sems.at[index])


def inner_forward(pos_w, pos_g, h, vec, bufs):
    tokens, width = h.shape
    hidden = bufs[0].shape[2] * 4
    export = shape((2, 2, 2, ZS, hidden // BLOCKS // 4, tokens), BF16)
    kept = (shape((tokens, hidden), BF16), export, export)
    return pl.pallas_call(
        functools.partial(inner_kernel, 384),
        out_shape=(shape((tokens, hidden), BF16),) + kept,
        in_specs=[SMEM, SMEM, VMEM, VMEM] + [ANY] * 2,
        out_specs=[VMEM] + [HBM] * 3,
        scratch_shapes=[
            wide_matrix(width, hidden),
            pltpu.VMEM((tokens, width), BF16),
            pltpu.VMEM((hidden, tokens), BF16),
        ]
        + [pltpu.VMEM(each.shape, each.dtype) for each in kept]
        + [pltpu.SemaphoreType.DMA, pltpu.SemaphoreType.DMA((3,))],
        compiler_params=params(VMEM_MB),
        cost_estimate=cost(),
        name="inner_forward",
    )(pos_w, pos_g, h, vec, *bufs)


def outer_kernel(last, *refs):
    pos_w, h_ref, active_ref, vec_ref = refs[:4]
    grad_ref = refs[4] if last else None
    refs = refs[4 + last :]
    bufs = refs[:2]
    outs, wu, acc_ref, sem = refs[2:-3], refs[-3], refs[-2], refs[-1]
    fetch_rows(pos_w, bufs, wu, sem)
    acc_ref[...] = h_ref[...] + row_of(vec_ref, UB)
    wait_full(wu, sem)
    tile = active_ref.shape[1] // ZS
    for z in range(ZS):
        acc_ref[...] += nn(active_ref[:, pl.ds(z * tile, tile)], flat(wu[z]))
    normed, inverse = normalize(acc_ref[...])
    result = normed * row_of(vec_ref, FG) + row_of(vec_ref, FS)
    outs[0][...] = result
    outs[1][...] = result.astype(BF16)
    if last:
        head_back(
            grad_ref[...].astype(F32), normed, inverse, row_of(vec_ref, FG), outs[2], outs[3], outs[4]
        )
    else:
        outs[2][...] = normed
        outs[3][...] = jnp.broadcast_to(inverse, outs[3].shape)


def outer_forward(pos_w, h, active, vec, bufs, grad):
    tokens, width = h.shape
    hidden = active.shape[1]
    last = grad is not None
    outs = (shape((tokens, width), F32), shape((tokens, width), BF16))
    if last:
        outs += head_shapes(tokens, width)
    else:
        outs += (shape((tokens, width), F32), shape((tokens, 128), F32))
    return pl.pallas_call(
        functools.partial(outer_kernel, int(last)),
        out_shape=outs,
        in_specs=[SMEM] + [VMEM] * (3 + last) + [ANY] * 2,
        out_specs=[VMEM] * len(outs),
        scratch_shapes=[
            tall_matrix(hidden, width),
            pltpu.VMEM((tokens, width), F32),
            pltpu.SemaphoreType.DMA,
        ],
        compiler_params=params(VMEM_MB),
        cost_estimate=cost(),
        name="outer_forward",
    )(pos_w, h, active, vec, *((grad,) if last else ()), *bufs)


def chain_kernel(tile, waits, *refs):
    pos_w, dyl_ref, dy_ref = refs[:3]
    sources, vec_ref = refs[3:6], refs[6]
    inner_bufs, outer_bufs, attn_bufs = refs[7:9], refs[9:11], refs[11:13]
    refs = refs[13 + waits :]
    pack_ref, da_ref, do_ref, sums_ref = refs[:4]
    wi, wu, wo, acc_ref = refs[4:8]
    held = refs[8:11]
    gp_ref, n1_ref, c1_ref = held
    sems, load_sems = refs[11:]
    width, hidden = dy_ref.shape[1], wi.shape[3]
    for index in range(3):
        load(sources[index], held[index], load_sems.at[index])
    du_ref = pack_ref.at[:, pl.ds(0, hidden)]
    dal_ref = pack_ref.at[:, pl.ds(hidden, width)]
    fetch_rows(pos_w, outer_bufs, wu, sems.at[0])
    fetch_columns(pos_w, inner_bufs, wi, sems.at[1])
    fetch_member(pos_w, attn_bufs, 3, wo, sems.at[2])
    sums_ref[...] = jnp.zeros_like(sums_ref)
    acc_ref[...] = dy_ref[...]
    wait_full(gp_ref, load_sems.at[0])
    wait_full(wu, sems.at[0])
    wait_full(wi, sems.at[1])
    per_row = width // tile

    for index in range(hidden // tile):
        lane = index * tile
        rows = wu[index * ZS * tile // hidden, pl.ds(lane % (hidden // ZS) * BLOCKS // hidden, tile * BLOCKS // hidden)]
        part = nt(dyl_ref[...], flat(rows))
        part = (part * gp_ref[:, pl.ds(lane, tile)].astype(F32)).astype(BF16)
        du_ref[:, pl.ds(lane, tile)] = part
        acc_ref[...] += nt(part, flat(wi[:, :, :, pl.ds(lane, tile)]))
        sums_ref[
            pl.ds(IB + index // per_row, 1), pl.ds(index % per_row * tile, tile)
        ] = colsum(part.astype(F32))

    grad = acc_ref[...]
    wait_full(n1_ref, load_sems.at[1])
    wait_full(c1_ref, load_sems.at[2])
    normed = n1_ref[...]
    sums_ref[pl.ds(AG, 1), :] = colsum(grad * normed)
    sums_ref[pl.ds(AS, 1), :] = colsum(grad)
    back = norm_back(normed, c1_ref[:, :1], grad * row_of(vec_ref, AG))
    da_ref[...] = back
    low = back.astype(BF16)
    dal_ref[...] = low
    sums_ref[pl.ds(OB, 1), :] = colsum(low.astype(F32))
    wait_full(wo, sems.at[2])
    do_ref[...] = nt(low, flat(wo[...])).astype(BF16)


def chain_backward(pos_w, dyl, dy, gp, n1, c1, vec, inner_bufs, outer_bufs, attn_bufs, after=()):
    tokens, width = n1.shape
    hidden = gp.shape[1]
    return pl.pallas_call(
        functools.partial(chain_kernel, 384, len(after)),
        out_shape=(
            shape((tokens, hidden + width), BF16),
            shape((tokens, width), F32),
            shape((tokens, width), BF16),
            shape((16, width), F32),
        ),
        in_specs=[SMEM] + [VMEM] * 2 + [HBM] * 3 + [VMEM] + [ANY] * (6 + len(after)),
        out_specs=[VMEM] * 4,
        scratch_shapes=[
            wide_matrix(width, hidden),
            tall_matrix(hidden, width),
            square(width),
            pltpu.VMEM((tokens, width), F32),
        ]
        + [pltpu.VMEM(each.shape, each.dtype) for each in (gp, n1, c1)]
        + [pltpu.SemaphoreType.DMA((3,)), pltpu.SemaphoreType.DMA((3,))],
        compiler_params=params(VMEM_MB),
        cost_estimate=cost(),
        name="chain_backward",
    )(pos_w, dyl, dy, gp, n1, c1, vec, *inner_bufs, *outer_bufs, *attn_bufs, *after)


def attn_back_kernel(waits, *refs):
    sources, do_ref = refs[:4], refs[4]
    refs = refs[waits:]
    pack_ref, sum_ref, wide_ref = refs[5], refs[6], refs[7]
    held, sems, pair_sems = refs[8:12], refs[12], refs[13]
    q_ref, kt_ref, v_ref, p_ref = held
    tokens, width = q_ref.shape
    for index in range(3):
        load(sources[index], held[index], sems.at[index])
    for index in range(width // 128):
        both = pl.ds(index * 2, 2)
        load(sources[3].at[both], p_ref.at[both], pair_sems.at[index])
    for index in range(3):
        wait_full(held[index], sems.at[index])

    def pair(index, carry):
        lane = pl.multiple_of(index * 128, 128)
        values = v_ref[:, pl.ds(lane, 128)]
        queries = q_ref[:, pl.ds(lane, 128)]
        grads = do_ref[:, pl.ds(lane, 128)]
        first = lax.broadcasted_iota(jnp.int32, grads.shape, 1) < HD
        keys_back, values_back = [], []
        wait_full(p_ref.at[pl.ds(index * 2, 2)], pair_sems.at[index])
        for which in range(2):
            mine = jnp.where(first if which == 0 else ~first, grads, jnp.zeros_like(grads))
            probs_low = p_ref[index * 2 + which]
            probs = probs_low.astype(F32)
            weighted = probs * nt(values, mine)
            back = weighted - probs * jnp.sum(weighted, axis=0, keepdims=True)
            low = back.astype(BF16)
            keys_back.append(nn(low, queries))
            values_back.append(nn(probs_low, grads))
            row = pl.multiple_of(index * 128 + which * HD, HD)
            wide_ref[pl.ds(row, HD), :] = nn(kt_ref[pl.ds(row, HD), :], low)
        split = lax.broadcasted_iota(jnp.int32, keys_back[0].shape, 1) < HD
        for at, back in ((1, keys_back), (3, values_back)):
            low = jnp.where(split, back[0], back[1]).astype(BF16)
            pack_ref[at, :, pl.ds(lane, 128)] = low[:tokens]
            pack_ref[at + 1, :, pl.ds(lane, 128)] = low[tokens:]
        return carry

    lax.fori_loop(0, width // 128, pair, 0)
    low = (wide_ref[...].T * HD ** (-0.5)).astype(BF16)
    pack_ref[0] = low
    sum_ref[...] = jnp.broadcast_to(colsum(low.astype(F32)), sum_ref.shape)


def attn_backward(q, kt, v, p, do, after=()):
    tokens, width = q.shape
    return pl.pallas_call(
        functools.partial(attn_back_kernel, len(after)),
        out_shape=(
            shape((5, tokens, width), BF16),
            shape((8, width), F32),
        ),
        in_specs=[HBM] * 4 + [VMEM] + [ANY] * len(after),
        out_specs=[VMEM] * 2,
        scratch_shapes=[pltpu.VMEM((width, tokens), F32)]
        + [pltpu.VMEM(each.shape, each.dtype) for each in (q, kt, v, p)]
        + [pltpu.SemaphoreType.DMA((3,)), pltpu.SemaphoreType.DMA((width // 128,))],
        compiler_params=params(VMEM_MB),
        cost_estimate=cost(),
        name="attn_backward",
    )(q, kt, v, p, do, *after)


def input_kernel(first, *refs):
    pos_w, da_ref, pack_ref, got_ref = refs[:4]
    bufs = refs[4:6]
    refs = refs[6:]
    if not first:
        n2_ref, c2_ref, vec_ref = refs[:3]
        refs = refs[3:]
    total_ref, sum_ref = refs[:2]
    heads = refs[2:-4]
    wq, wk, wv, sems = refs[-4:]
    tokens, width = da_ref.shape
    for member, full in enumerate((wq, wk, wv)):
        fetch_member(pos_w, bufs, member, full, sems.at[member])
    for at, (mine, theirs) in enumerate(((1, 2), (2, 1), (3, 4), (4, 3))):
        total_ref[at] = (pack_ref[mine].astype(F32) + got_ref[theirs].astype(F32)).astype(BF16)
    sum_ref[...] = jnp.broadcast_to(colsum(total_ref[2].astype(F32)), sum_ref.shape)
    wait_full(wq, sems.at[0])
    dx = da_ref[...] + nt(pack_ref[0], flat(wq[...]))
    wait_full(wk, sems.at[1])
    dx += nt(total_ref[0], flat(wk[...]))
    wait_full(wv, sems.at[2])
    dx += nt(total_ref[2], flat(wv[...]))
    if first:
        heads[0][...] = dx.astype(BF16)
    else:
        head_back(dx, n2_ref[...], c2_ref[:, :1], row_of(vec_ref, FG), *heads)


def input_backward(pos_w, da, pack, got, bufs, below):
    tokens, width = da.shape
    first = below is None
    outs = (shape((4, tokens, width), BF16), shape((8, width), F32))
    outs += (shape((tokens, width), BF16),) if first else head_shapes(tokens, width)
    return pl.pallas_call(
        functools.partial(input_kernel, first),
        out_shape=outs,
        in_specs=[SMEM] + [VMEM] * 3 + [ANY] * 2 + ([] if first else [VMEM] * 3),
        out_specs=[VMEM] * len(outs),
        scratch_shapes=[square(width)] * 3 + [pltpu.SemaphoreType.DMA((3,))],
        compiler_params=params(VMEM_MB),
        cost_estimate=cost(),
        name="input_backward",
    )(pos_w, da, pack, got, *bufs, *(() if first else below))


def place(outs, part, dy, value):
    a_keep, a_send, b_keep, b_send = outs
    if part == 0:
        a_keep[dy] = value[0]
        a_send[dy] = value[1]
    else:
        (b_send if dy else b_keep)[...] = value


def grad_shapes(rows, width):
    return (shape((2, ZS, rows, width), BF16),) * 4


def inner_grad_kernel(pos_ref, ta_ref, tb_ref, da_ref, db_ref, *refs):
    outs, left, sems = refs[:4], refs[4], refs[5]
    _, _, rows, width = outs[0].shape
    tokens = ta_ref.shape[-1]
    for side, source in enumerate((ta_ref, tb_ref)):
        load(source.at[2], left.at[side], sems.at[side])
    for side in range(2):
        wait_full(left.at[side], sems.at[side])
    left_a = left[0].reshape(2 * ZS * rows, tokens)
    left_b = left[1].reshape(2 * ZS * rows, tokens)
    for dy in range(2):
        for part in range(2):
            lanes = pl.ds(pl.multiple_of((half_at(pos_ref, dy) * 2 + part) * width, 128), width)
            value = nn(left_a, da_ref[:, lanes]) + nn(left_b, db_ref[:, lanes])
            place(outs, part, dy, value.astype(BF16).reshape(2, ZS, rows, width))


def inner_grad(pos_g, ta, tb, da, db):
    rows = ta.shape[3]
    return pl.pallas_call(
        inner_grad_kernel,
        out_shape=grad_shapes(rows, rows * BLOCKS),
        in_specs=[SMEM] + [HBM] * 2 + [VMEM] * 2,
        out_specs=[VMEM] * 4,
        scratch_shapes=[pltpu.VMEM((2,) + ta.shape[1:], BF16), pltpu.SemaphoreType.DMA((2,))],
        compiler_params=params(VMEM_MB),
        cost_estimate=cost(),
        name="inner_grad",
    )(pos_g, ta, tb, da, db)


def outer_grad_kernel(ta_ref, tb_ref, da_ref, db_ref, *refs):
    outs, left, sems = refs[:4], refs[4], refs[5]
    _, _, rows, width = outs[0].shape
    tokens = ta_ref.shape[-1]
    for side, source in enumerate((ta_ref, tb_ref)):
        load(source, left.at[side], sems.at[side])
    for side in range(2):
        wait_full(left.at[side], sems.at[side])
    for dy in range(2):
        for part in range(2):
            values = []
            for dx in range(2):
                left_a = left[0, dx, dy, part].reshape(ZS * rows, tokens)
                left_b = left[1, dx, dy, part].reshape(ZS * rows, tokens)
                value = nn(left_a, da_ref[...]) + nn(left_b, db_ref[...])
                values.append(value.astype(BF16).reshape(ZS, rows, width))
            place(outs, part, dy, jnp.stack(values))


def outer_grad(ta, tb, da, db):
    rows, width = ta.shape[4], da.shape[1]
    return pl.pallas_call(
        outer_grad_kernel,
        out_shape=grad_shapes(rows, width),
        in_specs=[HBM] * 2 + [VMEM] * 2,
        out_specs=[VMEM] * 4,
        scratch_shapes=[pltpu.VMEM((2,) + ta.shape, BF16), pltpu.SemaphoreType.DMA((2,))],
        compiler_params=params(VMEM_MB),
        cost_estimate=cost(),
        name="outer_grad",
    )(ta, tb, da, db)


def attn_grad_kernel(pos_ref, xa_ref, xb_ref, qa_ref, qb_ref, total_ref, da_ref, db_ref, *refs):
    outs, left, sems = refs[:4], refs[4], refs[5]
    for side, source in enumerate((xa_ref, xb_ref)):
        load(source.at[pl.ds(0, 2)], left.at[side], sems.at[side])
    for side in range(2):
        wait_full(left.at[side], sems.at[side])
    _, _, rows, width = outs[0].shape
    half = width // 2
    tokens = xa_ref.shape[-1]
    height = 2 * ZS * rows
    x_a = left[0, 0].reshape(height, tokens)
    x_b = left[1, 0].reshape(height, tokens)
    o_a = left[0, 1].reshape(height, tokens)
    o_b = left[1, 1].reshape(height, tokens)
    last = da_ref.shape[1] - width
    for dy in range(2):
        start = half_at(pos_ref, dy) * half
        lanes = pl.ds(pl.multiple_of(start, 128), half)
        tail = pl.ds(pl.multiple_of(start + last, 128), half)
        members = (
            nn(x_a, qa_ref[0, :, lanes]) + nn(x_b, qb_ref[0, :, lanes]),
            nn(x_a, total_ref[0, :, lanes]) + nn(x_b, total_ref[1, :, lanes]),
            nn(x_a, total_ref[2, :, lanes]) + nn(x_b, total_ref[3, :, lanes]),
            nn(o_a, da_ref[:, tail]) + nn(o_b, db_ref[:, tail]),
        )
        for part in range(2):
            value = jnp.concatenate(members[part * 2 : part * 2 + 2], axis=1)
            place(outs, part, dy, value.astype(BF16).reshape(2, ZS, rows, width))


def attn_grad(pos_g, xa, xb, qa, qb, total, da, db):
    rows = xa.shape[3]
    return pl.pallas_call(
        attn_grad_kernel,
        out_shape=grad_shapes(rows, rows * BLOCKS),
        in_specs=[SMEM] + [HBM] * 2 + [VMEM] * 5,
        out_specs=[VMEM] * 4,
        scratch_shapes=[pltpu.VMEM((2, 2) + xa.shape[1:], BF16), pltpu.SemaphoreType.DMA((2,))],
        compiler_params=params(VMEM_MB),
        cost_estimate=cost(),
        name="attn_grad",
    )(pos_g, xa, xb, qa, qb, total, da, db)


def copy_kernel(plan, inputs, pos_ref, *refs):
    ins, outs, sems = refs[:inputs], refs[inputs:-1], refs[-1]
    copies = []
    for index, (out, to, source, at, size, by_z) in enumerate(plan):
        if by_z:
            z = pos_ref[0]
            to = flip(lax.div(z, 2), to // 2) * 2 + flip(lax.rem(z, 2), to % 2)
        copies.append(
            pltpu.make_async_copy(
                ins[source].at[pl.ds(at, size)], outs[out].at[pl.ds(to, size)], sems.at[index]
            )
        )
    for each in copies:
        each.start()
    for each in copies:
        each.wait()


def copy_blocks(pos, plan, inputs, sizes, name):
    piece = inputs[0].shape[1:]
    return pl.pallas_call(
        functools.partial(copy_kernel, plan, len(inputs)),
        out_shape=tuple(shape((size,) + piece, BF16) for size in sizes),
        in_specs=[SMEM] + [ANY] * len(inputs),
        out_specs=[VMEM] * len(sizes),
        scratch_shapes=[pltpu.SemaphoreType.DMA((len(plan),))],
        compiler_params=params(VMEM_MB),
        cost_estimate=cost(),
        name=name,
    )(pos, *inputs)


def pack_kernel(group, pos_ref, *refs):
    four, inner, outer = refs[:4], refs[4], refs[5]
    out, sem = refs[6], refs[7]
    rows, width = out.shape[1:]
    half = width // 2
    y = pos_ref[3]
    for j, chunk in enumerate(group):
        layer, kind = chunk // 3, chunk % 3
        for part in range(2):
            to = out.at[2 * j + part]
            if kind == 0:
                for side in range(2):
                    pltpu.make_async_copy(
                        four[2 * part + side].at[layer, :, pl.ds(pl.multiple_of(y * half, 128), half)],
                        to.at[:, pl.ds(side * half, half)],
                        sem,
                    ).start()
            elif kind == 1:
                lane = pl.multiple_of((2 * y + part) * width, 128)
                pltpu.make_async_copy(inner.at[layer, :, pl.ds(lane, width)], to, sem).start()
            else:
                row = pl.multiple_of((2 * y + part) * rows, 16)
                pltpu.make_async_copy(outer.at[layer, pl.ds(row, rows)], to, sem).start()
    wait_full(out, sem)


def pack_pieces(group, pos, weights):
    _, rows, width = weights[0].shape
    return pl.pallas_call(
        functools.partial(pack_kernel, group),
        out_shape=shape((2 * len(group), rows, width), BF16),
        in_specs=[SMEM] + [HBM] * 6,
        out_specs=VMEM,
        scratch_shapes=[pltpu.SemaphoreType.DMA],
        compiler_params=params(VMEM_MB),
        cost_estimate=cost(),
        name="pack",
    )(pos, *weights)


def table_kernel(at_ref, *refs):
    vectors, out = refs[:-1], refs[-1]
    width = out.shape[2]
    for index, vector in enumerate(vectors):
        size = vector.shape[1]
        start = at_ref[0] * size
        for piece in range(max(1, out.shape[1] - IB if index == IB else 1)):
            lanes = lax.broadcasted_iota(jnp.int32, (size, width), 1) + piece * width
            spot = lax.broadcasted_iota(jnp.int32, (size, width), 0) + start
            chosen = (lanes == spot).astype(F32).astype(BF16)
            out[:, index + piece, :] = nn(vector[...], chosen)


def vector_table(at, vectors, width):
    layers, last = vectors[-1].shape[0], vectors[-1].shape[1]
    rows = IB + last // vectors[0].shape[1]
    return pl.pallas_call(
        table_kernel,
        out_shape=shape((layers, rows, width), F32),
        in_specs=[SMEM] + [VMEM] * len(vectors),
        out_specs=VMEM,
        compiler_params=params(VMEM_MB),
        cost_estimate=cost(),
        name="vector_table",
    )(at, *vectors)


def finish_kernel(kind, offsets, pos_ref, *refs):
    layers = len(offsets)
    owns, gots = refs[: 2 * layers], refs[2 * layers : 4 * layers]
    outs, buf, sems = refs[4 * layers : -2], refs[-2], refs[-1]
    rows, width = buf.shape[2:]
    half = width // 2
    y = pos_ref[3]
    copies = []
    for layer in range(layers):
        for part, at in enumerate(offsets[layer]):
            copies.append(
                pltpu.make_async_copy(
                    gots[2 * layer + part].at[pl.ds(at, 2 - part)],
                    buf.at[layer, pl.ds(2 * part, 2 - part)],
                    sems.at[2 * layer + part],
                )
            )
            copies[-1].start()
    for each in copies:
        each.wait()
    for side in range(2):
        yy = y if side == 0 else 1 - y
        for layer in range(layers):
            for part in range(2):
                if part == 0:
                    value = owns[2 * layer][side].astype(BF16).astype(F32)
                    value = value + buf[layer, 1 - side].astype(F32)
                else:
                    value = (buf[layer, 2] if side else owns[2 * layer + 1][0].astype(BF16)).astype(F32)
                if kind == 0:
                    lanes = pl.ds(pl.multiple_of(yy * half, 128), half)
                    for member in range(2):
                        outs[2 * part + member][layer, :, lanes] = value[
                            :, member * half : (member + 1) * half
                        ]
                elif kind == 1:
                    lane = pl.multiple_of((2 * yy + part) * width, 128)
                    outs[0][layer, :, pl.ds(lane, width)] = value
                else:
                    row = pl.multiple_of((2 * yy + part) * rows, 16)
                    outs[0][layer, pl.ds(row, rows), :] = value


def finish(kind, pos, results):
    layers = len(results)
    _, rows, width = results[0][0][0].shape
    outs = {
        0: (shape((layers, rows, width), F32),) * 4,
        1: (shape((layers, rows, 4 * width), F32),),
        2: (shape((layers, 4 * rows, width), F32),),
    }[kind]
    return pl.pallas_call(
        functools.partial(finish_kernel, kind, tuple((a[2], b[2]) for a, b in results)),
        out_shape=outs,
        in_specs=[SMEM] + [VMEM] * (2 * layers) + [ANY] * (2 * layers),
        out_specs=[VMEM] * len(outs),
        scratch_shapes=[
            pltpu.VMEM((layers, 3, rows, width), BF16),
            pltpu.SemaphoreType.DMA((2 * layers,)),
        ],
        compiler_params=params(VMEM_MB),
        cost_estimate=cost(),
        name="finish",
    )(pos, *[part[0] for value in results for part in value], *[part[1] for value in results for part in value])


def sum_kernel(config, *refs):
    fresh, first, second, third_a, third_b, fourth_a, fourth_b, small, waits = config
    refs = list(refs)

    def take(count):
        out = refs[:count]
        del refs[:count]
        return out

    sends = take(2) if fresh else None
    got_x = take(1)[0] if first or second else None
    got_y = take(1)[0] if first else None
    keeps = take(2) if first else None
    rest = take(1)[0] if second else None
    got_z1 = take(1)[0] if third_a or third_b else None
    pair_a = take(1)[0] if third_a else None
    pair_b = take(1)[0] if third_b else None
    got_z2 = take(1)[0] if fourth_a or fourth_b else None
    last_a = take(1)[0] if fourth_a else None
    last_b = take(1)[0] if fourth_b else None
    tables = take(2 if small == 1 else 1) if small else None
    take(waits)
    to_x = take(1)[0] if fresh or first else None
    to_y = take(1)[0] if fresh or fourth_a or fourth_b else None
    to_z1 = take(1)[0] if first or second else None
    to_z2 = take(1)[0] if third_a or third_b else None
    at = 0
    if fresh:
        for out, send in ((to_x, sends[0]), (to_y, sends[1])):
            for half in range(2):
                out[half * ZS : (half + 1) * ZS] = send[half]
        at = 2 * ZS
    if first:
        b_rest, hold = take(2)
        for k in range(ZS):
            for half in range(2):
                value = keeps[0][half, k].astype(F32) + got_x[half * ZS + k].astype(F32)
                (to_z1 if k % 2 else hold)[k // 2 * 2 + half] = value.astype(BF16)
        b_rest[...] = (keeps[1][0].astype(F32) + got_y[:ZS].astype(F32)).astype(BF16)
        value = keeps[1][1].astype(F32) + got_y[ZS : 2 * ZS].astype(F32)
        to_x[at : at + ZS] = value.astype(BF16)
    if second:
        (hold,) = take(1)
        begin = 2 * ZS if first else 0
        for k in range(ZS):
            value = (rest[k].astype(F32) + got_x[begin + k].astype(F32)).astype(BF16)
            if k % 2:
                to_z1[4 * first + k // 2] = value
            else:
                hold[k // 2] = value
    for here, pair, begin, size, to in (
        (third_a, pair_a, 0, 2, 0),
        (third_b, pair_b, 4 * third_a, 1, 2 * third_a),
    ):
        if here:
            (hold,) = take(1)
            for index in range(size):
                hold[index] = pair[index].astype(F32) + got_z1[begin + index].astype(F32)
                value = pair[size + index].astype(F32) + got_z1[begin + size + index].astype(F32)
                to_z2[to + index] = value.astype(BF16)
    for here, last, begin, size in ((fourth_a, last_a, 0, 2), (fourth_b, last_b, 2 * fourth_a, 1)):
        if here:
            (total,) = take(1)
            for index in range(size):
                value = last[index] + got_z2[begin + index].astype(F32)
                total[index] = value
                to_y[at + begin + index] = value.astype(BF16)
    if small:
        come = (None, None, got_x, got_z1, got_z2)[small]
        come = tables[1][...] if small == 1 else come[come.shape[0] - 1]
        value = tables[0][...] + come.astype(F32)
        refs[0][...] = value
        to = (None, to_x, to_z1, to_z2, to_y)[small]
        to[to.shape[0] - 1] = value.astype(BF16)


def sum_round(fresh, past, small, after):
    names = ("first", "second", "third_a", "third_b", "fourth_a", "fourth_b")
    stage, table = small
    config = (fresh is not None,) + tuple(name in past for name in names) + (stage, len(after))
    is_fresh, first, second, third_a, third_b, fourth_a, fourth_b = (int(value) for value in config[:7])
    sample = fresh[1] if fresh is not None else past[[name for name in names if name in past][0]][0]
    rows, width = sample.shape[-2:]
    inputs = []
    if is_fresh:
        inputs += [fresh[1], fresh[3]]
    if first or second:
        inputs += [past["got_x"]]
    if first:
        inputs += [past["got_y"]] + list(past["first"])
    if second:
        inputs += list(past["second"])
    if third_a or third_b:
        inputs += [past["got_z1"]]
    for name in ("third_a", "third_b"):
        inputs += list(past.get(name, ()))
    if fourth_a or fourth_b:
        inputs += [past["got_z2"]]
    for name in ("fourth_a", "fourth_b"):
        inputs += list(past.get(name, ()))
    if table is not None:
        inputs += list(table)
    begin = 2 * ZS * is_fresh
    sizes = (
        (is_fresh or first, begin + ZS * first + (stage == 1)),
        (is_fresh or fourth_a or fourth_b, begin + 2 * fourth_a + fourth_b + (stage == 4)),
        (first or second, 4 * first + 2 * second + (stage == 2)),
        (third_a or third_b, 2 * third_a + third_b + (stage == 3)),
    )
    outputs = [shape((size, rows, width), BF16) for there, size in sizes if there]
    if first:
        outputs += [shape((ZS, rows, width), BF16), shape((4, rows, width), BF16)]
    if second:
        outputs += [shape((2, rows, width), BF16)]
    if third_a:
        outputs += [shape((2, rows, width), F32)]
    if third_b:
        outputs += [shape((1, rows, width), F32)]
    if fourth_a:
        outputs += [shape((2, rows, width), F32)]
    if fourth_b:
        outputs += [shape((1, rows, width), F32)]
    if stage:
        outputs += [shape(table[0].shape, F32)]
    outs = list(
        pl.pallas_call(
            functools.partial(sum_kernel, config),
            out_shape=tuple(outputs),
            in_specs=[VMEM] * len(inputs) + [ANY] * len(after),
            out_specs=[VMEM] * len(outputs),
            compiler_params=params(VMEM_MB),
            cost_estimate=cost(),
            name="sum_round",
        )(*inputs, *after)
    )

    def take(wanted, count):
        if not wanted:
            return None
        out = tuple(outs[:count])
        del outs[:count]
        return out

    sends = tuple(take(there, 1) for there, _ in sizes)
    b_rest = take(first, 1)
    holds = (take(first, 1), take(second, 1))
    lasts = (take(third_a, 1), take(third_b, 1))
    totals = (take(fourth_a, 1), take(fourth_b, 1))
    return sends, begin, b_rest, holds, lasts, totals, take(stage > 0, 1)


def collect_kernel(*refs):
    out = refs[-1]
    for layer in range(out.shape[0]):
        query_ref, value_ref, head_ref, chain_ref = refs[4 * layer : 4 * layer + 4]
        out[layer] = chain_ref[...]
        out[layer, pl.ds(QB, 1), :] = query_ref[:1]
        out[layer, pl.ds(VB, 1), :] = value_ref[:1]
        for at, index in enumerate((FG, FS, UB)):
            out[layer, pl.ds(index, 1), :] = head_ref[at : at + 1]


def collect(vectors, rows):
    flat = [value for layer in vectors for value in layer]
    width = flat[0].shape[1]
    return pl.pallas_call(
        collect_kernel,
        out_shape=shape((len(vectors), rows, width), F32),
        in_specs=[VMEM] * len(flat),
        out_specs=VMEM,
        compiler_params=params(VMEM_MB),
        cost_estimate=cost(),
        name="collect",
    )(*flat)


def vectors_kernel(last, at_ref, table_ref, got_ref, *outs):
    layers, width = outs[0].shape[0], table_ref.shape[1]
    at = at_ref[0]
    for index, out in enumerate(outs):
        size = out.shape[1]
        start = at * size
        shift = lax.rem(width - lax.rem(start, width), width)
        for layer in range(layers):
            spot = pl.ds(layer * 16 + index + lax.div(start, width), 1)
            value = table_ref[spot, :]
            if last is not None:
                value = value.astype(BF16).astype(F32) + got_ref[spot, :]
            value = jnp.broadcast_to(value, (8, width))
            out[pl.ds(layer, 1), :] = pltpu.roll(value, shift, 1)[:1, :size]


def own_vectors(at, table, got, layers, size, wide):
    sizes = [size] * IB + [wide]
    last = None if got is None else 0
    return pl.pallas_call(
        functools.partial(vectors_kernel, last),
        out_shape=tuple(shape((layers, each), F32) for each in sizes),
        in_specs=[SMEM, VMEM, VMEM],
        out_specs=[VMEM] * len(sizes),
        compiler_params=params(VMEM_MB),
        cost_estimate=cost(),
        name="own_vectors",
    )(at, table, table if got is None else got)


def fence(values):
    return lax.optimization_barrier(values)


def build(mesh):
    count = mesh.shape["dp"]

    def flat(dp, seq):
        return dp * 2 + seq

    def pairs(source_of):
        out = []
        for dp in range(count):
            for seq in range(2):
                out.append((flat(*source_of(dp, seq)), flat(dp, seq)))
        return out

    swap_pairs = pairs(lambda dp, seq: (dp // 2 * 2 + seq, dp % 2))
    core_pairs = pairs(lambda dp, seq: (dp ^ 1, seq))
    x_pairs = pairs(lambda dp, seq: (dp ^ 2, seq))
    y_pairs = pairs(lambda dp, seq: (dp, 1 - seq))
    z_pairs = [pairs(lambda dp, seq, k=k: ((dp // 4 ^ k) * 4 + dp % 4, seq)) for k in (1, 2)]

    def move(value, perm):
        return lax.ppermute(value, AXES, perm)

    return dict(
        count=count,
        swap=swap_pairs,
        core=core_pairs,
        x=x_pairs,
        y=y_pairs,
        z1=z_pairs[0],
        z2=z_pairs[1],
        move=move,
    )


def body(
    net,
    tokens,
    segment_ids,
    padding,
    query_weight,
    key_weight,
    value_weight,
    output_weight,
    query_bias,
    value_bias,
    output_bias,
    attn_gain,
    attn_shift,
    inner_weight,
    inner_bias,
    outer_weight,
    outer_bias,
    ffn_gain,
    ffn_shift,
    upstream,
):
    layers, small, width = query_weight.shape
    hidden = inner_weight.shape[2]
    count = net["count"]
    move = net["move"]
    staged = count == BLOCKS and small == 16 * layers
    dp = lax.axis_index("dp").astype(jnp.int32)
    y = lax.axis_index("seq").astype(jnp.int32)
    core = lax.rem(dp, 2)
    if staged:
        pos_g = jnp.stack([lax.div(dp, 4), lax.rem(lax.div(dp, 2), 2), core, y])
        pos_w = pos_g
    else:
        zero = jnp.zeros((), jnp.int32)
        pos_g = jnp.stack([zero, zero, core, zero])
        pos_w = jnp.stack([zero, zero, zero, zero])

    labels = jnp.where(padding == 1, segment_ids, -1)
    small_own = move(jnp.concatenate([segment_ids, labels]), net["swap"])
    token_low = move(tokens[0], net["swap"])

    vector_args = [query_bias, value_bias, output_bias, attn_gain, attn_shift, outer_bias]
    vector_args += [ffn_gain, ffn_shift, inner_bias]
    table = vector_table(dp[None], vector_args, width)
    if staged:
        table = table + move(table, net["x"])
    else:
        table = lax.psum(table, "dp")

    raw = (query_weight, key_weight, value_weight, output_weight, inner_weight, outer_weight)
    chunks = []
    for layer in range(layers):
        four = (query_weight[layer], key_weight[layer], value_weight[layer], output_weight[layer])
        if not staged:
            full = [lax.all_gather(value, "dp", axis=0, tiled=True) for value in four]
            inner = lax.all_gather(inner_weight[layer], "dp", axis=0, tiled=True)
            outer = lax.all_gather(outer_weight[layer], "dp", axis=0, tiled=True)
            rows = width // BLOCKS

            def cut(value, dy, dx, dc):
                value = value.reshape(ZS, 2, 2, rows, 2, -1)
                return value[:, dx, dc, :, dy, :]

            lists = [[[], []], [[], []], [[], []]]
            for dc in range(2):
                for part, dy, dx in UNITS:
                    lists[0][dc].append(
                        jnp.concatenate([cut(value, dy, dx, dc) for value in full[part * 2 : part * 2 + 2]], axis=2)
                    )
                    lists[1][dc].append(cut(inner, dy, dx, dc)[..., part * width : (part + 1) * width])
                    lists[2][dc].append(
                        outer.reshape(ZS, 2, 2, 2, 2, hidden // BLOCKS // 4, width)[:, dx, dc, dy, part]
                    )
            chunks.extend(tuple(jnp.concatenate(side) for side in value) for value in lists)

    total_chunks = 3 * layers
    groups = []
    if staged:
        edges = [0, 1, 2, 3] + list(range(4, total_chunks, 2)) + [total_chunks]
        groups = [range(low, high) for low, high in zip(edges[:-1], edges[1:])]
    where_of = {i: (g, i - group[0]) for g, group in enumerate(groups) for i in group}
    stage_z = [None] * len(groups)

    def start_z2(g):
        own = pack_pieces(groups[g], pos_g, raw)
        stage_z[g] = (own, move(own, net["z2"]))

    def start_z1(g):
        own, come = stage_z[g]
        size = own.shape[0]
        both = copy_blocks(
            pos_g,
            [(0, 0, 0, 0, size, False), (0, size, 1, 0, size, False)],
            (own, come),
            [2 * size],
            "gather_z",
        )[0]
        stage_z[g] = (both, move(both, net["z1"]))

    if staged:
        start_z2(0)
        stage_z[0], raw, table, small_own, token_low = fence(
            (stage_z[0], raw, table, small_own, token_low)
        )
        start_z1(0)
        start_z2(1)
        table = table + move(table, net["core"])
    small_other = move(small_own, net["core"])
    token_other = move(token_low, net["core"])
    if staged:
        stage_z[:2], raw, table, small_own, small_other, token_low, token_other, upstream = fence(
            (stage_z[:2], raw, table, small_own, small_other, token_low, token_other, upstream)
        )
    seg = small_own[0:1]
    lab = jnp.concatenate([small_own[1], small_other[1]])[:, None]
    current = token_low.astype(F32)
    other = token_other
    kept = [None] * layers
    todo = []
    for layer in range(layers):
        todo.append(("attn", layer, 3 * layer))
        todo.append(("inner", layer, 3 * layer + 1))
        todo.append(("outer", layer, 3 * layer + 2))
    low = None
    attn_out = None
    arrived = 0 if staged else total_chunks

    mid = None

    def compute():
        nonlocal current, other, low, attn_out, mid, head
        if not todo or todo[0][2] >= arrived:
            return
        kind, layer, _ = todo.pop(0)
        vec = table[layer]
        if kind == "attn":
            attn_out = attn_forward(pos_w, pos_g, current, other, seg, lab, vec, chunks[3 * layer])
            return
        h, n1, c1, q, kt, v, p, xoh, far_xoh = attn_out
        if kind == "inner":
            active, gp, gt, far_gt = inner_forward(pos_w, pos_g, h, vec, chunks[3 * layer + 1])
            mid = (active, gp, gt, move(far_gt, net["core"]), move(far_xoh, net["core"]))
            return
        active, gp, gt, far_gt, far_xoh = mid
        last = layer + 1 == layers
        current, low, *rest = outer_forward(
            pos_w, h, active, vec, chunks[3 * layer + 2], upstream if last else None
        )
        if last:
            head, rest = rest, (None, None)
        else:
            other = move(low, net["core"])
        kept[layer] = (n1, c1, q, kt, v, p, *rest, gp, xoh, gt, far_xoh, far_gt)

    head = None
    if not staged:
        upstream = move(upstream[0], net["swap"])
    if staged:
        sent, got = {}, {}
        zplan = {r: [(1, r + 2), (2, r + 3)] for r in range(-1, 2)}
        for r in range(2, 2 * len(groups)):
            g = (r + 6) // 2 + (r % 2)
            zplan[r] = [(1 + r % 2, g)]
        spread = [net["z2"], net["z1"]]
        for r in range(-LAG, total_chunks + LAG):
            inputs, plan = [], []
            sizes = [0, 0]
            use = lambda value: (inputs.append(value), len(inputs) - 1)[1]
            fresh = r + LAG < total_chunks
            if fresh:
                g, j = where_of[r + LAG]
                n = len(groups[g])
                mine, theirs = use(stage_z[g][0]), use(stage_z[g][1])
                for out, part in ((0, 1), (1, 0)):
                    for k, (source, slot) in enumerate(((mine, 0), (theirs, 0), (mine, 1), (theirs, 1))):
                        plan.append((out, k, source, (slot * n + j) * 2 + part, 1, True))
                    sizes[out] = ZS
            before = r - LAG
            home = 0 <= before < total_chunks
            if before >= -LAG and (r < total_chunks or home):
                sx, sy = use(sent[before][0]), use(sent[before][1])
                rx, ry = use(got[before][0]), use(got[before][1])
                first = ZS if before + LAG < total_chunks else 0
                if r < total_chunks:
                    for out, send, come in ((0, sy, ry), (1, sx, rx)):
                        plan.append((out, sizes[out], send, 0, ZS, False))
                        plan.append((out, sizes[out] + ZS, come, 0, ZS, False))
                        sizes[out] += 2 * ZS
                if home:
                    sizes.append(8 * ZS)
                    slot = 2
                    for at, (send, come) in enumerate(((sx, rx), (sy, ry))):
                        plan.append((slot, at * 4 * ZS, send, first, 2 * ZS, False))
                        plan.append((slot, at * 4 * ZS + 2 * ZS, come, first, 2 * ZS, False))
            live = [index for index, size in enumerate(sizes) if size]
            outs = copy_blocks(
                pos_g,
                [(live.index(each[0]),) + each[1:] for each in plan],
                inputs,
                [sizes[index] for index in live],
                "gather_round",
            )
            outs = dict(zip(live, outs))
            if 0 in outs:
                sent[r] = (outs[0], outs[1])
                got[r] = (move(outs[0], net["x"]), move(outs[1], net["y"]))
            core_pair = None
            if home:
                core_pair = (outs[2], move(outs[2], net["core"]))
            for stage, g in zplan.get(r, ()):
                if g < len(groups):
                    (start_z2 if stage == 2 else start_z1)(g)
            if spread and r >= 0:
                table = table + move(table, spread.pop(0))
            if r == total_chunks - 1:
                upstream = move(upstream[0], net["swap"])
            compute()
            ready = r + 1 - LAG
            state = (got.get(ready), core_pair, stage_z, current, other, attn_out, raw, table, upstream, mid)
            state = fence(state)
            if ready in got:
                got[ready] = state[0]
            if home:
                chunks.append(state[1])
                arrived += 1
            stage_z, current, other, attn_out, raw, table, upstream, mid = (list(state[2]),) + tuple(state[3:])
    while todo:
        compute()
    range_ids = jnp.arange(SEGS, dtype=jnp.int32)
    own = (small_own[1][None, :] == range_ids[:, None]).astype(F32)
    sums = jnp.dot(own, current, precision=lax.Precision.HIGHEST)
    pool_sums = sums
    counts = jnp.sum((lab[:, 0][None, :] == range_ids[:, None]).astype(F32), axis=1)
    loose = {}
    if staged:
        loose["hidden"] = move(low, net["swap"])
        loose["pool"] = pool_sums + move(pool_sums, net["core"])

    parts = []
    vectors = [None] * layers
    rounds = []
    ends = [], []
    table_stage = 1

    def side_work():
        step = len(rounds)
        last = total_chunks + 1
        if step == 2:
            loose["after"] = (loose["hidden"], loose["pool"])
        if step == 3:
            loose["pooled"] = move(loose.pop("pool") / counts[:, None], net["swap"])
            loose["after"] = (loose["pooled"],)
        if step == last + 1:
            loose["grad"] = move(loose.pop("grad"), net["swap"])
            loose["after"] = (loose["grad"],)
        if step == last + 2:
            done = list(finish(2, pos_g, ended()[0::3][::-1]))
            loose["outer"] = done
            loose["after"] = (done[0],)

    def ended():
        out = []
        for each in zip(*ends):
            if each[1][0] < len(rounds):
                out.append(tuple((own, rounds[s]["got_y"], at) for s, own, at in each))
        return out

    def settle(state):
        return fence(state)

    def advance(fresh, state):
        if not staged:
            if fresh is not None:
                parts.append(fresh)
            return state(()) if callable(state) else state
        s = len(rounds)
        past = rounds[s - 1] if s else {}
        sends, begin, b_rest, holds, lasts, totals, small = sum_round(
            fresh, past, loose.pop("small", (0, None)), tuple(loose.pop("after", ()))
        )
        now = {}
        for name, way, value in zip(
            ("got_x", "got_y", "got_z1", "got_z2"), ("x", "y", "z1", "z2"), sends
        ):
            if value is not None:
                now[name] = move(value[0], net[way])
        for name, value in (
            ("first", fresh and (fresh[0], fresh[2])),
            ("second", b_rest),
            ("third_a", holds[0]),
            ("third_b", holds[1]),
            ("fourth_a", lasts[0]),
            ("fourth_b", lasts[1]),
        ):
            if value is not None:
                now[name] = value
        for part, value in enumerate(totals):
            if value is not None:
                ends[part].append((s, value[0], begin + (2 if part and totals[0] is not None else 0)))
        sends = tuple(value[0] for value in sends if value is not None)
        if "vectors" in loose:
            small = loose.pop("vectors").reshape(-1, width)
            loose["small"] = (1, (small, move(small, net["core"])))
        elif small is not None:
            nonlocal table_stage
            table_stage += 1
            loose["small"] = (table_stage, small)
        side_work()
        if callable(state):
            state = state(sends)
        rounds.append(now)
        ready = s + 1 - LAG
        if ready < 0:
            return fence(state)
        rounds[ready], state = fence((rounds[ready], state))
        return state

    top = layers - 1
    ready = []
    dyl, dy, head_sums = head
    for layer in reversed(range(layers)):
        attn_bufs, inner_bufs, outer_bufs = chunks[3 * layer : 3 * layer + 3]
        n1, c1, q, kt, v, p, n2, c2, gp, xoh, gt, far_xoh, far_gt = kept[layer]
        got_dyl = move(dyl, net["core"])
        chain_args = (pos_w, dyl, dy, gp, n1, c1, table[layer], inner_bufs, outer_bufs, attn_bufs)
        if layer == top:
            outer_parts = settle(outer_grad(gt, far_gt, dyl, got_dyl))

            def first_round(sends):
                return chain_backward(*chain_args, after=sends)

            pack, da, do, sums = advance(outer_parts, first_round)
            got_pack = move(pack, net["core"])

            def second_round(sends):
                back, qsum = attn_backward(q, kt, v, p, do, after=sends)
                return back, qsum, got_pack, inner_grad(pos_g, xoh, far_xoh, pack, got_pack)

            back, qsum, got_pack, inner_parts = advance(None, second_round)
            ready.append(inner_parts)
            got_back = move(back, net["core"])
        else:
            pack, da, do, sums = chain_backward(*chain_args)
            outer_parts = outer_grad(gt, far_gt, dyl, got_dyl)
            state = advance(ready.pop(0), (pack, da, do, sums, outer_parts))
            pack, da, do, sums, outer_parts = state
            ready.append(outer_parts)
            got_pack = move(pack, net["core"])
            back, qsum = attn_backward(q, kt, v, p, do)
            inner_parts = inner_grad(pos_g, xoh, far_xoh, pack, got_pack)
            state = advance(ready.pop(0), (back, qsum, got_pack, inner_parts))
            back, qsum, got_pack, inner_parts = state
            ready.append(inner_parts)
            got_back = move(back, net["core"])
        below = None if layer == 0 else (kept[layer - 1][6], kept[layer - 1][7], table[layer - 1])
        total, vsum, *head = input_backward(pos_w, da, back, got_back, attn_bufs, below)
        attn_parts = attn_grad(pos_g, xoh, far_xoh, back, got_back, total, pack, got_pack)
        attn_parts, head, vsum = advance(ready.pop(0), (attn_parts, head, vsum))
        ready.append(attn_parts)
        vectors[layer] = (qsum, vsum, head_sums, sums)
        if layer:
            dyl, dy, head_sums = head
    grad = head[0]
    vectors = collect(vectors, 16)
    loose["grad"] = grad
    while ready:
        if len(ready) == 1:
            loose["vectors"] = vectors
        advance(ready.pop(0), None)
    results = []
    if staged:
        for _ in range(4 * LAG):
            advance(None, None)
        results = ended()

    if staged:
        stacked = []
        for kind, first in ((0, 2), (1, 1)):
            stacked += list(finish(kind, pos_g, results[first::3][::-1]))
        stacked += loose["outer"]
        hidden_out, pooled, tokens_grad = (loose[key] for key in ("hidden", "pooled", "grad"))
        vectors = loose["small"][1][0]
        got_vectors = rounds[-1]["got_y"][-1].astype(F32)
    else:
        collected = [None] * layers
        for place_at, layer in enumerate(reversed(range(layers))):
            outer_parts, inner_parts, attn_parts = parts[3 * place_at : 3 * place_at + 3]

            def spread(outs):
                a_keep, a_send, b_keep, b_send = outs
                a = jnp.stack([a_keep, a_send])
                b = jnp.stack([b_keep, b_send], axis=1)
                return jnp.stack([a, b], axis=2)

            def total(out):
                out = out.reshape(ZS * 2, 1, out.shape[2], out.shape[3])
                mine = (jnp.arange(2, dtype=jnp.int32) == core)[None, :, None, None]
                out = jnp.where(mine, out, jnp.zeros_like(out)).reshape(-1, out.shape[-1])
                out = lax.psum_scatter(out, "dp", scatter_dimension=0, tiled=True)
                return lax.psum(out.astype(F32), "seq")

            outer = spread(outer_parts).transpose(3, 0, 1, 2, 4, 5)
            outer = total(outer.reshape(ZS, 2, -1, width))
            inner = spread(inner_parts).transpose(3, 0, 4, 1, 2, 5)
            inner = total(inner.reshape(ZS, 2, inner.shape[2], -1))
            attn = spread(attn_parts)
            attn = attn.reshape(attn.shape[:5] + (2, width // 2)).transpose(2, 5, 3, 0, 4, 1, 6)
            attn = attn.reshape(4, ZS, 2, attn.shape[4], width)
            four = [total(attn[index]) for index in range(4)]
            collected[layer] = four + [inner, outer]
        stacked = [
            jnp.stack([collected[layer][member] for layer in range(layers)]) for member in range(6)
        ]
        hidden_out = move(low, net["swap"])
        pooled = move((pool_sums + move(pool_sums, net["core"])) / counts[:, None], net["swap"])
        tokens_grad = move(grad, net["swap"])
        vectors = lax.psum(vectors, AXES).reshape(-1, width)
        got_vectors = None
    own = own_vectors(dp[None], vectors, got_vectors, layers, small, hidden // count)
    return (
        hidden_out[None],
        pooled[None],
        tokens_grad.astype(F32)[None],
        stacked[0],
        stacked[1],
        stacked[2],
        stacked[3],
        own[QB],
        own[VB],
        own[OB],
        own[AG],
        own[AS],
        stacked[4],
        own[IB],
        stacked[5],
        own[UB],
        own[FG],
        own[FS],
    )


def solution(mesh):
    cube = P(None, "dp", None)
    flat = P(None, "dp")
    acts = P("dp", "seq", None)
    ids = P("dp", "seq")
    return jax.shard_map(
        functools.partial(body, build(mesh)),
        mesh=mesh,
        in_specs=(acts, ids, ids, cube, cube, cube, cube, flat, flat, flat, flat, flat, cube, flat, cube)
        + (flat, flat, flat, acts),
        out_specs=(acts, P("dp", None, None), acts, cube, cube, cube, cube)
        + (flat, flat, flat, flat, flat, cube, flat, cube, flat, flat, flat),
        check_vma=False,
    )
```
